32 devices in a mesh: dp: 16 (over z, y, x), tensor: 2 (over core).
Axes of the slice: x: 2, y: 2, z: 4, core: 2. Of those that a mesh axis runs over, the one named last changes fastest.
Arguments:
- tokens: bfloat16 [50176, 192], P(('dp', 'tensor')), may hold values from -6 to 6
- cotangent: bfloat16 [50176, 192], P(('dp', 'tensor')), may hold values from -6 to 6
- keep_mask: int32 [256, 196], P('dp'), may hold values from 0 to 1, as said below
- triple_weight: float32 [3, 192, 192], P(None, None, 'tensor'), may hold values from -0.4375 to 0.4375
- outward_weight: float32 [192, 192], P('tensor'), may hold values from -3.5 to 3.5
- widen_weight: float32 [192, 768], P(None, 'tensor'), may hold values from -0.4375 to 0.4375
- narrow_weight: float32 [768, 192], P('tensor'), may hold values from -0.21875 to 0.21875
- vectors: float32 [6, 192], replicated, may hold values from -0.5 to 2.26
- hidden_bias: float32 [768], P('tensor'), may hold values from -0.5 to 0.5
- head_params: float32 [4, 4], P(None, 'tensor'), may hold values from -1.5 to 1.5
- triple_moment: float32 [2, 55296], P('tensor', 'dp'), may hold values from -0.0009765625 to 0.0009765625
- triple_square: float32 [2, 55296], P('tensor', 'dp'), may hold values from 1.2e-07 to 4.7e-07
- outward_moment: float32 [2, 18432], P('tensor', 'dp'), may hold values from -0.0009765625 to 0.0009765625
- outward_square: float32 [2, 18432], P('tensor', 'dp'), may hold values from 1.2e-07 to 4.7e-07
- widen_moment: float32 [2, 73728], P('tensor', 'dp'), may hold values from -0.0009765625 to 0.0009765625
- widen_square: float32 [2, 73728], P('tensor', 'dp'), may hold values from 1.2e-07 to 4.7e-07
- narrow_moment: float32 [2, 73728], P('tensor', 'dp'), may hold values from -0.0009765625 to 0.0009765625
- narrow_square: float32 [2, 73728], P('tensor', 'dp'), may hold values from 1.2e-07 to 4.7e-07
- vector_moment: float32 [6, 192], replicated, may hold values from -0.0048828125 to 0.0048828125
- vector_square: float32 [6, 192], replicated, may hold values from 3.4e-06 to 1.35e-05
- hidden_moment: float32 [768], P('tensor'), may hold values from -0.0048828125 to 0.0048828125
- hidden_square: float32 [768], P('tensor'), may hold values from 6e-08 to 2.4e-07
- head_moment: float32 [4, 4], P(None, 'tensor'), may hold values from -0.0048828125 to 0.0048828125
- head_square: float32 [4, 4], P(None, 'tensor'), may hold values from 3.4e-06 to 1.35e-05
Outputs:
- result: float32 [50176, 192], P(('dp', 'tensor'))
- grad_input: float32 [50176, 192], P(('dp', 'tensor'))
- triple_moments: float32 [2, 55296], P('tensor', 'dp')
- triple_squares: float32 [2, 55296], P('tensor', 'dp')
- triple_updated: float32 [2, 55296], P('tensor', 'dp')
- outward_moments: float32 [2, 18432], P('tensor', 'dp')
- outward_squares: float32 [2, 18432], P('tensor', 'dp')
- outward_updated: float32 [2, 18432], P('tensor', 'dp')
- widen_moments: float32 [2, 73728], P('tensor', 'dp')
- widen_squares: float32 [2, 73728], P('tensor', 'dp')
- widen_updated: float32 [2, 73728], P('tensor', 'dp')
- narrow_moments: float32 [2, 73728], P('tensor', 'dp')
- narrow_squares: float32 [2, 73728], P('tensor', 'dp')
- narrow_updated: float32 [2, 73728], P('tensor', 'dp')
- vector_moments: float32 [6, 192], replicated
- vector_squares: float32 [6, 192], replicated
- vector_updated: float32 [6, 192], replicated
- hidden_moments: float32 [768], P('tensor')
- hidden_squares: float32 [768], P('tensor')
- hidden_updated: float32 [768], P('tensor')
- head_moments: float32 [4, 4], P(None, 'tensor')
- head_squares: float32 [4, 4], P(None, 'tensor')
- head_updated: float32 [4, 4], P(None, 'tensor')
- grad_norm: float32 [], replicated
The draws below stay inside these ranges and needn't reach their ends.
Inputs may be any that keep to these rules, and one draw needn't show every extreme that they name: `keep_mask`: each image keeps at least one of its 196 patches.
All inputs are finite; a program needn't handle non-finite values.
Results may differ from the reference program's by a relative error of at most 0.006.
The reference program's roundings to bfloat16 on the way count: a program that leaves them out, or rounds other values in their place, can miss the bound.
Values may be sent and summed in bfloat16 or wider, within the bound.
No kernel may reach another device: no remote copies, remote signals or barrier semaphores. Data moves between devices by JAX's collectives and lax.ppermute only.
A program may use at most 128 MiB of HBM per device.

```python
import math
import jax
import jax.numpy as jnp
from jax import lax

D = 192
HEADS = 4
HD = 48
FF = 768
GRID = 14
STEP = 10
PATCHES = 196
IMAGES = 256
TOKENS = 50176
N_TENSOR = 2


def draw_keep_mask(key, part):
    key = jax.random.fold_in(key, 11)
    roll_key, spot_key = jax.random.split(key)
    image = jnp.arange(IMAGES, dtype=jnp.int32)[:, None]
    level = 300 + 600 * image // max(IMAGES - 1, 1)
    roll = jax.random.randint(roll_key, (IMAGES, PATCHES), 0, 1000)
    spot = jax.random.randint(spot_key, (IMAGES, 1), 0, PATCHES)
    placing = jnp.arange(PATCHES, dtype=jnp.int32)[None, :]
    return ((roll < level) | (placing == spot)).astype(jnp.int32)


def draw_vectors(key, part):
    key = jax.random.fold_in(key, 23)
    gain_key, shift_key = jax.random.split(key)
    across = jnp.arange(D, dtype=jnp.float32) / D
    rising = jnp.exp(jnp.log(3.0) * (across - 0.5))
    gains = jax.random.uniform(gain_key, (2, D), jnp.float32, 0.7, 1.3) * rising
    shifts = jax.random.uniform(shift_key, (4, D), jnp.float32, -0.5, 0.5)
    return jnp.stack([gains[0], shifts[0], gains[1], shifts[1], shifts[2], shifts[3]])


def draw_head_params(key, part):
    key = jax.random.fold_in(key, 37)
    keys = jax.random.split(key, 3)
    reach = jax.random.uniform(keys[0], (2, HEADS), jnp.float32, -1.0, 1.0) * (2.0 / GRID)
    nearness = -jax.random.uniform(keys[1], (1, HEADS), jnp.float32, 1.0, 3.0) * (4.0 / (GRID * GRID))
    mixing = jax.random.uniform(keys[2], (1, HEADS), jnp.float32, -1.5, 1.5)
    return jnp.concatenate([reach, nearness, mixing])


def level_of(own_key, extent, shards, smallest, high):
    factor_of, own = 1.0, jax.random.fold_in(own_key, 6)
    for axis_at, blocks in shards:
        steps = jnp.exp(jax.random.uniform(jax.random.fold_in(own, axis_at), (blocks,), jnp.float32, smallest / len(shards), high / len(shards)))
        factor_of = factor_of * jnp.repeat(steps, extent[axis_at] // blocks).reshape([-1 if axis == axis_at else 1 for axis in range(len(extent))])
    return factor_of


def gaussian(rng, dims, spread, most, cuts=(), held_as=jnp.bfloat16):
    values = spread * jax.random.normal(rng, dims, jnp.float32)
    if cuts:
        values = values * level_of(rng, dims, cuts, -0.22, 0.18)
    return jnp.clip(values, -most, most).astype(held_as)


def setup_inputs(seed: int = 0) -> dict:
    seeds = jax.random.split(jax.random.key(seed), 25)
    return {
        "tokens": gaussian(seeds[0], (TOKENS, D), 1.0, 6.0, ((0, 32),)),
        "cotangent": gaussian(seeds[1], (TOKENS, D), 1.0, 6.0, ((0, 32),)),
        "keep_mask": draw_keep_mask(jax.random.fold_in(seeds[24], 71), 0),
        "triple_weight": gaussian(seeds[3], (3, D, HEADS * HD), D ** -0.5, 0.4375, ((2, 2),), jnp.float32),
        "outward_weight": gaussian(seeds[4], (HEADS * HD, D), (HEADS * HD * 4 // PATCHES) ** -0.5, 3.5, ((0, 2),), jnp.float32),
        "widen_weight": gaussian(seeds[5], (D, FF), D ** -0.5, 0.4375, ((1, 2),), jnp.float32),
        "narrow_weight": gaussian(seeds[6], (FF, D), FF ** -0.5, 0.21875, ((0, 2),), jnp.float32),
        "vectors": draw_vectors(jax.random.fold_in(seeds[24], 71), 0),
        "hidden_bias": jnp.clip(jax.random.uniform(seeds[8], (FF,), jnp.float32, -0.5, 0.5) * level_of(seeds[8], (FF,), ((0, 2),), -0.4, 0.0), -0.5, 0.5),
        "head_params": draw_head_params(jax.random.fold_in(seeds[24], 71), 0),
        "triple_moment": gaussian(seeds[10], (N_TENSOR, 3 * D * HEADS * HD // N_TENSOR), 0.00017, 0.0009765625, ((0, 2), (1, 16)), jnp.float32),
        "triple_square": jnp.clip(jnp.exp(math.log(4.700000033608376e-07) - 1.365241 * jax.random.uniform(seeds[11], (N_TENSOR, 3 * D * HEADS * HD // N_TENSOR), jnp.float32) ** level_of(seeds[11], (N_TENSOR, 3 * D * HEADS * HD // N_TENSOR), ((0, 2), (1, 16)), -0.2, 0.2)), 1.199999957179898e-07, 4.700000033608376e-07),
        "outward_moment": gaussian(seeds[12], (N_TENSOR, HEADS * HD * D // N_TENSOR), 0.00017, 0.0009765625, ((0, 2), (1, 16)), jnp.float32),
        "outward_square": jnp.clip(jnp.exp(math.log(4.700000033608376e-07) - 1.365241 * jax.random.uniform(seeds[13], (N_TENSOR, HEADS * HD * D // N_TENSOR), jnp.float32) ** level_of(seeds[13], (N_TENSOR, HEADS * HD * D // N_TENSOR), ((0, 2), (1, 16)), -0.2, 0.2)), 1.199999957179898e-07, 4.700000033608376e-07),
        "widen_moment": gaussian(seeds[14], (N_TENSOR, D * FF // N_TENSOR), 0.00017, 0.0009765625, ((0, 2), (1, 16)), jnp.float32),
        "widen_square": jnp.clip(jnp.exp(math.log(4.700000033608376e-07) - 1.365241 * jax.random.uniform(seeds[15], (N_TENSOR, D * FF // N_TENSOR), jnp.float32) ** level_of(seeds[15], (N_TENSOR, D * FF // N_TENSOR), ((0, 2), (1, 16)), -0.2, 0.2)), 1.199999957179898e-07, 4.700000033608376e-07),
        "narrow_moment": gaussian(seeds[16], (N_TENSOR, FF * D // N_TENSOR), 0.00017, 0.0009765625, ((0, 2), (1, 16)), jnp.float32),
        "narrow_square": jnp.clip(jnp.exp(math.log(4.700000033608376e-07) - 1.365241 * jax.random.uniform(seeds[17], (N_TENSOR, FF * D // N_TENSOR), jnp.float32) ** level_of(seeds[17], (N_TENSOR, FF * D // N_TENSOR), ((0, 2), (1, 16)), -0.2, 0.2)), 1.199999957179898e-07, 4.700000033608376e-07),
        "vector_moment": gaussian(seeds[18], (6, D), 0.0009, 0.0048828125, (), jnp.float32),
        "vector_square": jnp.clip(jnp.exp(jax.random.uniform(seeds[19], (6, D), jnp.float32, math.log(3.3999999686784577e-06), math.log(1.3500000022759195e-05))), 3.3999999686784577e-06, 1.3500000022759195e-05),
        "hidden_moment": gaussian(seeds[20], (FF,), 0.0009, 0.0048828125, ((0, 2),), jnp.float32),
        "hidden_square": jnp.clip(jnp.exp(math.log(2.399999914359796e-07) - 1.3862944 * jax.random.uniform(seeds[21], (FF,), jnp.float32) ** level_of(seeds[21], (FF,), ((0, 2),), -0.2, 0.2)), 5.99999978589949e-08, 2.399999914359796e-07),
        "head_moment": gaussian(seeds[22], (4, HEADS), 0.0009, 0.0048828125, ((1, 2),), jnp.float32),
        "head_square": jnp.clip(jnp.exp(math.log(1.3500000022759195e-05) - 1.37891426 * jax.random.uniform(seeds[23], (4, HEADS), jnp.float32) ** level_of(seeds[23], (4, HEADS), ((1, 2),), -0.2, 0.2)), 3.3999999686784577e-06, 1.3500000022759195e-05),
    }


EPS_NORM = 1e-06
NEG_FILL = -1e+30
CLIP_AT = 1.0
BETA_ONE = 0.9
BETA_TWO = 0.95
ADAM_EPS = 1e-08
RATES = (0.1, 0.5, 0.1, 0.05, 0.3, 0.1, 0.3)
DECAYS = (0.05, 0.05, 0.05, 0.05, 0.0, 0.0, 0.0)
PRECISE = lax.Precision.HIGHEST

@jax.custom_vjp
def low(v):
    return lax.optimization_barrier(v.astype(jnp.bfloat16)).astype(jnp.float32)

@jax.custom_vjp
def low_back(v):
    return v

def low_keep(v):
    return (low(v), None)

def low_pass(kept, grad):
    return (grad,)

def back_keep(v):
    return (v, None)

def back_low(kept, grad):
    return (low(grad),)
low.defvjp(low_keep, low_pass)
low_back.defvjp(back_keep, back_low)

def layer_norm(features, gains, shifts):
    average = lax.optimization_barrier(jnp.mean(features, axis=-1, keepdims=True))
    centred = features - average
    variance = lax.optimization_barrier(jnp.mean(centred * centred, axis=-1, keepdims=True))
    return centred * lax.rsqrt(variance + EPS_NORM) * gains + shifts

def offsets_table(patch_count, grid_side):
    placing = jnp.arange(patch_count, dtype=jnp.int32)
    column = (placing % grid_side).astype(jnp.float32)
    rowpos = (placing // grid_side).astype(jnp.float32)
    across = column[None, :] - column[:, None]
    upward = rowpos[None, :] - rowpos[:, None]
    return jnp.stack([across, upward, across * across + upward * upward])

def masked_softmax(scores, kept_keys):
    scores = jnp.where(kept_keys, scores, NEG_FILL)
    highest = lax.optimization_barrier(jnp.max(scores, axis=-1, keepdims=True))
    exponent = jnp.exp(scores - highest)
    return exponent / lax.optimization_barrier(jnp.sum(exponent, axis=-1, keepdims=True))

def exact_gelu(values_in):
    return jax.nn.gelu(values_in, approximate=False)

def forward(inputs, triple_weight, outward_weight, widen_weight, narrow_weight, vectors, hidden_bias, head_params, keep_mask):
    images = keep_mask.shape[0]
    kept_keys = (keep_mask > 0)[:, None, None, :]
    scaling = 1.0 / math.sqrt(HD)
    first_in = low(layer_norm(inputs, vectors[0], vectors[1]))
    projected = jnp.einsum('td,cdf->ctf', first_in, low(triple_weight), precision=PRECISE)
    projected = low_back(low(projected)).reshape(3, images, PATCHES, HEADS, HD)
    queries = projected[0]
    key_rows = projected[1]
    value_rows = projected[2]
    scores = low_back(jnp.einsum('iqhe,ikhe->ihqk', queries, key_rows, precision=PRECISE) * scaling)
    content = masked_softmax(scores, kept_keys)
    placed = jnp.einsum('ch,cqk->hqk', head_params[:3], offsets_table(PATCHES, GRID), precision=PRECISE)
    located = masked_softmax(placed[None], kept_keys)
    gating = jax.nn.sigmoid(head_params[3])[None, :, None, None]
    attention = low((1.0 - gating) * content + gating * located)
    mixture = jnp.einsum('ihqk,ikhe->iqhe', attention, value_rows, precision=PRECISE)
    mixture = low_back(low(mixture.reshape(images * PATCHES, HEADS * HD)))
    middle = inputs + low_back(jnp.dot(mixture, low(outward_weight), precision=PRECISE)) + vectors[4]
    second_in = low(layer_norm(middle, vectors[2], vectors[3]))
    before = low_back(jnp.dot(second_in, low(widen_weight), precision=PRECISE)) + hidden_bias
    activated = low(exact_gelu(before))
    return middle + low_back(jnp.dot(activated, low(narrow_weight), precision=PRECISE)) + vectors[5]

def flat_triple(matrix):
    return matrix.reshape(3, D, N_TENSOR, HEADS * HD // N_TENSOR).transpose(2, 0, 1, 3).reshape(N_TENSOR, -1)

def flat_rows(matrix):
    return matrix.reshape(N_TENSOR, -1)

def flat_columns(matrix):
    return matrix.reshape(D, N_TENSOR, FF // N_TENSOR).transpose(1, 0, 2).reshape(N_TENSOR, -1)

def keep_same(matrix):
    return matrix

def adam_update(weight, gradient, moment, squares, learn_rate, decay_rate):
    moment_new = BETA_ONE * moment + (1.0 - BETA_ONE) * gradient
    squares_new = BETA_TWO * squares + (1.0 - BETA_TWO) * gradient * gradient
    quotient = moment_new / (1.0 - BETA_ONE ** STEP) / (jnp.sqrt(squares_new / (1.0 - BETA_TWO ** STEP)) + ADAM_EPS)
    return (moment_new, squares_new, weight - learn_rate * (quotient + decay_rate * weight))

def reference(tokens, cotangent, keep_mask, triple_weight, outward_weight, widen_weight, narrow_weight, vectors, hidden_bias, head_params, triple_moment, triple_square, outward_moment, outward_square, widen_moment, widen_square, narrow_moment, narrow_square, vector_moment, vector_square, hidden_moment, hidden_square, head_moment, head_square):
    inputs = tokens.astype(jnp.float32)
    params = (triple_weight, outward_weight, widen_weight, narrow_weight, vectors, hidden_bias, head_params)

    def run_layer(inputs_in, *weights):
        return forward(inputs_in, *weights, keep_mask)
    result, pull_back = jax.vjp(run_layer, inputs, *params)
    row_weight = keep_mask.reshape(-1).astype(jnp.float32)[:, None]
    gradients = pull_back(cotangent.astype(jnp.float32) * row_weight)
    grad_input = gradients[0]
    grads_all = gradients[1:]
    grad_norm = jnp.sqrt(sum((jnp.sum(member * member) for member in grads_all)))
    factor = CLIP_AT / jnp.maximum(grad_norm, CLIP_AT)
    layouts = (flat_triple, flat_rows, flat_columns, flat_rows, keep_same, keep_same, keep_same)
    states = ((triple_moment, triple_square), (outward_moment, outward_square), (widen_moment, widen_square), (narrow_moment, narrow_square), (vector_moment, vector_square), (hidden_moment, hidden_square), (head_moment, head_square))
    updates = []
    for group_index in range(7):
        shaping = layouts[group_index]
        renewed = adam_update(shaping(params[group_index]), shaping(grads_all[group_index]) * factor, states[group_index][0], states[group_index][1], RATES[group_index], DECAYS[group_index])
        updates.extend(renewed)
    return (result, grad_input, updates[0], updates[1], updates[2], updates[3], updates[4], updates[5], updates[6], updates[7], updates[8], updates[9], updates[10], updates[11], updates[12], updates[13], updates[14], updates[15], updates[16], updates[17], updates[18], updates[19], updates[20], grad_norm)
```

```python
import math

import jax
import jax.numpy as jnp
from jax import lax
from jax.sharding import PartitionSpec as P

GRID = 14
STEP = 10


EPS_NORM = 1e-06
NEG_FILL = -1e30
CLIP_AT = 1.0
BETA_ONE = 0.9
BETA_TWO = 0.95
ADAM_EPS = 1e-08
RATES = (0.1, 0.5, 0.1, 0.05, 0.3, 0.1, 0.3)
DECAYS = (0.05, 0.05, 0.05, 0.05, 0.0, 0.0, 0.0)
PRECISE = lax.Precision.HIGHEST


def layer_norm(features, gains, shifts):
    average = jnp.mean(features, axis=-1, keepdims=True)
    centred = features - average
    variance = jnp.mean(centred * centred, axis=-1, keepdims=True)
    return centred * lax.rsqrt(variance + EPS_NORM) * gains + shifts


def offsets_table(patch_count, grid_side):
    placing = jnp.arange(patch_count, dtype=jnp.int32)
    column = (placing % grid_side).astype(jnp.float32)
    rowpos = (placing // grid_side).astype(jnp.float32)
    across = column[None, :] - column[:, None]
    upward = rowpos[None, :] - rowpos[:, None]
    return jnp.stack([across, upward, across * across + upward * upward])


def masked_softmax(scores, kept_keys):
    scores = jnp.where(kept_keys, scores, NEG_FILL)
    highest = jnp.max(scores, axis=-1, keepdims=True)
    exponent = jnp.exp(scores - highest)
    return exponent / jnp.sum(exponent, axis=-1, keepdims=True)


def softmax_back(probability, upstream):
    return probability * (upstream - jnp.sum(upstream * probability, axis=-1, keepdims=True))


def exact_gelu(values_in):
    return jax.nn.gelu(values_in, approximate=False)


def adam_update(weight, gradient, moment, squares, learn_rate, decay_rate):
    moment_new = BETA_ONE * moment + (1.0 - BETA_ONE) * gradient
    squares_new = BETA_TWO * squares + (1.0 - BETA_TWO) * gradient * gradient
    quotient = (
        moment_new
        / (1.0 - BETA_ONE**STEP)
        / (jnp.sqrt(squares_new / (1.0 - BETA_TWO**STEP)) + ADAM_EPS)
    )
    return (moment_new, squares_new, weight - learn_rate * (quotient + decay_rate * weight))

def layer_pass(
    tokens,
    cotangent,
    keep_here,
    triple_low,
    outward_low,
    widen_low,
    narrow_low,
    vectors,
    hidden_bias,
    head_params,
):
    images, patches = keep_here.shape
    heads = head_params.shape[1]
    width = triple_low.shape[2]
    head_size = width // heads
    all_rows = images * patches
    scaling = 1.0 / math.sqrt(head_size)
    kept_keys = (keep_here > 0)[:, None, None, :]
    row_kept = keep_here.reshape(-1).astype(jnp.float32)[:, None]
    offsets = offsets_table(patches, GRID)
    inputs = tokens.astype(jnp.float32)
    normed_one, norm_one_pull = jax.vjp(layer_norm, inputs, vectors[0], vectors[1])
    first_in = normed_one.astype(jnp.bfloat16)
    projected = jnp.einsum(
        "td,cdf->ctf", first_in, triple_low, preferred_element_type=jnp.float32
    ).astype(jnp.bfloat16)
    projected = projected.reshape(3, images, patches, heads, head_size)
    queries = projected[0]
    key_rows = projected[1]
    value_rows = projected[2]
    scores = (
        jnp.einsum("iqhe,ikhe->ihqk", queries, key_rows, preferred_element_type=jnp.float32)
        * scaling
    )
    content = masked_softmax(scores, kept_keys)
    placed = jnp.einsum("ch,cqk->hqk", head_params[:3], offsets, precision=PRECISE)
    located = masked_softmax(placed[None], kept_keys)
    gating_flat = jax.nn.sigmoid(head_params[3])
    gating = gating_flat[None, :, None, None]
    attention = ((1.0 - gating) * content + gating * located).astype(jnp.bfloat16)
    mixture = jnp.einsum(
        "ihqk,ikhe->iqhe", attention, value_rows, preferred_element_type=jnp.float32
    )
    mixture = mixture.astype(jnp.bfloat16).reshape(all_rows, width)
    middle = inputs + jnp.dot(mixture, outward_low, preferred_element_type=jnp.float32) + vectors[4]
    normed_two, norm_two_pull = jax.vjp(layer_norm, middle, vectors[2], vectors[3])
    second_in = normed_two.astype(jnp.bfloat16)
    before = jnp.dot(second_in, widen_low, preferred_element_type=jnp.float32) + hidden_bias
    activated, gelu_pull = jax.vjp(exact_gelu, before)
    activated_low = activated.astype(jnp.bfloat16)
    result = (
        middle + jnp.dot(activated_low, narrow_low, preferred_element_type=jnp.float32) + vectors[5]
    )
    incoming = cotangent.astype(jnp.float32) * row_kept
    incoming_low = incoming.astype(jnp.bfloat16)
    narrow_grad = jnp.einsum(
        "tf,td->fd", activated_low, incoming_low, preferred_element_type=jnp.float32
    )
    grad_activated = jnp.einsum(
        "td,fd->tf", incoming_low, narrow_low, preferred_element_type=jnp.float32
    )
    grad_before = gelu_pull(grad_activated)[0]
    hidden_grad = jnp.sum(grad_before, axis=0)
    grad_low = grad_before.astype(jnp.bfloat16)
    widen_grad = jnp.einsum("td,tf->df", second_in, grad_low, preferred_element_type=jnp.float32)
    grad_second = jnp.einsum("tf,df->td", grad_low, widen_low, preferred_element_type=jnp.float32)
    grad_middle, gain_two_grad, shift_two_grad = norm_two_pull(grad_second)
    grad_middle = grad_middle + incoming
    middle_low = grad_middle.astype(jnp.bfloat16)
    outward_grad = jnp.einsum("tf,td->fd", mixture, middle_low, preferred_element_type=jnp.float32)
    grad_mixture = jnp.einsum(
        "td,fd->tf", middle_low, outward_low, preferred_element_type=jnp.float32
    )
    grad_mixture = grad_mixture.astype(jnp.bfloat16).reshape(images, patches, heads, head_size)
    grad_attention = jnp.einsum(
        "iqhe,ikhe->ihqk", grad_mixture, value_rows, preferred_element_type=jnp.float32
    )
    grad_values = jnp.einsum(
        "ihqk,iqhe->ikhe", attention, grad_mixture, preferred_element_type=jnp.float32
    ).astype(jnp.bfloat16)
    gating_raw = jnp.sum(grad_attention * (located - content), axis=(0, 2, 3))
    mixing_grad = gating_raw * gating_flat * (1.0 - gating_flat)
    grad_scores = softmax_back(content, (1.0 - gating) * grad_attention).astype(jnp.bfloat16)
    grad_placed = jnp.sum(softmax_back(located, gating * grad_attention), axis=0)
    reach_grad = jnp.einsum("hqk,cqk->ch", grad_placed, offsets, precision=PRECISE)
    grad_queries = (
        jnp.einsum("ihqk,ikhe->iqhe", grad_scores, key_rows, preferred_element_type=jnp.float32)
        * scaling
    ).astype(jnp.bfloat16)
    grad_keys = (
        jnp.einsum("ihqk,iqhe->ikhe", grad_scores, queries, preferred_element_type=jnp.float32)
        * scaling
    ).astype(jnp.bfloat16)
    grad_projected = jnp.stack([grad_queries, grad_keys, grad_values]).reshape(3, all_rows, width)
    triple_grad = jnp.einsum(
        "td,ctf->cdf", first_in, grad_projected, preferred_element_type=jnp.float32
    )
    grad_first = jnp.einsum(
        "ctf,cdf->td", grad_projected, triple_low, preferred_element_type=jnp.float32
    )
    grad_inner, gain_one_grad, shift_one_grad = norm_one_pull(grad_first)
    grad_input = grad_inner + grad_middle
    early_vectors = jnp.stack(
        [gain_two_grad, shift_two_grad, jnp.sum(grad_middle, axis=0), jnp.sum(incoming, axis=0)]
    )
    late_vectors = jnp.stack([gain_one_grad, shift_one_grad])
    head_grads = jnp.concatenate([reach_grad, mixing_grad[None, :]])
    matrices = (triple_grad, outward_grad, widen_grad, narrow_grad)
    return (result, grad_input, matrices, hidden_grad, head_grads, early_vectors, late_vectors)


def as_chunks(flat, count, dtype):
    rows = -(-flat.shape[-1] // 128)
    flat = jnp.pad(flat.astype(dtype), ((0, 0), (0, 0), (0, rows * 128 - flat.shape[-1])))
    return flat.reshape(count, rows, 128)


def on_device(
    tokens,
    cotangent,
    keep_mask,
    triple_weight,
    outward_weight,
    widen_weight,
    narrow_weight,
    vectors,
    hidden_bias,
    head_params,
    triple_moment,
    triple_square,
    outward_moment,
    outward_square,
    widen_moment,
    widen_square,
    narrow_moment,
    narrow_square,
    vector_moment,
    vector_square,
    hidden_moment,
    hidden_square,
    head_moment,
    head_square,
):
    tensor_rank = lax.axis_index("tensor")
    data_rank = lax.axis_index("dp")
    data_count = lax.axis_size("dp")
    all_count = 2 * data_count
    axes = ("dp", "tensor")
    images = keep_mask.shape[0] // 2
    keep_here = lax.dynamic_slice_in_dim(keep_mask, tensor_rank * images, images)

    def widened(own, axis):
        other = lax.ppermute(own, "tensor", [(0, 1), (1, 0)])
        return jnp.concatenate([own, other], axis=axis)

    def in_order(halves):
        return jnp.where(tensor_rank == 0, halves, jnp.stack([halves[1], halves[0]]))

    result, grad_input, matrices, hidden_grad, head_grads, early_vectors, late_vectors = layer_pass(
        tokens,
        cotangent,
        keep_here,
        widened(triple_weight.astype(jnp.bfloat16), 2),
        widened(outward_weight.astype(jnp.bfloat16), 0),
        widened(widen_weight.astype(jnp.bfloat16), 1),
        widened(narrow_weight.astype(jnp.bfloat16), 0),
        vectors,
        widened(hidden_bias, 0),
        widened(head_params, 1),
    )
    triple_grad, outward_grad, widen_grad, narrow_grad = matrices
    depth = triple_weight.shape[1]
    half = triple_weight.shape[2]
    half_hidden = widen_weight.shape[1]

    def split(halves):
        return in_order(halves.reshape(2, -1)).reshape(2, data_count, -1).transpose(1, 0, 2)

    triple_parts = split(triple_grad.reshape(3, depth, 2, half).transpose(2, 0, 1, 3))
    outward_parts = split(outward_grad)
    widen_parts = split(widen_grad.reshape(depth, 2, half_hidden).transpose(1, 0, 2))
    narrow_parts = split(narrow_grad)
    hidden_parts = jnp.broadcast_to(
        in_order(hidden_grad.reshape(2, -1))[None], (data_count, 2, half_hidden)
    )
    early_parts = jnp.broadcast_to(
        early_vectors.reshape(1, 1, -1), (data_count, 2, early_vectors.size)
    )
    early_sent = jnp.concatenate(
        [widen_parts, narrow_parts, outward_parts, early_parts, hidden_parts], axis=2
    )
    sizes = [member.shape[2] for member in (widen_parts, narrow_parts, outward_parts, early_parts)]
    early_got = lax.all_to_all(
        as_chunks(early_sent, all_count, jnp.bfloat16), axes, 0, 0, tiled=False
    )
    early_sum = jnp.sum(early_got.astype(jnp.float32), axis=0).reshape(-1)
    cuts = [sum(sizes[:at]) for at in range(5)]
    widen_share, narrow_share, outward_share, early_total = (
        early_sum[cuts[at] : cuts[at + 1]] for at in range(4)
    )
    bias_here = early_sum[cuts[4] : cuts[4] + half_hidden]
    early_total = early_total.reshape(4, depth)
    triple_got = lax.all_to_all(
        as_chunks(triple_parts, all_count, jnp.bfloat16), axes, 0, 0, tiled=False
    )
    triple_share = jnp.sum(triple_got.astype(jnp.float32), axis=0).reshape(-1)
    triple_share = triple_share[: triple_parts.shape[2]]
    shares = [triple_share, outward_share, widen_share, narrow_share]
    partial_squares = sum((jnp.sum(member * member) for member in shares)) + jnp.where(
        data_rank == 0, jnp.sum(bias_here * bias_here), 0.0
    )
    heads_here = head_params.shape[1]
    late_heads = in_order(head_grads.reshape(4, 2, heads_here).transpose(1, 0, 2))
    late_sent = jnp.concatenate(
        [late_vectors.reshape(-1), late_heads.reshape(-1), partial_squares[None]]
    )
    late_chunks = as_chunks(
        jnp.broadcast_to(late_sent, (data_count, 2, late_sent.shape[0])), all_count, jnp.float32
    )
    late_got = lax.all_to_all(late_chunks, axes, 0, 0, tiled=False)
    late_sum = jnp.sum(late_got, axis=0).reshape(-1)
    late_total = late_sum[: 2 * depth].reshape(2, depth)
    heads_total = late_sum[2 * depth : 2 * depth + 8 * heads_here].reshape(2, 4, heads_here)
    vector_sum = jnp.concatenate([late_total, early_total])
    squares_all = (
        late_sum[2 * depth + 8 * heads_here]
        + jnp.sum(vector_sum * vector_sum)
        + jnp.sum(heads_total * heads_total)
    )
    head_here = jnp.where(tensor_rank == 0, heads_total[0], heads_total[1])
    grad_norm = jnp.sqrt(squares_all)
    factor = CLIP_AT / jnp.maximum(grad_norm, CLIP_AT)
    masters = (triple_weight, outward_weight, widen_weight, narrow_weight)
    states = (
        (triple_moment, triple_square),
        (outward_moment, outward_square),
        (widen_moment, widen_square),
        (narrow_moment, narrow_square),
    )
    updates = []
    for group_index in range(4):
        master = masters[group_index].reshape(-1)
        share_len = shares[group_index].shape[0]
        weight_share = lax.dynamic_slice_in_dim(master, data_rank * share_len, share_len)
        renewed = adam_update(
            weight_share,
            shares[group_index] * factor,
            states[group_index][0].reshape(-1),
            states[group_index][1].reshape(-1),
            RATES[group_index],
            DECAYS[group_index],
        )
        updates.extend([member.reshape(1, -1) for member in renewed])
    small_params = (vectors, hidden_bias, head_params)
    small_grads = (vector_sum, bias_here, head_here)
    small_states = (
        (vector_moment, vector_square),
        (hidden_moment, hidden_square),
        (head_moment, head_square),
    )
    for small_index in range(3):
        renewed = adam_update(
            small_params[small_index],
            small_grads[small_index] * factor,
            small_states[small_index][0],
            small_states[small_index][1],
            RATES[4 + small_index],
            DECAYS[4 + small_index],
        )
        updates.extend(renewed)
    return (
        result,
        grad_input,
        updates[0],
        updates[1],
        updates[2],
        updates[3],
        updates[4],
        updates[5],
        updates[6],
        updates[7],
        updates[8],
        updates[9],
        updates[10],
        updates[11],
        updates[12],
        updates[13],
        updates[14],
        updates[15],
        updates[16],
        updates[17],
        updates[18],
        updates[19],
        updates[20],
        grad_norm,
    )


def solution(mesh):
    return jax.shard_map(
        on_device,
        mesh=mesh,
        in_specs=(
            P(("dp", "tensor"), None),
            P(("dp", "tensor"), None),
            P("dp", None),
            P(None, None, "tensor"),
            P("tensor", None),
            P(None, "tensor"),
            P("tensor", None),
            P(),
            P("tensor"),
            P(None, "tensor"),
            P("tensor", "dp"),
            P("tensor", "dp"),
            P("tensor", "dp"),
            P("tensor", "dp"),
            P("tensor", "dp"),
            P("tensor", "dp"),
            P("tensor", "dp"),
            P("tensor", "dp"),
            P(),
            P(),
            P("tensor"),
            P("tensor"),
            P(None, "tensor"),
            P(None, "tensor"),
        ),
        out_specs=(
            P(("dp", "tensor"), None),
            P(("dp", "tensor"), None),
            P("tensor", "dp"),
            P("tensor", "dp"),
            P("tensor", "dp"),
            P("tensor", "dp"),
            P("tensor", "dp"),
            P("tensor", "dp"),
            P("tensor", "dp"),
            P("tensor", "dp"),
            P("tensor", "dp"),
            P("tensor", "dp"),
            P("tensor", "dp"),
            P("tensor", "dp"),
            P(),
            P(),
            P(),
            P("tensor"),
            P("tensor"),
            P("tensor"),
            P(None, "tensor"),
            P(None, "tensor"),
            P(None, "tensor"),
            P(),
        ),
        check_vma=False,
    )
```

```python
import functools
import math

import jax
import jax.numpy as jnp
from jax import lax
from jax.experimental import pallas as pl
from jax.experimental.pallas import tpu as pltpu
from jax.sharding import PartitionSpec as P

GRID = 14
STEP = 10
EPS_NORM = 1e-06
CLIP_AT = 1.0
BETA_ONE = 0.9
BETA_TWO = 0.95
ADAM_EPS = 1e-08
RATES = (0.1, 0.5, 0.1, 0.05, 0.3, 0.1, 0.3)
DECAYS = (0.05, 0.05, 0.05, 0.05, 0.0, 0.0, 0.0)
LOG2E = 1.4426950408889634
BF = jnp.bfloat16
F32 = jnp.float32
VMEM_LIMIT = 56 * 1024 * 1024
EARLY_ROWS = 96
LATE_ROWS = 32
VM = pl.BlockSpec(memory_space=pltpu.VMEM)
SM = pl.BlockSpec(memory_space=pltpu.SMEM)
PARAMS = pltpu.CompilerParams(vmem_limit_bytes=VMEM_LIMIT)


def sds(*dims, dtype=F32):
    return jax.ShapeDtypeStruct(dims, dtype)


def nn(a, b):
    return lax.dot_general(a, b, (((1,), (0,)), ((), ())), preferred_element_type=F32)


def nt(a, b):
    return lax.dot_general(a, b, (((1,), (1,)), ((), ())), preferred_element_type=F32)


def norm_parts(v):
    width = v.shape[-1]
    average = jnp.sum(v, axis=-1, keepdims=True) * (1.0 / width)
    centred = v - average
    variance = jnp.sum(centred * centred, axis=-1, keepdims=True) * (1.0 / width)
    spread = lax.rsqrt(variance + EPS_NORM)
    return centred * spread, spread


def norm_back(e, n, spread):
    width = e.shape[-1]
    mean_e = jnp.sum(e, axis=-1, keepdims=True) * (1.0 / width)
    mean_en = jnp.sum(e * n, axis=-1, keepdims=True) * (1.0 / width)
    return spread * (e - mean_e - n * mean_en)


def fold(v):
    rows = v.shape[0]
    return jnp.sum(v.reshape(rows // 8, 8, v.shape[1]), axis=0)


def gelu_parts(x):
    y = jnp.abs(x)
    t = 1.0 / (1.0 + (0.3275911 / math.sqrt(2.0)) * y)
    e = jnp.exp2((x * x) * (-0.5 * LOG2E))
    poly = t * (
        0.5 * 0.254829592
        + t
        * (
            0.5 * -0.284496736
            + t * (0.5 * 1.421413741 + t * (0.5 * -1.453152027 + t * (0.5 * 1.061405429)))
        )
    )
    q = poly * e
    phi = jnp.where(x > 0.0, 1.0 - q, q)
    return x * phi, phi + x * (e * (1.0 / math.sqrt(2.0 * math.pi)))


def offsets(kp, qp):
    def side(dim):
        at = lax.broadcasted_iota(jnp.int32, (kp, qp), dim).astype(F32)
        row = jnp.floor((at + 0.5) * (1.0 / GRID))
        return at - row * GRID, row

    kc, kr = side(0)
    qc, qr = side(1)
    a = kc - qc
    b = kr - qr
    return a, b, a * a + b * b


def head_mask(rows, width, hd, h):
    lane = lax.broadcasted_iota(jnp.int32, (rows, width), 1)
    return ((lane >= h * hd) & (lane < (h + 1) * hd)).astype(BF)


def gate_of(hp_ref, h, lanes):
    return 1.0 / (1.0 + jnp.exp(-jnp.broadcast_to(hp_ref[h : h + 1, 3:4], (1, lanes))))


def fill_places(place, hp_ref, heads, kp, qp):
    parts = offsets(kp, qp)
    for h in range(heads):
        place[h] = LOG2E * sum(
            jnp.broadcast_to(hp_ref[h : h + 1, at : at + 1], (kp, qp)) * parts[at] for at in range(3)
        )
    return parts


def pair_rows(j, patches, kp):
    return pl.ds(pl.multiple_of(j * 2 * patches, 8), patches + kp + (-(patches + kp)) % 8)


def put_planes(ref, value):
    width = value.shape[1]
    ref[0] = value[:, :128]
    ref[1, :, 0 : width - 128] = value[:, 128:]


def even_odd_tiles(ref, start, pairs):
    even = [ref[at, pl.ds(start, pairs, stride=2), :] for at in range(2)]
    odd = [ref[at, pl.ds(start + 1, pairs, stride=2), :] for at in range(2)]
    return (
        even[0],
        jnp.concatenate([even[1][:, :64], odd[0][:, :64]], axis=1),
        jnp.concatenate([odd[0][:, 64:], odd[1][:, :64]], axis=1),
    )


def four_row_tiles(ref, plane, start, groups):
    r = [ref[plane, pl.ds(start + at, groups, stride=4), :] for at in range(4)]
    return (
        jnp.concatenate([r[0][:, :96], r[1][:, :32]], axis=1),
        jnp.concatenate([r[1][:, 32:96], r[2][:, :64]], axis=1),
        jnp.concatenate([r[2][:, 64:96], r[3][:, :96]], axis=1),
    )


def pack_kernel(tri_ref, out_ref, wid_ref, nar_ref, hb_ref, hp_ref, pack_ref):
    depth, wide = wid_ref.shape
    pack_ref[0:depth, :] = wid_ref[...].astype(BF)
    pack_ref[depth : 2 * depth, :] = nar_ref[...].astype(BF)
    pack_ref[2 * depth : 3 * depth, :] = jnp.concatenate(
        [tri_ref[0], tri_ref[1], tri_ref[2], out_ref[...].T], axis=1
    ).astype(BF)
    heads_here = hp_ref.shape[0]
    hp = jnp.concatenate([hp_ref[...], jnp.zeros((heads_here, wide - 4), F32)], axis=1)
    left = jnp.concatenate([hb_ref[...], hp], axis=0)
    parts = []
    for _ in range(3):
        part = left.astype(BF).astype(F32)
        parts.append(part)
        left = left - part
    parts.append(jnp.zeros((16 - 3 * (1 + heads_here), wide), F32))
    pack_ref[3 * depth : 3 * depth + 16, :] = jnp.concatenate(parts, axis=0).astype(BF)


def run_pack(tri, out, wid, nar_t, hb, hp_t):
    depth, wide = wid.shape
    return pl.pallas_call(
        pack_kernel,
        out_shape=sds(3 * depth + 16, wide, dtype=BF),
        in_specs=[VM] * 6,
        out_specs=VM,
        compiler_params=PARAMS,
        name="pack_weights",
    )(tri, out, wid, nar_t, hb, hp_t)


def forward_kernel(*refs, patches, heads, data_count):
    (rank_ref, tok_ref, cot_ref, keep_ref, own_ref, oth_ref, vec_ref) = refs[:7]
    (res_ref, gm_ref, first_ref, q_ref, k_ref, v_ref, kt_ref, dm_ref, lse_ref, hp_ref) = refs[7:17]
    outs = refs[17:22] if not data_count else refs[17:18]
    (xs, cs, wq, wk, wv, wkt, wvt, wo, wi, wn, place, act_s, low_s, inc_s, sec_s, og) = refs[
        17 + len(outs) : 33 + len(outs)
    ]
    if data_count:
        nar_p, out_p, wid_g, vec_g, hid_g, tmp = refs[33 + len(outs) :]
    else:
        nar_g, wid_g, out_g, vec_g, hid_g = outs
    images, kp, _ = keep_ref.shape
    qp = lse_ref.shape[2]
    rows = images * patches
    width = tok_ref.shape[1]
    hd = width // heads
    half = width // 2
    half_heads = heads // 2
    wide = own_ref.shape[1]
    c_scale = LOG2E / math.sqrt(hd)
    xs[pl.ds(0, rows), :] = tok_ref[...].astype(F32)
    cs[pl.ds(0, rows), :] = cot_ref[...].astype(F32)
    xs[pl.ds(rows, 16), :] = jnp.zeros((16, width), F32)
    cs[pl.ds(rows, 16), :] = jnp.zeros((16, width), F32)
    wi[:, pl.ds(0, wide)] = own_ref[0:width, :]
    wi[:, pl.ds(wide, wide)] = oth_ref[0:width, :]
    wn[:, pl.ds(0, wide)] = own_ref[width : 2 * width, :]
    wn[:, pl.ds(wide, wide)] = oth_ref[width : 2 * width, :]
    own_tri = own_ref[2 * width : 3 * width, :]
    oth_tri = oth_ref[2 * width : 3 * width, :]
    for at, w in enumerate((wq, wk, wv, wo)):
        span = slice(at * half, (at + 1) * half)
        w[...] = jnp.concatenate([own_tri[:, span], oth_tri[:, span]], axis=1)
    wkt[...] = wk[...].T
    wvt[...] = wv[...].T
    small = []
    for ref in (own_ref, oth_ref):
        tail = ref[3 * width : 3 * width + 16, :].astype(F32)
        step = 1 + half_heads
        small.append(tail[0:step] + tail[step : 2 * step] + tail[2 * step : 3 * step])
    hb = jnp.concatenate([member[0:1] for member in small], axis=1)
    hp_ref[...] = jnp.concatenate(
        [member[1:, :128] for member in small] + [jnp.zeros((8 - heads, 128), F32)], axis=0
    )
    fill_places(place, hp_ref, heads, kp, qp)
    hid_g[...] = jnp.zeros_like(hid_g)
    vec_g[...] = jnp.zeros_like(vec_g)
    og[...] = jnp.zeros_like(og)
    v = [vec_ref[at : at + 1, :] for at in range(6)]

    def image(i, x, cot):
        keep = keep_ref[i]
        bias = (keep - 1.0) * 1e30
        bias2 = jnp.concatenate([bias, bias], axis=1)
        keep_w = jnp.concatenate([keep, keep[:, : width - 128]], axis=1)
        n1, _ = norm_parts(x)
        first = (n1 * v[0] + v[1]).astype(BF)
        first_ref[i] = first
        first_q = jnp.concatenate([first, jnp.zeros((qp - kp, width), BF)], axis=0)
        queries = nn(first_q, wq[...]).astype(BF)
        keys = nn(first, wk[...]).astype(BF)
        values = nn(first, wv[...]).astype(BF)
        keys_t = nt(wkt[...], first_q).astype(BF)
        values_t = nt(wvt[...], first_q).astype(BF)
        q_ref[i] = queries
        k_ref[i] = keys
        v_ref[i] = values
        kt_ref[i] = keys_t
        mixed = []
        for h in range(heads):
            gate = gate_of(hp_ref, h, qp)
            qm = queries * head_mask(qp, width, hd, h)
            s = nt(keys, qm) * c_scale + bias2
            m = jnp.max(s, axis=0, keepdims=True)
            e = jnp.exp2(s - m)
            z = jnp.sum(e, axis=0, keepdims=True)
            p = place[h] + bias2
            pm = jnp.max(p, axis=0, keepdims=True)
            pe = jnp.exp2(p - pm)
            pz = jnp.sum(pe, axis=0, keepdims=True)
            att = (e * ((1.0 - gate) / z) + pe * (gate / pz)).astype(BF)
            lse_ref[i, h : h + 1, :] = m + jnp.log2(z / (1.0 - gate))
            lse_ref[i, heads + h : heads + h + 1, :] = pm + jnp.log2(pz / gate)
            att_k = jnp.concatenate([att, jnp.zeros((qp - kp, qp), BF)], axis=0)
            mixed.append(nn(values_t[h * hd : (h + 1) * hd, :], att_k))
        mix_t = jnp.concatenate(mixed, axis=0)
        mix = mix_t.T[:kp].astype(BF)
        middle = x + nt(mix, wo[...]) + v[4]
        n2, spread2 = norm_parts(middle)
        second = (n2 * v[2] + v[3]).astype(BF)
        before = nn(second, wi[...]) + hb
        gelu, slope = gelu_parts(before)
        act = gelu.astype(BF)
        result = middle + nt(act, wn[...]) + v[5]
        incoming = cot * keep_w
        inc_low = incoming.astype(BF)
        grad_before = nn(inc_low, wn[...]) * slope
        hid_g[...] += fold(grad_before)
        grad_low = grad_before.astype(BF)
        grad_second = nt(grad_low, wi[...])
        grad_middle = incoming + norm_back(grad_second * v[2], n2, spread2)
        vec_g[0] += fold(grad_second * n2)
        vec_g[1] += fold(grad_second)
        vec_g[2] += fold(grad_middle)
        vec_g[3] += fold(incoming)
        gm_ref[i] = grad_middle
        mid_low = jnp.concatenate(
            [grad_middle.astype(BF), jnp.zeros((qp - kp, width), BF)], axis=0
        )
        dm_ref[i] = nn(mid_low, wo[...]).astype(BF)
        og[...] += nn(mix_t.astype(BF), mid_low)
        span = pl.ds(pl.multiple_of(i * kp, 16), kp)
        act_s[span, :] = act
        low_s[span, :] = grad_low
        inc_s[span, :] = inc_low
        sec_s[span, :] = second
        return result

    def body(j, carry):
        x = xs[pair_rows(j, patches, kp), :]
        cot = cs[pair_rows(j, patches, kp), :]
        done = [
            image(
                2 * j + at,
                x[at * patches : at * patches + kp],
                cot[at * patches : at * patches + kp],
            )
            for at in range(2)
        ]
        res_ref[pl.ds(pl.multiple_of(j * 2 * patches, 8), 2 * patches), :] = jnp.concatenate(
            [member[:patches] for member in done], axis=0
        )
        return carry

    lax.fori_loop(0, images // 2, body, 0)
    narrow = nn(inc_s[...].T, act_s[...]).T
    wid_g[...] = nn(sec_s[...].T, low_s[...])
    if not data_count:
        nar_g[...] = narrow
        out_g[...] = og[...]
        return
    put_planes(nar_p, narrow)
    put_planes(out_p, og[...])
    chunk_ref = outs[0]
    tmp[...] = jnp.zeros_like(tmp)
    early = jnp.sum(vec_g[...], axis=1)
    hidden = jnp.sum(hid_g[...], axis=0, keepdims=True)
    rest = width - 128
    wp, np_, op = width // data_count, wide // data_count // 2, half // data_count // 2
    at = 3 * (wp + np_ + op)
    for side in range(2):
        for slot in range(2):
            tmp[2 * side + slot, at : at + 4, :] = early[:, :128]
            tmp[2 * side + slot, at + 4 : at + 8, 0:rest] = early[:, 128:]
            for k in range(3):
                lane = side * wide + 128 * k
                tmp[2 * side + slot, at + 8 + k : at + 9 + k, :] = hidden[:, lane : lane + 128]
    rank = rank_ref[0]
    for r in range(data_count):
        for side in range(2):
            piece = tmp.at[2 * side + r % 2]
            for k in range(3):
                lane = side * wide + 128 * k
                piece[k * wp : (k + 1) * wp, :] = wid_g[r * wp : (r + 1) * wp, lane : lane + 128]
            base = 3 * wp
            tiles = even_odd_tiles(nar_p, side * wide + 2 * np_ * r, np_)
            for k in range(3):
                piece[base + k * np_ : base + (k + 1) * np_, :] = tiles[k]
            base += 3 * np_
            tiles = even_odd_tiles(out_p, side * half + 2 * op * r, op)
            for k in range(3):
                piece[base + k * op : base + (k + 1) * op, :] = tiles[k]
            chunk_ref[2 * r + (rank + side) % 2] = piece[...].astype(BF)


def run_forward(rank, tok, cot, keep, own, oth, vec, heads, patches, data_count):
    images, kp, _ = keep.shape
    qp = -(-patches // 128) * 128
    width = tok.shape[1]
    hidden = 2 * own.shape[1]
    rows = images * patches
    full = images * kp
    sums = [
        sds(hidden, width),
        sds(width, hidden),
        sds(width, width),
        sds(4, 8, width),
        sds(8, hidden),
    ]
    scratch = [
        pltpu.VMEM((rows + 16, width), F32),
        pltpu.VMEM((rows + 16, width), F32),
        *[pltpu.VMEM((width, width), BF)] * 6,
        pltpu.VMEM((width, hidden), BF),
        pltpu.VMEM((width, hidden), BF),
        pltpu.VMEM((heads, kp, qp), F32),
        pltpu.VMEM((full, hidden), BF),
        pltpu.VMEM((full, hidden), BF),
        pltpu.VMEM((full, width), BF),
        pltpu.VMEM((full, width), BF),
        pltpu.VMEM((width, width), F32),
    ]
    if data_count:
        outs = [sds(2 * data_count, EARLY_ROWS, 128, dtype=BF)]
        scratch += [pltpu.VMEM((2, hidden, 128), F32), pltpu.VMEM((2, width, 128), F32)]
        scratch += [pltpu.VMEM(sums[at].shape, F32) for at in (1, 3, 4)]
        scratch.append(pltpu.VMEM((4, EARLY_ROWS, 128), F32))
    else:
        outs = sums
    return pl.pallas_call(
        functools.partial(forward_kernel, patches=patches, heads=heads, data_count=data_count),
        out_shape=(
            sds(rows, width),
            sds(images, kp, width),
            sds(images, kp, width, dtype=BF),
            sds(images, qp, width, dtype=BF),
            sds(images, kp, width, dtype=BF),
            sds(images, kp, width, dtype=BF),
            sds(images, width, qp, dtype=BF),
            sds(images, qp, width, dtype=BF),
            sds(images, 2 * heads, qp),
            sds(8, 128),
            *outs,
        ),
        in_specs=[SM] + [VM] * 6,
        out_specs=(VM,) * (10 + len(outs)),
        scratch_shapes=scratch,
        compiler_params=PARAMS,
        name="forward",
    )(rank, tok, cot, keep, own, oth, vec)


def backward_kernel(*refs, patches, heads, data_count):
    (rank_ref, hp_ref, keep_ref, first_ref, q_ref, k_ref, v_ref, kt_ref, dm_ref, lse_ref) = refs[:10]
    (dp_ref, head_ref, tri_out) = refs[10:13]
    (place, place_g, gate_g, first_s, dp_s) = refs[13:18]
    images, kp, _ = keep_ref.shape
    qp = lse_ref.shape[2]
    width = first_ref.shape[2]
    hd = width // heads
    half = width // 2
    c_scale = LOG2E / math.sqrt(hd)
    back_scale = 1.0 / math.sqrt(hd)
    parts = fill_places(place, hp_ref, heads, kp, qp)
    place_g[...] = jnp.zeros_like(place_g)
    gate_g[...] = jnp.zeros_like(gate_g)

    def body(i, carry):
        keep = keep_ref[i]
        bias = (keep - 1.0) * 1e30
        bias2 = jnp.concatenate([bias, bias], axis=1)
        queries, keys, values, keys_t, dm = q_ref[i], k_ref[i], v_ref[i], kt_ref[i], dm_ref[i]
        dq_t = []
        dk = jnp.zeros((kp, width), F32)
        dv = jnp.zeros((kp, width), F32)
        for h in range(heads):
            gate = gate_of(hp_ref, h, qp)
            mask = head_mask(qp, width, hd, h)
            qm = queries * mask
            dmm = dm * mask
            s = nt(keys, qm) * c_scale + bias2
            c = jnp.exp2(s - lse_ref[i, h : h + 1, :])
            l = jnp.exp2(place[h] + bias2 - lse_ref[i, heads + h : heads + h + 1, :])
            att = (c + l).astype(BF)
            da = nt(values, dmm)
            pc = c * da
            pt = l * da
            rc = jnp.sum(pc, axis=0, keepdims=True) / (1.0 - gate)
            rl = jnp.sum(pt, axis=0, keepdims=True) / gate
            ds = (pc - c * rc).astype(BF)
            place_g[h] += pt - l * rl
            gate_g[h : h + 1, :] += rl - rc
            dv = dv + nn(att, dmm)
            dk = dk + nn(ds, qm)
            ds_k = jnp.concatenate([ds, jnp.zeros((qp - kp, qp), BF)], axis=0)
            dq_t.append(nn(keys_t[h * hd : (h + 1) * hd, :], ds_k))
        dq = (jnp.concatenate(dq_t, axis=0) * back_scale).T[:kp]
        span = pl.ds(pl.multiple_of(i * kp, 16), kp)
        for at, d in enumerate((dq, dk * back_scale, dv)):
            low = d.astype(BF)
            dp_ref[at, i] = low
            dp_s[at, span, :] = low
        first_s[span, :] = first_ref[i]
        return carry

    lax.fori_loop(0, images, body, 0)
    first_t = first_s[...].T
    for at in range(3):
        part = nn(first_t, dp_s[at])
        rows = pl.ds(at * width, width)
        if data_count:
            tri_s = refs[18]
            tri_s[0, rows, 0:half] = part[:, :half]
            tri_s[1, rows, 0:half] = part[:, half:]
        else:
            tri_out[rows, :] = part
    rank = rank_ref[0]
    lane = lax.broadcasted_iota(jnp.int32, (1, 128), 1)
    row = jnp.zeros((1, 128), F32)
    half_heads = heads // 2
    for h in range(heads):
        base = ((rank + h // half_heads) % 2) * (4 * half_heads) + h % half_heads
        g = place_g[h]
        for at in range(3):
            row = row + jnp.where(lane == base + at * half_heads, jnp.sum(g * parts[at]), 0.0)
        gate = gate_of(hp_ref, h, 128)
        total = jnp.sum(gate_g[h : h + 1, :])
        row = row + jnp.where(lane == base + 3 * half_heads, total * gate * (1.0 - gate), 0.0)
    head_ref[...] = row
    if not data_count:
        return
    tmp = refs[19]
    tmp[...] = jnp.zeros_like(tmp)
    groups = 3 * width // data_count // 4
    for r in range(data_count):
        for side in range(2):
            piece = tmp.at[2 * side + r % 2]
            tiles = four_row_tiles(tri_s, side, 4 * groups * r, groups)
            for k in range(3):
                piece[k * groups : (k + 1) * groups, :] = tiles[k]
            tri_out[2 * r + (rank + side) % 2] = piece[...].astype(BF)


def run_backward(rank, hp, keep, first, q, k, v, kt, dm, lse, heads, patches, data_count):
    images, kp, _ = keep.shape
    qp = lse.shape[2]
    width = first.shape[2]
    full = images * kp
    scratch = [
        pltpu.VMEM((heads, kp, qp), F32),
        pltpu.VMEM((heads, kp, qp), F32),
        pltpu.VMEM((8, qp), F32),
        pltpu.VMEM((full, width), BF),
        pltpu.VMEM((3, full, width), BF),
    ]
    if data_count:
        last = sds(2 * data_count, LATE_ROWS, 128, dtype=BF)
        scratch += [pltpu.VMEM((2, 3 * width, 128), F32), pltpu.VMEM((4, LATE_ROWS, 128), F32)]
    else:
        last = sds(3 * width, width)
    return pl.pallas_call(
        functools.partial(backward_kernel, patches=patches, heads=heads, data_count=data_count),
        out_shape=(sds(3, images, kp, width, dtype=BF), sds(1, 128), last),
        in_specs=[SM] + [VM] * 9,
        out_specs=(VM,) * 3,
        scratch_shapes=scratch,
        compiler_params=PARAMS,
        name="attention_backward",
    )(rank, hp, keep, first, q, k, v, kt, dm, lse)


def input_kernel(tok_ref, gm_ref, dp_ref, own_ref, oth_ref, vec_ref, gi_ref, vec_out, xs, w, vec_g, *, patches):
    images, kp, width = gm_ref.shape
    rows = images * patches
    half = width // 2
    xs[pl.ds(0, rows), :] = tok_ref[...].astype(F32)
    xs[pl.ds(rows, 16), :] = jnp.zeros((16, width), F32)
    own_tri = own_ref[2 * width : 3 * width, :]
    oth_tri = oth_ref[2 * width : 3 * width, :]
    for at in range(3):
        span = slice(at * half, (at + 1) * half)
        w[at] = jnp.concatenate([own_tri[:, span], oth_tri[:, span]], axis=1)
    vec_g[...] = jnp.zeros_like(vec_g)
    gain = vec_ref[0:1, :]

    def image(i, x):
        n1, spread = norm_parts(x)
        g = nt(dp_ref[0, i], w[0]) + nt(dp_ref[1, i], w[1]) + nt(dp_ref[2, i], w[2])
        vec_g[0] += fold(g * n1)
        vec_g[1] += fold(g)
        return gm_ref[i] + norm_back(g * gain, n1, spread)

    def body(j, carry):
        x = xs[pair_rows(j, patches, kp), :]
        done = [image(2 * j + at, x[at * patches : at * patches + kp]) for at in range(2)]
        gi_ref[pl.ds(pl.multiple_of(j * 2 * patches, 8), 2 * patches), :] = jnp.concatenate(
            [member[:patches] for member in done], axis=0
        )
        return carry

    lax.fori_loop(0, images // 2, body, 0)
    vec_out[...] = jnp.sum(vec_g[...], axis=1)


def run_input(tok, gm, dp, own, oth, vec, patches):
    images, kp, width = gm.shape
    rows = images * patches
    return pl.pallas_call(
        functools.partial(input_kernel, patches=patches),
        out_shape=(sds(rows, width), sds(2, width)),
        in_specs=[VM] * 6,
        out_specs=(VM,) * 2,
        scratch_shapes=[
            pltpu.VMEM((rows + 16, width), F32),
            pltpu.VMEM((3, width, width), BF),
            pltpu.VMEM((2, 8, width), F32),
        ],
        compiler_params=PARAMS,
        name="input_gradient",
    )(tok, gm, dp, own, oth, vec)


def spread_rows(flat_ref, from_ref, base, blocks):
    for p in range(blocks):
        for k in range(3):
            at = base + k * blocks + p
            tile = 128 * (3 * p + k)
            flat_ref[0:1, tile : tile + 128] = from_ref[at : at + 1, :]


def pick_rows(ref, start, count, flip=False):
    total = ref.shape[1] if flip else ref.shape[0]
    row = lax.broadcasted_iota(jnp.int32, (count, total), 0) + start
    col = lax.broadcasted_iota(jnp.int32, (count, total), 1)
    chosen = (row == col).astype(F32)
    return lax.dot_general(
        chosen,
        ref[...],
        (((1,), (1 if flip else 0,)), ((), ())),
        preferred_element_type=F32,
        precision=lax.Precision.HIGHEST,
    )


def early_kernel(rank_ref, got_ref, tri_ref, out_ref, wid_ref, nar_ref, *refs, data_count):
    (wid_f, nar_f, out_f, wt_f, wo_f, ww_f, wn_f, vec_ref, hid_ref, sq_ref, tot, st, so, sw, sn) = refs
    width, wide = wid_ref.shape
    half = out_ref.shape[0]
    wp, np_, op = width // data_count, wide // data_count // 2, half // data_count // 2
    tot[...] = jnp.sum(got_ref[...].astype(F32), axis=0)
    spread_rows(wid_f, tot, 0, wp)
    spread_rows(nar_f, tot, 3 * wp, np_)
    spread_rows(out_f, tot, 3 * (wp + np_), op)
    at = 3 * (wp + np_ + op)
    vec_ref[...] = jnp.concatenate([tot[at : at + 4, :], tot[at + 4 : at + 8, : width - 128]], axis=1)
    hid = [tot[at + 8 + k : at + 9 + k, :] for k in range(3)]
    hid_ref[...] = jnp.concatenate(hid, axis=1)
    matrices = tot[0:at, :]
    squares = jnp.sum(matrices * matrices)
    hidden = sum(jnp.sum(member * member) for member in hid)
    squares = squares + jnp.where(rank_ref[1] == 0, hidden, 0.0)
    sq_ref[...] = jnp.full((1, 128), squares)
    data_rank = rank_ref[1]
    groups = tri_ref.shape[0] // data_count // 4
    st[0, :, 0 : tri_ref.shape[1]] = pick_rows(tri_ref, data_rank * 4 * groups, 4 * groups)
    put_planes(so, pick_rows(out_ref, data_rank * 2 * op, 2 * op))
    sw[...] = pick_rows(wid_ref, data_rank * wp, wp)
    put_planes(sn, pick_rows(nar_ref, data_rank * 2 * np_, 2 * np_, flip=True))
    tiles = four_row_tiles(st, 0, 0, groups)
    for p in range(groups):
        for k in range(3):
            tile = 128 * (3 * p + k)
            wt_f[0:1, tile : tile + 128] = tiles[k][p : p + 1, :]
    for ref, flat, pairs in ((so, wo_f, op), (sn, wn_f, np_)):
        tiles = even_odd_tiles(ref, 0, pairs)
        for p in range(pairs):
            for k in range(3):
                tile = 128 * (3 * p + k)
                flat[0:1, tile : tile + 128] = tiles[k][p : p + 1, :]
    for p in range(wp):
        ww_f[0:1, wide * p : wide * (p + 1)] = sw[p : p + 1, :]


def run_early(rank, got, tri, out, wid, nar_t, data_count):
    width, wide = wid.shape
    half = out.shape[0]
    lens = [member.size // data_count for member in (wid, nar_t, out, tri, out, wid, nar_t)]
    share = [member.shape[0] // data_count for member in (tri, out, wid)]
    return pl.pallas_call(
        functools.partial(early_kernel, data_count=data_count),
        out_shape=(
            *[sds(1, member) for member in lens],
            sds(4, width),
            sds(1, wide),
            sds(1, 128),
        ),
        in_specs=[SM] + [VM] * 5,
        out_specs=(VM,) * 10,
        scratch_shapes=[
            pltpu.VMEM((EARLY_ROWS, 128), F32),
            pltpu.VMEM((1, share[0], 128), F32),
            pltpu.VMEM((2, share[1], 128), F32),
            pltpu.VMEM((share[2], wide), F32),
            pltpu.VMEM((2, wide // data_count, 128), F32),
        ],
        compiler_params=PARAMS,
        name="early_sums",
    )(rank, got, tri, out, wid, nar_t)


def late_kernel(got_ref, vec_ref, head_ref, sq_ref, tri_f, pay_ref, tot, *, blocks):
    width = vec_ref.shape[1]
    tot[...] = jnp.sum(got_ref[...].astype(F32), axis=0)
    spread_rows(tri_f, tot, 0, blocks)
    matrix = tot[0 : 3 * blocks, :]
    squares = sq_ref[...] + jnp.sum(matrix * matrix)
    lane = lax.broadcasted_iota(jnp.int32, (1, 128), 1)
    tails = jnp.concatenate([vec_ref[0:1, 128:], vec_ref[1:2, 128:]], axis=1)
    payload = jnp.concatenate(
        [vec_ref[:, :128], tails, jnp.where(lane == 127, squares, head_ref[...])], axis=0
    )
    pay_ref[...] = jnp.broadcast_to(payload[None], pay_ref.shape)


def run_late(got, vec, head, sq, blocks):
    count = got.shape[0]
    return pl.pallas_call(
        functools.partial(late_kernel, blocks=blocks),
        out_shape=(sds(1, 3 * 128 * blocks), sds(count, 4, 128)),
        in_specs=[VM] * 4,
        out_specs=(VM,) * 2,
        scratch_shapes=[pltpu.VMEM((LATE_ROWS, 128), F32)],
        compiler_params=PARAMS,
        name="late_sums",
    )(got, vec, head, sq)


def adam_parts(weight, gradient, moment, squares, rate, decay):
    moment_new = BETA_ONE * moment + (1.0 - BETA_ONE) * gradient
    squares_new = BETA_TWO * squares + (1.0 - BETA_TWO) * gradient * gradient
    quotient = (moment_new / (1.0 - BETA_ONE**STEP)) / (
        jnp.sqrt(squares_new / (1.0 - BETA_TWO**STEP)) + ADAM_EPS
    )
    return moment_new, squares_new, weight - rate * (quotient + decay * weight)


def adam_kernel(rank_ref, got_ref, early_ref, hid_ref, hp_ref, vec_ref, hb_ref, *refs):
    grads = refs[0:4]
    weights = refs[4:8]
    states = refs[8:22]
    outs = refs[22:43]
    norm_ref = refs[43]
    width = vec_ref.shape[1]
    half_heads = hp_ref.shape[0]
    tail = width - 128
    total = jnp.sum(got_ref[...], axis=0)
    late = jnp.concatenate(
        [
            total[0:2, :],
            jnp.concatenate([total[2:3, :tail], total[2:3, tail : 2 * tail]], axis=0),
        ],
        axis=1,
    )
    vector = jnp.concatenate([late, early_ref[...]], axis=0)
    lane = lax.broadcasted_iota(jnp.int32, (1, 128), 1)
    heads_row = jnp.where(lane < 8 * half_heads, total[3:4, :], 0.0)
    squares = (
        jnp.sum(jnp.where(lane == 127, total[3:4, :], 0.0))
        + jnp.sum(vector * vector)
        + jnp.sum(heads_row * heads_row)
    )
    norm = jnp.sqrt(jnp.full((1, 128), squares))
    norm_ref[...] = norm[:, 0:1]
    factor = (CLIP_AT / jnp.maximum(norm, CLIP_AT))[:, 0:1]
    span = 4 * half_heads
    mine = jnp.where(rank_ref[0] == 0, heads_row[:, :span], heads_row[:, span : 2 * span])
    head = jnp.concatenate(
        [
            jnp.concatenate(
                [mine[:, c * half_heads + h : c * half_heads + h + 1] for c in range(4)], axis=1
            )
            for h in range(half_heads)
        ],
        axis=0,
    )
    given = [ref[...] for ref in grads] + [vector, hid_ref[...], head]
    held = [ref[...] for ref in weights] + [vec_ref[...], hb_ref[...], hp_ref[...]]
    for at in range(7):
        renewed = adam_parts(
            held[at],
            given[at] * factor,
            states[2 * at][...],
            states[2 * at + 1][...],
            RATES[at],
            DECAYS[at],
        )
        for step in range(3):
            outs[3 * at + step][...] = renewed[step]


def run_adam(rank, got, early, hid, hp_t, vec, hb, grads, weights, states):
    shapes = []
    for at in range(7):
        shapes += [sds(*states[2 * at].shape)] * 3
    return pl.pallas_call(
        adam_kernel,
        out_shape=(*shapes, sds(1, 1)),
        in_specs=[SM] + [VM] * (6 + 4 + 4 + 14),
        out_specs=(VM,) * 22,
        compiler_params=PARAMS,
        name="adam",
    )(rank, got, early, hid, hp_t, vec, hb, *grads, *weights, *states)


def plain_chunks(halves, tensor_rank, data_count, rows):
    parts = []
    for own_first in halves:
        turned = jnp.where(
            tensor_rank == 0, own_first, jnp.concatenate([own_first[1:], own_first[:1]])
        )
        parts.append(turned.reshape(2, data_count, -1).transpose(1, 0, 2))
    flat = jnp.concatenate(parts, axis=2)
    flat = jnp.pad(flat, ((0, 0), (0, 0), (0, rows * 128 - flat.shape[2])))
    return flat.astype(BF).reshape(2 * data_count, rows, 128)


def on_device(
    tokens,
    cotangent,
    keep_mask,
    triple_weight,
    outward_weight,
    widen_weight,
    narrow_weight,
    vectors,
    hidden_bias,
    head_params,
    triple_moment,
    triple_square,
    outward_moment,
    outward_square,
    widen_moment,
    widen_square,
    narrow_moment,
    narrow_square,
    vector_moment,
    vector_square,
    hidden_moment,
    hidden_square,
    head_moment,
    head_square,
):
    tensor_rank = lax.axis_index("tensor")
    data_rank = lax.axis_index("dp")
    data_count = lax.axis_size("dp")
    axes = ("dp", "tensor")
    images = keep_mask.shape[0] // 2
    patches = keep_mask.shape[1]
    heads = 2 * head_params.shape[1]
    depth = triple_weight.shape[1]
    half = triple_weight.shape[2]
    wide = widen_weight.shape[1]
    rank = jnp.stack([tensor_rank, data_rank]).astype(jnp.int32)
    triple_rows = triple_weight.reshape(3 * depth, half)
    narrow_t = narrow_weight.T
    bias_row = hidden_bias.reshape(1, wide)
    head_t = head_params.T
    fast = (
        depth == 192
        and half == 96
        and wide == 384
        and depth % data_count == 0
        and wide % (2 * data_count) == 0
        and half % (2 * data_count) == 0
        and 3 * depth % (4 * data_count) == 0
    )
    chunked = data_count if fast else 0

    own = run_pack(triple_weight, outward_weight, widen_weight, narrow_t, bias_row, head_t)
    other = lax.ppermute(own, "tensor", [(0, 1), (1, 0)])
    keep_here = lax.dynamic_slice_in_dim(keep_mask, tensor_rank * images, images).astype(F32)
    kp = -(-patches // 16) * 16
    keep_cols = jnp.broadcast_to(
        jnp.pad(keep_here, ((0, 0), (0, kp - patches)))[:, :, None], (images, kp, 128)
    )
    result, grad_middle, first, q, k, v, kt, dm, lse, hp, *sums = run_forward(
        rank, tokens, cotangent, keep_cols, own, other, vectors, heads, patches, chunked
    )
    if fast:
        early_sent = sums[0]
    else:
        nar_g, wid_g, out_g, vec_g, hid_g = sums
        early_mine = jnp.sum(vec_g, axis=1).reshape(1, 1, -1)
        early_sent = plain_chunks(
            [
                wid_g.reshape(depth, 2, wide).transpose(1, 0, 2).reshape(2, -1),
                nar_g.reshape(2, -1),
                out_g.reshape(2, -1),
                jnp.broadcast_to(early_mine, (2, data_count, early_mine.size)).reshape(2, -1),
                jnp.broadcast_to(
                    jnp.sum(hid_g, axis=0).reshape(2, 1, wide), (2, data_count, wide)
                ).reshape(2, -1),
            ],
            tensor_rank,
            data_count,
            EARLY_ROWS,
        )
    early_got = lax.all_to_all(early_sent, axes, 0, 0, tiled=False)
    dp, head_row, late = run_backward(
        rank, hp, keep_cols, first, q, k, v, kt, dm, lse, heads, patches, chunked
    )
    if not fast:
        halves = late.reshape(3 * depth, 2, half).transpose(1, 0, 2).reshape(2, -1)
        late = plain_chunks([halves], tensor_rank, data_count, LATE_ROWS)
    late_got = lax.all_to_all(late, axes, 0, 0, tiled=False)
    grad_input, late_vec = run_input(tokens, grad_middle, dp, own, other, vectors, patches)
    if fast:
        wid_f, nar_f, out_f, wt_f, wo_f, ww_f, wn_f, early_vec, hid, sq = run_early(
            rank, early_got, triple_rows, outward_weight, widen_weight, narrow_t, data_count
        )
        tri_f, payload = run_late(late_got, late_vec, head_row, sq, 3 * depth // data_count // 4)
    else:
        early_sum = jnp.sum(early_got.astype(F32), axis=0).reshape(1, -1)
        masters = (widen_weight, narrow_weight, outward_weight)
        sizes = [member.size // data_count for member in masters] + [4 * depth, wide]
        cuts = [sum(sizes[:at]) for at in range(6)]
        wid_f, nar_f, out_f, early_vec, hid = (
            early_sum[:, cuts[at] : cuts[at + 1]] for at in range(5)
        )
        early_vec = early_vec.reshape(4, depth)
        share = triple_rows.size // data_count
        tri_f = jnp.sum(late_got.astype(F32), axis=0).reshape(1, -1)[:, :share]

        def weight_share(member):
            length = member.size // data_count
            return lax.dynamic_slice_in_dim(member.reshape(1, -1), data_rank * length, length, 1)

        ww_f, wn_f, wo_f = (weight_share(member) for member in masters)
        wt_f = weight_share(triple_rows)
        squares = sum(jnp.sum(member * member) for member in (wid_f, nar_f, out_f, tri_f))
        squares = squares + jnp.where(data_rank == 0, jnp.sum(hid * hid), 0.0)
        lane = lax.broadcasted_iota(jnp.int32, (1, 128), 1)
        payload = jnp.concatenate(
            [
                late_vec[:, :128],
                late_vec[:, 128:].reshape(1, 128),
                jnp.where(lane == 127, squares, head_row),
            ]
        )
        payload = jnp.broadcast_to(payload[None], (2 * data_count, 4, 128))
    last_got = lax.all_to_all(payload, axes, 0, 0, tiled=False)
    renewed = run_adam(
        rank,
        last_got,
        early_vec,
        hid,
        head_t,
        vectors,
        bias_row,
        (tri_f, out_f, wid_f, nar_f),
        (wt_f, wo_f, ww_f, wn_f),
        (
            triple_moment,
            triple_square,
            outward_moment,
            outward_square,
            widen_moment,
            widen_square,
            narrow_moment,
            narrow_square,
            vector_moment,
            vector_square,
            hidden_moment.reshape(1, wide),
            hidden_square.reshape(1, wide),
            head_moment.T,
            head_square.T,
        ),
    )
    hidden_new = [member.reshape(wide) for member in renewed[15:18]]
    head_new = [member.T for member in renewed[18:21]]
    return (result, grad_input, *renewed[:15], *hidden_new, *head_new, renewed[21].reshape(()))


def solution(mesh):
    return jax.shard_map(
        on_device,
        mesh=mesh,
        in_specs=(
            P(("dp", "tensor"), None),
            P(("dp", "tensor"), None),
            P("dp", None),
            P(None, None, "tensor"),
            P("tensor", None),
            P(None, "tensor"),
            P("tensor", None),
            P(),
            P("tensor"),
            P(None, "tensor"),
            P("tensor", "dp"),
            P("tensor", "dp"),
            P("tensor", "dp"),
            P("tensor", "dp"),
            P("tensor", "dp"),
            P("tensor", "dp"),
            P("tensor", "dp"),
            P("tensor", "dp"),
            P(),
            P(),
            P("tensor"),
            P("tensor"),
            P(None, "tensor"),
            P(None, "tensor"),
        ),
        out_specs=(
            P(("dp", "tensor"), None),
            P(("dp", "tensor"), None),
            P("tensor", "dp"),
            P("tensor", "dp"),
            P("tensor", "dp"),
            P("tensor", "dp"),
            P("tensor", "dp"),
            P("tensor", "dp"),
            P("tensor", "dp"),
            P("tensor", "dp"),
            P("tensor", "dp"),
            P("tensor", "dp"),
            P("tensor", "dp"),
            P("tensor", "dp"),
            P(),
            P(),
            P(),
            P("tensor"),
            P("tensor"),
            P("tensor"),
            P(None, "tensor"),
            P(None, "tensor"),
            P(None, "tensor"),
            P(),
        ),
        check_vma=False,
    )
```

```python
import functools
import math

import jax
import jax.numpy as jnp
from jax import lax
from jax.experimental import pallas as pl
from jax.experimental.pallas import tpu as pltpu
from jax.sharding import PartitionSpec as P

GRID = 14
STEP = 10
EPS_NORM = 1e-06
CLIP_AT = 1.0
BETA_ONE = 0.9
BETA_TWO = 0.95
ADAM_EPS = 1e-08
RATES = (0.1, 0.5, 0.1, 0.05, 0.3, 0.1, 0.3)
DECAYS = (0.05, 0.05, 0.05, 0.05, 0.0, 0.0, 0.0)
LOG2E = 1.4426950408889634
BF = jnp.bfloat16
F32 = jnp.float32
VMEM_LIMIT = 56 * 1024 * 1024
EARLY_ROWS = 96
LATE_ROWS = 32
CHUNK_ROWS = EARLY_ROWS + LATE_ROWS
PAIR = 2
VM = pl.BlockSpec(memory_space=pltpu.VMEM)
SM = pl.BlockSpec(memory_space=pltpu.SMEM)
PARAMS = pltpu.CompilerParams(vmem_limit_bytes=VMEM_LIMIT)


def sds(*dims, dtype=F32):
    return jax.ShapeDtypeStruct(dims, dtype)


def nn(a, b):
    return lax.dot_general(a, b, (((1,), (0,)), ((), ())), preferred_element_type=F32)


def nt(a, b):
    return lax.dot_general(a, b, (((1,), (1,)), ((), ())), preferred_element_type=F32)


def norm_parts(v):
    width = v.shape[-1]
    average = jnp.sum(v, axis=-1, keepdims=True) * (1.0 / width)
    centred = v - average
    variance = jnp.sum(centred * centred, axis=-1, keepdims=True) * (1.0 / width)
    spread = lax.rsqrt(variance + EPS_NORM)
    return centred * spread, spread


def norm_back(e, n, spread):
    width = e.shape[-1]
    mean_e = jnp.sum(e, axis=-1, keepdims=True) * (1.0 / width)
    mean_en = jnp.sum(e * n, axis=-1, keepdims=True) * (1.0 / width)
    return spread * (e - mean_e - n * mean_en)


def fold(v):
    rows = v.shape[0]
    return jnp.sum(v.reshape(rows // 8, 8, v.shape[1]), axis=0)


def gelu_parts(x):
    phi = 0.5 + 0.5 * lax.erf(x * math.sqrt(0.5))
    density = jnp.exp2((x * x) * (-0.5 * LOG2E)) * (1.0 / math.sqrt(2.0 * math.pi))
    return x * phi, phi + x * density


def places(count, lanes, dim):
    at = lax.broadcasted_iota(jnp.int32, (count, lanes), dim).astype(F32)
    row = jnp.floor((at + 0.5) * (1.0 / GRID))
    return at - row * GRID, row


def offsets(kp, qp):
    kc, kr = places(kp, qp, 0)
    qc, qr = places(kp, qp, 1)
    a = kc - qc
    b = kr - qr
    return a, b, a * a + b * b


def head_mask(rows, width, hd, h):
    lane = lax.broadcasted_iota(jnp.int32, (rows, width), 1)
    return ((lane >= h * hd) & (lane < (h + 1) * hd)).astype(BF)


def gate_of(hp_ref, h, lanes):
    return 1.0 / (1.0 + jnp.exp(-jnp.broadcast_to(hp_ref[h : h + 1, 3:4], (1, lanes))))


def bf_parts(value, count=3):
    parts = []
    for _ in range(count):
        part = value.astype(BF).astype(F32)
        parts.append(part)
        value = value - part
    return parts


def key_operand(kp):
    kc, kr = places(kp, 128, 0)
    lane = lax.broadcasted_iota(jnp.int32, (kp, 128), 1)
    value = jnp.where(lane < 3, kc, jnp.where(lane < 6, kr, jnp.where(lane < 9, kc * kc, kr * kr)))
    return jnp.where(lane < 12, value, 0.0).astype(BF)


def query_operand(hp_ref, h, qp):
    p = [LOG2E * jnp.broadcast_to(hp_ref[h : h + 1, at : at + 1], (16, qp)) for at in range(3)]
    qc, qr = places(16, qp, 1)
    row = lax.broadcasted_iota(jnp.int32, (16, qp), 0)
    value = jnp.where(row < 3, p[0] - 2.0 * p[2] * qc, jnp.where(row < 6, p[1] - 2.0 * p[2] * qr, p[2]))
    parts = bf_parts(value)
    place = row - 3 * ((row >= 3).astype(jnp.int32) + (row >= 6) + (row >= 9))
    value = jnp.where(place == 0, parts[0], jnp.where(place == 1, parts[1], parts[2]))
    return jnp.where(row < 12, value, jnp.where(row == 12, 1.0, 0.0)).astype(BF)


STRIP = 16


def interleave(*streams):
    streams = [member for member in streams if member is not None]
    while streams:
        alive = []
        for member in streams:
            try:
                next(member)
                alive.append(member)
            except StopIteration:
                pass
        streams = alive


def slow(stream, count):
    for _ in range(count):
        yield
        try:
            next(stream)
        except StopIteration:
            return


def cut(value, r):
    return value[r * STRIP : (r + 1) * STRIP]


def rows_of(r):
    return pl.ds(r * STRIP, STRIP)


def put_planes(ref, value):
    width = value.shape[1]
    ref[0] = value[:, :128]
    ref[1, :, 0 : width - 128] = value[:, 128:]


def even_odd_tiles(ref, start, pairs):
    even = [ref[at, pl.ds(start, pairs, stride=2), :] for at in range(2)]
    odd = [ref[at, pl.ds(start + 1, pairs, stride=2), :] for at in range(2)]
    return (
        even[0],
        jnp.concatenate([even[1][:, :64], odd[0][:, :64]], axis=1),
        jnp.concatenate([odd[0][:, 64:], odd[1][:, :64]], axis=1),
    )


def four_row_tiles(ref, plane, start, groups):
    r = [ref[plane, pl.ds(start + at, groups, stride=4), :] for at in range(4)]
    return (
        jnp.concatenate([r[0][:, :96], r[1][:, :32]], axis=1),
        jnp.concatenate([r[1][:, 32:96], r[2][:, :64]], axis=1),
        jnp.concatenate([r[2][:, 64:96], r[3][:, :96]], axis=1),
    )


def pack_kernel(tri_ref, out_ref, wid_ref, nar_ref, hb_ref, hp_ref, pack_ref):
    depth, wide = wid_ref.shape
    pack_ref[0:depth, :] = wid_ref[...].astype(BF)
    pack_ref[depth : 2 * depth, :] = nar_ref[...].astype(BF)
    pack_ref[2 * depth : 3 * depth, :] = jnp.concatenate(
        [tri_ref[0], tri_ref[1], tri_ref[2], out_ref[...].T], axis=1
    ).astype(BF)
    heads_here = hp_ref.shape[0]
    hp = jnp.concatenate([hp_ref[...], jnp.zeros((heads_here, wide - 4), F32)], axis=1)
    left = jnp.concatenate([hb_ref[...].reshape(1, wide), hp], axis=0)
    parts = []
    for _ in range(3):
        part = left.astype(BF).astype(F32)
        parts.append(part)
        left = left - part
    parts.append(jnp.zeros((16 - 3 * (1 + heads_here), wide), F32))
    pack_ref[3 * depth : 3 * depth + 16, :] = jnp.concatenate(parts, axis=0).astype(BF)


def run_pack(tri, out, wid, nar_t, hb, hp_t):
    depth, wide = wid.shape
    return pl.pallas_call(
        pack_kernel,
        out_shape=sds(3 * depth + 16, wide, dtype=BF),
        in_specs=[VM] * 6,
        out_specs=VM,
        compiler_params=PARAMS,
        name="pack_weights",
    )(tri, out, wid, nar_t, hb, hp_t)


def prepare_kernel(rank_ref, tok_ref, cot_ref, keep_ref, x_ref, inc_ref, bias_ref, xs, cs):
    images, kp, width = x_ref.shape
    patches = keep_ref.shape[1]
    rows = images * patches
    qp = -(-patches // 128) * 128
    mine = keep_ref[pl.ds(pl.multiple_of(rank_ref[0] * images, 8), images), :].astype(F32)
    columns = jnp.concatenate([mine, jnp.zeros((images, qp - patches), F32)], axis=1).T
    xs[0:rows, :] = tok_ref[...].T.astype(F32)
    cs[0:rows, :] = cot_ref[...].T.astype(F32)
    xs[rows : rows + 16, :] = jnp.zeros((16, width), F32)
    cs[rows : rows + 16, :] = jnp.zeros((16, width), F32)
    for i in range(images):
        span = slice(i * patches, i * patches + kp)
        keep = jnp.broadcast_to(columns[:kp, i : i + 1], (kp, 128))
        keep_wide = jnp.concatenate([keep, keep[:, : width - 128]], axis=1)
        x_ref[i] = xs[span, :].astype(BF)
        inc_ref[i] = (cs[span, :] * keep_wide).astype(BF)
        bias_ref[i] = ((keep - 1.0) * 1e30).astype(BF)


def run_prepare(rank, tok_t, cot_t, keep_mask):
    images = keep_mask.shape[0] // 2
    kp = -(-keep_mask.shape[1] // 16) * 16
    width, rows_here = tok_t.shape
    rows = sds(images, kp, width, dtype=BF)
    return pl.pallas_call(
        prepare_kernel,
        out_shape=(rows, rows, sds(images, kp, 128, dtype=BF)),
        in_specs=[SM] + [VM] * 3,
        out_specs=(VM,) * 3,
        scratch_shapes=[pltpu.VMEM((rows_here + 16, width), F32)] * 2,
        compiler_params=PARAMS,
        name="prepare",
    )(rank, tok_t, cot_t, keep_mask)


def layer_kernel(*refs, patches, heads, data_count):
    (rank_ref, x_ref, inc_ref, bias_ref, own_ref, oth_ref, vec_ref) = refs[:7]
    (res_ref, gm_ref, dp_ref, head_ref) = refs[7:11]
    outs = refs[11:13] if data_count else refs[11:17]
    at = 11 + len(outs)
    (wq, wk, wv, wkt, wvt, wo, wi, wn, hb_s, hp_s, key_p, query_p) = refs[at : at + 12]
    at += 12
    (fst_s, keys_s, vt_s, qm_s, dmm_s, v_s, kt_s, soft_s, mix_s, mid_s, n2_s) = refs[at : at + 11]
    at += 11
    (first_t, left_t, right_s, res_s, gm_s, dp_s, s_buf, p_buf, att_buf) = refs[at : at + 9]
    at += 9
    (place_g, gate_g, da_buf, att_s, ds_s, wide_g, vec_g, hid_g, og, sems) = refs[at : at + 10]
    at += 10
    images, kp, width = x_ref.shape
    qp = soft_s.shape[4]
    hd = width // heads
    half = width // 2
    half_heads = heads // 2
    wide = own_ref.shape[1]
    hidden = 2 * wide
    strips = kp // STRIP
    c_scale = LOG2E / math.sqrt(hd)
    back_scale = 1.0 / math.sqrt(hd)
    v = [vec_ref[k : k + 1, :] for k in range(6)]

    wi[:, pl.ds(0, wide)] = own_ref[0:width, :]
    wi[:, pl.ds(wide, wide)] = oth_ref[0:width, :]
    wn[:, pl.ds(0, wide)] = own_ref[width : 2 * width, :]
    wn[:, pl.ds(wide, wide)] = oth_ref[width : 2 * width, :]
    own_tri = own_ref[2 * width : 3 * width, :]
    oth_tri = oth_ref[2 * width : 3 * width, :]
    for k, w in enumerate((wq, wk, wv, wo)):
        lanes = slice(k * half, (k + 1) * half)
        w[...] = jnp.concatenate([own_tri[:, lanes], oth_tri[:, lanes]], axis=1)
    wkt[...] = wk[...].T
    wvt[...] = wv[...].T
    small = []
    for ref in (own_ref, oth_ref):
        tail = ref[3 * width : 3 * width + 16, :].astype(F32)
        each = 1 + half_heads
        small.append(tail[0:each] + tail[each : 2 * each] + tail[2 * each : 3 * each])
    hb_s[0:1, :] = jnp.concatenate([member[0:1] for member in small], axis=1)
    hp_s[...] = jnp.concatenate(
        [member[1:, :128] for member in small] + [jnp.zeros((8 - heads, 128), F32)], axis=0
    )
    key_p[...] = key_operand(kp)
    query_p[...] = jnp.zeros_like(query_p)
    for h in range(heads):
        query_p[h, 0:16, :] = query_operand(hp_s, h, qp)
    for ref in (hid_g, vec_g, og, place_g, gate_g, mix_s, att_buf):
        ref[...] = jnp.zeros_like(ref)
    fst_s[kp:, :] = jnp.zeros((qp - kp, width), BF)
    for k in range(images):
        for side in range(2):
            right_s[side, k * qp + kp : (k + 1) * qp, :] = jnp.zeros((qp - kp, hidden), BF)
        for c in range(3):
            dp_s[c, k * qp + kp : (k + 1) * qp, :] = jnp.zeros((qp - kp, width), BF)
    gap = jnp.zeros((qp - kp, width), BF)
    one_lane = (lax.broadcasted_iota(jnp.int32, (qp, qp - width), 1) == 0).astype(BF)
    bias_lane = (lax.broadcasted_iota(jnp.int32, (kp, 128), 1) == 12).astype(BF)

    def columns_at(i):
        return pl.ds(pl.multiple_of(i * qp, 128), qp)


    def first_norm(i):
        for r in range(strips):
            n1, _ = norm_parts(x_ref[i, rows_of(r), :].astype(F32))
            fst_s[rows_of(r), :] = (n1 * v[0] + v[1]).astype(BF)
            yield

    def project(i):
        slot = i % 2
        first_q = fst_s[...]
        first = fst_s[0:kp, :]
        queries = nn(first_q, wq[...]).astype(BF)
        yield
        for h in range(heads):
            qm_s[i, h] = jnp.concatenate([queries * head_mask(qp, width, hd, h), one_lane], axis=1)
            yield
        keys_s[slot, :, 0:width] = nn(first, wk[...]).astype(BF)
        keys_s[slot, :, width:] = bias_ref[i, :, 0 : qp - width]
        yield
        vt_s[slot] = nt(wvt[...], first_q).astype(BF)
        yield
        v_s[i] = nn(first, wv[...]).astype(BF)
        yield
        kt_s[i] = nt(wkt[...], first_q).astype(BF)
        yield
        first_t[:, columns_at(i)] = first_q.T
        yield


    def forward_attention(i):
        held = {}
        slot_i = i % 2

        def scores(h):
            slot = h % 3
            s = nt(keys_s[slot_i], qm_s[i, h])
            p = nn(key_p[...] + bias_ref[i] * bias_lane, query_p[h])
            m, pm = cut(s, 0), cut(p, 0)
            for r in range(strips):
                yield
                s_buf[slot, rows_of(r), :] = cut(s, r)
                p_buf[slot, rows_of(r), :] = cut(p, r)
                m = jnp.maximum(m, cut(s, r))
                pm = jnp.maximum(pm, cut(p, r))
            held["m", h] = jnp.max(m, axis=0, keepdims=True)
            held["pm", h] = jnp.max(pm, axis=0, keepdims=True)

        def exponents(h):
            slot = h % 3
            m, pm = held["m", h], held["pm", h]
            z = jnp.zeros((STRIP, qp), F32)
            pz = jnp.zeros((STRIP, qp), F32)
            for r in range(strips):
                yield
                e = jnp.exp2((s_buf[slot, rows_of(r), :] - m) * c_scale)
                pe = jnp.exp2(p_buf[slot, rows_of(r), :] - pm)
                s_buf[slot, rows_of(r), :] = e
                p_buf[slot, rows_of(r), :] = pe
                z = z + e
                pz = pz + pe
            gate = gate_of(hp_s, h, qp)
            held["a", h] = (1.0 - gate) / jnp.sum(z, axis=0, keepdims=True)
            held["b", h] = gate / jnp.sum(pz, axis=0, keepdims=True)

        def mixing(h):
            slot = h % 3
            a, b = held["a", h], held["b", h]
            for r in range(strips):
                yield
                content = s_buf[slot, rows_of(r), :] * a
                located = p_buf[slot, rows_of(r), :] * b
                soft_s[i, h, 0, rows_of(r), :] = content
                soft_s[i, h, 1, rows_of(r), :] = located
                att_buf[h % 2, rows_of(r), :] = (content + located).astype(BF)
            yield
            mix_s[slot_i, h * hd : (h + 1) * hd, :] = nn(
                vt_s[slot_i, h * hd : (h + 1) * hd, :], att_buf[h % 2]
            ).astype(BF)

        return scores, exponents, mixing


    def feed_forward(i, slot, on):
        spreads = {}

        def strip_rows(r):
            return pl.ds(pl.multiple_of(i * qp + r * STRIP, 16), STRIP)

        rows = pl.ds(pl.multiple_of(i * qp, 16), kp)
        second = {}

        def start():
            attn = nt(mix_s[slot].T[:kp], wo[...])
            for r in range(strips):
                yield
                middle = x_ref[i, rows_of(r), :].astype(F32) + cut(attn, r) + v[4]
                n2, spread = norm_parts(middle)
                mid_s[rows_of(r), :] = middle
                n2_s[rows_of(r), :] = n2
                spreads[r] = spread
                second[r] = (n2 * v[2] + v[3]).astype(BF)
            inc_q = jnp.concatenate([inc_ref[i], gap], axis=0)
            left_t[0, :, columns_at(i)] = inc_q.T
            yield
            second["all"] = jnp.concatenate([second[r] for r in range(strips)], axis=0)
            left_t[1, :, columns_at(i)] = jnp.concatenate([second["all"], gap], axis=0).T

        def chunk(c):
            lanes = pl.ds(c * 256, 256)
            before = nn(second["all"], wi[:, lanes])
            back = nn(inc_ref[i] * on, wn[:, lanes])
            bias_row = hb_s[0:1, lanes]
            total = jnp.zeros((8, 256), F32)
            for r in range(strips):
                yield
                gelu, slope = gelu_parts(cut(before, r) + bias_row)
                right_s[0, strip_rows(r), lanes] = gelu.astype(BF)
                grad_before = cut(back, r) * slope
                right_s[1, strip_rows(r), lanes] = grad_before.astype(BF)
                total = total + fold(grad_before)
            hid_g[:, lanes] += total

        def end():
            grad_second = nt(right_s[1, rows, :], wi[...])
            product = nt(right_s[0, rows, :], wn[...])
            totals = [jnp.zeros((8, width), F32)] * 4
            mids = []
            for r in range(strips):
                yield
                n2 = n2_s[rows_of(r), :]
                res_s[i, rows_of(r), :] = mid_s[rows_of(r), :] + cut(product, r) + v[5]
                incoming = (inc_ref[i, rows_of(r), :] * on).astype(F32)
                g = cut(grad_second, r)
                grad_middle = incoming + norm_back(g * v[2], n2, spreads[r])
                gm_s[i, rows_of(r), :] = grad_middle
                mids.append(grad_middle.astype(BF))
                for k, term in enumerate((g * n2, g, grad_middle, incoming)):
                    totals[k] = totals[k] + fold(term)
            for k in range(4):
                vec_g[k] += totals[k]
            mid_low = jnp.concatenate([*mids, gap], axis=0)
            yield
            dm = nn(mid_low, wo[...]).astype(BF)
            for h in range(heads):
                yield
                dmm_s[i, h] = dm * head_mask(qp, width, hd, h)
            yield
            og[...] += nn(mix_s[slot], mid_low)

        return start, chunk, end

    def together(scores, exponents, mixing, feed, extra):
        for tick in range(heads + 2):
            interleave(
                scores(tick) if tick < heads else None,
                exponents(tick - 1) if 0 <= tick - 1 < heads else None,
                mixing(tick - 2) if 0 <= tick - 2 < heads else None,
                feed[tick] if tick < len(feed) else None,
                extra.get(tick),
            )

    blocks = hidden // 256

    def forward_step(i, carry):
        behind = jnp.maximum(i - 1, 0)
        after = jnp.minimum(i + 1, images - 1)
        start, chunk, end = feed_forward(behind, (i + 1) % 2, (i > 0).astype(BF))
        together(
            *forward_attention(i),
            [start(), *[chunk(c) for c in range(blocks)], end()],
            {heads: first_norm(after), heads + 1: project(after)},
        )
        return carry

    interleave(first_norm(0))
    interleave(project(0))
    lax.fori_loop(0, images, forward_step, 0)
    start, chunk, end = feed_forward(images - 1, (images - 1) % 2, jnp.ones((), BF))
    interleave(start())
    for c in range(blocks):
        interleave(chunk(c))
    interleave(end())
    sent = [
        pltpu.make_async_copy(res_s, res_ref, sems.at[0]),
        pltpu.make_async_copy(gm_s, gm_ref, sems.at[1]),
    ]
    for member in sent:
        member.start()


    def attention_back(i):
        held = {}
        here = i % 2

        def scores(h):
            slot = h % 2
            da = nt(v_s[i], dmm_s[i, h])
            rc = jnp.zeros((STRIP, qp), F32)
            rl = jnp.zeros((STRIP, qp), F32)
            for r in range(strips):
                yield
                part = cut(da, r)
                da_buf[slot, rows_of(r), :] = part
                rc = rc + soft_s[i, h, 0, rows_of(r), :] * part
                rl = rl + soft_s[i, h, 1, rows_of(r), :] * part
            gate = gate_of(hp_s, h, qp)
            held["c", h] = jnp.sum(rc, axis=0, keepdims=True) / (1.0 - gate)
            held["l", h] = jnp.sum(rl, axis=0, keepdims=True) / gate
            gate_g[h : h + 1, :] += held["l", h] - held["c", h]

        def spread(h):
            slot = h % 2
            rc, rl = held["c", h], held["l", h]
            lanes = pl.ds(h * qp, qp)
            for r in range(strips):
                yield
                rows = rows_of(r)
                c = soft_s[i, h, 0, rows, :]
                l = soft_s[i, h, 1, rows, :]
                part = da_buf[slot, rows, :]
                ds_s[here, rows, lanes] = (c * (part - rc)).astype(BF)
                att_s[here, rows, lanes] = (c + l).astype(BF)
                place_g[h, rows, :] += l * (part - rl)

        return scores, spread

    def products(i, there):
        rows = pl.ds(pl.multiple_of(i * qp, 16), kp)
        dq_t = []
        pad = jnp.zeros((qp - kp, qp), BF)
        for h in range(heads):
            yield
            ds = jnp.concatenate([ds_s[there, :, h * qp : (h + 1) * qp], pad], axis=0)
            dq_t.append(nn(kt_s[i, h * hd : (h + 1) * hd, :], ds))
        yield
        dq = (jnp.concatenate(dq_t, axis=0) * back_scale).astype(BF).T[:kp]
        yield
        dp_s[0, rows, :] = dq
        yield
        dk = nn(ds_s[there], qm_s[i].reshape(heads * qp, qp))[:, :width]
        dp_s[1, rows, :] = (dk * back_scale).astype(BF)
        yield
        dv = nn(att_s[there], dmm_s[i].reshape(heads * qp, width))
        dp_s[2, rows, :] = dv.astype(BF)

    def weight_gradient(unit):
        side = unit // blocks
        lanes = pl.ds(pl.multiple_of((unit % blocks) * 256, 128), 256)
        wide_g[side, :, lanes] = nn(left_t[side], right_s[side, :, lanes])
        yield

    def backward_step(i, carry):
        scores, spread = attention_back(i)
        work = products(jnp.maximum(i - 1, 0), (i + 1) % 2)
        for tick in range(heads + 1):
            interleave(
                scores(tick) if tick < heads else None,
                spread(tick - 1) if tick >= 1 else None,
                slow(work, 2),
                weight_gradient(jnp.minimum(i, 2 * blocks - 1)) if tick == 2 else None,
            )
        interleave(work)
        return carry

    lax.fori_loop(0, images, backward_step, 0)
    interleave(products(images - 1, (images - 1) % 2))
    for unit in range(images, 2 * blocks):
        interleave(weight_gradient(unit))
    sent.append(pltpu.make_async_copy(dp_s, dp_ref, sems.at[2]))
    sent[-1].start()

    triple = [nn(first_t[...], dp_s[c]) for c in range(3)]
    parts = offsets(kp, qp)
    rank = rank_ref[0]
    lane = lax.broadcasted_iota(jnp.int32, (1, 128), 1)
    row = jnp.zeros((1, 128), F32)
    for h in range(heads):
        base = ((rank + h // half_heads) % 2) * (4 * half_heads) + h % half_heads
        g = place_g[h]
        for k in range(3):
            total = jnp.sum(g * parts[k])
            row = row + jnp.where(lane == base + k * half_heads, total, 0.0)
        gate = gate_of(hp_s, h, 128)
        total = jnp.sum(gate_g[h : h + 1, :])
        row = row + jnp.where(lane == base + 3 * half_heads, total * gate * (1.0 - gate), 0.0)
    head_ref[...] = row
    if data_count:
        nar_p, out_p, tri_p, tmp = refs[at : at + 4]
        put_planes(nar_p, wide_g[0].T)
        put_planes(out_p, og[...])
        for c in range(3):
            tri_p[0, c * width : (c + 1) * width, 0:half] = triple[c][:, :half]
            tri_p[1, c * width : (c + 1) * width, 0:half] = triple[c][:, half:]
        early = jnp.sum(vec_g[...], axis=1)
        hidden_sum = jnp.sum(hid_g[...], axis=0, keepdims=True)
        rest = width - 128
        wp, np_, op = width // data_count, wide // data_count // 2, half // data_count // 2
        groups = 3 * width // data_count // 4
        small_at = 3 * (wp + np_ + op)
        for r in range(data_count):
            for side in range(2):
                piece = outs[0].at[r] if side == 0 else tmp.at[r % 4]
                for k in range(3):
                    lanes = slice(side * wide + 128 * k, side * wide + 128 * (k + 1))
                    piece[k * wp : (k + 1) * wp, :] = wide_g[1, r * wp : (r + 1) * wp, lanes]
                    piece[small_at + 8 + k : small_at + 9 + k, :] = hidden_sum[:, lanes]
                base = 3 * wp
                tiles = even_odd_tiles(nar_p, side * wide + 2 * np_ * r, np_)
                for k in range(3):
                    piece[base + k * np_ : base + (k + 1) * np_, :] = tiles[k]
                base += 3 * np_
                tiles = even_odd_tiles(out_p, side * half + 2 * op * r, op)
                for k in range(3):
                    piece[base + k * op : base + (k + 1) * op, :] = tiles[k]
                piece[small_at : small_at + 4, :] = early[:, :128]
                piece[small_at + 4 : small_at + 8, 0:rest] = early[:, 128:]
                piece[small_at + 4 : small_at + 8, rest:] = jnp.zeros((4, 128 - rest), F32)
                piece[small_at + 11 : EARLY_ROWS, :] = jnp.zeros(
                    (EARLY_ROWS - small_at - 11, 128), F32
                )
                tiles = four_row_tiles(tri_p, side, 4 * groups * r, groups)
                for k in range(3):
                    at_row = EARLY_ROWS + k * groups
                    piece[at_row : at_row + groups, :] = tiles[k]
                at_row = EARLY_ROWS + 3 * groups
                piece[at_row:CHUNK_ROWS, :] = jnp.zeros((CHUNK_ROWS - at_row, 128), F32)
                if side:
                    outs[1][r] = piece[...].astype(BF)
    else:
        outs[0][...] = wide_g[0].T
        outs[1][...] = wide_g[1]
        outs[2][...] = og[...]
        outs[3][...] = vec_g[...]
        outs[4][...] = hid_g[...]
        for c in range(3):
            outs[5][c * width : (c + 1) * width, :] = triple[c]
    for member in sent:
        member.wait()


def run_layer(rank, x, inc, bias, own, oth, vec, heads, patches, data_count):
    images, kp, width = x.shape
    qp = -(-patches // 128) * 128
    hidden = 2 * own.shape[1]
    full = images * qp
    if data_count:
        outs = [sds(data_count, CHUNK_ROWS, 128), sds(data_count, CHUNK_ROWS, 128, dtype=BF)]
    else:
        outs = [
            sds(hidden, width),
            sds(width, hidden),
            sds(width, width),
            sds(4, 8, width),
            sds(8, hidden),
            sds(3 * width, width),
        ]

    def bf(*dims):
        return pltpu.VMEM(dims, BF)

    def f32(*dims):
        return pltpu.VMEM(dims, F32)

    scratch = [
        *[bf(width, width)] * 6,
        bf(width, hidden),
        bf(width, hidden),
        f32(8, hidden),
        f32(8, 128),
        bf(kp, 128),
        bf(heads, 128, qp),
        bf(qp, width),
        bf(2, kp, qp),
        bf(2, width, qp),
        bf(images, heads, qp, qp),
        bf(images, heads, qp, width),
        bf(images, kp, width),
        bf(images, width, qp),
        f32(images, heads, 2, kp, qp),
        bf(2, width, qp),
        f32(kp, width),
        f32(kp, width),
        bf(width, full),
        bf(2, width, full),
        bf(2, full, hidden),
        f32(images, kp, width),
        f32(images, kp, width),
        bf(3, full, width),
        f32(3, kp, qp),
        f32(3, kp, qp),
        bf(2, qp, qp),
        f32(heads, kp, qp),
        f32(8, qp),
        f32(2, kp, qp),
        bf(2, kp, heads * qp),
        bf(2, kp, heads * qp),
        f32(2, width, hidden),
        f32(4, 8, width),
        f32(8, hidden),
        f32(width, width),
        pltpu.SemaphoreType.DMA((3,)),
    ]
    if data_count:
        scratch += [f32(2, hidden, 128), f32(2, width, 128), f32(2, 3 * width, 128)]
        scratch.append(f32(4, CHUNK_ROWS, 128))
    anywhere = pl.BlockSpec(memory_space=pl.ANY)
    return pl.pallas_call(
        functools.partial(layer_kernel, patches=patches, heads=heads, data_count=data_count),
        out_shape=(
            sds(images, kp, width),
            sds(images, kp, width),
            sds(3, full, width, dtype=BF),
            sds(1, 128),
            *outs,
        ),
        in_specs=[SM] + [VM] * 6,
        out_specs=(anywhere,) * 3 + (VM,) * (1 + len(outs)),
        scratch_shapes=scratch,
        compiler_params=PARAMS,
        name="layer",
    )(rank, x, inc, bias, own, oth, vec)


def whole(*dims):
    return pl.BlockSpec(dims, lambda i: (0,) * len(dims))


def paired(*dims):
    return pl.BlockSpec((PAIR, *dims), lambda i: (i,) + (0,) * len(dims))


def input_kernel(x_ref, gm_ref, dp_ref, own_ref, oth_ref, vec_ref, gi_ref, vec_out, w, vec_g, *, patches):
    step = pl.program_id(0)
    kp, width = gm_ref.shape[1:]
    qp = dp_ref.shape[1] // PAIR
    half = width // 2

    @pl.when(step == 0)
    def _():
        own_tri = own_ref[2 * width : 3 * width, :]
        oth_tri = oth_ref[2 * width : 3 * width, :]
        for at in range(3):
            span = slice(at * half, (at + 1) * half)
            w[at] = jnp.concatenate([own_tri[:, span], oth_tri[:, span]], axis=1)
        vec_g[...] = jnp.zeros_like(vec_g)

    gain = vec_ref[0:1, :]
    done = []
    for at in range(PAIR):
        n1, spread = norm_parts(x_ref[at].astype(F32))
        g = sum(nt(dp_ref[c, at * qp : at * qp + kp, :], w[c]) for c in range(3))
        vec_g[0] += fold(g * n1)
        vec_g[1] += fold(g)
        done.append(gm_ref[at] + norm_back(g * gain, n1, spread))
    gi_ref[...] = jnp.concatenate([member[:patches] for member in done], axis=0)

    @pl.when(step == pl.num_programs(0) - 1)
    def _():
        vec_out[...] = jnp.sum(vec_g[...], axis=1)


def run_input(x, gm, dp, own, oth, vec, patches):
    images, kp, width = gm.shape
    qp = dp.shape[1] // images
    return pl.pallas_call(
        functools.partial(input_kernel, patches=patches),
        grid=(images // PAIR,),
        out_shape=(sds(images * patches, width), sds(2, width)),
        in_specs=[
            paired(kp, width),
            paired(kp, width),
            pl.BlockSpec((3, PAIR * qp, width), lambda i: (0, i, 0)),
            whole(*own.shape),
            whole(*own.shape),
            whole(*vec.shape),
        ],
        out_specs=(
            pl.BlockSpec((PAIR * patches, width), lambda i: (i, 0)),
            whole(2, width),
        ),
        scratch_shapes=[pltpu.VMEM((3, width, width), BF), pltpu.VMEM((2, 8, width), F32)],
        compiler_params=PARAMS,
        name="input_gradient",
    )(x, gm, dp, own, oth, vec)


def combine_kernel(own_ref, got_ref, out_ref):
    out_ref[...] = (own_ref[...] + got_ref[...].astype(F32)).astype(BF)


def run_combine(own, got):
    return pl.pallas_call(
        combine_kernel,
        out_shape=sds(*own.shape, dtype=BF),
        in_specs=[VM] * 2,
        out_specs=VM,
        compiler_params=PARAMS,
        name="combine",
    )(own, got)


def pick_rows(ref, start, count, flip=False):
    total = ref.shape[1] if flip else ref.shape[0]
    row = lax.broadcasted_iota(jnp.int32, (count, total), 0) + start
    col = lax.broadcasted_iota(jnp.int32, (count, total), 1)
    chosen = (row == col).astype(F32)
    return lax.dot_general(
        chosen,
        ref[...],
        (((1,), (1 if flip else 0,)), ((), ())),
        preferred_element_type=F32,
        precision=lax.Precision.HIGHEST,
    )


def share_kernel(rank_ref, _, tri_ref, out_ref, wid_ref, nar_ref, *refs, data_count):
    (wt_f, wo_f, ww_f, wn_f, st, so, sw, sn) = refs
    width, wide = wid_ref.shape
    half = out_ref.shape[0]
    wp, np_, op = width // data_count, wide // data_count // 2, half // data_count // 2
    data_rank = rank_ref[1]
    groups = tri_ref.shape[0] // data_count // 4
    st[0, :, 0 : tri_ref.shape[1]] = pick_rows(tri_ref, data_rank * 4 * groups, 4 * groups)
    put_planes(so, pick_rows(out_ref, data_rank * 2 * op, 2 * op))
    sw[...] = pick_rows(wid_ref, data_rank * wp, wp)
    put_planes(sn, pick_rows(nar_ref, data_rank * 2 * np_, 2 * np_, flip=True))
    tiles = four_row_tiles(st, 0, 0, groups)
    for p in range(groups):
        for k in range(3):
            tile = 128 * (3 * p + k)
            wt_f[0:1, tile : tile + 128] = tiles[k][p : p + 1, :]
    for ref, flat, pairs in ((so, wo_f, op), (sn, wn_f, np_)):
        tiles = even_odd_tiles(ref, 0, pairs)
        for p in range(pairs):
            for k in range(3):
                tile = 128 * (3 * p + k)
                flat[0:1, tile : tile + 128] = tiles[k][p : p + 1, :]
    for p in range(wp):
        ww_f[0:1, wide * p : wide * (p + 1)] = sw[p : p + 1, :]


def run_shares(rank, after, tri, out, wid, nar_t, data_count):
    wide = wid.shape[1]
    share = [member.shape[0] // data_count for member in (tri, out, wid)]
    return pl.pallas_call(
        functools.partial(share_kernel, data_count=data_count),
        out_shape=tuple(sds(1, member.size // data_count) for member in (tri, out, wid, nar_t)),
        in_specs=[SM] + [VM] * 5,
        out_specs=(VM,) * 4,
        scratch_shapes=[
            pltpu.VMEM((1, share[0], 128), F32),
            pltpu.VMEM((2, share[1], 128), F32),
            pltpu.VMEM((share[2], wide), F32),
            pltpu.VMEM((2, wide // data_count, 128), F32),
        ],
        compiler_params=PARAMS,
        name="weight_shares",
    )(rank, after, tri, out, wid, nar_t)


def spread_rows(flat_ref, from_ref, base, blocks):
    for p in range(blocks):
        for k in range(3):
            at = base + k * blocks + p
            tile = 128 * (3 * p + k)
            flat_ref[0:1, tile : tile + 128] = from_ref[at : at + 1, :]


def sum_kernel(rank_ref, got_ref, late_ref, head_ref, _, *refs, blocks):
    (tri_f, out_f, wid_f, nar_f, vec_ref, hid_ref, pay_ref, tot) = refs
    width = late_ref.shape[1]
    tri_b, out_b, wid_b, nar_b = blocks
    tot[...] = jnp.sum(got_ref[...].astype(F32), axis=0)
    spread_rows(wid_f, tot, 0, wid_b)
    spread_rows(nar_f, tot, 3 * wid_b, nar_b)
    spread_rows(out_f, tot, 3 * (wid_b + nar_b), out_b)
    spread_rows(tri_f, tot, EARLY_ROWS, tri_b)
    at = 3 * (wid_b + nar_b + out_b)
    vec_ref[...] = jnp.concatenate(
        [tot[at : at + 4, :], tot[at + 4 : at + 8, : width - 128]], axis=1
    )
    hid = jnp.concatenate([tot[at + 8 + k : at + 9 + k, :] for k in range(3)], axis=1)
    hid_ref[...] = hid
    early = tot[0:at, :]
    late = tot[EARLY_ROWS : EARLY_ROWS + 3 * tri_b, :]
    squares = jnp.sum(early * early) + jnp.sum(late * late)
    squares = squares + jnp.where(rank_ref[1] == 0, jnp.sum(hid * hid), 0.0)
    lane = lax.broadcasted_iota(jnp.int32, (1, 128), 1)
    tails = jnp.concatenate([late_ref[0:1, 128:], late_ref[1:2, 128:]], axis=1)
    payload = jnp.concatenate(
        [late_ref[:, :128], tails, jnp.where(lane == 127, squares, head_ref[...])], axis=0
    )
    pay_ref[...] = jnp.broadcast_to(payload[None], pay_ref.shape)


def run_sums(rank, got, late_vec, head, after, blocks, wide):
    count = got.shape[0]
    width = late_vec.shape[1]
    return pl.pallas_call(
        functools.partial(sum_kernel, blocks=blocks),
        out_shape=(
            *[sds(1, 3 * 128 * member) for member in blocks],
            sds(4, width),
            sds(1, wide),
            sds(2 * count, 4, 128),
        ),
        in_specs=[SM] + [VM] * 4,
        out_specs=(VM,) * 7,
        scratch_shapes=[pltpu.VMEM((EARLY_ROWS + LATE_ROWS, 128), F32)],
        compiler_params=PARAMS,
        name="sums",
    )(rank, got, late_vec, head, after)


def adam_parts(weight, gradient, moment, squares, rate, decay):
    moment_new = BETA_ONE * moment + (1.0 - BETA_ONE) * gradient
    squares_new = BETA_TWO * squares + (1.0 - BETA_TWO) * gradient * gradient
    quotient = (moment_new / (1.0 - BETA_ONE**STEP)) / (
        jnp.sqrt(squares_new / (1.0 - BETA_TWO**STEP)) + ADAM_EPS
    )
    return moment_new, squares_new, weight - rate * (quotient + decay * weight)


def adam_kernel(rank_ref, got_ref, early_ref, hid_ref, hp_ref, vec_ref, hb_ref, *refs):
    grads = refs[0:4]
    weights = refs[4:8]
    states = refs[8:22]
    outs = refs[22:43]
    norm_ref = refs[43]
    width = vec_ref.shape[1]
    half_heads = hp_ref.shape[0]
    tail = width - 128
    total = jnp.sum(got_ref[...], axis=0)
    late = jnp.concatenate(
        [
            total[0:2, :],
            jnp.concatenate([total[2:3, :tail], total[2:3, tail : 2 * tail]], axis=0),
        ],
        axis=1,
    )
    vector = jnp.concatenate([late, early_ref[...]], axis=0)
    lane = lax.broadcasted_iota(jnp.int32, (1, 128), 1)
    heads_row = jnp.where(lane < 8 * half_heads, total[3:4, :], 0.0)
    squares = (
        jnp.sum(jnp.where(lane == 127, total[3:4, :], 0.0))
        + jnp.sum(vector * vector)
        + jnp.sum(heads_row * heads_row)
    )
    norm = jnp.sqrt(jnp.full((1, 128), squares))
    norm_ref[0] = jnp.sum(norm[:, 0:1])
    factor = (CLIP_AT / jnp.maximum(norm, CLIP_AT))[:, 0:1]
    span = 4 * half_heads
    mine = jnp.where(rank_ref[0] == 0, heads_row[:, :span], heads_row[:, span : 2 * span])
    head = jnp.concatenate(
        [
            jnp.concatenate(
                [mine[:, c * half_heads + h : c * half_heads + h + 1] for c in range(4)], axis=1
            )
            for h in range(half_heads)
        ],
        axis=0,
    )
    given = [ref[...] for ref in grads] + [vector, hid_ref[...], head]
    wide = hid_ref.shape[1]
    held = [ref[...] for ref in weights] + [vec_ref[...], hb_ref[...].reshape(1, wide), hp_ref[...]]
    for at in range(7):
        renewed = adam_parts(
            held[at],
            given[at] * factor,
            states[2 * at][...].reshape(held[at].shape),
            states[2 * at + 1][...].reshape(held[at].shape),
            RATES[at],
            DECAYS[at],
        )
        for step in range(3):
            out = outs[3 * at + step]
            out[...] = renewed[step].reshape(out.shape)


def run_adam(rank, got, early, hid, hp_t, vec, hb, grads, weights, states):
    shapes = []
    for at in range(7):
        shapes += [sds(*states[2 * at].shape)] * 3
    return pl.pallas_call(
        adam_kernel,
        out_shape=(*shapes, sds(1)),
        in_specs=[SM] + [VM] * (6 + 4 + 4 + 14),
        out_specs=(VM,) * 21 + (SM,),
        compiler_params=PARAMS,
        name="adam",
    )(rank, got, early, hid, hp_t, vec, hb, *grads, *weights, *states)


def plain_chunks(halves, data_count, rows):
    sides = []
    for side in range(2):
        flat = jnp.concatenate([own_first[side].reshape(data_count, -1) for own_first in halves], axis=1)
        flat = jnp.pad(flat, ((0, 0), (0, rows * 128 - flat.shape[1])))
        sides.append(flat.reshape(data_count, rows, 128))
    return sides[0], sides[1].astype(BF)


def on_device(
    tokens,
    cotangent,
    keep_mask,
    triple_weight,
    outward_weight,
    widen_weight,
    narrow_weight,
    vectors,
    hidden_bias,
    head_params,
    triple_moment,
    triple_square,
    outward_moment,
    outward_square,
    widen_moment,
    widen_square,
    narrow_moment,
    narrow_square,
    vector_moment,
    vector_square,
    hidden_moment,
    hidden_square,
    head_moment,
    head_square,
):
    tensor_rank = lax.axis_index("tensor")
    data_rank = lax.axis_index("dp")
    data_count = lax.axis_size("dp")
    images = keep_mask.shape[0] // 2
    patches = keep_mask.shape[1]
    heads = 2 * head_params.shape[1]
    depth = triple_weight.shape[1]
    half = triple_weight.shape[2]
    wide = widen_weight.shape[1]
    rank = jnp.stack([tensor_rank, data_rank]).astype(jnp.int32)
    triple_rows = triple_weight.reshape(3 * depth, half)
    narrow_t = narrow_weight.T
    head_t = head_params.T
    fast = (
        depth == 192
        and half == 96
        and wide == 384
        and depth % data_count == 0
        and wide % (2 * data_count) == 0
        and half % (2 * data_count) == 0
        and 3 * depth % (4 * data_count) == 0
    )
    chunked = data_count if fast else 0
    swap = [(0, 1), (1, 0)]

    own = run_pack(triple_weight, outward_weight, widen_weight, narrow_t, hidden_bias, head_t)
    other = lax.ppermute(own, "tensor", swap)
    x, inc, bias = run_prepare(rank, tokens.T, cotangent.T, keep_mask)
    result, grad_middle, dp, head_row, *sums = run_layer(
        rank, x, inc, bias, own, other, vectors, heads, patches, chunked
    )
    if fast:
        mine, theirs = sums
    else:
        nar_g, wid_g, out_g, vec_g, hid_g, tri_g = sums
        early_mine = jnp.sum(vec_g, axis=1).reshape(1, -1)
        early_both = jnp.broadcast_to(early_mine, (data_count, early_mine.size))
        hidden_both = jnp.broadcast_to(
            jnp.sum(hid_g, axis=0).reshape(2, 1, wide), (2, data_count, wide)
        )
        early = plain_chunks(
            [
                wid_g.reshape(depth, 2, wide).transpose(1, 0, 2),
                nar_g.reshape(2, -1),
                out_g.reshape(2, -1),
                (early_both, early_both),
                hidden_both,
            ],
            data_count,
            EARLY_ROWS,
        )
        late = plain_chunks(
            [tri_g.reshape(3 * depth, 2, half).transpose(1, 0, 2)], data_count, LATE_ROWS
        )
        mine, theirs = (jnp.concatenate(pair, axis=1) for pair in zip(early, late))
    chunks = run_combine(mine, lax.ppermute(theirs, "tensor", swap))
    got = lax.all_to_all(chunks, "dp", 0, 0, tiled=False)
    grad_input, late_vec = run_input(x, grad_middle, dp, own, other, vectors, patches)
    if fast:
        wt_f, wo_f, ww_f, wn_f = run_shares(
            rank, head_row, triple_rows, outward_weight, widen_weight, narrow_t, data_count
        )
        blocks = [
            member.size // data_count // 384
            for member in (triple_rows, outward_weight, widen_weight, narrow_t)
        ]
        tri_f, out_f, wid_f, nar_f, early_vec, hid, payload = run_sums(
            rank, got, late_vec, head_row, wo_f, blocks, wide
        )
    else:
        total = jnp.sum(got.astype(F32), axis=0)
        early_sum = total[:EARLY_ROWS].reshape(1, -1)
        masters = (widen_weight, narrow_weight, outward_weight)
        sizes = [member.size // data_count for member in masters] + [4 * depth, wide]
        cuts = [sum(sizes[:at]) for at in range(6)]
        wid_f, nar_f, out_f, early_vec, hid = (
            early_sum[:, cuts[at] : cuts[at + 1]] for at in range(5)
        )
        early_vec = early_vec.reshape(4, depth)
        share = triple_rows.size // data_count
        tri_f = total[EARLY_ROWS:].reshape(1, -1)[:, :share]

        def weight_share(member):
            length = member.size // data_count
            return lax.dynamic_slice_in_dim(member.reshape(1, -1), data_rank * length, length, 1)

        ww_f, wn_f, wo_f = (weight_share(member) for member in masters)
        wt_f = weight_share(triple_rows)
        squares = sum(jnp.sum(member * member) for member in (wid_f, nar_f, out_f, tri_f))
        squares = squares + jnp.where(data_rank == 0, jnp.sum(hid * hid), 0.0)
        lane = lax.broadcasted_iota(jnp.int32, (1, 128), 1)
        payload = jnp.concatenate(
            [
                late_vec[:, :128],
                late_vec[:, 128:].reshape(1, 128),
                jnp.where(lane == 127, squares, head_row),
            ]
        )
        payload = jnp.broadcast_to(payload[None], (2 * data_count, 4, 128))
    last_got = lax.all_to_all(payload, ("dp", "tensor"), 0, 0, tiled=False)
    renewed = run_adam(
        rank,
        last_got,
        early_vec,
        hid,
        head_t,
        vectors,
        hidden_bias,
        (tri_f, out_f, wid_f, nar_f),
        (wt_f, wo_f, ww_f, wn_f),
        (
            triple_moment,
            triple_square,
            outward_moment,
            outward_square,
            widen_moment,
            widen_square,
            narrow_moment,
            narrow_square,
            vector_moment,
            vector_square,
            hidden_moment,
            hidden_square,
            head_moment.T,
            head_square.T,
        ),
    )
    hidden_new = renewed[15:18]
    head_new = [member.T for member in renewed[18:21]]
    result = result[:, :patches].reshape(images * patches, depth)
    return (result, grad_input, *renewed[:15], *hidden_new, *head_new, renewed[21].reshape(()))


def solution(mesh):
    return jax.shard_map(
        on_device,
        mesh=mesh,
        in_specs=(
            P(("dp", "tensor"), None),
            P(("dp", "tensor"), None),
            P("dp", None),
            P(None, None, "tensor"),
            P("tensor", None),
            P(None, "tensor"),
            P("tensor", None),
            P(),
            P("tensor"),
            P(None, "tensor"),
            P("tensor", "dp"),
            P("tensor", "dp"),
            P("tensor", "dp"),
            P("tensor", "dp"),
            P("tensor", "dp"),
            P("tensor", "dp"),
            P("tensor", "dp"),
            P("tensor", "dp"),
            P(),
            P(),
            P("tensor"),
            P("tensor"),
            P(None, "tensor"),
            P(None, "tensor"),
        ),
        out_specs=(
            P(("dp", "tensor"), None),
            P(("dp", "tensor"), None),
            P("tensor", "dp"),
            P("tensor", "dp"),
            P("tensor", "dp"),
            P("tensor", "dp"),
            P("tensor", "dp"),
            P("tensor", "dp"),
            P("tensor", "dp"),
            P("tensor", "dp"),
            P("tensor", "dp"),
            P("tensor", "dp"),
            P("tensor", "dp"),
            P("tensor", "dp"),
            P(),
            P(),
            P(),
            P("tensor"),
            P("tensor"),
            P("tensor"),
            P(None, "tensor"),
            P(None, "tensor"),
            P(None, "tensor"),
            P(),
        ),
        check_vma=False,
    )
```

```python
import functools
import math

import jax
import jax.numpy as jnp
from jax import lax
from jax.experimental import pallas as pl
from jax.experimental.pallas import tpu as pltpu
from jax.sharding import PartitionSpec as P

GRID = 14
STEP = 10
EPS_NORM = 1e-06
CLIP_AT = 1.0
BETA_ONE = 0.9
BETA_TWO = 0.95
ADAM_EPS = 1e-08
RATES = (0.1, 0.5, 0.1, 0.05, 0.3, 0.1, 0.3)
DECAYS = (0.05, 0.05, 0.05, 0.05, 0.0, 0.0, 0.0)
LOG2E = 1.4426950408889634
BF = jnp.bfloat16
F32 = jnp.float32
LAYER_VMEM = 55 * 1024 * 1024
SMALL_VMEM = 16 * 1024 * 1024
EARLY_ROWS = 96
LATE_ROWS = 32
CHUNK_ROWS = EARLY_ROWS + LATE_ROWS
PAIR = 2
VM = pl.BlockSpec(memory_space=pltpu.VMEM)
ANYWHERE = pl.BlockSpec(memory_space=pl.ANY)
SM = pl.BlockSpec(memory_space=pltpu.SMEM)
PARAMS = pltpu.CompilerParams(vmem_limit_bytes=SMALL_VMEM)


def sds(*dims, dtype=F32):
    return jax.ShapeDtypeStruct(dims, dtype)


def near(*arrays):
    return [pltpu.with_memory_space_constraint(member, pltpu.VMEM) for member in arrays]


def far(*arrays):
    return [pltpu.with_memory_space_constraint(member, pltpu.HBM) for member in arrays]


def nn(a, b):
    return lax.dot_general(a, b, (((1,), (0,)), ((), ())), preferred_element_type=F32)


def nt(a, b):
    return lax.dot_general(a, b, (((1,), (1,)), ((), ())), preferred_element_type=F32)


def norm_parts(v):
    width = v.shape[-1]
    average = jnp.sum(v, axis=-1, keepdims=True) * (1.0 / width)
    centred = v - average
    variance = jnp.sum(centred * centred, axis=-1, keepdims=True) * (1.0 / width)
    spread = lax.rsqrt(variance + EPS_NORM)
    return centred * spread, spread


def norm_back(e, n, spread):
    width = e.shape[-1]
    mean_e = jnp.sum(e, axis=-1, keepdims=True) * (1.0 / width)
    mean_en = jnp.sum(e * n, axis=-1, keepdims=True) * (1.0 / width)
    return spread * (e - mean_e - n * mean_en)


def fold(v):
    rows = v.shape[0]
    return jnp.sum(v.reshape(rows // 8, 8, v.shape[1]), axis=0)


def gelu_parts(x):
    phi = 0.5 + 0.5 * lax.erf(x * math.sqrt(0.5))
    density = jnp.exp2((x * x) * (-0.5 * LOG2E)) * (1.0 / math.sqrt(2.0 * math.pi))
    return x * phi, phi + x * density


def places(count, lanes, dim):
    at = lax.broadcasted_iota(jnp.int32, (count, lanes), dim).astype(F32)
    row = jnp.floor((at + 0.5) * (1.0 / GRID))
    return at - row * GRID, row


def offsets(kp, qp):
    kc, kr = places(kp, qp, 0)
    qc, qr = places(kp, qp, 1)
    a = kc - qc
    b = kr - qr
    return a, b, a * a + b * b


def head_mask(width, hd, h):
    lane = lax.broadcasted_iota(jnp.int32, (STRIP, width), 1)
    return ((lane >= h * hd) & (lane < (h + 1) * hd)).astype(BF)


def gate_of(hp_ref, h, lanes):
    return 1.0 / (1.0 + jnp.exp(-jnp.broadcast_to(hp_ref[h : h + 1, 3:4], (1, lanes))))


def bf_parts(value, count=3):
    parts = []
    for _ in range(count):
        part = value.astype(BF).astype(F32)
        parts.append(part)
        value = value - part
    return parts


def key_operand(kp):
    kc, kr = places(kp, 128, 0)
    lane = lax.broadcasted_iota(jnp.int32, (kp, 128), 1)
    value = jnp.where(lane < 3, kc, jnp.where(lane < 6, kr, jnp.where(lane < 9, kc * kc, kr * kr)))
    return jnp.where(lane < 12, value, 0.0).astype(BF)


def query_operand(hp_ref, h, qp):
    p = [LOG2E * jnp.broadcast_to(hp_ref[h : h + 1, at : at + 1], (16, qp)) for at in range(3)]
    qc, qr = places(16, qp, 1)
    row = lax.broadcasted_iota(jnp.int32, (16, qp), 0)
    value = jnp.where(row < 3, p[0] - 2.0 * p[2] * qc, jnp.where(row < 6, p[1] - 2.0 * p[2] * qr, p[2]))
    parts = bf_parts(value)
    place = row - 3 * ((row >= 3).astype(jnp.int32) + (row >= 6) + (row >= 9))
    value = jnp.where(place == 0, parts[0], jnp.where(place == 1, parts[1], parts[2]))
    return jnp.where(row < 12, value, jnp.where(row == 12, 1.0, 0.0)).astype(BF)


STRIP = 16
LAG = 3
WAIT = 3


def interleave(*streams):
    streams = [member for member in streams if member is not None]
    while streams:
        alive = []
        for member in streams:
            try:
                next(member)
                alive.append(member)
            except StopIteration:
                pass
        streams = alive


def staged(count, lag, *stages):
    for t in range(count + lag * (len(stages) - 1)):
        for k, stage in enumerate(stages):
            if 0 <= t - k * lag < count:
                stage(t - k * lag)
        yield


def slow(stream, count):
    for _ in range(count):
        yield
        try:
            next(stream)
        except StopIteration:
            return


def cut(value, r):
    return value[r * STRIP : (r + 1) * STRIP]


def rows_of(r):
    return pl.ds(r * STRIP, STRIP)


def put_planes(ref, value):
    width = value.shape[1]
    ref[0] = value[:, :128]
    ref[1, :, 0 : width - 128] = value[:, 128:]


def even_odd_tiles(ref, start, pairs):
    even = [ref[at, pl.ds(start, pairs, stride=2), :] for at in range(2)]
    odd = [ref[at, pl.ds(start + 1, pairs, stride=2), :] for at in range(2)]
    return (
        even[0],
        jnp.concatenate([even[1][:, :64], odd[0][:, :64]], axis=1),
        jnp.concatenate([odd[0][:, 64:], odd[1][:, :64]], axis=1),
    )


def four_row_tiles(ref, plane, start, groups):
    r = [ref[plane, pl.ds(start + at, groups, stride=4), :] for at in range(4)]
    return (
        jnp.concatenate([r[0][:, :96], r[1][:, :32]], axis=1),
        jnp.concatenate([r[1][:, 32:96], r[2][:, :64]], axis=1),
        jnp.concatenate([r[2][:, 64:96], r[3][:, :96]], axis=1),
    )


def pack_kernel(*refs):
    given, pack_ref, passed, held, sems = refs[:9], refs[9], refs[10:13], refs[13:19], refs[19]
    copies = [
        pltpu.make_async_copy(source, target, sems.at[at])
        for at, (source, target) in enumerate(zip(given, [*held, *passed]))
    ]
    for member in copies:
        member.start()
    for member in copies[:6]:
        member.wait()
    tri_ref, out_ref, wid_ref, nar_ref, hb_ref, hp_ref = held
    depth, wide = wid_ref.shape
    pack_ref[0:depth, :] = wid_ref[...].astype(BF)
    pack_ref[depth : 2 * depth, :] = nar_ref[...].astype(BF)
    pack_ref[2 * depth : 3 * depth, :] = jnp.concatenate(
        [tri_ref[0], tri_ref[1], tri_ref[2], out_ref[...].T], axis=1
    ).astype(BF)
    heads_here = hp_ref.shape[0]
    hp = jnp.concatenate([hp_ref[...], jnp.zeros((heads_here, wide - 4), F32)], axis=1)
    left = jnp.concatenate([hb_ref[...].reshape(1, wide), hp], axis=0)
    parts = []
    for _ in range(3):
        part = left.astype(BF).astype(F32)
        parts.append(part)
        left = left - part
    parts.append(jnp.zeros((16 - 3 * (1 + heads_here), wide), F32))
    pack_ref[3 * depth : 3 * depth + 16, :] = jnp.concatenate(parts, axis=0).astype(BF)
    for member in copies[6:]:
        member.wait()


def run_pack(tri, out, wid, nar_t, hb, hp_t, *passed):
    depth, wide = wid.shape
    given = (tri, out, wid, nar_t, hb, hp_t)
    return pl.pallas_call(
        pack_kernel,
        out_shape=(
            pltpu.VMEM((3 * depth + 16, wide), BF),
            *[pltpu.VMEM(member.shape, member.dtype) for member in passed],
        ),
        in_specs=[pl.BlockSpec(memory_space=pltpu.HBM)] * 9,
        out_specs=(VM,) * 4,
        scratch_shapes=[
            *[pltpu.VMEM(member.shape, member.dtype) for member in given],
            pltpu.SemaphoreType.DMA((9,)),
        ],
        compiler_params=PARAMS,
        name="pack_weights",
    )(*far(*given, *passed))


def prepare_kernel(tok_ref, cot_ref, keep_ref, x_ref, inc_ref, bias_ref, xs, cs):
    images, kp, width = x_ref.shape
    patches = keep_ref.shape[1]
    rows = images * patches
    qp = -(-patches // 128) * 128
    mine = keep_ref[pl.ds(pl.multiple_of(lax.axis_index("tensor") * images, 8), images), :].astype(F32)
    columns = jnp.concatenate([mine, jnp.zeros((images, qp - patches), F32)], axis=1).T
    xs[0:rows, :] = tok_ref[...].T.astype(F32)
    cs[0:rows, :] = cot_ref[...].T.astype(F32)
    xs[rows : rows + 16, :] = jnp.zeros((16, width), F32)
    cs[rows : rows + 16, :] = jnp.zeros((16, width), F32)
    for i in range(images):
        span = slice(i * patches, i * patches + kp)
        keep = jnp.broadcast_to(columns[:kp, i : i + 1], (kp, 128))
        keep_wide = jnp.concatenate([keep, keep[:, : width - 128]], axis=1)
        x_ref[i] = xs[span, :].astype(BF)
        inc_ref[i] = (cs[span, :] * keep_wide).astype(BF)
        bias_ref[i] = ((keep - 1.0) * 1e30).astype(BF)


def run_prepare(tok_t, cot_t, keep_mask):
    images = keep_mask.shape[0] // 2
    kp = -(-keep_mask.shape[1] // 16) * 16
    width, rows_here = tok_t.shape
    rows = pltpu.VMEM((images, kp, width), BF)
    return pl.pallas_call(
        prepare_kernel,
        out_shape=(rows, rows, pltpu.VMEM((images, kp, 128), BF)),
        in_specs=[VM] * 3,
        out_specs=(VM,) * 3,
        scratch_shapes=[pltpu.VMEM((rows_here + 16, width), F32)] * 2,
        compiler_params=PARAMS,
        name="prepare",
    )(*near(tok_t, cot_t, keep_mask))


def layer_kernel(*refs, patches, heads, data_count):
    (x_ref, inc_ref, bias_ref, own_ref, oth_ref, vec_ref) = refs[:6]
    (res_ref, gm_ref, dp_ref, head_ref) = refs[6:10]
    outs = refs[10:12] if data_count else refs[10:16]
    at = 10 + len(outs)
    (wq, wk, wv, wo, wi, wn, hb_s, hp_s, key_p, query_p) = refs[at : at + 10]
    at += 10
    (fst_s, keys_s, vt_s, qm_s, dmm_s, v_s, kt_s, soft_s, mid_s, n2_s) = refs[at : at + 10]
    at += 10
    (sec_s, spr_s, low_s, stat_s, back_s) = refs[at : at + 5]
    at += 5
    (first_t, left_t, right_s, res_s, gm_s, dp_s, s_buf, p_buf, att_buf) = refs[at : at + 9]
    at += 9
    (place_g, gate_g, da_buf, att_s, ds_s, wide_g, vec_g, hid_g, sems) = refs[at : at + 9]
    at += 9
    images, kp, width = x_ref.shape
    qp = soft_s.shape[4]
    hd = width // heads
    half = width // 2
    half_heads = heads // 2
    wide = own_ref.shape[1]
    hidden = 2 * wide
    strips = kp // STRIP
    c_scale = LOG2E / math.sqrt(hd)
    back_scale = 1.0 / math.sqrt(hd)
    v = [vec_ref[k : k + 1, :] for k in range(6)]

    key_p[...] = key_operand(kp)
    query_p[...] = jnp.zeros_like(query_p)
    for ref in (hid_g, vec_g, place_g, gate_g, att_buf, mid_s, n2_s, sec_s, spr_s, stat_s):
        ref[...] = jnp.zeros_like(ref)
    s_buf[heads - 2 :] = jnp.zeros((2, kp, qp), F32)
    p_buf[heads - 2 :] = jnp.zeros((2, kp, qp), F32)
    left_t[2, :, 0:qp] = jnp.zeros((width, qp), BF)
    right_s[1, 0:qp, :] = jnp.zeros((qp, hidden), BF)
    vt_s[...] = jnp.zeros((width, qp), BF)
    for k in range(2):
        fst_s[k, kp:, :] = jnp.zeros((qp - kp, width), BF)
    for k in range(images):
        for side in range(2):
            right_s[side, k * qp + kp : (k + 1) * qp, :] = jnp.zeros((qp - kp, hidden), BF)
        for c in range(3):
            dp_s[c, k * qp + kp : (k + 1) * qp, :] = jnp.zeros((qp - kp, width), BF)
    gap = jnp.zeros((qp - kp, width), BF)
    one_lane = (lax.broadcasted_iota(jnp.int32, (STRIP, qp - width), 1) == 0).astype(BF)
    masks = [head_mask(width, hd, h) for h in range(heads)]
    bias_lane = (lax.broadcasted_iota(jnp.int32, (kp, 128), 1) == 12).astype(BF)

    def columns_at(i):
        return pl.ds(pl.multiple_of(i * qp, 128), qp)


    def first_norm(i):
        kept = {}

        def mean(r):
            x = x_ref[i, rows_of(r), :].astype(F32)
            kept[r] = x - jnp.sum(x, axis=-1, keepdims=True) * (1.0 / width)

        def spread(r):
            kept[r] = (kept[r], jnp.sum(kept[r] * kept[r], axis=-1, keepdims=True) * (1.0 / width))

        def put(r):
            centred, variance = kept[r]
            fst_s[i % 2, rows_of(r), :] = (centred * lax.rsqrt(variance + EPS_NORM) * v[0] + v[1]).astype(BF)

        yield from staged(strips, LAG, mean, spread, put)

    def project(i, part):
        first_q = fst_s[i % 2]
        if part == 0:
            queries = nn(first_q, wq[...]).astype(BF)
            yield
            for r in range(qp // STRIP):
                for h in range(heads):
                    qm_s[i, h, rows_of(r), 0:width] = cut(queries, r) * masks[h]
                    qm_s[i, h, rows_of(r), width:] = one_lane
                yield
        elif part == 1:
            keys = nn(first_q, wk[...]).astype(BF)
            yield
            keys_s[:, 0:width] = keys[:kp]
            keys_s[:, width:] = bias_ref[i, :, 0 : qp - width]
            yield
            kt_s[i] = keys.T
            yield
        else:
            values = nn(first_q, wv[...]).astype(BF)
            yield
            v_s[i] = values[:kp]
            vt_s[...] = values.T
            yield
            yield
            first_t[:, columns_at(i)] = first_q.T
            yield


    def scores(i, h):
        s = nt(keys_s[...], qm_s[i, h])
        p = nn(key_p[...] + bias_ref[i] * bias_lane, query_p[h])
        m, pm = cut(s, 0), cut(p, 0)
        for r in range(strips):
            yield
            s_buf[h, rows_of(r), :] = cut(s, r)
            p_buf[h, rows_of(r), :] = cut(p, r)
            m = jnp.maximum(m, cut(s, r))
            pm = jnp.maximum(pm, cut(p, r))
        stat_s[4 * h : 4 * h + 1, :] = jnp.max(m, axis=0, keepdims=True)
        stat_s[4 * h + 1 : 4 * h + 2, :] = jnp.max(pm, axis=0, keepdims=True)

    def exponents(h):
        m, pm = stat_s[4 * h : 4 * h + 1, :], stat_s[4 * h + 1 : 4 * h + 2, :]
        z = jnp.zeros((STRIP, qp), F32)
        pz = jnp.zeros((STRIP, qp), F32)
        for r in range(strips):
            yield
            e = jnp.exp2((s_buf[h, rows_of(r), :] - m) * c_scale)
            pe = jnp.exp2(p_buf[h, rows_of(r), :] - pm)
            s_buf[h, rows_of(r), :] = e
            p_buf[h, rows_of(r), :] = pe
            z = z + e
            pz = pz + pe
        gate = gate_of(hp_s, h, qp)
        stat_s[4 * h + 2 : 4 * h + 3, :] = (1.0 - gate) / jnp.sum(z, axis=0, keepdims=True)
        stat_s[4 * h + 3 : 4 * h + 4, :] = gate / jnp.sum(pz, axis=0, keepdims=True)

    def mixing(i, h):
        a, b = stat_s[4 * h + 2 : 4 * h + 3, :], stat_s[4 * h + 3 : 4 * h + 4, :]
        for r in range(strips):
            yield
            content = s_buf[h, rows_of(r), :] * a
            located = p_buf[h, rows_of(r), :] * b
            soft_s[i, h, 0, rows_of(r), :] = content
            soft_s[i, h, 1, rows_of(r), :] = located
            att_buf[h % 2, rows_of(r), :] = (content + located).astype(BF)
        yield
        left_t[2, h * hd : (h + 1) * hd, columns_at(i)] = nn(
            vt_s[h * hd : (h + 1) * hd, :], att_buf[h % 2]
        ).astype(BF)


    def strip_rows(i, r):
        return pl.ds(pl.multiple_of(i * qp + r * STRIP, 16), STRIP)

    def image_rows(i):
        return pl.ds(pl.multiple_of(i * qp, 16), kp)

    def start(i):
        attn = nt(left_t[2, :, columns_at(i)].T[:kp], wo[...])
        for _ in range(WAIT + 2):
            yield
        kept = {}

        def mean(r):
            middle = x_ref[i, rows_of(r), :].astype(F32) + cut(attn, r) + v[4]
            mid_s[rows_of(r), :] = middle
            kept[r] = middle - jnp.sum(middle, axis=-1, keepdims=True) * (1.0 / width)

        def vary(r):
            kept[r] = (kept[r], jnp.sum(kept[r] * kept[r], axis=-1, keepdims=True) * (1.0 / width))

        def put(r):
            centred, variance = kept[r]
            spread = lax.rsqrt(variance + EPS_NORM)
            n2 = centred * spread
            n2_s[rows_of(r), :] = n2
            spr_s[rows_of(r), :] = spread
            sec_s[rows_of(r), :] = (n2 * v[2] + v[3]).astype(BF)

        yield from staged(strips, LAG, mean, vary, put)
        left_t[0, :, columns_at(i)] = jnp.concatenate([inc_ref[i], gap], axis=0).T
        yield
        left_t[1, :, columns_at(i)] = jnp.concatenate([sec_s[...], gap], axis=0).T

    def chunk(i, c, on):
        lanes = pl.ds(c * 256, 256)
        before = nn(sec_s[...], wi[:, lanes])
        back = nn(inc_ref[i] * on, wn[:, lanes])
        bias_row = hb_s[0:1, lanes]
        total = jnp.zeros((8, 256), F32)
        for r in range(strips):
            yield
            gelu, slope = gelu_parts(cut(before, r) + bias_row)
            right_s[0, strip_rows(i, r), lanes] = gelu.astype(BF)
            grad_before = cut(back, r) * slope
            right_s[1, strip_rows(i, r), lanes] = grad_before.astype(BF)
            total = total + fold(grad_before)
        hid_g[:, lanes] += total

    def end(i, on):
        grad_second = nt(right_s[1, image_rows(i), :], wi[...])
        totals = [jnp.zeros((8, width), F32)] * 4
        mids = []
        for _ in range(WAIT):
            yield
        kept = {}

        def means(r):
            n2 = n2_s[rows_of(r), :]
            g = cut(grad_second, r)
            e = g * v[2]
            mean_e = jnp.sum(e, axis=-1, keepdims=True) * (1.0 / width)
            mean_en = jnp.sum(e * n2, axis=-1, keepdims=True) * (1.0 / width)
            kept[r] = (e, mean_e, mean_en)
            for k, term in enumerate((g * n2, g)):
                totals[k] = totals[k] + fold(term)

        def put(r):
            e, mean_e, mean_en = kept[r]
            n2 = n2_s[rows_of(r), :]
            incoming = (inc_ref[i, rows_of(r), :] * on).astype(F32)
            spread = spr_s[rows_of(r), :]
            grad_middle = incoming + spread * (e - mean_e - n2 * mean_en)
            gm_s[i, rows_of(r), :] = grad_middle
            mids.append(grad_middle.astype(BF))
            for k, term in enumerate((grad_middle, incoming)):
                totals[2 + k] = totals[2 + k] + fold(term)

        yield from staged(strips, LAG, means, put)
        for k in range(4):
            vec_g[k] += totals[k]
        mid_low = jnp.concatenate([*mids, gap], axis=0)
        yield
        dm = nn(mid_low, wo[...]).astype(BF)
        for r in range(qp // STRIP):
            yield
            for h in range(heads):
                dmm_s[i, h, rows_of(r), :] = cut(dm, r) * masks[h]
        yield
        low_s[pl.ds(pl.multiple_of(i * qp, 16), qp), :] = mid_low

    def outcome(i):
        product = nt(right_s[0, image_rows(i), :], wn[...])
        for _ in range(WAIT):
            yield
        for r in range(strips):
            res_s[i, rows_of(r), :] = mid_s[rows_of(r), :] + cut(product, r) + v[5]
            yield

    blocks = hidden // 256

    def forward_step(i, carry):
        one, two = jnp.maximum(i - 1, 0), jnp.maximum(i - 2, 0)
        after = jnp.minimum(i + 1, images - 1)
        on_one, on_two = (i > 0).astype(BF), (i > 1).astype(BF)
        interleave(scores(i, 0), exponents(3), mixing(one, 2), chunk(two, 1, on_two), first_norm(after))
        interleave(scores(i, 1), exponents(0), mixing(one, 3), chunk(two, 2, on_two))
        interleave(
            scores(i, 2),
            exponents(1),
            mixing(i, 0),
            end(two, on_two),
            outcome(two),
            start(one),
            project(i, 2),
        )
        interleave(
            scores(i, 3),
            exponents(2),
            mixing(i, 1),
            chunk(one, 0, on_one),
            project(after, 0),
            project(after, 1),
        )
        return carry

    interleave(first_norm(0))
    wi[:, pl.ds(0, wide)] = own_ref[0:width, :]
    wi[:, pl.ds(wide, wide)] = oth_ref[0:width, :]
    wn[:, pl.ds(0, wide)] = own_ref[width : 2 * width, :]
    wn[:, pl.ds(wide, wide)] = oth_ref[width : 2 * width, :]
    own_tri = own_ref[2 * width : 3 * width, :]
    oth_tri = oth_ref[2 * width : 3 * width, :]
    for k, w in enumerate((wq, wk, wv, wo)):
        lanes = slice(k * half, (k + 1) * half)
        w[...] = jnp.concatenate([own_tri[:, lanes], oth_tri[:, lanes]], axis=1)
    small = []
    for ref in (own_ref, oth_ref):
        tail = ref[3 * width : 3 * width + 16, :].astype(F32)
        each = 1 + half_heads
        small.append(tail[0:each] + tail[each : 2 * each] + tail[2 * each : 3 * each])
    hb_s[0:1, :] = jnp.concatenate([member[0:1] for member in small], axis=1)
    hp_s[...] = jnp.concatenate(
        [member[1:, :128] for member in small] + [jnp.zeros((8 - heads, 128), F32)], axis=0
    )
    for h in range(heads):
        query_p[h, 0:16, :] = query_operand(hp_s, h, qp)
    for part in range(2):
        interleave(project(0, part))
    lax.fori_loop(0, images, forward_step, 0)


    def back_scores(i, h):
        da = nt(v_s[i], dmm_s[i, h])
        rc = jnp.zeros((STRIP, qp), F32)
        rl = jnp.zeros((STRIP, qp), F32)
        for r in range(strips):
            yield
            part = cut(da, r)
            da_buf[h % 2, rows_of(r), :] = part
            rc = rc + soft_s[i, h, 0, rows_of(r), :] * part
            rl = rl + soft_s[i, h, 1, rows_of(r), :] * part
        gate = gate_of(hp_s, h, qp)
        rc = jnp.sum(rc, axis=0, keepdims=True) / (1.0 - gate)
        rl = jnp.sum(rl, axis=0, keepdims=True) / gate
        back_s[2 * h : 2 * h + 1, :] = rc
        back_s[2 * h + 1 : 2 * h + 2, :] = rl
        gate_g[h : h + 1, :] += rl - rc

    def back_spread(i, h):
        rc, rl = back_s[2 * h : 2 * h + 1, :], back_s[2 * h + 1 : 2 * h + 2, :]
        lanes = pl.ds(h * qp, qp)
        for r in range(strips):
            yield
            rows = rows_of(r)
            c = soft_s[i, h, 0, rows, :]
            l = soft_s[i, h, 1, rows, :]
            part = da_buf[h % 2, rows, :]
            ds_s[i % 2, rows, lanes] = (c * (part - rc)).astype(BF)
            att_s[i % 2, rows, lanes] = (c + l).astype(BF)
            place_g[h, rows, :] += l * (part - rl)

    def keys_back(i):
        dk = nn(ds_s[i % 2], qm_s[i].reshape(heads * qp, qp))[:, :width]
        yield
        dp_s[1, image_rows(i), :] = (dk * back_scale).astype(BF)

    def values_back(i):
        dv = nn(att_s[i % 2], dmm_s[i].reshape(heads * qp, width))
        yield
        dp_s[2, image_rows(i), :] = dv.astype(BF)

    def queries_back(i):
        pad = jnp.zeros((qp - kp, qp), BF)
        dq_t = []
        for h in range(heads):
            ds = jnp.concatenate([ds_s[i % 2, :, h * qp : (h + 1) * qp], pad], axis=0)
            dq_t.append(nn(kt_s[i, h * hd : (h + 1) * hd, :], ds))
            yield
        dp_s[0, image_rows(i), :] = (jnp.concatenate(dq_t, axis=0) * back_scale).astype(BF).T[:kp]

    def weight_gradient(unit):
        side = unit // blocks
        lanes = pl.ds(pl.multiple_of((unit % blocks) * 256, 128), 256)
        wide_g[side, :, lanes] = nn(left_t[side], right_s[side, :, lanes])
        yield

    def backward_step(i, carry):
        unit = jnp.minimum(i - 1, 2 * blocks - 1)
        interleave(back_scores(i, 0), back_spread(i - 1, 3), weight_gradient(unit))
        interleave(back_scores(i, 1), back_spread(i, 0), keys_back(i - 1))
        interleave(back_scores(i, 2), back_spread(i, 1), values_back(i - 1))
        interleave(back_scores(i, 3), back_spread(i, 2), queries_back(i - 1))
        return carry

    last = images - 1
    on = jnp.ones((), BF)
    interleave(exponents(3), mixing(last, 2), chunk(last - 1, 1, on), back_scores(0, 0))
    interleave(mixing(last, 3), chunk(last - 1, 2, on), back_scores(0, 1), back_spread(0, 0))
    interleave(end(last - 1, on), outcome(last - 1), start(last), back_scores(0, 2), back_spread(0, 1))
    interleave(chunk(last, 0, on), back_scores(0, 3), back_spread(0, 2))
    interleave(chunk(last, 1, on))
    interleave(chunk(last, 2, on))
    interleave(end(last, on), outcome(last))
    sent = [
        pltpu.make_async_copy(res_s, res_ref, sems.at[0]),
        pltpu.make_async_copy(gm_s, gm_ref, sems.at[1]),
    ]
    for member in sent:
        member.start()

    lax.fori_loop(1, images, backward_step, 0)
    interleave(back_spread(last, 3))
    interleave(keys_back(last), values_back(last), queries_back(last))
    for unit in range(images - 1, 2 * blocks):
        interleave(weight_gradient(unit))
    sent.append(pltpu.make_async_copy(dp_s, dp_ref, sems.at[2]))
    sent[-1].start()

    triple = [nn(first_t[...], dp_s[c]) for c in range(3)]
    parts = offsets(kp, qp)
    rank = lax.axis_index("tensor")
    lane = lax.broadcasted_iota(jnp.int32, (1, 128), 1)
    row = jnp.zeros((1, 128), F32)
    for h in range(heads):
        base = ((rank + h // half_heads) % 2) * (4 * half_heads) + h % half_heads
        g = place_g[h]
        for k in range(3):
            total = jnp.sum(g * parts[k])
            row = row + jnp.where(lane == base + k * half_heads, total, 0.0)
        gate = gate_of(hp_s, h, 128)
        total = jnp.sum(gate_g[h : h + 1, :])
        row = row + jnp.where(lane == base + 3 * half_heads, total * gate * (1.0 - gate), 0.0)
    head_ref[...] = row
    if data_count:
        nar_p, out_p, tri_p, tmp = refs[at : at + 4]
        put_planes(nar_p, wide_g[0].T)
        put_planes(out_p, nn(left_t[2], low_s[...]))
        for c in range(3):
            tri_p[0, c * width : (c + 1) * width, 0:half] = triple[c][:, :half]
            tri_p[1, c * width : (c + 1) * width, 0:half] = triple[c][:, half:]
        early = jnp.sum(vec_g[...], axis=1)
        hidden_sum = jnp.sum(hid_g[...], axis=0, keepdims=True)
        rest = width - 128
        wp, np_, op = width // data_count, wide // data_count // 2, half // data_count // 2
        groups = 3 * width // data_count // 4
        small_at = 3 * (wp + np_ + op)
        for r in range(data_count):
            for side in range(2):
                piece = outs[0].at[r] if side == 0 else tmp.at[r % 4]
                for k in range(3):
                    lanes = slice(side * wide + 128 * k, side * wide + 128 * (k + 1))
                    piece[k * wp : (k + 1) * wp, :] = wide_g[1, r * wp : (r + 1) * wp, lanes]
                    piece[small_at + 8 + k : small_at + 9 + k, :] = hidden_sum[:, lanes]
                base = 3 * wp
                tiles = even_odd_tiles(nar_p, side * wide + 2 * np_ * r, np_)
                for k in range(3):
                    piece[base + k * np_ : base + (k + 1) * np_, :] = tiles[k]
                base += 3 * np_
                tiles = even_odd_tiles(out_p, side * half + 2 * op * r, op)
                for k in range(3):
                    piece[base + k * op : base + (k + 1) * op, :] = tiles[k]
                piece[small_at : small_at + 4, :] = early[:, :128]
                piece[small_at + 4 : small_at + 8, 0:rest] = early[:, 128:]
                piece[small_at + 4 : small_at + 8, rest:] = jnp.zeros((4, 128 - rest), F32)
                piece[small_at + 11 : EARLY_ROWS, :] = jnp.zeros(
                    (EARLY_ROWS - small_at - 11, 128), F32
                )
                tiles = four_row_tiles(tri_p, side, 4 * groups * r, groups)
                for k in range(3):
                    at_row = EARLY_ROWS + k * groups
                    piece[at_row : at_row + groups, :] = tiles[k]
                at_row = EARLY_ROWS + 3 * groups
                piece[at_row:CHUNK_ROWS, :] = jnp.zeros((CHUNK_ROWS - at_row, 128), F32)
                if side:
                    outs[1][r] = piece[...].astype(BF)
    else:
        outs[0][...] = wide_g[0].T
        outs[1][...] = wide_g[1]
        outs[2][...] = nn(left_t[2], low_s[...])
        outs[3][...] = vec_g[...]
        outs[4][...] = hid_g[...]
        for c in range(3):
            outs[5][c * width : (c + 1) * width, :] = triple[c]
    for member in sent:
        member.wait()


def run_layer(x, inc, bias, own, oth, vec, heads, patches, data_count):
    images, kp, width = x.shape
    qp = -(-patches // 128) * 128
    hidden = 2 * own.shape[1]
    full = images * qp
    if data_count:
        outs = [
            pltpu.VMEM((data_count, CHUNK_ROWS, 128), F32),
            pltpu.VMEM((data_count, CHUNK_ROWS, 128), BF),
        ]
    else:
        outs = [
            sds(hidden, width),
            sds(width, hidden),
            sds(width, width),
            sds(4, 8, width),
            sds(8, hidden),
            sds(3 * width, width),
        ]

    def bf(*dims):
        return pltpu.VMEM(dims, BF)

    def f32(*dims):
        return pltpu.VMEM(dims, F32)

    scratch = [
        *[bf(width, width)] * 4,
        bf(width, hidden),
        bf(width, hidden),
        f32(8, hidden),
        f32(8, 128),
        bf(kp, 128),
        bf(heads, 128, qp),
        bf(2, qp, width),
        bf(kp, qp),
        bf(width, qp),
        bf(images, heads, qp, qp),
        bf(images, heads, qp, width),
        bf(images, kp, width),
        bf(images, width, qp),
        f32(images, heads, 2, kp, qp),
        f32(kp, width),
        f32(kp, width),
        bf(kp, width),
        f32(kp, 1),
        bf(full, width),
        f32(4 * heads, qp),
        f32(2 * heads, qp),
        bf(width, full),
        bf(3, width, full),
        bf(2, full, hidden),
        f32(images, kp, width),
        f32(images, kp, width),
        bf(3, full, width),
        f32(heads, kp, qp),
        f32(heads, kp, qp),
        bf(2, qp, qp),
        f32(heads, kp, qp),
        f32(8, qp),
        f32(2, kp, qp),
        bf(2, kp, heads * qp),
        bf(2, kp, heads * qp),
        f32(2, width, hidden),
        f32(4, 8, width),
        f32(8, hidden),
        pltpu.SemaphoreType.DMA((3,)),
    ]
    if data_count:
        scratch += [f32(2, hidden, 128), f32(2, width, 128), f32(2, 3 * width, 128)]
        scratch.append(f32(4, CHUNK_ROWS, 128))
    return pl.pallas_call(
        functools.partial(layer_kernel, patches=patches, heads=heads, data_count=data_count),
        out_shape=(
            sds(images, kp, width),
            sds(images, kp, width),
            sds(3, full, width, dtype=BF),
            sds(1, 128),
            *outs,
        ),
        in_specs=[VM] * 6,
        out_specs=(ANYWHERE,) * 3 + (VM,) * (1 + len(outs)),
        scratch_shapes=scratch,
        compiler_params=pltpu.CompilerParams(vmem_limit_bytes=LAYER_VMEM),
        name="layer",
    )(*near(x, inc, bias, own, oth), vec)


def finish_kernel(
    x_ref, own_ref, oth_ref, vec_ref, res_hbm, gm_hbm, dp_hbm, res_out, gi_out, vec_out,
    res_s, gm_s, dp_s, w, vec_g, rows_s, sems, *, patches,
):
    images, kp, width = x_ref.shape
    qp = dp_s.shape[1] // images
    half = width // 2
    copies = [
        pltpu.make_async_copy(source, target, sems.at[at])
        for at, (source, target) in enumerate(
            ((res_hbm, res_s), (gm_hbm, gm_s), (dp_hbm, dp_s))
        )
    ]
    for member in copies:
        member.start()
    own_tri = own_ref[2 * width : 3 * width, :]
    oth_tri = oth_ref[2 * width : 3 * width, :]
    for at in range(3):
        span = slice(at * half, (at + 1) * half)
        w[at] = jnp.concatenate([own_tri[:, span], oth_tri[:, span]], axis=1)
    vec_g[...] = jnp.zeros_like(vec_g)
    gain = vec_ref[0:1, :]
    copies[0].wait()
    for i in range(images):
        rows_s[i * patches : (i + 1) * patches, :] = res_s[i, 0:patches, :]
    res_out[...] = rows_s[...].T
    copies[1].wait()
    copies[2].wait()
    for i in range(images):
        n1, spread = norm_parts(x_ref[i].astype(F32))
        g = sum(nt(dp_s[c, i * qp : i * qp + kp, :], w[c]) for c in range(3))
        vec_g[0] += fold(g * n1)
        vec_g[1] += fold(g)
        rows = gm_s[i] + norm_back(g * gain, n1, spread)
        rows_s[i * patches : (i + 1) * patches, :] = rows[0:patches]
    gi_out[...] = rows_s[...].T
    vec_out[...] = jnp.sum(vec_g[...], axis=1)


def run_finish(x, own, oth, vec, res, gm, dp, patches):
    images, kp, width = x.shape
    rows = images * patches
    return pl.pallas_call(
        functools.partial(finish_kernel, patches=patches),
        out_shape=(sds(width, rows), sds(width, rows), sds(2, width)),
        in_specs=[VM] * 4 + [ANYWHERE] * 3,
        out_specs=(VM,) * 3,
        scratch_shapes=[
            pltpu.VMEM(res.shape, F32),
            pltpu.VMEM(gm.shape, F32),
            pltpu.VMEM(dp.shape, BF),
            pltpu.VMEM((3, width, width), BF),
            pltpu.VMEM((2, 8, width), F32),
            pltpu.VMEM((rows, width), F32),
            pltpu.SemaphoreType.DMA((3,)),
        ],
        compiler_params=pltpu.CompilerParams(vmem_limit_bytes=32 * 1024 * 1024),
        name="finish",
    )(*near(x, own, oth), vec, *far(res, gm, dp))


def combine_kernel(own_ref, got_ref, out_ref):
    out_ref[...] = (own_ref[...] + got_ref[...].astype(F32)).astype(BF)


def run_combine(own, got):
    return pl.pallas_call(
        combine_kernel,
        out_shape=pltpu.VMEM(own.shape, BF),
        in_specs=[VM] * 2,
        out_specs=VM,
        compiler_params=PARAMS,
        name="combine",
    )(*near(own, got))


def pick_rows(ref, start, count, flip=False):
    total = ref.shape[1] if flip else ref.shape[0]
    row = lax.broadcasted_iota(jnp.int32, (count, total), 0) + start
    col = lax.broadcasted_iota(jnp.int32, (count, total), 1)
    chosen = (row == col).astype(F32)
    return lax.dot_general(
        chosen,
        ref[...],
        (((1,), (1 if flip else 0,)), ((), ())),
        preferred_element_type=F32,
        precision=lax.Precision.HIGHEST,
    )


def share_kernel(_, tri_ref, out_ref, wid_ref, nar_ref, *refs, data_count):
    (wt_f, wo_f, ww_f, wn_f, st, so, sw, sn) = refs
    width, wide = wid_ref.shape
    half = out_ref.shape[0]
    wp, np_, op = width // data_count, wide // data_count // 2, half // data_count // 2
    data_rank = lax.axis_index("dp")
    groups = tri_ref.shape[0] // data_count // 4
    st[0, :, 0 : tri_ref.shape[1]] = pick_rows(tri_ref, data_rank * 4 * groups, 4 * groups)
    put_planes(so, pick_rows(out_ref, data_rank * 2 * op, 2 * op))
    sw[...] = pick_rows(wid_ref, data_rank * wp, wp)
    put_planes(sn, pick_rows(nar_ref, data_rank * 2 * np_, 2 * np_, flip=True))
    tiles = four_row_tiles(st, 0, 0, groups)
    for p in range(groups):
        for k in range(3):
            tile = 128 * (3 * p + k)
            wt_f[0:1, tile : tile + 128] = tiles[k][p : p + 1, :]
    for ref, flat, pairs in ((so, wo_f, op), (sn, wn_f, np_)):
        tiles = even_odd_tiles(ref, 0, pairs)
        for p in range(pairs):
            for k in range(3):
                tile = 128 * (3 * p + k)
                flat[0:1, tile : tile + 128] = tiles[k][p : p + 1, :]
    for p in range(wp):
        ww_f[0:1, wide * p : wide * (p + 1)] = sw[p : p + 1, :]


def run_shares(after, tri, out, wid, nar_t, data_count):
    wide = wid.shape[1]
    share = [member.shape[0] // data_count for member in (tri, out, wid)]
    return pl.pallas_call(
        functools.partial(share_kernel, data_count=data_count),
        out_shape=tuple(sds(1, member.size // data_count) for member in (tri, out, wid, nar_t)),
        in_specs=[VM] * 5,
        out_specs=(VM,) * 4,
        scratch_shapes=[
            pltpu.VMEM((1, share[0], 128), F32),
            pltpu.VMEM((2, share[1], 128), F32),
            pltpu.VMEM((share[2], wide), F32),
            pltpu.VMEM((2, wide // data_count, 128), F32),
        ],
        compiler_params=PARAMS,
        name="weight_shares",
    )(after, tri, out, wid, nar_t)


def spread_rows(flat_ref, from_ref, base, blocks):
    for p in range(blocks):
        for k in range(3):
            at = base + k * blocks + p
            tile = 128 * (3 * p + k)
            flat_ref[0:1, tile : tile + 128] = from_ref[at : at + 1, :]


def sum_kernel(got_ref, late_ref, head_ref, _, *refs, blocks):
    (tri_f, out_f, wid_f, nar_f, vec_ref, hid_ref, pay_ref, tot) = refs
    width = late_ref.shape[1]
    tri_b, out_b, wid_b, nar_b = blocks
    tot[...] = jnp.sum(got_ref[...].astype(F32), axis=0)
    spread_rows(wid_f, tot, 0, wid_b)
    spread_rows(nar_f, tot, 3 * wid_b, nar_b)
    spread_rows(out_f, tot, 3 * (wid_b + nar_b), out_b)
    spread_rows(tri_f, tot, EARLY_ROWS, tri_b)
    at = 3 * (wid_b + nar_b + out_b)
    vec_ref[...] = jnp.concatenate(
        [tot[at : at + 4, :], tot[at + 4 : at + 8, : width - 128]], axis=1
    )
    hid = jnp.concatenate([tot[at + 8 + k : at + 9 + k, :] for k in range(3)], axis=1)
    hid_ref[...] = hid
    early = tot[0:at, :]
    late = tot[EARLY_ROWS : EARLY_ROWS + 3 * tri_b, :]
    squares = jnp.sum(early * early) + jnp.sum(late * late)
    squares = squares + jnp.where(lax.axis_index("dp") == 0, jnp.sum(hid * hid), 0.0)
    lane = lax.broadcasted_iota(jnp.int32, (1, 128), 1)
    tails = jnp.concatenate([late_ref[0:1, 128:], late_ref[1:2, 128:]], axis=1)
    payload = jnp.concatenate(
        [late_ref[:, :128], tails, jnp.where(lane == 127, squares, head_ref[...])], axis=0
    )
    pay_ref[...] = jnp.broadcast_to(payload[None], pay_ref.shape)


def run_sums(got, late_vec, head, after, blocks, wide):
    count = got.shape[0]
    width = late_vec.shape[1]
    return pl.pallas_call(
        functools.partial(sum_kernel, blocks=blocks),
        out_shape=(
            *[sds(1, 3 * 128 * member) for member in blocks],
            sds(4, width),
            sds(1, wide),
            sds(2 * count, 4, 128),
        ),
        in_specs=[VM] * 4,
        out_specs=(VM,) * 7,
        scratch_shapes=[pltpu.VMEM((CHUNK_ROWS, 128), F32)],
        compiler_params=PARAMS,
        name="sums",
    )(got, late_vec, head, after)


def adam_parts(weight, gradient, moment, squares, rate, decay):
    moment_new = BETA_ONE * moment + (1.0 - BETA_ONE) * gradient
    squares_new = BETA_TWO * squares + (1.0 - BETA_TWO) * gradient * gradient
    quotient = (moment_new / (1.0 - BETA_ONE**STEP)) / (
        jnp.sqrt(squares_new / (1.0 - BETA_TWO**STEP)) + ADAM_EPS
    )
    return moment_new, squares_new, weight - rate * (quotient + decay * weight)


def adam_kernel(got_ref, early_ref, hid_ref, hp_ref, vec_ref, hb_ref, *refs):
    grads = refs[0:4]
    weights = refs[4:8]
    states = refs[8:22]
    outs = refs[22:43]
    norm_ref = refs[43]
    width = vec_ref.shape[1]
    half_heads = hp_ref.shape[0]
    tail = width - 128
    total = jnp.sum(got_ref[...], axis=0)
    late = jnp.concatenate(
        [
            total[0:2, :],
            jnp.concatenate([total[2:3, :tail], total[2:3, tail : 2 * tail]], axis=0),
        ],
        axis=1,
    )
    vector = jnp.concatenate([late, early_ref[...]], axis=0)
    lane = lax.broadcasted_iota(jnp.int32, (1, 128), 1)
    heads_row = jnp.where(lane < 8 * half_heads, total[3:4, :], 0.0)
    squares = (
        jnp.sum(jnp.where(lane == 127, total[3:4, :], 0.0))
        + jnp.sum(vector * vector)
        + jnp.sum(heads_row * heads_row)
    )
    norm = jnp.sqrt(jnp.full((1, 128), squares))
    norm_ref[0] = jnp.sum(norm[:, 0:1])
    factor = (CLIP_AT / jnp.maximum(norm, CLIP_AT))[:, 0:1]
    span = 4 * half_heads
    mine = jnp.where(lax.axis_index("tensor") == 0, heads_row[:, :span], heads_row[:, span : 2 * span])
    head = jnp.concatenate(
        [
            jnp.concatenate(
                [mine[:, c * half_heads + h : c * half_heads + h + 1] for c in range(4)], axis=1
            )
            for h in range(half_heads)
        ],
        axis=0,
    )
    given = [ref[...] for ref in grads] + [vector, hid_ref[...], head]
    wide = hid_ref.shape[1]
    held = [ref[...] for ref in weights] + [vec_ref[...], hb_ref[...].reshape(1, wide), hp_ref[...]]
    for at in range(7):
        renewed = adam_parts(
            held[at],
            given[at] * factor,
            states[2 * at][...].reshape(held[at].shape),
            states[2 * at + 1][...].reshape(held[at].shape),
            RATES[at],
            DECAYS[at],
        )
        for step in range(3):
            out = outs[3 * at + step]
            out[...] = renewed[step].reshape(out.shape)


def run_adam(got, early, hid, hp_t, vec, hb, grads, weights, states):
    shapes = []
    for at in range(7):
        shapes += [sds(*states[2 * at].shape)] * 3
    return pl.pallas_call(
        adam_kernel,
        out_shape=(*shapes, sds(1)),
        in_specs=[VM] * (6 + 4 + 4 + 14),
        out_specs=(VM,) * 21 + (SM,),
        compiler_params=PARAMS,
        name="adam",
    )(got, early, hid, hp_t, vec, hb, *grads, *weights, *states)


def plain_chunks(halves, data_count, rows):
    sides = []
    for side in range(2):
        flat = jnp.concatenate([own_first[side].reshape(data_count, -1) for own_first in halves], axis=1)
        flat = jnp.pad(flat, ((0, 0), (0, rows * 128 - flat.shape[1])))
        sides.append(flat.reshape(data_count, rows, 128))
    return sides[0], sides[1].astype(BF)


def on_device(
    tokens,
    cotangent,
    keep_mask,
    triple_weight,
    outward_weight,
    widen_weight,
    narrow_weight,
    vectors,
    hidden_bias,
    head_params,
    triple_moment,
    triple_square,
    outward_moment,
    outward_square,
    widen_moment,
    widen_square,
    narrow_moment,
    narrow_square,
    vector_moment,
    vector_square,
    hidden_moment,
    hidden_square,
    head_moment,
    head_square,
):
    tensor_rank = lax.axis_index("tensor")
    data_rank = lax.axis_index("dp")
    data_count = lax.axis_size("dp")
    images = keep_mask.shape[0] // 2
    patches = keep_mask.shape[1]
    heads = 2 * head_params.shape[1]
    depth = triple_weight.shape[1]
    half = triple_weight.shape[2]
    wide = widen_weight.shape[1]
    triple_rows = triple_weight.reshape(3 * depth, half)
    narrow_t = narrow_weight.T
    head_t = head_params.T
    fast = (
        depth == 192
        and half == 96
        and wide == 384
        and depth % data_count == 0
        and wide % (2 * data_count) == 0
        and half % (2 * data_count) == 0
        and 3 * depth % (4 * data_count) == 0
    )
    chunked = data_count if fast else 0
    swap = [(0, 1), (1, 0)]

    own, *rows_near = run_pack(
        triple_weight,
        outward_weight,
        widen_weight,
        narrow_t,
        hidden_bias,
        head_t,
        tokens.T,
        cotangent.T,
        keep_mask,
    )
    other = lax.ppermute(own, "tensor", swap)
    x, inc, bias = run_prepare(*rows_near)
    result, grad_middle, dp, head_row, *sums = run_layer(
        x, inc, bias, own, other, vectors, heads, patches, chunked
    )
    if fast:
        mine, theirs = sums
    else:
        nar_g, wid_g, out_g, vec_g, hid_g, tri_g = sums
        early_mine = jnp.sum(vec_g, axis=1).reshape(1, -1)
        early_both = jnp.broadcast_to(early_mine, (data_count, early_mine.size))
        hidden_both = jnp.broadcast_to(
            jnp.sum(hid_g, axis=0).reshape(2, 1, wide), (2, data_count, wide)
        )
        early = plain_chunks(
            [
                wid_g.reshape(depth, 2, wide).transpose(1, 0, 2),
                nar_g.reshape(2, -1),
                out_g.reshape(2, -1),
                (early_both, early_both),
                hidden_both,
            ],
            data_count,
            EARLY_ROWS,
        )
        late = plain_chunks(
            [tri_g.reshape(3 * depth, 2, half).transpose(1, 0, 2)], data_count, LATE_ROWS
        )
        mine, theirs = (jnp.concatenate(pair, axis=1) for pair in zip(early, late))
    received = lax.ppermute(theirs, "tensor", swap)
    chunks = run_combine(mine, received)
    got = lax.all_to_all(chunks, "dp", 0, 0, tiled=False)
    result_t, grad_input_t, late_vec = run_finish(
        x, own, other, vectors, result, grad_middle, dp, patches
    )
    if fast:
        wt_f, wo_f, ww_f, wn_f = run_shares(
            head_row, triple_rows, outward_weight, widen_weight, narrow_t, data_count
        )
        blocks = [
            member.size // data_count // 384
            for member in (triple_rows, outward_weight, widen_weight, narrow_t)
        ]
        tri_f, out_f, wid_f, nar_f, early_vec, hid, payload = run_sums(
            got, late_vec, head_row, wo_f, blocks, wide
        )
    else:
        total = jnp.sum(got.astype(F32), axis=0)
        early_sum = total[:EARLY_ROWS].reshape(1, -1)
        masters = (widen_weight, narrow_weight, outward_weight)
        sizes = [member.size // data_count for member in masters] + [4 * depth, wide]
        cuts = [sum(sizes[:at]) for at in range(6)]
        wid_f, nar_f, out_f, early_vec, hid = (
            early_sum[:, cuts[at] : cuts[at + 1]] for at in range(5)
        )
        early_vec = early_vec.reshape(4, depth)
        share = triple_rows.size // data_count
        tri_f = total[EARLY_ROWS:].reshape(1, -1)[:, :share]

        def weight_share(member):
            length = member.size // data_count
            return lax.dynamic_slice_in_dim(member.reshape(1, -1), data_rank * length, length, 1)

        ww_f, wn_f, wo_f = (weight_share(member) for member in masters)
        wt_f = weight_share(triple_rows)
        squares = sum(jnp.sum(member * member) for member in (wid_f, nar_f, out_f, tri_f))
        squares = squares + jnp.where(data_rank == 0, jnp.sum(hid * hid), 0.0)
        lane = lax.broadcasted_iota(jnp.int32, (1, 128), 1)
        payload = jnp.concatenate(
            [
                late_vec[:, :128],
                late_vec[:, 128:].reshape(1, 128),
                jnp.where(lane == 127, squares, head_row),
            ]
        )
        payload = jnp.broadcast_to(payload[None], (2 * data_count, 4, 128))
    last_got = lax.all_to_all(payload, ("dp", "tensor"), 0, 0, tiled=False)
    renewed = run_adam(
        last_got,
        early_vec,
        hid,
        head_t,
        vectors,
        hidden_bias,
        (tri_f, out_f, wid_f, nar_f),
        (wt_f, wo_f, ww_f, wn_f),
        (
            triple_moment,
            triple_square,
            outward_moment,
            outward_square,
            widen_moment,
            widen_square,
            narrow_moment,
            narrow_square,
            vector_moment,
            vector_square,
            hidden_moment,
            hidden_square,
            head_moment.T,
            head_square.T,
        ),
    )
    hidden_new = renewed[15:18]
    head_new = [member.T for member in renewed[18:21]]
    return (result_t.T, grad_input_t.T, *renewed[:15], *hidden_new, *head_new, renewed[21].reshape(()))


def solution(mesh):
    return jax.shard_map(
        on_device,
        mesh=mesh,
        in_specs=(
            P(("dp", "tensor"), None),
            P(("dp", "tensor"), None),
            P("dp", None),
            P(None, None, "tensor"),
            P("tensor", None),
            P(None, "tensor"),
            P("tensor", None),
            P(),
            P("tensor"),
            P(None, "tensor"),
            P("tensor", "dp"),
            P("tensor", "dp"),
            P("tensor", "dp"),
            P("tensor", "dp"),
            P("tensor", "dp"),
            P("tensor", "dp"),
            P("tensor", "dp"),
            P("tensor", "dp"),
            P(),
            P(),
            P("tensor"),
            P("tensor"),
            P(None, "tensor"),
            P(None, "tensor"),
        ),
        out_specs=(
            P(("dp", "tensor"), None),
            P(("dp", "tensor"), None),
            P("tensor", "dp"),
            P("tensor", "dp"),
            P("tensor", "dp"),
            P("tensor", "dp"),
            P("tensor", "dp"),
            P("tensor", "dp"),
            P("tensor", "dp"),
            P("tensor", "dp"),
            P("tensor", "dp"),
            P("tensor", "dp"),
            P("tensor", "dp"),
            P("tensor", "dp"),
            P(),
            P(),
            P(),
            P("tensor"),
            P("tensor"),
            P("tensor"),
            P(None, "tensor"),
            P(None, "tensor"),
            P(None, "tensor"),
            P(),
        ),
        check_vma=False,
    )
```

```python
import functools
import math

import jax
import jax.numpy as jnp
from jax import lax
from jax.experimental import pallas as pl
from jax.experimental.pallas import tpu as pltpu
from jax.sharding import PartitionSpec as P

GRID = 14
STEP = 10
EPS_NORM = 1e-06
CLIP_AT = 1.0
BETA_ONE = 0.9
BETA_TWO = 0.95
ADAM_EPS = 1e-08
RATES = (0.1, 0.5, 0.1, 0.05, 0.3, 0.1, 0.3)
DECAYS = (0.05, 0.05, 0.05, 0.05, 0.0, 0.0, 0.0)
LOG2E = 1.4426950408889634
BF = jnp.bfloat16
F32 = jnp.float32
LAYER_VMEM = 52 * 1024 * 1024
SMALL_VMEM = 16 * 1024 * 1024
EARLY_ROWS = 96
LATE_ROWS = 32
CHUNK_ROWS = EARLY_ROWS + LATE_ROWS
PAIR = 2
VM = pl.BlockSpec(memory_space=pltpu.VMEM)
ANYWHERE = pl.BlockSpec(memory_space=pl.ANY)
SM = pl.BlockSpec(memory_space=pltpu.SMEM)
PARAMS = pltpu.CompilerParams(vmem_limit_bytes=SMALL_VMEM)


def sds(*dims, dtype=F32):
    return jax.ShapeDtypeStruct(dims, dtype)


def near(*arrays):
    return [pltpu.with_memory_space_constraint(member, pltpu.VMEM) for member in arrays]


def far(*arrays):
    return [pltpu.with_memory_space_constraint(member, pltpu.HBM) for member in arrays]


def nn(a, b):
    return lax.dot_general(a, b, (((1,), (0,)), ((), ())), preferred_element_type=F32)


def nt(a, b):
    return lax.dot_general(a, b, (((1,), (1,)), ((), ())), preferred_element_type=F32)


def norm_parts(v):
    width = v.shape[-1]
    average = jnp.sum(v, axis=-1, keepdims=True) * (1.0 / width)
    centred = v - average
    variance = jnp.sum(centred * centred, axis=-1, keepdims=True) * (1.0 / width)
    spread = lax.rsqrt(variance + EPS_NORM)
    return centred * spread, spread


def norm_back(e, n, spread):
    width = e.shape[-1]
    mean_e = jnp.sum(e, axis=-1, keepdims=True) * (1.0 / width)
    mean_en = jnp.sum(e * n, axis=-1, keepdims=True) * (1.0 / width)
    return spread * (e - mean_e - n * mean_en)


def fold(v):
    rows = v.shape[0]
    return jnp.sum(v.reshape(rows // 8, 8, v.shape[1]), axis=0)


def gelu_parts(x):
    phi = 0.5 + 0.5 * lax.erf(x * math.sqrt(0.5))
    density = jnp.exp2((x * x) * (-0.5 * LOG2E)) * (1.0 / math.sqrt(2.0 * math.pi))
    return x * phi, phi + x * density


def places(count, lanes, dim):
    at = lax.broadcasted_iota(jnp.int32, (count, lanes), dim).astype(F32)
    row = jnp.floor((at + 0.5) * (1.0 / GRID))
    return at - row * GRID, row


def offsets(kp, qp):
    kc, kr = places(kp, qp, 0)
    qc, qr = places(kp, qp, 1)
    a = kc - qc
    b = kr - qr
    return a, b, a * a + b * b


def head_mask(hd, h):
    lane = lax.broadcasted_iota(jnp.int32, (STRIP, 128), 1)
    return ((lane >= h * hd) & (lane < (h + 1) * hd)).astype(BF)


def in_tiles(own, oth):
    gap = jnp.zeros((own.shape[0], 128 - own.shape[1]), own.dtype)
    return jnp.concatenate([own, gap, oth, gap], axis=1)


def gate_of(hp_ref, h, lanes):
    return 1.0 / (1.0 + jnp.exp(-jnp.broadcast_to(hp_ref[h : h + 1, 3:4], (1, lanes))))


def bf_parts(value, count=3):
    parts = []
    for _ in range(count):
        part = value.astype(BF).astype(F32)
        parts.append(part)
        value = value - part
    return parts


def key_operand(kp):
    kc, kr = places(kp, 128, 0)
    lane = lax.broadcasted_iota(jnp.int32, (kp, 128), 1)
    value = jnp.where(lane < 3, kc, jnp.where(lane < 6, kr, jnp.where(lane < 9, kc * kc, kr * kr)))
    return jnp.where(lane < 12, value, 0.0).astype(BF)


def query_operand(hp_ref, h, qp):
    p = [LOG2E * jnp.broadcast_to(hp_ref[h : h + 1, at : at + 1], (16, qp)) for at in range(3)]
    qc, qr = places(16, qp, 1)
    row = lax.broadcasted_iota(jnp.int32, (16, qp), 0)
    value = jnp.where(row < 3, p[0] - 2.0 * p[2] * qc, jnp.where(row < 6, p[1] - 2.0 * p[2] * qr, p[2]))
    parts = bf_parts(value)
    place = row - 3 * ((row >= 3).astype(jnp.int32) + (row >= 6) + (row >= 9))
    value = jnp.where(place == 0, parts[0], jnp.where(place == 1, parts[1], parts[2]))
    return jnp.where(row < 12, value, jnp.where(row == 12, 1.0, 0.0)).astype(BF)


STRIP = 16
LAG = 3
WAIT = 3


def interleave(*streams):
    streams = [member for member in streams if member is not None]
    while streams:
        alive = []
        for member in streams:
            try:
                next(member)
                alive.append(member)
            except StopIteration:
                pass
        streams = alive


def staged(count, lag, *stages):
    for t in range(count + lag * (len(stages) - 1)):
        for k, stage in enumerate(stages):
            if 0 <= t - k * lag < count:
                stage(t - k * lag)
        yield


def slow(stream, count):
    for _ in range(count):
        yield
        try:
            next(stream)
        except StopIteration:
            return


def cut(value, r):
    return value[r * STRIP : (r + 1) * STRIP]


def rows_of(r):
    return pl.ds(r * STRIP, STRIP)


def put_planes(ref, value):
    width = value.shape[1]
    ref[0] = value[:, :128]
    ref[1, :, 0 : width - 128] = value[:, 128:]


def even_odd_tiles(ref, start, pairs):
    even = [ref[at, pl.ds(start, pairs, stride=2), :] for at in range(2)]
    odd = [ref[at, pl.ds(start + 1, pairs, stride=2), :] for at in range(2)]
    return (
        even[0],
        jnp.concatenate([even[1][:, :64], odd[0][:, :64]], axis=1),
        jnp.concatenate([odd[0][:, 64:], odd[1][:, :64]], axis=1),
    )


def four_row_tiles(ref, plane, start, groups):
    r = [ref[plane, pl.ds(start + at, groups, stride=4), :] for at in range(4)]
    return (
        jnp.concatenate([r[0][:, :96], r[1][:, :32]], axis=1),
        jnp.concatenate([r[1][:, 32:96], r[2][:, :64]], axis=1),
        jnp.concatenate([r[2][:, 64:96], r[3][:, :96]], axis=1),
    )


def pack_kernel(*refs):
    given, pack_ref, passed, held, sems = refs[:9], refs[9], refs[10:13], refs[13:19], refs[19]
    copies = [
        pltpu.make_async_copy(source, target, sems.at[at])
        for at, (source, target) in enumerate(zip(given, [*held, *passed]))
    ]
    for member in copies:
        member.start()
    for member in copies[:6]:
        member.wait()
    tri_ref, out_ref, wid_ref, nar_ref, hb_ref, hp_ref = held
    depth, wide = wid_ref.shape
    pack_ref[0:depth, :] = wid_ref[...].astype(BF)
    pack_ref[depth : 2 * depth, :] = nar_ref[...].astype(BF)
    pack_ref[2 * depth : 3 * depth, :] = jnp.concatenate(
        [tri_ref[0], tri_ref[1], tri_ref[2], out_ref[...].T], axis=1
    ).astype(BF)
    heads_here = hp_ref.shape[0]
    hp = jnp.concatenate([hp_ref[...], jnp.zeros((heads_here, wide - 4), F32)], axis=1)
    left = jnp.concatenate([hb_ref[...].reshape(1, wide), hp], axis=0)
    parts = []
    for _ in range(3):
        part = left.astype(BF).astype(F32)
        parts.append(part)
        left = left - part
    parts.append(jnp.zeros((16 - 3 * (1 + heads_here), wide), F32))
    pack_ref[3 * depth : 3 * depth + 16, :] = jnp.concatenate(parts, axis=0).astype(BF)
    for member in copies[6:]:
        member.wait()


def run_pack(tri, out, wid, nar_t, hb, hp_t, *passed):
    depth, wide = wid.shape
    given = (tri, out, wid, nar_t, hb, hp_t)
    return pl.pallas_call(
        pack_kernel,
        out_shape=(
            pltpu.VMEM((3 * depth + 16, wide), BF),
            *[pltpu.VMEM(member.shape, member.dtype) for member in passed],
        ),
        in_specs=[pl.BlockSpec(memory_space=pltpu.HBM)] * 9,
        out_specs=(VM,) * 4,
        scratch_shapes=[
            *[pltpu.VMEM(member.shape, member.dtype) for member in given],
            pltpu.SemaphoreType.DMA((9,)),
        ],
        compiler_params=PARAMS,
        name="pack_weights",
    )(*far(*given, *passed))


def prepare_kernel(tok_ref, cot_ref, keep_ref, x_ref, inc_ref, bias_ref, xs, cs):
    images, kp, width = x_ref.shape
    patches = keep_ref.shape[1]
    rows = images * patches
    qp = -(-patches // 128) * 128
    mine = keep_ref[pl.ds(pl.multiple_of(lax.axis_index("tensor") * images, 8), images), :].astype(F32)
    columns = jnp.concatenate([mine, jnp.zeros((images, qp - patches), F32)], axis=1).T
    xs[0:rows, :] = tok_ref[...].T.astype(F32)
    cs[0:rows, :] = cot_ref[...].T.astype(F32)
    xs[rows : rows + 16, :] = jnp.zeros((16, width), F32)
    cs[rows : rows + 16, :] = jnp.zeros((16, width), F32)
    for i in range(images):
        span = slice(i * patches, i * patches + kp)
        keep = jnp.broadcast_to(columns[:kp, i : i + 1], (kp, 128))
        keep_wide = jnp.concatenate([keep, keep[:, : width - 128]], axis=1)
        x_ref[i] = xs[span, :].astype(BF)
        inc_ref[i] = (cs[span, :] * keep_wide).astype(BF)
        bias_ref[i] = ((keep - 1.0) * 1e30).astype(BF)


def run_prepare(tok_t, cot_t, keep_mask):
    images = keep_mask.shape[0] // 2
    kp = -(-keep_mask.shape[1] // 16) * 16
    width, rows_here = tok_t.shape
    rows = pltpu.VMEM((images, kp, width), BF)
    return pl.pallas_call(
        prepare_kernel,
        out_shape=(rows, rows, pltpu.VMEM((images, kp, 128), BF)),
        in_specs=[VM] * 3,
        out_specs=(VM,) * 3,
        scratch_shapes=[pltpu.VMEM((rows_here + 16, width), F32)] * 2,
        compiler_params=PARAMS,
        name="prepare",
    )(*near(tok_t, cot_t, keep_mask))


def layer_kernel(*refs, patches, heads, data_count):
    (x_ref, inc_ref, bias_ref, own_ref, oth_ref, vec_ref) = refs[:6]
    far_refs = refs[6:11]
    gate_ref, hp_ref = refs[11:13]
    outs = refs[13:15] if data_count else refs[13:19]
    at = 13 + len(outs)
    (wq, wk, wv, wo, wop, wi, wn, hb_s, hp_s, key_p, key_i, query_p) = refs[at : at + 12]
    at += 12
    (fst_s, keys_s, vt_s, qm_s, dmm_s, v_s, kt_s, soft_s, mid_s, n2_s) = refs[at : at + 10]
    at += 10
    (sec_s, spr_s, low_s, stat_s, back_s) = refs[at : at + 5]
    at += 5
    (first_t, mix_t, left_t, right_s, gm_s, dp_s, s_buf, p_buf, att_buf) = refs[at : at + 9]
    at += 9
    (place_g, gate_g, da_buf, att_s, ds_s, wide_g, out_g, vec_g, hid_g, tri_p, sems) = refs[at : at + 11]
    at += 11
    if data_count:
        nar_p, out_p, tmp = refs[at : at + 3]
    images, kp, width = x_ref.shape
    qp = soft_s.shape[4]
    hd = width // heads
    half = width // 2
    half_heads = heads // 2
    wide = own_ref.shape[1]
    hidden = 2 * wide
    strips = kp // STRIP
    c_scale = LOG2E / math.sqrt(hd)
    back_scale = 1.0 / math.sqrt(hd)
    v = [vec_ref[k : k + 1, :] for k in range(6)]

    key_p[...] = key_operand(kp)
    query_p[...] = jnp.zeros_like(query_p)
    for ref in (hid_g, vec_g, place_g, gate_g):
        ref[...] = jnp.zeros_like(ref)
    for k in range(2):
        att_buf[k, kp:, :] = jnp.zeros((qp - kp, qp), BF)
    for k in range(2):
        fst_s[k, kp:, :] = jnp.zeros((qp - kp, width), BF)
    for k in range(images):
        for side in range(2):
            right_s[side, k * qp + kp : (k + 1) * qp, :] = jnp.zeros((qp - kp, hidden), BF)
        for c in range(3):
            dp_s[c, k * qp + kp : (k + 1) * qp, :] = jnp.zeros((qp - kp, 256), BF)
    gap = jnp.zeros((qp - kp, width), BF)
    one_lane = (lax.broadcasted_iota(jnp.int32, (STRIP, 128), 1) == half).astype(BF)
    masks = [head_mask(hd, h) for h in range(half_heads)]
    tiles = [slice(128 * t, 128 * (t + 1)) for t in range(2)]
    bias_lane = (lax.broadcasted_iota(jnp.int32, (kp, 128), 1) == 12).astype(BF)

    def columns_at(i):
        return pl.ds(pl.multiple_of(i * qp, 128), qp)


    def first_norm(i):
        kept = {}

        def mean(r):
            x = x_ref[i, rows_of(r), :].astype(F32)
            kept[r] = x - jnp.sum(x, axis=-1, keepdims=True) * (1.0 / width)

        def spread(r):
            kept[r] = (kept[r], jnp.sum(kept[r] * kept[r], axis=-1, keepdims=True) * (1.0 / width))

        def put(r):
            centred, variance = kept[r]
            fst_s[i % 2, rows_of(r), :] = (centred * lax.rsqrt(variance + EPS_NORM) * v[0] + v[1]).astype(BF)

        yield from staged(strips, LAG, mean, spread, put)

    def project(i, part):
        first_q = fst_s[i % 2]
        if part == 0:
            queries = nn(first_q, wq[...]).astype(BF)
            yield
            for r in range(qp // STRIP):
                for h in range(heads):
                    tile = cut(queries[:, tiles[h // half_heads]], r)
                    qm_s[i, h, rows_of(r), :] = tile * masks[h % half_heads] + one_lane
                yield
        elif part == 1:
            keys = nn(first_q, wk[...]).astype(BF)
            yield
            for r in range(strips):
                bias = bias_ref[i, rows_of(r), :]
                key_i[rows_of(r), :] = key_p[rows_of(r), :] + bias * cut(bias_lane, r)
                for t in range(2):
                    keys_s[rows_of(r), tiles[t]] = cut(keys[:, tiles[t]], r) + bias * one_lane
                yield
            kt_s[i] = keys.T
            yield
        else:
            values = nn(first_q, wv[...]).astype(BF)
            yield
            v_s[i] = values[:kp]
            vt_s[...] = values.T
            yield
            yield
            first_t[:, columns_at(i)] = first_q.T
            yield

    def head_rows(h):
        first_row = 128 * (h // half_heads) + hd * (h % half_heads)
        return slice(first_row, first_row + hd)


    def scores(i, h):
        s = nt(keys_s[:, tiles[h // half_heads]], qm_s[i, h])
        p = nn(key_i[...], query_p[h])
        m, pm = cut(s, 0), cut(p, 0)
        for r in range(strips):
            yield
            s_buf[h, rows_of(r), :] = cut(s, r)
            p_buf[h, rows_of(r), :] = cut(p, r)
            m = jnp.maximum(m, cut(s, r))
            pm = jnp.maximum(pm, cut(p, r))
        stat_s[4 * h : 4 * h + 1, :] = jnp.max(m, axis=0, keepdims=True)
        stat_s[4 * h + 1 : 4 * h + 2, :] = jnp.max(pm, axis=0, keepdims=True)

    def exponents(h):
        m, pm = stat_s[4 * h : 4 * h + 1, :], stat_s[4 * h + 1 : 4 * h + 2, :]
        z = jnp.zeros((STRIP, qp), F32)
        pz = jnp.zeros((STRIP, qp), F32)
        for r in range(strips):
            yield
            e = jnp.exp2((s_buf[h, rows_of(r), :] - m) * c_scale)
            pe = jnp.exp2(p_buf[h, rows_of(r), :] - pm)
            s_buf[h, rows_of(r), :] = e
            p_buf[h, rows_of(r), :] = pe
            z = z + e
            pz = pz + pe
        gate = gate_of(hp_s, h, qp)
        stat_s[4 * h + 2 : 4 * h + 3, :] = (1.0 - gate) / jnp.sum(z, axis=0, keepdims=True)
        stat_s[4 * h + 3 : 4 * h + 4, :] = gate / jnp.sum(pz, axis=0, keepdims=True)

    def mixing(i, h):
        a, b = stat_s[4 * h + 2 : 4 * h + 3, :], stat_s[4 * h + 3 : 4 * h + 4, :]
        for r in range(strips):
            yield
            content = s_buf[h, rows_of(r), :] * a
            located = p_buf[h, rows_of(r), :] * b
            soft_s[i, h, 0, rows_of(r), :] = content
            soft_s[i, h, 1, rows_of(r), :] = located
            att_buf[h % 2, rows_of(r), :] = (content + located).astype(BF)
        yield
        mix_t[h * hd : (h + 1) * hd, columns_at(i)] = nn(
            vt_s[head_rows(h), :], att_buf[h % 2]
        ).astype(BF)


    def strip_rows(i, r):
        return pl.ds(pl.multiple_of(i * qp + r * STRIP, 16), STRIP)

    def image_rows(i):
        return pl.ds(pl.multiple_of(i * qp, 16), kp)

    def start(i):
        attn = nt(mix_t[:, columns_at(i)].T[:kp], wo[...])
        for _ in range(WAIT + 2):
            yield
        kept = {}

        def mean(r):
            middle = x_ref[i, rows_of(r), :].astype(F32) + cut(attn, r) + v[4]
            mid_s[i, rows_of(r), :] = middle
            kept[r] = middle - jnp.sum(middle, axis=-1, keepdims=True) * (1.0 / width)

        def vary(r):
            kept[r] = (kept[r], jnp.sum(kept[r] * kept[r], axis=-1, keepdims=True) * (1.0 / width))

        def put(r):
            centred, variance = kept[r]
            spread = lax.rsqrt(variance + EPS_NORM)
            n2 = centred * spread
            n2_s[rows_of(r), :] = n2
            spr_s[rows_of(r), :] = spread
            sec_s[rows_of(r), :] = (n2 * v[2] + v[3]).astype(BF)

        yield from staged(strips, LAG, mean, vary, put)
        left_t[0, :, columns_at(i)] = jnp.concatenate([inc_ref[i], gap], axis=0).T
        yield
        left_t[1, :, columns_at(i)] = jnp.concatenate([sec_s[...], gap], axis=0).T

    def chunk(i, c, on):
        lanes = pl.ds(c * 256, 256)
        before = nn(sec_s[...], wi[:, lanes])
        back = nn(inc_ref[i], wn[:, lanes])
        bias_row = hb_s[0:1, lanes]
        total = jnp.zeros((8, 256), F32)
        for r in range(strips):
            yield
            gelu, slope = gelu_parts(cut(before, r) + bias_row)
            right_s[0, strip_rows(i, r), lanes] = gelu.astype(BF)
            grad_before = cut(back, r) * slope
            right_s[1, strip_rows(i, r), lanes] = grad_before.astype(BF)
            total = total + fold(grad_before)
        hid_g[:, lanes] += jnp.where(on, total, 0.0)

    def end(i, on):
        grad_second = nt(right_s[1, image_rows(i), :], wi[...])
        totals = [jnp.zeros((8, width), F32)] * 4
        mids = []
        for _ in range(WAIT):
            yield
        kept = {}

        def means(r):
            n2 = n2_s[rows_of(r), :]
            g = cut(grad_second, r)
            e = g * v[2]
            mean_e = jnp.sum(e, axis=-1, keepdims=True) * (1.0 / width)
            mean_en = jnp.sum(e * n2, axis=-1, keepdims=True) * (1.0 / width)
            kept[r] = (e, mean_e, mean_en)
            for k, term in enumerate((g * n2, g)):
                totals[k] = totals[k] + fold(term)

        def put(r):
            e, mean_e, mean_en = kept[r]
            n2 = n2_s[rows_of(r), :]
            incoming = inc_ref[i, rows_of(r), :].astype(F32)
            spread = spr_s[rows_of(r), :]
            grad_middle = incoming + spread * (e - mean_e - n2 * mean_en)
            gm_s[i, rows_of(r), :] = grad_middle
            mids.append(grad_middle.astype(BF))
            for k, term in enumerate((grad_middle, incoming)):
                totals[2 + k] = totals[2 + k] + fold(term)

        yield from staged(strips, LAG, means, put)
        for k in range(4):
            vec_g[k] += jnp.where(on, totals[k], 0.0)
        mid_low = jnp.concatenate([*mids, gap], axis=0)
        yield
        dm = nn(mid_low, wop[...]).astype(BF)
        for r in range(qp // STRIP):
            yield
            for h in range(heads):
                tile = cut(dm[:, tiles[h // half_heads]], r)
                dmm_s[i, h, rows_of(r), :] = tile * masks[h % half_heads]
        yield
        low_s[pl.ds(pl.multiple_of(i * qp, 16), qp), :] = mid_low

    blocks = hidden // 256

    def forward_step(i, carry):
        one, two = jnp.maximum(i - 1, 0), jnp.maximum(i - 2, 0)
        after = jnp.minimum(i + 1, images - 1)
        on_one, on_two = i > 0, i > 1
        interleave(scores(i, 0), exponents(3), mixing(one, 2), chunk(two, 1, on_two), first_norm(after))
        interleave(scores(i, 1), exponents(0), mixing(one, 3), chunk(two, 2, on_two))
        interleave(
            scores(i, 2),
            exponents(1),
            mixing(i, 0),
            end(two, on_two),
            start(one),
            project(i, 2),
        )
        interleave(
            scores(i, 3),
            exponents(2),
            mixing(i, 1),
            chunk(one, 0, on_one),
            project(after, 0),
            project(after, 1),
        )
        return carry

    interleave(first_norm(0))
    wi[:, pl.ds(0, wide)] = own_ref[0:width, :]
    wi[:, pl.ds(wide, wide)] = oth_ref[0:width, :]
    wn[:, pl.ds(0, wide)] = own_ref[width : 2 * width, :]
    wn[:, pl.ds(wide, wide)] = oth_ref[width : 2 * width, :]
    own_tri = own_ref[2 * width : 3 * width, :]
    oth_tri = oth_ref[2 * width : 3 * width, :]
    for k, w in enumerate((wq, wk, wv, wop)):
        lanes = slice(k * half, (k + 1) * half)
        w[...] = in_tiles(own_tri[:, lanes], oth_tri[:, lanes])
    wo[...] = jnp.concatenate([own_tri[:, 3 * half :], oth_tri[:, 3 * half :]], axis=1)
    small = []
    for ref in (own_ref, oth_ref):
        tail = ref[3 * width : 3 * width + 16, :].astype(F32)
        each = 1 + half_heads
        small.append(tail[0:each] + tail[each : 2 * each] + tail[2 * each : 3 * each])
    hb_s[0:1, :] = jnp.concatenate([member[0:1] for member in small], axis=1)
    hp_s[...] = jnp.concatenate(
        [member[1:, :128] for member in small] + [jnp.zeros((8 - heads, 128), F32)], axis=0
    )
    for h in range(heads):
        query_p[h, 0:16, :] = query_operand(hp_s, h, qp)
    for part in range(2):
        interleave(project(0, part))
    def forward_pair(j, carry):
        return forward_step(2 * j + 1, forward_step(2 * j, carry))

    lax.fori_loop(0, images // 2, forward_pair, 0)


    def back_scores(i, h):
        da = nt(v_s[i, :, tiles[h // half_heads]], dmm_s[i, h])
        rc = jnp.zeros((STRIP, qp), F32)
        rl = jnp.zeros((STRIP, qp), F32)
        for r in range(strips):
            yield
            part = cut(da, r)
            da_buf[h % 2, rows_of(r), :] = part
            rc = rc + soft_s[i, h, 0, rows_of(r), :] * part
            rl = rl + soft_s[i, h, 1, rows_of(r), :] * part
        gate = gate_of(hp_s, h, qp)
        rc = jnp.sum(rc, axis=0, keepdims=True) / (1.0 - gate)
        rl = jnp.sum(rl, axis=0, keepdims=True) / gate
        back_s[2 * h : 2 * h + 1, :] = rc
        back_s[2 * h + 1 : 2 * h + 2, :] = rl
        gate_g[h : h + 1, :] += rl - rc

    def back_spread(i, h):
        rc, rl = back_s[2 * h : 2 * h + 1, :], back_s[2 * h + 1 : 2 * h + 2, :]
        lanes = pl.ds(h * qp, qp)
        for r in range(strips):
            yield
            rows = rows_of(r)
            c = soft_s[i, h, 0, rows, :]
            l = soft_s[i, h, 1, rows, :]
            part = da_buf[h % 2, rows, :]
            ds_s[rows, lanes] = (c * (part - rc)).astype(BF)
            att_s[rows, lanes] = (c + l).astype(BF)
            place_g[h, rows, :] += l * (part - rl)

    def products(i, t):
        lanes = slice(t * half_heads * qp, (t + 1) * half_heads * qp)
        heads_in = slice(t * half_heads, (t + 1) * half_heads)
        dk = nn(ds_s[:, lanes], qm_s[i, heads_in].reshape(half_heads * qp, 128))
        dv = nn(att_s[:, lanes], dmm_s[i, heads_in].reshape(half_heads * qp, 128))
        yield
        pad = jnp.zeros((qp - kp, qp), BF)
        dq_t = []
        for h in range(t * half_heads, (t + 1) * half_heads):
            ds = jnp.concatenate([ds_s[:, h * qp : (h + 1) * qp], pad], axis=0)
            dq_t.append(nn(kt_s[i, head_rows(h), :], ds))
        yield
        dp_s[1, image_rows(i), tiles[t]] = (dk * back_scale).astype(BF)
        yield
        dp_s[2, image_rows(i), tiles[t]] = dv.astype(BF)
        yield
        dq_t.append(jnp.zeros((128 - half, qp), F32))
        dq = (jnp.concatenate(dq_t, axis=0) * back_scale).astype(BF)
        dp_s[0, image_rows(i), tiles[t]] = dq.T[:kp]

    cut_at = (images - 2) * qp
    spans = (slice(0, cut_at), slice(cut_at, images * qp))

    def weight_gradient(unit, part):
        side = unit // blocks
        lanes = slice((unit % blocks) * 256, (unit % blocks) * 256 + 256)
        value = nn(left_t[side, :, spans[part]], right_s[side, spans[part], lanes])
        yield
        if part:
            wide_g[side, :, lanes] += value
        else:
            wide_g[side, :, lanes] = value

    def outward_gradient(part):
        value = nn(mix_t[:, spans[part]], low_s[spans[part], :])
        yield
        if part:
            out_g[...] += value
        else:
            out_g[...] = value

    def triple_gradient(c, part):
        value = nn(first_t[:, spans[part]], dp_s[c, spans[part], :])
        yield
        rows = pl.ds(c * width, width)
        for t in range(2):
            if part:
                tri_p[t, rows, :] += value[:, tiles[t]]
            else:
                tri_p[t, rows, :] = value[:, tiles[t]]

    last = images - 1
    on = True
    partial = [weight_gradient(unit, 0) for unit in range(2 * blocks)] + [outward_gradient(0)]
    interleave(
        exponents(3), mixing(last, 2), chunk(last - 1, 1, on), back_scores(0, 0), partial[0]
    )
    interleave(
        mixing(last, 3),
        chunk(last - 1, 2, on),
        back_scores(0, 1),
        back_spread(0, 0),
        partial[1],
    )
    interleave(
        end(last - 1, on), start(last), back_scores(0, 2), back_spread(0, 1), partial[2]
    )
    interleave(chunk(last, 0, on), back_scores(0, 3), back_spread(0, 2), partial[3])
    interleave(chunk(last, 1, on), back_spread(0, 3), partial[4])
    interleave(chunk(last, 2, on), products(0, 0), partial[5])
    interleave(end(last, on), products(0, 1), *partial[6:])

    def send(slots, *sources):
        copies = [
            pltpu.make_async_copy(source, far_refs[k], sems.at[k])
            for k, source in zip(slots, sources)
        ]
        for member in copies:
            member.start()
        return copies

    sent = send((0, 1, 2), right_s.at[0], mid_s, gm_s)


    def piece_of(r, side):
        return outs[0].at[r] if side == 0 else tmp.at[r % 4]

    def early_chunks():
        put_planes(nar_p, wide_g[0].T)
        yield
        put_planes(out_p, out_g[...])
        early = jnp.sum(vec_g[...], axis=1)
        hidden_sum = jnp.sum(hid_g[...], axis=0, keepdims=True)
        rest = width - 128
        wp, np_, op = width // data_count, wide // data_count // 2, half // data_count // 2
        small_at = 3 * (wp + np_ + op)
        for r in range(data_count):
            for side in range(2):
                yield
                piece = piece_of(r, side)
                for k in range(3):
                    lanes = slice(side * wide + 128 * k, side * wide + 128 * (k + 1))
                    piece[k * wp : (k + 1) * wp, :] = wide_g[1, r * wp : (r + 1) * wp, lanes]
                    piece[small_at + 8 + k : small_at + 9 + k, :] = hidden_sum[:, lanes]
                base = 3 * wp
                parts = even_odd_tiles(nar_p, side * wide + 2 * np_ * r, np_)
                for k in range(3):
                    piece[base + k * np_ : base + (k + 1) * np_, :] = parts[k]
                base += 3 * np_
                parts = even_odd_tiles(out_p, side * half + 2 * op * r, op)
                for k in range(3):
                    piece[base + k * op : base + (k + 1) * op, :] = parts[k]
                piece[small_at : small_at + 4, :] = early[:, :128]
                piece[small_at + 4 : small_at + 8, 0:rest] = early[:, 128:]
                piece[small_at + 4 : small_at + 8, rest:] = jnp.zeros((4, 128 - rest), F32)
                piece[small_at + 11 : EARLY_ROWS, :] = jnp.zeros(
                    (EARLY_ROWS - small_at - 11, 128), F32
                )
                if side:
                    outs[1][r, 0:EARLY_ROWS, :] = piece[0:EARLY_ROWS, :].astype(BF)

    def late_chunks():
        groups = 3 * width // data_count // 4
        for r in range(data_count):
            for side in range(2):
                yield
                piece = piece_of(r, side)
                parts = four_row_tiles(tri_p, side, 4 * groups * r, groups)
                for k in range(3):
                    row = EARLY_ROWS + k * groups
                    piece[row : row + groups, :] = parts[k]
                row = EARLY_ROWS + 3 * groups
                piece[row:CHUNK_ROWS, :] = jnp.zeros((CHUNK_ROWS - row, 128), F32)
                if side:
                    outs[1][r, EARLY_ROWS:, :] = piece[EARLY_ROWS:, :].astype(BF)

    chunking = early_chunks() if data_count else iter(())
    for i in range(1, images):
        before = i > 1
        done = i == last
        interleave(
            back_scores(i, 0),
            back_spread(i - 1, 3) if before else None,
            outward_gradient(1) if i == 1 else None,
        )
        interleave(
            back_scores(i, 1),
            products(i - 1, 0) if before else None,
            back_spread(i, 0),
        )
        interleave(
            back_scores(i, 2),
            products(i - 1, 1) if before else None,
            back_spread(i, 1),
        )
        interleave(
            back_scores(i, 3),
            back_spread(i, 2),
            weight_gradient(i - 1, 1) if i <= 2 * blocks else None,
        )
    for unit in range(last, 2 * blocks):
        interleave(weight_gradient(unit, 1))
    interleave(back_spread(last, 3), *[triple_gradient(c, 0) for c in range(3)])
    interleave(products(last, 0), products(last, 1))
    interleave(chunking)
    sent += send((3, 4), dp_s, place_g)
    gate_ref[...] = gate_g[...]
    hp_ref[...] = hp_s[...]
    for c in range(3):
        interleave(triple_gradient(c, 1))
    if data_count:
        interleave(late_chunks())
    else:
        outs[0][...] = wide_g[0].T
        outs[1][...] = wide_g[1]
        outs[2][...] = out_g[...]
        outs[3][...] = vec_g[...]
        outs[4][...] = hid_g[...]
        for c in range(3):
            rows = pl.ds(c * width, width)
            outs[5][rows, :] = jnp.concatenate(
                [tri_p[0, rows, 0:half], tri_p[1, rows, 0:half]], axis=1
            )
    for member in sent:
        member.wait()


def run_layer(x, inc, bias, own, oth, vec, heads, patches, data_count):
    images, kp, width = x.shape
    qp = -(-patches // 128) * 128
    hidden = 2 * own.shape[1]
    full = images * qp
    if data_count:
        outs = [
            pltpu.VMEM((data_count, CHUNK_ROWS, 128), F32),
            pltpu.VMEM((data_count, CHUNK_ROWS, 128), BF),
        ]
    else:
        outs = [
            sds(hidden, width),
            sds(width, hidden),
            sds(width, width),
            sds(4, 8, width),
            sds(8, hidden),
            sds(3 * width, width),
        ]

    def bf(*dims):
        return pltpu.VMEM(dims, BF)

    def f32(*dims):
        return pltpu.VMEM(dims, F32)

    scratch = [
        *[bf(width, 256)] * 3,
        bf(width, width),
        bf(width, 256),
        bf(width, hidden),
        bf(width, hidden),
        f32(8, hidden),
        f32(8, 128),
        bf(kp, 128),
        bf(kp, 128),
        bf(heads, 128, qp),
        bf(2, qp, width),
        bf(kp, 256),
        bf(256, qp),
        bf(images, heads, qp, 128),
        bf(images, heads, qp, 128),
        bf(images, kp, 256),
        bf(images, 256, qp),
        f32(images, heads, 2, kp, qp),
        f32(images, kp, width),
        f32(kp, width),
        bf(kp, width),
        f32(kp, 1),
        bf(full, width),
        f32(4 * heads, qp),
        f32(2 * heads, qp),
        bf(width, full),
        bf(width, full),
        bf(2, width, full),
        bf(2, full, hidden),
        f32(images, kp, width),
        bf(3, full, 256),
        f32(heads, kp, qp),
        f32(heads, kp, qp),
        bf(2, qp, qp),
        f32(heads, kp, qp),
        f32(8, qp),
        f32(2, kp, qp),
        bf(kp, heads * qp),
        bf(kp, heads * qp),
        f32(2, width, hidden),
        f32(width, width),
        f32(4, 8, width),
        f32(8, hidden),
        f32(2, 3 * width, 128),
        pltpu.SemaphoreType.DMA((5,)),
    ]
    if data_count:
        scratch += [f32(2, hidden, 128), f32(2, width, 128)]
        scratch.append(f32(4, CHUNK_ROWS, 128))
    return pl.pallas_call(
        functools.partial(layer_kernel, patches=patches, heads=heads, data_count=data_count),
        out_shape=(
            sds(full, hidden, dtype=BF),
            sds(images, kp, width),
            sds(images, kp, width),
            sds(3, full, 256, dtype=BF),
            sds(heads, kp, qp),
            pltpu.VMEM((8, qp), F32),
            pltpu.VMEM((8, 128), F32),
            *outs,
        ),
        in_specs=[VM] * 6,
        out_specs=(ANYWHERE,) * 5 + (VM,) * (2 + len(outs)),
        scratch_shapes=scratch,
        compiler_params=pltpu.CompilerParams(vmem_limit_bytes=LAYER_VMEM),
        name="layer",
    )(*near(x, inc, bias, own, oth), vec)


def finish_kernel(*refs, patches, heads):
    (x_ref, own_ref, oth_ref, vec_ref, gate_ref, hp_ref), far_refs = refs[:6], refs[6:11]
    (res_out, gi_out, vec_out, head_ref) = refs[11:15]
    (act_s, mid_s, gm_s, dp_s, place_s), (w, wn, vec_g, rows_s, sems) = refs[15:20], refs[20:]
    images, kp, width = x_ref.shape
    qp = dp_s.shape[1] // images
    half = width // 2
    wide = own_ref.shape[1]
    copies = [
        pltpu.make_async_copy(source, target, sems.at[at])
        for at, (source, target) in enumerate(
            zip(far_refs, (act_s, mid_s, gm_s, dp_s, place_s))
        )
    ]
    for member in copies:
        member.start()
    own_tri = own_ref[2 * width : 3 * width, :]
    oth_tri = oth_ref[2 * width : 3 * width, :]
    for at in range(3):
        span = slice(at * half, (at + 1) * half)
        w[at] = in_tiles(own_tri[:, span], oth_tri[:, span])
    wn[:, 0:wide] = own_ref[width : 2 * width, :]
    wn[:, wide : 2 * wide] = oth_ref[width : 2 * width, :]
    vec_g[...] = jnp.zeros_like(vec_g)
    gain = vec_ref[0:1, :]
    shift = vec_ref[5:6, :]
    for member in copies[:2]:
        member.wait()
    for i in range(images):
        rows = mid_s[i] + nt(act_s[i * qp : i * qp + kp, :], wn[...]) + shift
        rows_s[i * patches : (i + 1) * patches, :] = rows[0:patches]
    res_out[...] = rows_s[...].T
    for member in copies[2:]:
        member.wait()
    for i in range(images):
        n1, spread = norm_parts(x_ref[i].astype(F32))
        g = sum(nt(dp_s[c, i * qp : i * qp + kp, :], w[c]) for c in range(3))
        vec_g[0] += fold(g * n1)
        vec_g[1] += fold(g)
        rows = gm_s[i] + norm_back(g * gain, n1, spread)
        rows_s[i * patches : (i + 1) * patches, :] = rows[0:patches]
    gi_out[...] = rows_s[...].T
    vec_out[...] = jnp.sum(vec_g[...], axis=1)
    parts = offsets(kp, qp)
    rank = lax.axis_index("tensor")
    lane = lax.broadcasted_iota(jnp.int32, (1, 128), 1)
    row = jnp.zeros((1, 128), F32)
    half_heads = heads // 2
    for h in range(heads):
        base = ((rank + h // half_heads) % 2) * (4 * half_heads) + h % half_heads
        g = place_s[h]
        for k in range(3):
            total = jnp.sum(g * parts[k])
            row = row + jnp.where(lane == base + k * half_heads, total, 0.0)
        gate = gate_of(hp_ref, h, 128)
        total = jnp.sum(gate_ref[h : h + 1, :])
        row = row + jnp.where(lane == base + 3 * half_heads, total * gate * (1.0 - gate), 0.0)
    head_ref[...] = row


def run_finish(x, own, oth, vec, gate, hp, act, mid, gm, dp, place, patches):
    images, kp, width = x.shape
    rows = images * patches
    fetched = (act, mid, gm, dp, place)
    return pl.pallas_call(
        functools.partial(finish_kernel, patches=patches, heads=place.shape[0]),
        out_shape=(sds(width, rows), sds(width, rows), sds(2, width), sds(1, 128)),
        in_specs=[VM] * 6 + [ANYWHERE] * 5,
        out_specs=(VM,) * 4,
        scratch_shapes=[
            *[pltpu.VMEM(member.shape, member.dtype) for member in fetched],
            pltpu.VMEM((3, width, 256), BF),
            pltpu.VMEM((width, 2 * own.shape[1]), BF),
            pltpu.VMEM((2, 8, width), F32),
            pltpu.VMEM((rows, width), F32),
            pltpu.SemaphoreType.DMA((5,)),
        ],
        compiler_params=pltpu.CompilerParams(vmem_limit_bytes=32 * 1024 * 1024),
        name="finish",
    )(*near(x, own, oth), vec, gate, hp, *far(*fetched))


def combine_kernel(own_ref, got_ref, out_ref):
    out_ref[...] = (own_ref[...] + got_ref[...].astype(F32)).astype(BF)


def run_combine(own, got):
    return pl.pallas_call(
        combine_kernel,
        out_shape=pltpu.VMEM(own.shape, BF),
        in_specs=[VM] * 2,
        out_specs=VM,
        compiler_params=PARAMS,
        name="combine",
    )(*near(own, got))


def pick_rows(ref, start, count, flip=False):
    total = ref.shape[1] if flip else ref.shape[0]
    row = lax.broadcasted_iota(jnp.int32, (count, total), 0) + start
    col = lax.broadcasted_iota(jnp.int32, (count, total), 1)
    chosen = (row == col).astype(F32)
    return lax.dot_general(
        chosen,
        ref[...],
        (((1,), (1 if flip else 0,)), ((), ())),
        preferred_element_type=F32,
        precision=lax.Precision.HIGHEST,
    )


def share_kernel(_, tri_ref, out_ref, wid_ref, nar_ref, *refs, data_count):
    (wt_f, wo_f, ww_f, wn_f, st, so, sw, sn) = refs
    width, wide = wid_ref.shape
    half = out_ref.shape[0]
    wp, np_, op = width // data_count, wide // data_count // 2, half // data_count // 2
    data_rank = lax.axis_index("dp")
    groups = tri_ref.shape[0] // data_count // 4
    st[0, :, 0 : tri_ref.shape[1]] = pick_rows(tri_ref, data_rank * 4 * groups, 4 * groups)
    put_planes(so, pick_rows(out_ref, data_rank * 2 * op, 2 * op))
    sw[...] = pick_rows(wid_ref, data_rank * wp, wp)
    put_planes(sn, pick_rows(nar_ref, data_rank * 2 * np_, 2 * np_, flip=True))
    tiles = four_row_tiles(st, 0, 0, groups)
    for p in range(groups):
        for k in range(3):
            tile = 128 * (3 * p + k)
            wt_f[0:1, tile : tile + 128] = tiles[k][p : p + 1, :]
    for ref, flat, pairs in ((so, wo_f, op), (sn, wn_f, np_)):
        tiles = even_odd_tiles(ref, 0, pairs)
        for p in range(pairs):
            for k in range(3):
                tile = 128 * (3 * p + k)
                flat[0:1, tile : tile + 128] = tiles[k][p : p + 1, :]
    for p in range(wp):
        ww_f[0:1, wide * p : wide * (p + 1)] = sw[p : p + 1, :]


def run_shares(after, tri, out, wid, nar_t, data_count):
    wide = wid.shape[1]
    share = [member.shape[0] // data_count for member in (tri, out, wid)]
    return pl.pallas_call(
        functools.partial(share_kernel, data_count=data_count),
        out_shape=tuple(sds(1, member.size // data_count) for member in (tri, out, wid, nar_t)),
        in_specs=[VM] * 5,
        out_specs=(VM,) * 4,
        scratch_shapes=[
            pltpu.VMEM((1, share[0], 128), F32),
            pltpu.VMEM((2, share[1], 128), F32),
            pltpu.VMEM((share[2], wide), F32),
            pltpu.VMEM((2, wide // data_count, 128), F32),
        ],
        compiler_params=PARAMS,
        name="weight_shares",
    )(after, tri, out, wid, nar_t)


def spread_rows(flat_ref, from_ref, base, blocks):
    for p in range(blocks):
        for k in range(3):
            at = base + k * blocks + p
            tile = 128 * (3 * p + k)
            flat_ref[0:1, tile : tile + 128] = from_ref[at : at + 1, :]


def sum_kernel(got_ref, late_ref, head_ref, _, *refs, blocks):
    (tri_f, out_f, wid_f, nar_f, vec_ref, hid_ref, pay_ref, tot) = refs
    width = late_ref.shape[1]
    tri_b, out_b, wid_b, nar_b = blocks
    tot[...] = jnp.sum(got_ref[...].astype(F32), axis=0)
    spread_rows(wid_f, tot, 0, wid_b)
    spread_rows(nar_f, tot, 3 * wid_b, nar_b)
    spread_rows(out_f, tot, 3 * (wid_b + nar_b), out_b)
    spread_rows(tri_f, tot, EARLY_ROWS, tri_b)
    at = 3 * (wid_b + nar_b + out_b)
    vec_ref[...] = jnp.concatenate(
        [tot[at : at + 4, :], tot[at + 4 : at + 8, : width - 128]], axis=1
    )
    hid = jnp.concatenate([tot[at + 8 + k : at + 9 + k, :] for k in range(3)], axis=1)
    hid_ref[...] = hid
    early = tot[0:at, :]
    late = tot[EARLY_ROWS : EARLY_ROWS + 3 * tri_b, :]
    squares = jnp.sum(early * early) + jnp.sum(late * late)
    squares = squares + jnp.where(lax.axis_index("dp") == 0, jnp.sum(hid * hid), 0.0)
    lane = lax.broadcasted_iota(jnp.int32, (1, 128), 1)
    tails = jnp.concatenate([late_ref[0:1, 128:], late_ref[1:2, 128:]], axis=1)
    payload = jnp.concatenate(
        [late_ref[:, :128], tails, jnp.where(lane == 127, squares, head_ref[...])], axis=0
    )
    pay_ref[...] = jnp.broadcast_to(payload[None], pay_ref.shape)


def run_sums(got, late_vec, head, after, blocks, wide):
    count = got.shape[0]
    width = late_vec.shape[1]
    return pl.pallas_call(
        functools.partial(sum_kernel, blocks=blocks),
        out_shape=(
            *[sds(1, 3 * 128 * member) for member in blocks],
            sds(4, width),
            sds(1, wide),
            sds(2 * count, 4, 128),
        ),
        in_specs=[VM] * 4,
        out_specs=(VM,) * 7,
        scratch_shapes=[pltpu.VMEM((CHUNK_ROWS, 128), F32)],
        compiler_params=PARAMS,
        name="sums",
    )(got, late_vec, head, after)


def adam_parts(weight, gradient, moment, squares, rate, decay):
    moment_new = BETA_ONE * moment + (1.0 - BETA_ONE) * gradient
    squares_new = BETA_TWO * squares + (1.0 - BETA_TWO) * gradient * gradient
    quotient = (moment_new / (1.0 - BETA_ONE**STEP)) / (
        jnp.sqrt(squares_new / (1.0 - BETA_TWO**STEP)) + ADAM_EPS
    )
    return moment_new, squares_new, weight - rate * (quotient + decay * weight)


def adam_kernel(got_ref, early_ref, hid_ref, hp_ref, vec_ref, hb_ref, *refs):
    grads = refs[0:4]
    weights = refs[4:8]
    states = refs[8:22]
    outs = refs[22:43]
    norm_ref = refs[43]
    width = vec_ref.shape[1]
    half_heads = hp_ref.shape[0]
    tail = width - 128
    total = jnp.sum(got_ref[...], axis=0)
    late = jnp.concatenate(
        [
            total[0:2, :],
            jnp.concatenate([total[2:3, :tail], total[2:3, tail : 2 * tail]], axis=0),
        ],
        axis=1,
    )
    vector = jnp.concatenate([late, early_ref[...]], axis=0)
    lane = lax.broadcasted_iota(jnp.int32, (1, 128), 1)
    heads_row = jnp.where(lane < 8 * half_heads, total[3:4, :], 0.0)
    squares = (
        jnp.sum(jnp.where(lane == 127, total[3:4, :], 0.0))
        + jnp.sum(vector * vector)
        + jnp.sum(heads_row * heads_row)
    )
    norm = jnp.sqrt(jnp.full((1, 128), squares))
    norm_ref[0] = jnp.sum(norm[:, 0:1])
    factor = (CLIP_AT / jnp.maximum(norm, CLIP_AT))[:, 0:1]
    span = 4 * half_heads
    mine = jnp.where(lax.axis_index("tensor") == 0, heads_row[:, :span], heads_row[:, span : 2 * span])
    head = jnp.concatenate(
        [
            jnp.concatenate(
                [mine[:, c * half_heads + h : c * half_heads + h + 1] for c in range(4)], axis=1
            )
            for h in range(half_heads)
        ],
        axis=0,
    )
    given = [ref[...] for ref in grads] + [vector, hid_ref[...], head]
    wide = hid_ref.shape[1]
    held = [ref[...] for ref in weights] + [vec_ref[...], hb_ref[...].reshape(1, wide), hp_ref[...]]
    for at in range(7):
        renewed = adam_parts(
            held[at],
            given[at] * factor,
            states[2 * at][...].reshape(held[at].shape),
            states[2 * at + 1][...].reshape(held[at].shape),
            RATES[at],
            DECAYS[at],
        )
        for step in range(3):
            out = outs[3 * at + step]
            out[...] = renewed[step].reshape(out.shape)


def run_adam(got, early, hid, hp_t, vec, hb, grads, weights, states):
    shapes = []
    for at in range(7):
        shapes += [sds(*states[2 * at].shape)] * 3
    return pl.pallas_call(
        adam_kernel,
        out_shape=(*shapes, sds(1)),
        in_specs=[VM] * (6 + 4 + 4 + 14),
        out_specs=(VM,) * 21 + (SM,),
        compiler_params=PARAMS,
        name="adam",
    )(got, early, hid, hp_t, vec, hb, *grads, *weights, *states)


def plain_chunks(halves, data_count, rows):
    sides = []
    for side in range(2):
        flat = jnp.concatenate([own_first[side].reshape(data_count, -1) for own_first in halves], axis=1)
        flat = jnp.pad(flat, ((0, 0), (0, rows * 128 - flat.shape[1])))
        sides.append(flat.reshape(data_count, rows, 128))
    return sides[0], sides[1].astype(BF)


def on_device(
    tokens,
    cotangent,
    keep_mask,
    triple_weight,
    outward_weight,
    widen_weight,
    narrow_weight,
    vectors,
    hidden_bias,
    head_params,
    triple_moment,
    triple_square,
    outward_moment,
    outward_square,
    widen_moment,
    widen_square,
    narrow_moment,
    narrow_square,
    vector_moment,
    vector_square,
    hidden_moment,
    hidden_square,
    head_moment,
    head_square,
):
    tensor_rank = lax.axis_index("tensor")
    data_rank = lax.axis_index("dp")
    data_count = lax.axis_size("dp")
    images = keep_mask.shape[0] // 2
    patches = keep_mask.shape[1]
    heads = 2 * head_params.shape[1]
    depth = triple_weight.shape[1]
    half = triple_weight.shape[2]
    wide = widen_weight.shape[1]
    triple_rows = triple_weight.reshape(3 * depth, half)
    narrow_t = narrow_weight.T
    head_t = head_params.T
    fast = (
        depth == 192
        and half == 96
        and wide == 384
        and depth % data_count == 0
        and wide % (2 * data_count) == 0
        and half % (2 * data_count) == 0
        and 3 * depth % (4 * data_count) == 0
    )
    chunked = data_count if fast else 0
    swap = [(0, 1), (1, 0)]

    own, *rows_near = run_pack(
        triple_weight,
        outward_weight,
        widen_weight,
        narrow_t,
        hidden_bias,
        head_t,
        tokens.T,
        cotangent.T,
        keep_mask,
    )
    other = lax.ppermute(own, "tensor", swap)
    x, inc, bias = run_prepare(*rows_near)
    act, middle, grad_middle, dp, place, gate, hp, *sums = run_layer(
        x, inc, bias, own, other, vectors, heads, patches, chunked
    )
    if fast:
        mine, theirs = sums
    else:
        nar_g, wid_g, out_g, vec_g, hid_g, tri_g = sums
        early_mine = jnp.sum(vec_g, axis=1).reshape(1, -1)
        early_both = jnp.broadcast_to(early_mine, (data_count, early_mine.size))
        hidden_both = jnp.broadcast_to(
            jnp.sum(hid_g, axis=0).reshape(2, 1, wide), (2, data_count, wide)
        )
        early = plain_chunks(
            [
                wid_g.reshape(depth, 2, wide).transpose(1, 0, 2),
                nar_g.reshape(2, -1),
                out_g.reshape(2, -1),
                (early_both, early_both),
                hidden_both,
            ],
            data_count,
            EARLY_ROWS,
        )
        late = plain_chunks(
            [tri_g.reshape(3 * depth, 2, half).transpose(1, 0, 2)], data_count, LATE_ROWS
        )
        mine, theirs = (jnp.concatenate(pair, axis=1) for pair in zip(early, late))
    received = lax.ppermute(theirs, "tensor", swap)
    chunks = run_combine(mine, received)
    got = lax.all_to_all(chunks, "dp", 0, 0, tiled=False)
    result_t, grad_input_t, late_vec, head_row = run_finish(
        x, own, other, vectors, gate, hp, act, middle, grad_middle, dp, place, patches
    )
    if fast:
        wt_f, wo_f, ww_f, wn_f = run_shares(
            gate, triple_rows, outward_weight, widen_weight, narrow_t, data_count
        )
        blocks = [
            member.size // data_count // 384
            for member in (triple_rows, outward_weight, widen_weight, narrow_t)
        ]
        tri_f, out_f, wid_f, nar_f, early_vec, hid, payload = run_sums(
            got, late_vec, head_row, wo_f, blocks, wide
        )
    else:
        total = jnp.sum(got.astype(F32), axis=0)
        early_sum = total[:EARLY_ROWS].reshape(1, -1)
        masters = (widen_weight, narrow_weight, outward_weight)
        sizes = [member.size // data_count for member in masters] + [4 * depth, wide]
        cuts = [sum(sizes[:at]) for at in range(6)]
        wid_f, nar_f, out_f, early_vec, hid = (
            early_sum[:, cuts[at] : cuts[at + 1]] for at in range(5)
        )
        early_vec = early_vec.reshape(4, depth)
        share = triple_rows.size // data_count
        tri_f = total[EARLY_ROWS:].reshape(1, -1)[:, :share]

        def weight_share(member):
            length = member.size // data_count
            return lax.dynamic_slice_in_dim(member.reshape(1, -1), data_rank * length, length, 1)

        ww_f, wn_f, wo_f = (weight_share(member) for member in masters)
        wt_f = weight_share(triple_rows)
        squares = sum(jnp.sum(member * member) for member in (wid_f, nar_f, out_f, tri_f))
        squares = squares + jnp.where(data_rank == 0, jnp.sum(hid * hid), 0.0)
        lane = lax.broadcasted_iota(jnp.int32, (1, 128), 1)
        payload = jnp.concatenate(
            [
                late_vec[:, :128],
                late_vec[:, 128:].reshape(1, 128),
                jnp.where(lane == 127, squares, head_row),
            ]
        )
        payload = jnp.broadcast_to(payload[None], (2 * data_count, 4, 128))
    last_got = lax.all_to_all(payload, ("dp", "tensor"), 0, 0, tiled=False)
    renewed = run_adam(
        last_got,
        early_vec,
        hid,
        head_t,
        vectors,
        hidden_bias,
        (tri_f, out_f, wid_f, nar_f),
        (wt_f, wo_f, ww_f, wn_f),
        (
            triple_moment,
            triple_square,
            outward_moment,
            outward_square,
            widen_moment,
            widen_square,
            narrow_moment,
            narrow_square,
            vector_moment,
            vector_square,
            hidden_moment,
            hidden_square,
            head_moment.T,
            head_square.T,
        ),
    )
    hidden_new = renewed[15:18]
    head_new = [member.T for member in renewed[18:21]]
    return (result_t.T, grad_input_t.T, *renewed[:15], *hidden_new, *head_new, renewed[21].reshape(()))


def solution(mesh):
    return jax.shard_map(
        on_device,
        mesh=mesh,
        in_specs=(
            P(("dp", "tensor"), None),
            P(("dp", "tensor"), None),
            P("dp", None),
            P(None, None, "tensor"),
            P("tensor", None),
            P(None, "tensor"),
            P("tensor", None),
            P(),
            P("tensor"),
            P(None, "tensor"),
            P("tensor", "dp"),
            P("tensor", "dp"),
            P("tensor", "dp"),
            P("tensor", "dp"),
            P("tensor", "dp"),
            P("tensor", "dp"),
            P("tensor", "dp"),
            P("tensor", "dp"),
            P(),
            P(),
            P("tensor"),
            P("tensor"),
            P(None, "tensor"),
            P(None, "tensor"),
        ),
        out_specs=(
            P(("dp", "tensor"), None),
            P(("dp", "tensor"), None),
            P("tensor", "dp"),
            P("tensor", "dp"),
            P("tensor", "dp"),
            P("tensor", "dp"),
            P("tensor", "dp"),
            P("tensor", "dp"),
            P("tensor", "dp"),
            P("tensor", "dp"),
            P("tensor", "dp"),
            P("tensor", "dp"),
            P("tensor", "dp"),
            P("tensor", "dp"),
            P(),
            P(),
            P(),
            P("tensor"),
            P("tensor"),
            P("tensor"),
            P(None, "tensor"),
            P(None, "tensor"),
            P(None, "tensor"),
            P(),
        ),
        check_vma=False,
    )
```

```python
import functools
import math

import jax
import jax.numpy as jnp
from jax import lax
from jax.experimental import pallas as pl
from jax.experimental.pallas import tpu as pltpu
from jax.sharding import PartitionSpec as P

GRID = 14
STEP = 10
EPS_NORM = 1e-06
CLIP_AT = 1.0
BETA_ONE = 0.9
BETA_TWO = 0.95
ADAM_EPS = 1e-08
RATES = (0.1, 0.5, 0.1, 0.05, 0.3, 0.1, 0.3)
DECAYS = (0.05, 0.05, 0.05, 0.05, 0.0, 0.0, 0.0)
LOG2E = 1.4426950408889634
BF = jnp.bfloat16
F32 = jnp.float32
LAYER_VMEM = 52 * 1024 * 1024
SMALL_VMEM = 16 * 1024 * 1024
EARLY_ROWS = 96
LATE_ROWS = 32
SENT_EARLY = 80
SENT_ROWS = 112
SMALL_AT = 16
PAIR = 2
VM = pl.BlockSpec(memory_space=pltpu.VMEM)
ANYWHERE = pl.BlockSpec(memory_space=pl.ANY)
SM = pl.BlockSpec(memory_space=pltpu.SMEM)
PARAMS = pltpu.CompilerParams(vmem_limit_bytes=SMALL_VMEM)


def sds(*dims, dtype=F32):
    return jax.ShapeDtypeStruct(dims, dtype)


def near(*arrays):
    return [pltpu.with_memory_space_constraint(member, pltpu.VMEM) for member in arrays]


def far(*arrays):
    return [pltpu.with_memory_space_constraint(member, pltpu.HBM) for member in arrays]


def nn(a, b):
    return lax.dot_general(a, b, (((1,), (0,)), ((), ())), preferred_element_type=F32)


def nt(a, b):
    return lax.dot_general(a, b, (((1,), (1,)), ((), ())), preferred_element_type=F32)


def norm_parts(v):
    width = v.shape[-1]
    average = jnp.sum(v, axis=-1, keepdims=True) * (1.0 / width)
    centred = v - average
    variance = jnp.sum(centred * centred, axis=-1, keepdims=True) * (1.0 / width)
    spread = lax.rsqrt(variance + EPS_NORM)
    return centred * spread, spread


def norm_back(e, n, spread):
    width = e.shape[-1]
    mean_e = jnp.sum(e, axis=-1, keepdims=True) * (1.0 / width)
    mean_en = jnp.sum(e * n, axis=-1, keepdims=True) * (1.0 / width)
    return spread * (e - mean_e - n * mean_en)


def fold(v):
    rows = v.shape[0]
    return jnp.sum(v.reshape(rows // 8, 8, v.shape[1]), axis=0)


def gelu_parts(x):
    phi = 0.5 + 0.5 * lax.erf(x * math.sqrt(0.5))
    density = jnp.exp2((x * x) * (-0.5 * LOG2E)) * (1.0 / math.sqrt(2.0 * math.pi))
    return x * phi, phi + x * density


def places(count, lanes, dim):
    at = lax.broadcasted_iota(jnp.int32, (count, lanes), dim).astype(F32)
    row = jnp.floor((at + 0.5) * (1.0 / GRID))
    return at - row * GRID, row


def offsets(kp, qp):
    kc, kr = places(kp, qp, 0)
    qc, qr = places(kp, qp, 1)
    a = kc - qc
    b = kr - qr
    return a, b, a * a + b * b


def head_mask(hd, h):
    lane = lax.broadcasted_iota(jnp.int32, (STRIP, 128), 1)
    return ((lane >= h * hd) & (lane < (h + 1) * hd)).astype(BF)


def in_tiles(own, oth):
    gap = jnp.zeros((own.shape[0], 128 - own.shape[1]), own.dtype)
    return jnp.concatenate([own, gap, oth, gap], axis=1)


def gate_of(hp_ref, h, lanes):
    return 1.0 / (1.0 + jnp.exp(-jnp.broadcast_to(hp_ref[h : h + 1, 3:4], (1, lanes))))


def bf_parts(value, count=3):
    parts = []
    for _ in range(count):
        part = value.astype(BF).astype(F32)
        parts.append(part)
        value = value - part
    return parts


def key_operand(kp):
    kc, kr = places(kp, 128, 0)
    lane = lax.broadcasted_iota(jnp.int32, (kp, 128), 1)
    value = jnp.where(lane < 3, kc, jnp.where(lane < 6, kr, jnp.where(lane < 9, kc * kc, kr * kr)))
    return jnp.where(lane < 12, value, 0.0).astype(BF)


def query_operand(hp_ref, h, qp):
    p = [LOG2E * jnp.broadcast_to(hp_ref[h : h + 1, at : at + 1], (16, qp)) for at in range(3)]
    qc, qr = places(16, qp, 1)
    row = lax.broadcasted_iota(jnp.int32, (16, qp), 0)
    value = jnp.where(row < 3, p[0] - 2.0 * p[2] * qc, jnp.where(row < 6, p[1] - 2.0 * p[2] * qr, p[2]))
    parts = bf_parts(value)
    place = row - 3 * ((row >= 3).astype(jnp.int32) + (row >= 6) + (row >= 9))
    value = jnp.where(place == 0, parts[0], jnp.where(place == 1, parts[1], parts[2]))
    return jnp.where(row < 12, value, jnp.where(row == 12, 1.0, 0.0)).astype(BF)


STRIP = 16
LAG = 3
WAIT = 3


def interleave(*streams):
    streams = [member for member in streams if member is not None]
    while streams:
        alive = []
        for member in streams:
            try:
                next(member)
                alive.append(member)
            except StopIteration:
                pass
        streams = alive


def staged(count, lag, *stages):
    for t in range(count + lag * (len(stages) - 1)):
        for k, stage in enumerate(stages):
            if 0 <= t - k * lag < count:
                stage(t - k * lag)
        yield


def slow(stream, count):
    for _ in range(count):
        yield
        try:
            next(stream)
        except StopIteration:
            return


def cut(value, r):
    return value[r * STRIP : (r + 1) * STRIP]


def rows_of(r):
    return pl.ds(r * STRIP, STRIP)


def put_planes(ref, value):
    width = value.shape[1]
    ref[0] = value[:, :128]
    ref[1, :, 0 : width - 128] = value[:, 128:]


def even_odd_tiles(ref, start, pairs):
    even = [ref[at, pl.ds(start, pairs, stride=2), :] for at in range(2)]
    odd = [ref[at, pl.ds(start + 1, pairs, stride=2), :] for at in range(2)]
    return (
        even[0],
        jnp.concatenate([even[1][:, :64], odd[0][:, :64]], axis=1),
        jnp.concatenate([odd[0][:, 64:], odd[1][:, :64]], axis=1),
    )


def four_row_tiles(ref, plane, start, groups):
    r = [ref[plane, pl.ds(start + at, groups, stride=4), :] for at in range(4)]
    return (
        jnp.concatenate([r[0][:, :96], r[1][:, :32]], axis=1),
        jnp.concatenate([r[1][:, 32:96], r[2][:, :64]], axis=1),
        jnp.concatenate([r[2][:, 64:96], r[3][:, :96]], axis=1),
    )


def pack_kernel(*refs):
    given, pack_ref, passed, held, sems = refs[:9], refs[9], refs[10:13], refs[13:19], refs[19]
    copies = [
        pltpu.make_async_copy(source, target, sems.at[at])
        for at, (source, target) in enumerate(zip(given, [*held, *passed]))
    ]
    for member in copies:
        member.start()
    for member in copies[:6]:
        member.wait()
    tri_ref, out_ref, wid_ref, nar_ref, hb_ref, hp_ref = held
    depth, wide = wid_ref.shape
    pack_ref[0:depth, :] = wid_ref[...].astype(BF)
    pack_ref[depth : 2 * depth, :] = nar_ref[...].astype(BF)
    pack_ref[2 * depth : 3 * depth, :] = jnp.concatenate(
        [tri_ref[0], tri_ref[1], tri_ref[2], out_ref[...].T], axis=1
    ).astype(BF)
    heads_here = hp_ref.shape[0]
    hp = jnp.concatenate([hp_ref[...], jnp.zeros((heads_here, wide - 4), F32)], axis=1)
    left = jnp.concatenate([hb_ref[...].reshape(1, wide), hp], axis=0)
    parts = []
    for _ in range(3):
        part = left.astype(BF).astype(F32)
        parts.append(part)
        left = left - part
    parts.append(jnp.zeros((16 - 3 * (1 + heads_here), wide), F32))
    pack_ref[3 * depth : 3 * depth + 16, :] = jnp.concatenate(parts, axis=0).astype(BF)
    for member in copies[6:]:
        member.wait()


def run_pack(tri, out, wid, nar_t, hb, hp_t, *passed):
    depth, wide = wid.shape
    given = (tri, out, wid, nar_t, hb, hp_t)
    return pl.pallas_call(
        pack_kernel,
        out_shape=(
            pltpu.VMEM((3 * depth + 16, wide), BF),
            *[pltpu.VMEM(member.shape, member.dtype) for member in passed],
        ),
        in_specs=[pl.BlockSpec(memory_space=pltpu.HBM)] * 9,
        out_specs=(VM,) * 4,
        scratch_shapes=[
            *[pltpu.VMEM(member.shape, member.dtype) for member in given],
            pltpu.SemaphoreType.DMA((9,)),
        ],
        compiler_params=PARAMS,
        name="pack_weights",
    )(*far(*given, *passed))


def prepare_kernel(tok_ref, cot_ref, keep_ref, x_ref, inc_ref, bias_ref, xs, cs):
    images, kp, width = x_ref.shape
    patches = keep_ref.shape[1]
    rows = images * patches
    qp = -(-patches // 128) * 128
    mine = keep_ref[pl.ds(pl.multiple_of(lax.axis_index("tensor") * images, 8), images), :].astype(F32)
    columns = jnp.concatenate([mine, jnp.zeros((images, qp - patches), F32)], axis=1).T
    xs[0:rows, :] = tok_ref[...].T.astype(F32)
    cs[0:rows, :] = cot_ref[...].T.astype(F32)
    xs[rows : rows + 16, :] = jnp.zeros((16, width), F32)
    cs[rows : rows + 16, :] = jnp.zeros((16, width), F32)
    for i in range(images):
        span = slice(i * patches, i * patches + kp)
        keep = jnp.broadcast_to(columns[:kp, i : i + 1], (kp, 128))
        keep_wide = jnp.concatenate([keep, keep[:, : width - 128]], axis=1)
        x_ref[i] = xs[span, :].astype(BF)
        inc_ref[i] = (cs[span, :] * keep_wide).astype(BF)
        bias_ref[i] = ((keep - 1.0) * 1e30).astype(BF)


def run_prepare(tok_t, cot_t, keep_mask):
    images = keep_mask.shape[0] // 2
    kp = -(-keep_mask.shape[1] // 16) * 16
    width, rows_here = tok_t.shape
    rows = pltpu.VMEM((images, kp, width), BF)
    return pl.pallas_call(
        prepare_kernel,
        out_shape=(rows, rows, pltpu.VMEM((images, kp, 128), BF)),
        in_specs=[VM] * 3,
        out_specs=(VM,) * 3,
        scratch_shapes=[pltpu.VMEM((rows_here + 16, width), F32)] * 2,
        compiler_params=PARAMS,
        name="prepare",
    )(*near(tok_t, cot_t, keep_mask))


def layer_kernel(*refs, patches, heads, data_count):
    (x_ref, inc_ref, bias_ref, own_ref, oth_ref, vec_ref) = refs[:6]
    far_refs = refs[6:11]
    gate_ref, hp_ref = refs[11:13]
    outs = refs[13:15] if data_count else refs[13:19]
    at = 13 + len(outs)
    (wq, wk, wv, wo, wop, wi, wn, hp_s, key_p, key_i, query_p) = refs[at : at + 11]
    at += 11
    (fst_s, keys_s, vt_s, qm_s, dmm_s, v_s, kt_s, soft_s, mid_s, n2_s) = refs[at : at + 10]
    at += 10
    (sec_s, spr_s, low_s, stat_s, back_s) = refs[at : at + 5]
    at += 5
    (first_t, mix_t, left_t, right_s, gm_s, dp_s, s_buf, p_buf, att_buf) = refs[at : at + 9]
    at += 9
    (place_g, gate_g, da_buf, att_s, ds_s, wide_g, out_g, vec_g, hid_g, tri_p, sems) = refs[at : at + 11]
    at += 11
    if data_count:
        nar_p, out_p, nar_f, out_f, tri_f, tmp = refs[at : at + 6]
    images, kp, width = x_ref.shape
    qp = soft_s.shape[4]
    hd = width // heads
    half = width // 2
    half_heads = heads // 2
    wide = own_ref.shape[1]
    hidden = 2 * wide
    strips = kp // STRIP
    c_scale = LOG2E / math.sqrt(hd)
    back_scale = 1.0 / math.sqrt(hd)
    v = [vec_ref[k : k + 1, :] for k in range(6)]

    key_p[...] = key_operand(kp)
    query_p[...] = jnp.zeros_like(query_p)
    for ref in (hid_g, vec_g, place_g, gate_g):
        ref[...] = jnp.zeros_like(ref)
    for k in range(2):
        att_buf[k, kp:, :] = jnp.zeros((qp - kp, qp), BF)
    for k in range(2):
        fst_s[k, kp:, :] = jnp.zeros((qp - kp, width), BF)
    for k in range(images):
        for side in range(2):
            right_s[side, k * qp + kp : (k + 1) * qp, :] = jnp.zeros((qp - kp, hidden), BF)
        for c in range(3):
            dp_s[c, k * qp + kp : (k + 1) * qp, :] = jnp.zeros((qp - kp, 256), BF)
    sec_s[:, width:] = (lax.broadcasted_iota(jnp.int32, (kp, 256 - width), 1) < 3).astype(BF)
    gap = jnp.zeros((qp - kp, width), BF)
    one_lane = (lax.broadcasted_iota(jnp.int32, (STRIP, 128), 1) == half).astype(BF)
    masks = [head_mask(hd, h) for h in range(half_heads)]
    tiles = [slice(128 * t, 128 * (t + 1)) for t in range(2)]
    bias_lane = (lax.broadcasted_iota(jnp.int32, (kp, 128), 1) == 12).astype(BF)

    def columns_at(i):
        return pl.ds(pl.multiple_of(i * qp, 128), qp)


    def first_norm(i):
        kept = {}

        def mean(r):
            x = x_ref[i, rows_of(r), :].astype(F32)
            kept[r] = x - jnp.sum(x, axis=-1, keepdims=True) * (1.0 / width)

        def spread(r):
            kept[r] = (kept[r], jnp.sum(kept[r] * kept[r], axis=-1, keepdims=True) * (1.0 / width))

        def put(r):
            centred, variance = kept[r]
            fst_s[i % 2, rows_of(r), :] = (centred * lax.rsqrt(variance + EPS_NORM) * v[0] + v[1]).astype(BF)

        yield from staged(strips, LAG, mean, spread, put)

    def project(i, part):
        first_q = fst_s[i % 2]
        if part == 0:
            queries = nn(first_q, wq[...]).astype(BF)
            yield
            for r in range(qp // STRIP):
                for h in range(heads):
                    tile = cut(queries[:, tiles[h // half_heads]], r)
                    qm_s[i, h, rows_of(r), :] = tile * masks[h % half_heads] + one_lane
                yield
        elif part == 1:
            keys = nn(first_q, wk[...]).astype(BF)
            yield
            for r in range(strips):
                bias = bias_ref[i, rows_of(r), :]
                key_i[rows_of(r), :] = key_p[rows_of(r), :] + bias * cut(bias_lane, r)
                for t in range(2):
                    keys_s[rows_of(r), tiles[t]] = cut(keys[:, tiles[t]], r) + bias * one_lane
                yield
            kt_s[i] = keys.T
            yield
        else:
            values = nn(first_q, wv[...]).astype(BF)
            yield
            v_s[i] = values[:kp]
            vt_s[...] = values.T
            yield
            yield
            first_t[:, columns_at(i)] = first_q.T
            yield

    def head_rows(h):
        first_row = 128 * (h // half_heads) + hd * (h % half_heads)
        return slice(first_row, first_row + hd)


    def scores(i, h):
        s = nt(keys_s[:, tiles[h // half_heads]], qm_s[i, h])
        p = nn(key_i[...], query_p[h])
        m, pm = cut(s, 0), cut(p, 0)
        for r in range(strips):
            yield
            s_buf[h, rows_of(r), :] = cut(s, r)
            p_buf[h, rows_of(r), :] = cut(p, r)
            m = jnp.maximum(m, cut(s, r))
            pm = jnp.maximum(pm, cut(p, r))
        stat_s[4 * h : 4 * h + 1, :] = jnp.max(m, axis=0, keepdims=True)
        stat_s[4 * h + 1 : 4 * h + 2, :] = jnp.max(pm, axis=0, keepdims=True)

    def exponents(h):
        m, pm = stat_s[4 * h : 4 * h + 1, :], stat_s[4 * h + 1 : 4 * h + 2, :]
        z = jnp.zeros((STRIP, qp), F32)
        pz = jnp.zeros((STRIP, qp), F32)
        for r in range(strips):
            yield
            e = jnp.exp2((s_buf[h, rows_of(r), :] - m) * c_scale)
            pe = jnp.exp2(p_buf[h, rows_of(r), :] - pm)
            s_buf[h, rows_of(r), :] = e
            p_buf[h, rows_of(r), :] = pe
            z = z + e
            pz = pz + pe
        gate = gate_of(hp_s, h, qp)
        stat_s[4 * h + 2 : 4 * h + 3, :] = (1.0 - gate) / jnp.sum(z, axis=0, keepdims=True)
        stat_s[4 * h + 3 : 4 * h + 4, :] = gate / jnp.sum(pz, axis=0, keepdims=True)

    def mixing(i, h):
        a, b = stat_s[4 * h + 2 : 4 * h + 3, :], stat_s[4 * h + 3 : 4 * h + 4, :]
        for r in range(strips):
            yield
            content = s_buf[h, rows_of(r), :] * a
            located = p_buf[h, rows_of(r), :] * b
            soft_s[i, h, 0, rows_of(r), :] = content
            soft_s[i, h, 1, rows_of(r), :] = located
            att_buf[h % 2, rows_of(r), :] = (content + located).astype(BF)
        yield
        mix_t[h * hd : (h + 1) * hd, columns_at(i)] = nn(
            vt_s[head_rows(h), :], att_buf[h % 2]
        ).astype(BF)


    def strip_rows(i, r):
        return pl.ds(pl.multiple_of(i * qp + r * STRIP, 16), STRIP)

    def image_rows(i):
        return pl.ds(pl.multiple_of(i * qp, 16), kp)

    def start(i):
        attn = nt(mix_t[:, columns_at(i)].T[:kp], wo[...])
        for _ in range(WAIT + 2):
            yield
        kept = {}

        def mean(r):
            middle = x_ref[i, rows_of(r), :].astype(F32) + cut(attn, r) + v[4]
            mid_s[i, rows_of(r), :] = middle
            kept[r] = middle - jnp.sum(middle, axis=-1, keepdims=True) * (1.0 / width)

        def vary(r):
            kept[r] = (kept[r], jnp.sum(kept[r] * kept[r], axis=-1, keepdims=True) * (1.0 / width))

        def put(r):
            centred, variance = kept[r]
            spread = lax.rsqrt(variance + EPS_NORM)
            n2 = centred * spread
            n2_s[rows_of(r), :] = n2
            spr_s[rows_of(r), :] = spread
            sec_s[rows_of(r), 0:width] = (n2 * v[2] + v[3]).astype(BF)

        yield from staged(strips, LAG, mean, vary, put)
        left_t[0, :, columns_at(i)] = jnp.concatenate([inc_ref[i], gap], axis=0).T
        yield
        left_t[1, :, columns_at(i)] = jnp.concatenate([sec_s[:, 0:width], gap], axis=0).T

    def chunk(i, c, on):
        lanes = pl.ds(c * 256, 256)
        before = nn(sec_s[...], wi[:, lanes])
        back = nn(inc_ref[i], wn[:, lanes])
        total = jnp.zeros((8, 256), F32)
        for r in range(strips):
            yield
            gelu, slope = gelu_parts(cut(before, r))
            right_s[0, strip_rows(i, r), lanes] = gelu.astype(BF)
            grad_before = cut(back, r) * slope
            right_s[1, strip_rows(i, r), lanes] = grad_before.astype(BF)
            total = total + fold(grad_before)
        hid_g[:, lanes] += jnp.where(on, total, 0.0)

    def end(i, on):
        grad_second = nt(right_s[1, image_rows(i), :], wi[0:width, :])
        totals = [jnp.zeros((8, width), F32)] * 4
        mids = []
        for _ in range(WAIT):
            yield
        kept = {}

        def means(r):
            n2 = n2_s[rows_of(r), :]
            g = cut(grad_second, r)
            e = g * v[2]
            mean_e = jnp.sum(e, axis=-1, keepdims=True) * (1.0 / width)
            mean_en = jnp.sum(e * n2, axis=-1, keepdims=True) * (1.0 / width)
            kept[r] = (e, mean_e, mean_en)
            for k, term in enumerate((g * n2, g)):
                totals[k] = totals[k] + fold(term)

        def put(r):
            e, mean_e, mean_en = kept[r]
            n2 = n2_s[rows_of(r), :]
            incoming = inc_ref[i, rows_of(r), :].astype(F32)
            spread = spr_s[rows_of(r), :]
            grad_middle = incoming + spread * (e - mean_e - n2 * mean_en)
            gm_s[i, rows_of(r), :] = grad_middle
            mids.append(grad_middle.astype(BF))
            for k, term in enumerate((grad_middle, incoming)):
                totals[2 + k] = totals[2 + k] + fold(term)

        yield from staged(strips, LAG, means, put)
        for k in range(4):
            vec_g[k] += jnp.where(on, totals[k], 0.0)
        mid_low = jnp.concatenate([*mids, gap], axis=0)
        yield
        dm = nn(mid_low, wop[...]).astype(BF)
        for r in range(qp // STRIP):
            yield
            for h in range(heads):
                tile = cut(dm[:, tiles[h // half_heads]], r)
                dmm_s[i, h, rows_of(r), :] = tile * masks[h % half_heads]
        yield
        low_s[pl.ds(pl.multiple_of(i * qp, 16), qp), :] = mid_low

    blocks = hidden // 256

    def forward_step(i, carry):
        one, two = jnp.maximum(i - 1, 0), jnp.maximum(i - 2, 0)
        after = jnp.minimum(i + 1, images - 1)
        on_one, on_two = i > 0, i > 1
        interleave(scores(i, 0), exponents(3), mixing(one, 2), chunk(two, 1, on_two), first_norm(after))
        interleave(scores(i, 1), exponents(0), mixing(one, 3), chunk(two, 2, on_two))
        interleave(
            scores(i, 2),
            exponents(1),
            mixing(i, 0),
            end(two, on_two),
            start(one),
            project(i, 2),
        )
        interleave(
            scores(i, 3),
            exponents(2),
            mixing(i, 1),
            chunk(one, 0, on_one),
            project(after, 0),
            project(after, 1),
        )
        return carry

    interleave(first_norm(0))
    wi[0:width, pl.ds(0, wide)] = own_ref[0:width, :]
    wi[0:width, pl.ds(wide, wide)] = oth_ref[0:width, :]
    wn[:, pl.ds(0, wide)] = own_ref[width : 2 * width, :]
    wn[:, pl.ds(wide, wide)] = oth_ref[width : 2 * width, :]
    own_tri = own_ref[2 * width : 3 * width, :]
    oth_tri = oth_ref[2 * width : 3 * width, :]
    for k, w in enumerate((wq, wk, wv, wop)):
        lanes = slice(k * half, (k + 1) * half)
        w[...] = in_tiles(own_tri[:, lanes], oth_tri[:, lanes])
    wo[...] = jnp.concatenate([own_tri[:, 3 * half :], oth_tri[:, 3 * half :]], axis=1)
    small = []
    for ref in (own_ref, oth_ref):
        tail = ref[3 * width : 3 * width + 16, :].astype(F32)
        each = 1 + half_heads
        small.append(tail[0:each] + tail[each : 2 * each] + tail[2 * each : 3 * each])
    hb = jnp.concatenate([member[0:1] for member in small], axis=1)
    wi[width:, :] = jnp.concatenate(
        [*bf_parts(hb), jnp.zeros((256 - width - 3, hidden), F32)], axis=0
    ).astype(BF)
    hp_s[...] = jnp.concatenate(
        [member[1:, :128] for member in small] + [jnp.zeros((8 - heads, 128), F32)], axis=0
    )
    for h in range(heads):
        query_p[h, 0:16, :] = query_operand(hp_s, h, qp)
    for part in range(2):
        interleave(project(0, part))
    def leaving(first_image, count):
        rows = pl.ds(pl.multiple_of(first_image * qp, 16), count * qp)
        images_out = pl.ds(first_image, count)
        for k, (source, at_rows) in enumerate(
            ((right_s.at[0], rows), (mid_s, images_out), (gm_s, images_out))
        ):
            pltpu.make_async_copy(
                source.at[at_rows], far_refs[k].at[at_rows], sems.at[k]
            ).start()

    def forward_pair(j, carry):
        forward_step(2 * j + 1, forward_step(2 * j, carry))

        @pl.when(j > 0)
        def _():
            leaving(2 * j - 2, 2)

        return carry

    lax.fori_loop(0, images // 2, forward_pair, 0)


    def back_scores(i, h):
        da = nt(v_s[i, :, tiles[h // half_heads]], dmm_s[i, h])
        rc = jnp.zeros((STRIP, qp), F32)
        rl = jnp.zeros((STRIP, qp), F32)
        for r in range(strips):
            yield
            part = cut(da, r)
            da_buf[h % 2, rows_of(r), :] = part
            rc = rc + soft_s[i, h, 0, rows_of(r), :] * part
            rl = rl + soft_s[i, h, 1, rows_of(r), :] * part
        gate = gate_of(hp_s, h, qp)
        rc = jnp.sum(rc, axis=0, keepdims=True) / (1.0 - gate)
        rl = jnp.sum(rl, axis=0, keepdims=True) / gate
        back_s[2 * h : 2 * h + 1, :] = rc
        back_s[2 * h + 1 : 2 * h + 2, :] = rl
        gate_g[h : h + 1, :] += rl - rc

    def back_spread(i, h):
        rc, rl = back_s[2 * h : 2 * h + 1, :], back_s[2 * h + 1 : 2 * h + 2, :]
        lanes = pl.ds(h * qp, qp)
        for r in range(strips):
            yield
            rows = rows_of(r)
            c = soft_s[i, h, 0, rows, :]
            l = soft_s[i, h, 1, rows, :]
            part = da_buf[h % 2, rows, :]
            ds_s[rows, lanes] = (c * (part - rc)).astype(BF)
            att_s[rows, lanes] = (c + l).astype(BF)
            place_g[h, rows, :] += l * (part - rl)

    def products(i, t):
        lanes = slice(t * half_heads * qp, (t + 1) * half_heads * qp)
        heads_in = slice(t * half_heads, (t + 1) * half_heads)
        dk = nn(ds_s[:, lanes], qm_s[i, heads_in].reshape(half_heads * qp, 128))
        dv = nn(att_s[:, lanes], dmm_s[i, heads_in].reshape(half_heads * qp, 128))
        yield
        pad = jnp.zeros((qp - kp, qp), BF)
        dq_t = []
        for h in range(t * half_heads, (t + 1) * half_heads):
            ds = jnp.concatenate([ds_s[:, h * qp : (h + 1) * qp], pad], axis=0)
            dq_t.append(nn(kt_s[i, head_rows(h), :], ds))
        yield
        dp_s[1, image_rows(i), tiles[t]] = (dk * back_scale).astype(BF)
        yield
        dp_s[2, image_rows(i), tiles[t]] = dv.astype(BF)
        yield
        dq_t.append(jnp.zeros((128 - half, qp), F32))
        dq = (jnp.concatenate(dq_t, axis=0) * back_scale).astype(BF)
        dp_s[0, image_rows(i), tiles[t]] = dq.T[:kp]

    cut_at = (images - 2) * qp
    spans = (slice(0, cut_at), slice(cut_at, images * qp))

    def weight_gradient(unit, part):
        side = unit // blocks
        lanes = slice((unit % blocks) * 256, (unit % blocks) * 256 + 256)
        value = nn(left_t[side, :, spans[part]], right_s[side, spans[part], lanes])
        yield
        if part:
            wide_g[side, :, lanes] += value
        else:
            wide_g[side, :, lanes] = value

    def outward_gradient(part):
        value = nn(mix_t[:, spans[part]], low_s[spans[part], :])
        yield
        if part:
            out_g[...] += value
        else:
            out_g[...] = value

    def triple_gradient(c, part):
        value = nn(first_t[:, spans[part]], dp_s[c, spans[part], :])
        yield
        rows = pl.ds(c * width, width)
        for t in range(2):
            if part:
                tri_p[t, rows, :] += value[:, tiles[t]]
            else:
                tri_p[t, rows, :] = value[:, tiles[t]]

    last = images - 1
    on = True
    partial = [weight_gradient(unit, 0) for unit in range(2 * blocks)] + [outward_gradient(0)]
    interleave(
        exponents(3), mixing(last, 2), chunk(last - 1, 1, on), back_scores(0, 0), partial[0]
    )
    interleave(
        mixing(last, 3),
        chunk(last - 1, 2, on),
        back_scores(0, 1),
        back_spread(0, 0),
        partial[1],
    )
    interleave(
        end(last - 1, on), start(last), back_scores(0, 2), back_spread(0, 1), partial[2]
    )
    interleave(chunk(last, 0, on), back_scores(0, 3), back_spread(0, 2), partial[3])
    interleave(chunk(last, 1, on), back_spread(0, 3), partial[4])
    interleave(chunk(last, 2, on), products(0, 0), partial[5])
    interleave(end(last, on), products(0, 1), *partial[6:])

    leaving(images - 2, 2)


    def early_chunks():
        put_planes(nar_p, wide_g[0].T)
        put_planes(out_p, out_g[...])
        for side in range(2):
            for k, part in enumerate(even_odd_tiles(nar_p, side * wide, wide // 2)):
                nar_f[side, k] = part
            for k, part in enumerate(even_odd_tiles(out_p, side * half, half // 2)):
                out_f[side, k] = part
            yield
        for r in range(data_count):
            for side in range(2):
                yield
                piece = outs[0].at[r] if side == 0 else tmp.at[r]
                for k in range(3):
                    lanes = slice(side * wide + 128 * k, side * wide + 128 * (k + 1))
                    piece[k * wp : (k + 1) * wp, :] = wide_g[1, r * wp : (r + 1) * wp, lanes]
                    row = 3 * wp + k * np_
                    piece[row : row + np_, :] = nar_f[side, k, r * np_ : (r + 1) * np_, :]
                    row = 3 * (wp + np_) + k * op
                    piece[row : row + op, :] = out_f[side, k, r * op : (r + 1) * op, :]
                if side:
                    outs[1][r, 0:SENT_EARLY, :] = piece[0:SENT_EARLY, :].astype(BF)

    def late_chunks():
        early = jnp.sum(vec_g[...], axis=1)
        hidden_sum = jnp.sum(hid_g[...], axis=0, keepdims=True)
        vec_n, hid_n = 4 * width // data_count, wide // data_count
        rest = jnp.zeros((1, 128 - vec_n - hid_n), F32)
        groups = 3 * width // data_count // 4
        small_at = 3 * (wp + np_ + op)
        for side in range(2):
            for k, part in enumerate(four_row_tiles(tri_p, side, 0, 3 * width // 4)):
                tri_f[side, k] = part
            yield
        for r in range(data_count):
            for side in range(2):
                yield
                piece = outs[0].at[r] if side == 0 else tmp.at[r]
                row, lane = divmod(r * vec_n, width)
                at_hidden = side * wide + r * hid_n
                piece[small_at : small_at + 1, :] = jnp.concatenate(
                    [
                        early[row : row + 1, lane : lane + vec_n],
                        hidden_sum[:, at_hidden : at_hidden + hid_n],
                        rest,
                    ],
                    axis=1,
                )
                for k in range(3):
                    row = small_at + 1 + k * groups
                    piece[row : row + groups, :] = tri_f[side, k, r * groups : (r + 1) * groups, :]
                row = small_at + 1 + 3 * groups
                piece[row:SENT_ROWS, :] = jnp.zeros((SENT_ROWS - row, 128), F32)
                if side:
                    outs[1][r, SENT_EARLY:, :] = piece[SENT_EARLY:, :].astype(BF)

    if data_count:
        wp, np_, op = width // data_count, wide // data_count // 2, half // data_count // 2
    chunking = early_chunks() if data_count else iter(())
    for i in range(1, images):
        before = i > 1
        done = i == last
        interleave(
            back_scores(i, 0),
            back_spread(i - 1, 3) if before else None,
            outward_gradient(1) if i == 1 else None,
        )
        interleave(
            back_scores(i, 1),
            products(i - 1, 0) if before else None,
            back_spread(i, 0),
        )
        interleave(
            back_scores(i, 2),
            products(i - 1, 1) if before else None,
            back_spread(i, 1),
        )
        interleave(
            back_scores(i, 3),
            back_spread(i, 2),
            weight_gradient(i - 1, 1) if i <= 2 * blocks else None,
        )
    for unit in range(last, 2 * blocks):
        interleave(weight_gradient(unit, 1))
    interleave(back_spread(last, 3), *[triple_gradient(c, 0) for c in range(3)])
    interleave(products(last, 0), products(last, 1))
    interleave(chunking)
    for k, source in ((3, dp_s), (4, place_g)):
        pltpu.make_async_copy(source, far_refs[k], sems.at[k]).start()
    gate_ref[...] = gate_g[...]
    hp_ref[...] = hp_s[...]
    for c in range(3):
        interleave(triple_gradient(c, 1))
    if data_count:
        interleave(late_chunks())
    else:
        outs[0][...] = wide_g[0].T
        outs[1][...] = wide_g[1]
        outs[2][...] = out_g[...]
        outs[3][...] = vec_g[...]
        outs[4][...] = hid_g[...]
        for c in range(3):
            rows = pl.ds(c * width, width)
            outs[5][rows, :] = jnp.concatenate(
                [tri_p[0, rows, 0:half], tri_p[1, rows, 0:half]], axis=1
            )
    for k, source in enumerate((right_s.at[0], mid_s, gm_s, dp_s, place_g)):
        pltpu.make_async_copy(source, far_refs[k], sems.at[k]).wait()


def run_layer(x, inc, bias, own, oth, vec, heads, patches, data_count):
    images, kp, width = x.shape
    qp = -(-patches // 128) * 128
    wide, half = own.shape[1], width // 2
    hidden = 2 * wide
    full = images * qp
    if data_count:
        outs = [
            pltpu.VMEM((data_count, SENT_ROWS, 128), F32),
            pltpu.VMEM((data_count, SENT_ROWS, 128), BF),
        ]
    else:
        outs = [
            sds(hidden, width),
            sds(width, hidden),
            sds(width, width),
            sds(4, 8, width),
            sds(8, hidden),
            sds(3 * width, width),
        ]

    def bf(*dims):
        return pltpu.VMEM(dims, BF)

    def f32(*dims):
        return pltpu.VMEM(dims, F32)

    scratch = [
        *[bf(width, 256)] * 3,
        bf(width, width),
        bf(width, 256),
        bf(256, hidden),
        bf(width, hidden),
        f32(8, 128),
        bf(kp, 128),
        bf(kp, 128),
        bf(heads, 128, qp),
        bf(2, qp, width),
        bf(kp, 256),
        bf(256, qp),
        bf(images, heads, qp, 128),
        bf(images, heads, qp, 128),
        bf(images, kp, 256),
        bf(images, 256, qp),
        f32(images, heads, 2, kp, qp),
        f32(images, kp, width),
        f32(kp, width),
        bf(kp, 256),
        f32(kp, 1),
        bf(full, width),
        f32(4 * heads, qp),
        f32(2 * heads, qp),
        bf(width, full),
        bf(width, full),
        bf(2, width, full),
        bf(2, full, hidden),
        f32(images, kp, width),
        bf(3, full, 256),
        f32(heads, kp, qp),
        f32(heads, kp, qp),
        bf(2, qp, qp),
        f32(heads, kp, qp),
        f32(8, qp),
        f32(2, kp, qp),
        bf(kp, heads * qp),
        bf(kp, heads * qp),
        f32(2, width, hidden),
        f32(width, width),
        f32(4, 8, width),
        f32(8, hidden),
        f32(2, 3 * width, 128),
        pltpu.SemaphoreType.DMA((5,)),
    ]
    if data_count:
        scratch += [f32(2, hidden, 128), f32(2, width, 128)]
        scratch += [f32(2, 3, wide // 2, 128), f32(2, 3, half // 2, 128)]
        scratch += [f32(2, 3, 3 * width // 4, 128), f32(data_count, SENT_ROWS, 128)]
    return pl.pallas_call(
        functools.partial(layer_kernel, patches=patches, heads=heads, data_count=data_count),
        out_shape=(
            sds(full, hidden, dtype=BF),
            sds(images, kp, width),
            sds(images, kp, width),
            sds(3, full, 256, dtype=BF),
            sds(heads, kp, qp),
            pltpu.VMEM((8, qp), F32),
            pltpu.VMEM((8, 128), F32),
            *outs,
        ),
        in_specs=[VM] * 6,
        out_specs=(ANYWHERE,) * 5 + (VM,) * (2 + len(outs)),
        scratch_shapes=scratch,
        compiler_params=pltpu.CompilerParams(vmem_limit_bytes=LAYER_VMEM),
        name="layer",
    )(*near(x, inc, bias, own, oth), vec)


def finish_kernel(*refs, patches, heads):
    (x_ref, own_ref, oth_ref, vec_ref, gate_ref, hp_ref), far_refs = refs[:6], refs[6:11]
    (res_out, gi_out, vec_out, head_ref) = refs[11:15]
    (act_s, mid_s, gm_s, dp_s, place_s), (w, wn, vec_g, rows_s, sems) = refs[15:20], refs[20:]
    images, kp, width = x_ref.shape
    qp = dp_s.shape[1] // images
    half = width // 2
    wide = own_ref.shape[1]
    copies = [
        pltpu.make_async_copy(source, target, sems.at[at])
        for at, (source, target) in enumerate(
            zip(far_refs, (act_s, mid_s, gm_s, dp_s, place_s))
        )
    ]
    for member in copies:
        member.start()
    own_tri = own_ref[2 * width : 3 * width, :]
    oth_tri = oth_ref[2 * width : 3 * width, :]
    for at in range(3):
        span = slice(at * half, (at + 1) * half)
        w[at] = in_tiles(own_tri[:, span], oth_tri[:, span])
    wn[:, 0:wide] = own_ref[width : 2 * width, :]
    wn[:, wide : 2 * wide] = oth_ref[width : 2 * width, :]
    vec_g[...] = jnp.zeros_like(vec_g)
    gain = vec_ref[0:1, :]
    shift = vec_ref[5:6, :]
    for member in copies[:2]:
        member.wait()
    for i in range(images):
        rows = mid_s[i] + nt(act_s[i * qp : i * qp + kp, :], wn[...]) + shift
        rows_s[i * patches : (i + 1) * patches, :] = rows[0:patches]
    res_out[...] = rows_s[...].T
    for member in copies[2:]:
        member.wait()
    for i in range(images):
        n1, spread = norm_parts(x_ref[i].astype(F32))
        g = sum(nt(dp_s[c, i * qp : i * qp + kp, :], w[c]) for c in range(3))
        vec_g[0] += fold(g * n1)
        vec_g[1] += fold(g)
        rows = gm_s[i] + norm_back(g * gain, n1, spread)
        rows_s[i * patches : (i + 1) * patches, :] = rows[0:patches]
    gi_out[...] = rows_s[...].T
    vec_out[...] = jnp.sum(vec_g[...], axis=1)
    parts = offsets(kp, qp)
    rank = lax.axis_index("tensor")
    lane = lax.broadcasted_iota(jnp.int32, (1, 128), 1)
    row = jnp.zeros((1, 128), F32)
    half_heads = heads // 2
    for h in range(heads):
        base = ((rank + h // half_heads) % 2) * (4 * half_heads) + h % half_heads
        g = place_s[h]
        for k in range(3):
            total = jnp.sum(g * parts[k])
            row = row + jnp.where(lane == base + k * half_heads, total, 0.0)
        gate = gate_of(hp_ref, h, 128)
        total = jnp.sum(gate_ref[h : h + 1, :])
        row = row + jnp.where(lane == base + 3 * half_heads, total * gate * (1.0 - gate), 0.0)
    head_ref[...] = row


def run_finish(x, own, oth, vec, gate, hp, act, mid, gm, dp, place, patches):
    images, kp, width = x.shape
    rows = images * patches
    fetched = (act, mid, gm, dp, place)
    return pl.pallas_call(
        functools.partial(finish_kernel, patches=patches, heads=place.shape[0]),
        out_shape=(sds(width, rows), sds(width, rows), sds(2, width), sds(1, 128)),
        in_specs=[VM] * 6 + [ANYWHERE] * 5,
        out_specs=(VM,) * 4,
        scratch_shapes=[
            *[pltpu.VMEM(member.shape, member.dtype) for member in fetched],
            pltpu.VMEM((3, width, 256), BF),
            pltpu.VMEM((width, 2 * own.shape[1]), BF),
            pltpu.VMEM((2, 8, width), F32),
            pltpu.VMEM((rows, width), F32),
            pltpu.SemaphoreType.DMA((5,)),
        ],
        compiler_params=pltpu.CompilerParams(vmem_limit_bytes=32 * 1024 * 1024),
        name="finish",
    )(*near(x, own, oth), vec, gate, hp, *far(*fetched))


def combine_kernel(own_ref, got_ref, out_ref):
    out_ref[...] = (own_ref[...] + got_ref[...].astype(F32)).astype(BF)


def run_combine(own, got):
    return pl.pallas_call(
        combine_kernel,
        out_shape=pltpu.VMEM(own.shape, BF),
        in_specs=[VM] * 2,
        out_specs=VM,
        compiler_params=PARAMS,
        name="combine",
    )(*near(own, got))


def pick_rows(ref, start, count, flip=False):
    total = ref.shape[1] if flip else ref.shape[0]
    row = lax.broadcasted_iota(jnp.int32, (count, total), 0) + start
    col = lax.broadcasted_iota(jnp.int32, (count, total), 1)
    chosen = (row == col).astype(F32)
    return lax.dot_general(
        chosen,
        ref[...],
        (((1,), (1 if flip else 0,)), ((), ())),
        preferred_element_type=F32,
        precision=lax.Precision.HIGHEST,
    )


def share_kernel(_, tri_ref, out_ref, wid_ref, nar_ref, *refs, data_count):
    (wt_f, wo_f, ww_f, wn_f, st, so, sw, sn) = refs
    width, wide = wid_ref.shape
    half = out_ref.shape[0]
    wp, np_, op = width // data_count, wide // data_count // 2, half // data_count // 2
    data_rank = lax.axis_index("dp")
    groups = tri_ref.shape[0] // data_count // 4
    st[0, :, 0 : tri_ref.shape[1]] = pick_rows(tri_ref, data_rank * 4 * groups, 4 * groups)
    put_planes(so, pick_rows(out_ref, data_rank * 2 * op, 2 * op))
    sw[...] = pick_rows(wid_ref, data_rank * wp, wp)
    put_planes(sn, pick_rows(nar_ref, data_rank * 2 * np_, 2 * np_, flip=True))
    tiles = four_row_tiles(st, 0, 0, groups)
    for p in range(groups):
        for k in range(3):
            tile = 128 * (3 * p + k)
            wt_f[0:1, tile : tile + 128] = tiles[k][p : p + 1, :]
    for ref, flat, pairs in ((so, wo_f, op), (sn, wn_f, np_)):
        tiles = even_odd_tiles(ref, 0, pairs)
        for p in range(pairs):
            for k in range(3):
                tile = 128 * (3 * p + k)
                flat[0:1, tile : tile + 128] = tiles[k][p : p + 1, :]
    for p in range(wp):
        ww_f[0:1, wide * p : wide * (p + 1)] = sw[p : p + 1, :]


def run_shares(after, tri, out, wid, nar_t, data_count):
    wide = wid.shape[1]
    share = [member.shape[0] // data_count for member in (tri, out, wid)]
    return pl.pallas_call(
        functools.partial(share_kernel, data_count=data_count),
        out_shape=tuple(sds(1, member.size // data_count) for member in (tri, out, wid, nar_t)),
        in_specs=[VM] * 5,
        out_specs=(VM,) * 4,
        scratch_shapes=[
            pltpu.VMEM((1, share[0], 128), F32),
            pltpu.VMEM((2, share[1], 128), F32),
            pltpu.VMEM((share[2], wide), F32),
            pltpu.VMEM((2, wide // data_count, 128), F32),
        ],
        compiler_params=PARAMS,
        name="weight_shares",
    )(after, tri, out, wid, nar_t)


def spread_rows(flat_ref, from_ref, base, blocks):
    for p in range(blocks):
        for k in range(3):
            at = base + k * blocks + p
            tile = 128 * (3 * p + k)
            flat_ref[0:1, tile : tile + 128] = from_ref[at : at + 1, :]


def sum_kernel(got_ref, late_ref, head_ref, _, *refs, blocks, span):
    (tri_f, out_f, wid_f, nar_f, pay_ref, tot) = refs
    tri_b, out_b, wid_b, nar_b = blocks
    vec_n, hid_n = span
    tot[...] = jnp.sum(got_ref[...].astype(F32), axis=0)
    spread_rows(wid_f, tot, 0, wid_b)
    spread_rows(nar_f, tot, 3 * wid_b, nar_b)
    spread_rows(out_f, tot, 3 * (wid_b + nar_b), out_b)
    at = 3 * (wid_b + nar_b + out_b)
    spread_rows(tri_f, tot, at + 1, tri_b)
    early = tot[0:at, :]
    late = tot[at + 1 : at + 1 + 3 * tri_b, :]
    small = tot[at : at + 1, :]
    hid = small[:, vec_n : vec_n + hid_n]
    squares = jnp.sum(early * early) + jnp.sum(late * late) + jnp.sum(hid * hid)
    lane = lax.broadcasted_iota(jnp.int32, (1, 128), 1)
    tails = jnp.concatenate([late_ref[0:1, 128:], late_ref[1:2, 128:]], axis=1)
    last = jnp.concatenate([head_ref[:, 0:SMALL_AT], small[:, 0 : 128 - SMALL_AT]], axis=1)
    payload = jnp.concatenate(
        [late_ref[:, :128], tails, jnp.where(lane == 127, squares, last)], axis=0
    )
    pay_ref[...] = jnp.broadcast_to(payload[None], pay_ref.shape)


def run_sums(got, late_vec, head, after, blocks, span):
    count = got.shape[0]
    return pl.pallas_call(
        functools.partial(sum_kernel, blocks=blocks, span=span),
        out_shape=(
            *[sds(1, 3 * 128 * member) for member in blocks],
            sds(2 * count, 4, 128),
        ),
        in_specs=[VM] * 4,
        out_specs=(VM,) * 5,
        scratch_shapes=[pltpu.VMEM((SENT_ROWS, 128), F32)],
        compiler_params=PARAMS,
        name="sums",
    )(got, late_vec, head, after)


def adam_parts(weight, gradient, moment, squares, rate, decay):
    moment_new = BETA_ONE * moment + (1.0 - BETA_ONE) * gradient
    squares_new = BETA_TWO * squares + (1.0 - BETA_TWO) * gradient * gradient
    quotient = (moment_new / (1.0 - BETA_ONE**STEP)) / (
        jnp.sqrt(squares_new / (1.0 - BETA_TWO**STEP)) + ADAM_EPS
    )
    return moment_new, squares_new, weight - rate * (quotient + decay * weight)


def gathered(last, width, wide):
    count = last.shape[0] // 2
    vec_n, hid_n = 4 * width // count, wide // count
    even = last[pl.ds(0, count, stride=2), :]
    odd = last[pl.ds(1, count, stride=2), :]
    mine = jnp.where(lax.axis_index("tensor") == 0, even, odd)

    def placed(part, times):
        n = part.shape[1]
        value = jnp.concatenate([part] * times, axis=1)
        row = lax.broadcasted_iota(jnp.int32, value.shape, 0)
        lane = lax.broadcasted_iota(jnp.int32, value.shape, 1)
        at = jnp.floor((lane.astype(F32) + 0.5) * (1.0 / n)).astype(jnp.int32)
        return value, row, at

    per_row = width // vec_n
    value, row, at = placed(even[:, SMALL_AT : SMALL_AT + vec_n], per_row)
    vector = jnp.concatenate(
        [
            jnp.sum(jnp.where(row == at + v * per_row, value, 0.0), axis=0, keepdims=True)
            for v in range(4)
        ],
        axis=0,
    )
    at_hidden = SMALL_AT + vec_n
    value, row, at = placed(mine[:, at_hidden : at_hidden + hid_n], count)
    return vector, jnp.sum(jnp.where(row == at, value, 0.0), axis=0, keepdims=True)


def adam_kernel(got_ref, hp_ref, vec_ref, hb_ref, *refs, given_sums):
    refs = list(refs)
    sums = [refs.pop(0) for _ in range(2 * given_sums)]
    grads = refs[0:4]
    weights = refs[4:8]
    states = refs[8:22]
    outs = refs[22:43]
    norm_ref, last = refs[43:45]
    width = vec_ref.shape[1]
    half_heads = hp_ref.shape[0]
    tail = width - 128
    total = jnp.sum(got_ref[...], axis=0)
    if given_sums:
        early, hid = sums[0][...], sums[1][...]
    else:
        last[...] = got_ref[:, 3, :]
        early, hid = gathered(last, width, hb_ref.shape[0])
    late = jnp.concatenate(
        [
            total[0:2, :],
            jnp.concatenate([total[2:3, :tail], total[2:3, tail : 2 * tail]], axis=0),
        ],
        axis=1,
    )
    vector = jnp.concatenate([late, early], axis=0)
    lane = lax.broadcasted_iota(jnp.int32, (1, 128), 1)
    heads_row = jnp.where(lane < 8 * half_heads, total[3:4, :], 0.0)
    squares = (
        jnp.sum(jnp.where(lane == 127, total[3:4, :], 0.0))
        + jnp.sum(vector * vector)
        + jnp.sum(heads_row * heads_row)
    )
    norm = jnp.sqrt(jnp.full((1, 128), squares))
    norm_ref[0] = jnp.sum(norm[:, 0:1])
    factor = (CLIP_AT / jnp.maximum(norm, CLIP_AT))[:, 0:1]
    span = 4 * half_heads
    mine = jnp.where(lax.axis_index("tensor") == 0, heads_row[:, :span], heads_row[:, span : 2 * span])
    head = jnp.concatenate(
        [
            jnp.concatenate(
                [mine[:, c * half_heads + h : c * half_heads + h + 1] for c in range(4)], axis=1
            )
            for h in range(half_heads)
        ],
        axis=0,
    )
    given = [ref[...] for ref in grads] + [vector, hid, head]
    wide = hid.shape[1]
    held = [ref[...] for ref in weights] + [vec_ref[...], hb_ref[...].reshape(1, wide), hp_ref[...]]
    for at in range(7):
        renewed = adam_parts(
            held[at],
            given[at] * factor,
            states[2 * at][...].reshape(held[at].shape),
            states[2 * at + 1][...].reshape(held[at].shape),
            RATES[at],
            DECAYS[at],
        )
        for step in range(3):
            out = outs[3 * at + step]
            out[...] = renewed[step].reshape(out.shape)


def run_adam(got, hp_t, vec, hb, sums, grads, weights, states):
    shapes = []
    for at in range(7):
        shapes += [sds(*states[2 * at].shape)] * 3
    return pl.pallas_call(
        functools.partial(adam_kernel, given_sums=len(sums) // 2),
        out_shape=(*shapes, sds(1)),
        in_specs=[VM] * (4 + len(sums) + 4 + 4 + 14),
        out_specs=(VM,) * 21 + (SM,),
        scratch_shapes=[pltpu.VMEM((got.shape[0], 128), F32)],
        compiler_params=PARAMS,
        name="adam",
    )(got, hp_t, vec, hb, *sums, *grads, *weights, *states)


def plain_chunks(halves, data_count, rows):
    sides = []
    for side in range(2):
        flat = jnp.concatenate([own_first[side].reshape(data_count, -1) for own_first in halves], axis=1)
        flat = jnp.pad(flat, ((0, 0), (0, rows * 128 - flat.shape[1])))
        sides.append(flat.reshape(data_count, rows, 128))
    return sides[0], sides[1].astype(BF)


def on_device(
    tokens,
    cotangent,
    keep_mask,
    triple_weight,
    outward_weight,
    widen_weight,
    narrow_weight,
    vectors,
    hidden_bias,
    head_params,
    triple_moment,
    triple_square,
    outward_moment,
    outward_square,
    widen_moment,
    widen_square,
    narrow_moment,
    narrow_square,
    vector_moment,
    vector_square,
    hidden_moment,
    hidden_square,
    head_moment,
    head_square,
):
    tensor_rank = lax.axis_index("tensor")
    data_rank = lax.axis_index("dp")
    data_count = lax.axis_size("dp")
    images = keep_mask.shape[0] // 2
    patches = keep_mask.shape[1]
    heads = 2 * head_params.shape[1]
    depth = triple_weight.shape[1]
    half = triple_weight.shape[2]
    wide = widen_weight.shape[1]
    triple_rows = triple_weight.reshape(3 * depth, half)
    narrow_t = narrow_weight.T
    head_t = head_params.T
    fast = (
        depth == 192
        and half == 96
        and wide == 384
        and depth % data_count == 0
        and wide % (2 * data_count) == 0
        and half % (2 * data_count) == 0
        and 3 * depth % (4 * data_count) == 0
    )
    if fast:
        early_rows = (2 * depth * wide + half * depth) // data_count // 128
        late_rows = 3 * depth * half // data_count // 128
        fast = SENT_EARLY <= early_rows and early_rows + 1 + late_rows <= SENT_ROWS
    chunked = data_count if fast else 0
    swap = [(0, 1), (1, 0)]

    own, *rows_near = run_pack(
        triple_weight,
        outward_weight,
        widen_weight,
        narrow_t,
        hidden_bias,
        head_t,
        tokens.T,
        cotangent.T,
        keep_mask,
    )
    other = lax.ppermute(own, "tensor", swap)
    x, inc, bias = run_prepare(*rows_near)
    act, middle, grad_middle, dp, place, gate, hp, *sums = run_layer(
        x, inc, bias, own, other, vectors, heads, patches, chunked
    )
    if fast:
        mine, theirs = sums
    else:
        nar_g, wid_g, out_g, vec_g, hid_g, tri_g = sums
        early_mine = jnp.sum(vec_g, axis=1).reshape(1, -1)
        early_both = jnp.broadcast_to(early_mine, (data_count, early_mine.size))
        hidden_both = jnp.broadcast_to(
            jnp.sum(hid_g, axis=0).reshape(2, 1, wide), (2, data_count, wide)
        )
        early = plain_chunks(
            [
                wid_g.reshape(depth, 2, wide).transpose(1, 0, 2),
                nar_g.reshape(2, -1),
                out_g.reshape(2, -1),
                (early_both, early_both),
                hidden_both,
            ],
            data_count,
            EARLY_ROWS,
        )
        late = plain_chunks(
            [tri_g.reshape(3 * depth, 2, half).transpose(1, 0, 2)], data_count, LATE_ROWS
        )
        mine, theirs = (jnp.concatenate(pair, axis=1) for pair in zip(early, late))
    received = lax.ppermute(theirs, "tensor", swap)
    chunks = run_combine(mine, received)
    got = lax.all_to_all(chunks, "dp", 0, 0, tiled=False)
    result_t, grad_input_t, late_vec, head_row = run_finish(
        x, own, other, vectors, gate, hp, act, middle, grad_middle, dp, place, patches
    )
    if fast:
        wt_f, wo_f, ww_f, wn_f = run_shares(
            gate, triple_rows, outward_weight, widen_weight, narrow_t, data_count
        )
        blocks = [
            member.size // data_count // 384
            for member in (triple_rows, outward_weight, widen_weight, narrow_t)
        ]
        span = (4 * depth // data_count, wide // data_count)
        tri_f, out_f, wid_f, nar_f, payload = run_sums(
            got, late_vec, head_row, wo_f, blocks, span
        )
        sums = ()
    else:
        total = jnp.sum(got.astype(F32), axis=0)
        early_sum = total[:EARLY_ROWS].reshape(1, -1)
        masters = (widen_weight, narrow_weight, outward_weight)
        sizes = [member.size // data_count for member in masters] + [4 * depth, wide]
        cuts = [sum(sizes[:at]) for at in range(6)]
        wid_f, nar_f, out_f, early_vec, hid = (
            early_sum[:, cuts[at] : cuts[at + 1]] for at in range(5)
        )
        early_vec = early_vec.reshape(4, depth)
        share = triple_rows.size // data_count
        tri_f = total[EARLY_ROWS:].reshape(1, -1)[:, :share]

        def weight_share(member):
            length = member.size // data_count
            return lax.dynamic_slice_in_dim(member.reshape(1, -1), data_rank * length, length, 1)

        ww_f, wn_f, wo_f = (weight_share(member) for member in masters)
        wt_f = weight_share(triple_rows)
        squares = sum(jnp.sum(member * member) for member in (wid_f, nar_f, out_f, tri_f))
        squares = squares + jnp.where(data_rank == 0, jnp.sum(hid * hid), 0.0)
        lane = lax.broadcasted_iota(jnp.int32, (1, 128), 1)
        payload = jnp.concatenate(
            [
                late_vec[:, :128],
                late_vec[:, 128:].reshape(1, 128),
                jnp.where(lane == 127, squares, head_row),
            ]
        )
        payload = jnp.broadcast_to(payload[None], (2 * data_count, 4, 128))
        sums = (early_vec, hid)
    last_got = lax.all_to_all(payload, ("dp", "tensor"), 0, 0, tiled=False)
    renewed = run_adam(
        last_got,
        head_t,
        vectors,
        hidden_bias,
        sums,
        (tri_f, out_f, wid_f, nar_f),
        (wt_f, wo_f, ww_f, wn_f),
        (
            triple_moment,
            triple_square,
            outward_moment,
            outward_square,
            widen_moment,
            widen_square,
            narrow_moment,
            narrow_square,
            vector_moment,
            vector_square,
            hidden_moment,
            hidden_square,
            head_moment.T,
            head_square.T,
        ),
    )
    hidden_new = renewed[15:18]
    head_new = [member.T for member in renewed[18:21]]
    return (result_t.T, grad_input_t.T, *renewed[:15], *hidden_new, *head_new, renewed[21].reshape(()))


def solution(mesh):
    return jax.shard_map(
        on_device,
        mesh=mesh,
        in_specs=(
            P(("dp", "tensor"), None),
            P(("dp", "tensor"), None),
            P("dp", None),
            P(None, None, "tensor"),
            P("tensor", None),
            P(None, "tensor"),
            P("tensor", None),
            P(),
            P("tensor"),
            P(None, "tensor"),
            P("tensor", "dp"),
            P("tensor", "dp"),
            P("tensor", "dp"),
            P("tensor", "dp"),
            P("tensor", "dp"),
            P("tensor", "dp"),
            P("tensor", "dp"),
            P("tensor", "dp"),
            P(),
            P(),
            P("tensor"),
            P("tensor"),
            P(None, "tensor"),
            P(None, "tensor"),
        ),
        out_specs=(
            P(("dp", "tensor"), None),
            P(("dp", "tensor"), None),
            P("tensor", "dp"),
            P("tensor", "dp"),
            P("tensor", "dp"),
            P("tensor", "dp"),
            P("tensor", "dp"),
            P("tensor", "dp"),
            P("tensor", "dp"),
            P("tensor", "dp"),
            P("tensor", "dp"),
            P("tensor", "dp"),
            P("tensor", "dp"),
            P("tensor", "dp"),
            P(),
            P(),
            P(),
            P("tensor"),
            P("tensor"),
            P("tensor"),
            P(None, "tensor"),
            P(None, "tensor"),
            P(None, "tensor"),
            P(),
        ),
        check_vma=False,
    )
```

```python
import functools
import math

import jax
import jax.numpy as jnp
from jax import lax
from jax.experimental import pallas as pl
from jax.experimental.pallas import tpu as pltpu
from jax.sharding import PartitionSpec as P

GRID = 14
STEP = 10
EPS_NORM = 1e-06
CLIP_AT = 1.0
BETA_ONE = 0.9
BETA_TWO = 0.95
ADAM_EPS = 1e-08
RATES = (0.1, 0.5, 0.1, 0.05, 0.3, 0.1, 0.3)
DECAYS = (0.05, 0.05, 0.05, 0.05, 0.0, 0.0, 0.0)
LOG2E = 1.4426950408889634
BF = jnp.bfloat16
F32 = jnp.float32
LAYER_VMEM = 52 * 1024 * 1024
SMALL_VMEM = 16 * 1024 * 1024
EARLY_ROWS = 96
LATE_ROWS = 32
SENT_EARLY = 80
SENT_ROWS = 112
SMALL_AT = 16
PAIR = 2
VM = pl.BlockSpec(memory_space=pltpu.VMEM)
ANYWHERE = pl.BlockSpec(memory_space=pl.ANY)
SM = pl.BlockSpec(memory_space=pltpu.SMEM)
PARAMS = pltpu.CompilerParams(vmem_limit_bytes=SMALL_VMEM)


def sds(*dims, dtype=F32):
    return jax.ShapeDtypeStruct(dims, dtype)


def near(*arrays):
    return [pltpu.with_memory_space_constraint(member, pltpu.VMEM) for member in arrays]


def far(*arrays):
    return [pltpu.with_memory_space_constraint(member, pltpu.HBM) for member in arrays]


def nn(a, b):
    return lax.dot_general(a, b, (((1,), (0,)), ((), ())), preferred_element_type=F32)


def nt(a, b):
    return lax.dot_general(a, b, (((1,), (1,)), ((), ())), preferred_element_type=F32)


def norm_parts(v):
    width = v.shape[-1]
    average = jnp.sum(v, axis=-1, keepdims=True) * (1.0 / width)
    centred = v - average
    variance = jnp.sum(centred * centred, axis=-1, keepdims=True) * (1.0 / width)
    spread = lax.rsqrt(variance + EPS_NORM)
    return centred * spread, spread


def norm_back(e, n, spread):
    width = e.shape[-1]
    mean_e = jnp.sum(e, axis=-1, keepdims=True) * (1.0 / width)
    mean_en = jnp.sum(e * n, axis=-1, keepdims=True) * (1.0 / width)
    return spread * (e - mean_e - n * mean_en)


def fold(v):
    rows = v.shape[0]
    return jnp.sum(v.reshape(rows // 8, 8, v.shape[1]), axis=0)


def gelu_parts(x):
    phi = 0.5 + 0.5 * lax.erf(x * math.sqrt(0.5))
    density = jnp.exp2((x * x) * (-0.5 * LOG2E)) * (1.0 / math.sqrt(2.0 * math.pi))
    return x * phi, phi + x * density


def places(count, lanes, dim):
    at = lax.broadcasted_iota(jnp.int32, (count, lanes), dim).astype(F32)
    row = jnp.floor((at + 0.5) * (1.0 / GRID))
    return at - row * GRID, row


def offsets(kp, qp):
    kc, kr = places(kp, qp, 0)
    qc, qr = places(kp, qp, 1)
    a = kc - qc
    b = kr - qr
    return a, b, a * a + b * b


def head_mask(hd, h):
    lane = lax.broadcasted_iota(jnp.int32, (STRIP, 128), 1)
    return ((lane >= h * hd) & (lane < (h + 1) * hd)).astype(BF)


def in_tiles(own, oth):
    gap = jnp.zeros((own.shape[0], 128 - own.shape[1]), own.dtype)
    return jnp.concatenate([own, gap, oth, gap], axis=1)


def gate_of(hp_ref, h, lanes):
    return 1.0 / (1.0 + jnp.exp(-jnp.broadcast_to(hp_ref[h : h + 1, 3:4], (1, lanes))))


def bf_parts(value, count=3):
    parts = []
    for _ in range(count):
        part = value.astype(BF).astype(F32)
        parts.append(part)
        value = value - part
    return parts


def key_operand(kp):
    kc, kr = places(kp, 128, 0)
    lane = lax.broadcasted_iota(jnp.int32, (kp, 128), 1)
    value = jnp.where(lane < 3, kc, jnp.where(lane < 6, kr, jnp.where(lane < 9, kc * kc, kr * kr)))
    return jnp.where(lane < 12, value, 0.0).astype(BF)


def query_operand(hp_ref, h, qp):
    p = [LOG2E * jnp.broadcast_to(hp_ref[h : h + 1, at : at + 1], (16, qp)) for at in range(3)]
    qc, qr = places(16, qp, 1)
    row = lax.broadcasted_iota(jnp.int32, (16, qp), 0)
    value = jnp.where(row < 3, p[0] - 2.0 * p[2] * qc, jnp.where(row < 6, p[1] - 2.0 * p[2] * qr, p[2]))
    parts = bf_parts(value)
    place = row - 3 * ((row >= 3).astype(jnp.int32) + (row >= 6) + (row >= 9))
    value = jnp.where(place == 0, parts[0], jnp.where(place == 1, parts[1], parts[2]))
    return jnp.where(row < 12, value, jnp.where(row == 12, 1.0, 0.0)).astype(BF)


STRIP = 16
LAG = 3
WAIT = 3


def interleave(*streams):
    streams = [member for member in streams if member is not None]
    while streams:
        alive = []
        for member in streams:
            try:
                next(member)
                alive.append(member)
            except StopIteration:
                pass
        streams = alive


def staged(count, lag, *stages):
    for t in range(count + lag * (len(stages) - 1)):
        for k, stage in enumerate(stages):
            if 0 <= t - k * lag < count:
                stage(t - k * lag)
        yield


def slow(stream, count):
    for _ in range(count):
        yield
        try:
            next(stream)
        except StopIteration:
            return


def cut(value, r):
    return value[r * STRIP : (r + 1) * STRIP]


def rows_of(r):
    return pl.ds(r * STRIP, STRIP)


def put_planes(ref, value):
    width = value.shape[1]
    ref[0] = value[:, :128]
    ref[1, :, 0 : width - 128] = value[:, 128:]


def even_odd_tiles(ref, start, pairs):
    even = [ref[at, pl.ds(start, pairs, stride=2), :] for at in range(2)]
    odd = [ref[at, pl.ds(start + 1, pairs, stride=2), :] for at in range(2)]
    return (
        even[0],
        jnp.concatenate([even[1][:, :64], odd[0][:, :64]], axis=1),
        jnp.concatenate([odd[0][:, 64:], odd[1][:, :64]], axis=1),
    )


def four_row_tiles(ref, plane, start, groups):
    r = [ref[plane, pl.ds(start + at, groups, stride=4), :] for at in range(4)]
    return (
        jnp.concatenate([r[0][:, :96], r[1][:, :32]], axis=1),
        jnp.concatenate([r[1][:, 32:96], r[2][:, :64]], axis=1),
        jnp.concatenate([r[2][:, 64:96], r[3][:, :96]], axis=1),
    )


def pack_kernel(*refs):
    given, pack_ref, passed, held, sems = refs[:9], refs[9], refs[10:13], refs[13:19], refs[19]
    copies = [
        pltpu.make_async_copy(source, target, sems.at[at])
        for at, (source, target) in enumerate(zip(given, [*held, *passed]))
    ]
    for member in copies:
        member.start()
    for member in copies[:6]:
        member.wait()
    tri_ref, out_ref, wid_ref, nar_ref, hb_ref, hp_ref = held
    depth, wide = wid_ref.shape
    pack_ref[0:depth, :] = wid_ref[...].astype(BF)
    pack_ref[depth : 2 * depth, :] = nar_ref[...].astype(BF)
    pack_ref[2 * depth : 3 * depth, :] = jnp.concatenate(
        [tri_ref[0], tri_ref[1], tri_ref[2], out_ref[...].T], axis=1
    ).astype(BF)
    heads_here = hp_ref.shape[0]
    hp = jnp.concatenate([hp_ref[...], jnp.zeros((heads_here, wide - 4), F32)], axis=1)
    left = jnp.concatenate([hb_ref[...].reshape(1, wide), hp], axis=0)
    parts = []
    for _ in range(3):
        part = left.astype(BF).astype(F32)
        parts.append(part)
        left = left - part
    parts.append(jnp.zeros((16 - 3 * (1 + heads_here), wide), F32))
    pack_ref[3 * depth : 3 * depth + 16, :] = jnp.concatenate(parts, axis=0).astype(BF)
    for member in copies[6:]:
        member.wait()


def run_pack(tri, out, wid, nar_t, hb, hp_t, *passed):
    depth, wide = wid.shape
    given = (tri, out, wid, nar_t, hb, hp_t)
    return pl.pallas_call(
        pack_kernel,
        out_shape=(
            pltpu.VMEM((3 * depth + 16, wide), BF),
            *[pltpu.VMEM(member.shape, member.dtype) for member in passed],
        ),
        in_specs=[pl.BlockSpec(memory_space=pltpu.HBM)] * 9,
        out_specs=(VM,) * 4,
        scratch_shapes=[
            *[pltpu.VMEM(member.shape, member.dtype) for member in given],
            pltpu.SemaphoreType.DMA((9,)),
        ],
        compiler_params=PARAMS,
        name="pack_weights",
    )(*far(*given, *passed))


def prepare_kernel(tok_ref, cot_ref, keep_ref, x_ref, inc_ref, bias_ref, xs, cs):
    images, kp, width = x_ref.shape
    patches = keep_ref.shape[1]
    rows = images * patches
    qp = -(-patches // 128) * 128
    mine = keep_ref[pl.ds(pl.multiple_of(lax.axis_index("tensor") * images, 8), images), :].astype(F32)
    columns = jnp.concatenate([mine, jnp.zeros((images, qp - patches), F32)], axis=1).T
    xs[0:rows, :] = tok_ref[...].T.astype(F32)
    cs[0:rows, :] = cot_ref[...].T.astype(F32)
    xs[rows : rows + 16, :] = jnp.zeros((16, width), F32)
    cs[rows : rows + 16, :] = jnp.zeros((16, width), F32)
    for i in range(images):
        span = slice(i * patches, i * patches + kp)
        keep = jnp.broadcast_to(columns[:kp, i : i + 1], (kp, 128))
        keep_wide = jnp.concatenate([keep, keep[:, : width - 128]], axis=1)
        x_ref[i] = xs[span, :].astype(BF)
        inc_ref[i] = (cs[span, :] * keep_wide).astype(BF)
        bias_ref[i] = ((keep - 1.0) * 1e30).astype(BF)


def run_prepare(tok_t, cot_t, keep_mask):
    images = keep_mask.shape[0] // 2
    kp = -(-keep_mask.shape[1] // 16) * 16
    width, rows_here = tok_t.shape
    rows = pltpu.VMEM((images, kp, width), BF)
    return pl.pallas_call(
        prepare_kernel,
        out_shape=(rows, rows, pltpu.VMEM((images, kp, 128), BF)),
        in_specs=[VM] * 3,
        out_specs=(VM,) * 3,
        scratch_shapes=[pltpu.VMEM((rows_here + 16, width), F32)] * 2,
        compiler_params=PARAMS,
        name="prepare",
    )(*near(tok_t, cot_t, keep_mask))


def layer_kernel(*refs, patches, heads, data_count):
    (x_ref, inc_ref, bias_ref, own_ref, oth_ref, vec_ref) = refs[:6]
    far_refs = refs[6:11]
    gate_ref, hp_ref = refs[11:13]
    outs = refs[13:15] if data_count else refs[13:19]
    at = 13 + len(outs)
    (wq, wk, wv, wo, wop, wi, wn, hp_s, key_p, key_i, query_p) = refs[at : at + 11]
    at += 11
    (fst_s, keys_s, vt_s, qm_s, dmm_s, v_s, kt_s, soft_s, mid_s, n2_s) = refs[at : at + 10]
    at += 10
    (sec_s, spr_s, low_s, stat_s, back_s) = refs[at : at + 5]
    at += 5
    (first_t, mix_t, left_t, right_s, gm_s, dp_s, s_buf, p_buf, att_buf) = refs[at : at + 9]
    at += 9
    (place_g, gate_g, da_buf, att_s, ds_s, wide_g, out_g, vec_g, hid_g, tri_p, sems) = refs[at : at + 11]
    at += 11
    if data_count:
        nar_p, out_p, nar_f, out_f, tri_f, tmp = refs[at : at + 6]
    images, kp, width = x_ref.shape
    qp = soft_s.shape[4]
    hd = width // heads
    half = width // 2
    half_heads = heads // 2
    wide = own_ref.shape[1]
    hidden = 2 * wide
    strips = kp // STRIP
    c_scale = LOG2E / math.sqrt(hd)
    back_scale = 1.0 / math.sqrt(hd)
    v = [vec_ref[k : k + 1, :] for k in range(6)]

    key_p[...] = key_operand(kp)
    query_p[...] = jnp.zeros_like(query_p)
    for ref in (hid_g, vec_g, place_g, gate_g):
        ref[...] = jnp.zeros_like(ref)
    for k in range(2):
        att_buf[k, kp:, :] = jnp.zeros((qp - kp, qp), BF)
    for k in range(2):
        fst_s[k, kp:, :] = jnp.zeros((qp - kp, width), BF)
    for k in range(images):
        for side in range(2):
            right_s[side, k * qp + kp : (k + 1) * qp, :] = jnp.zeros((qp - kp, hidden), BF)
        for c in range(3):
            dp_s[c, k * qp + kp : (k + 1) * qp, :] = jnp.zeros((qp - kp, 256), BF)
    sec_s[:, width:] = (lax.broadcasted_iota(jnp.int32, (kp, 256 - width), 1) < 3).astype(BF)
    gap = jnp.zeros((qp - kp, width), BF)
    one_lane = (lax.broadcasted_iota(jnp.int32, (STRIP, 128), 1) == half).astype(BF)
    masks = [head_mask(hd, h) for h in range(half_heads)]
    tiles = [slice(128 * t, 128 * (t + 1)) for t in range(2)]
    bias_lane = (lax.broadcasted_iota(jnp.int32, (kp, 128), 1) == 12).astype(BF)

    def columns_at(i):
        return pl.ds(pl.multiple_of(i * qp, 128), qp)


    def first_norm(i):
        kept = {}

        def mean(r):
            x = x_ref[i, rows_of(r), :].astype(F32)
            kept[r] = x - jnp.sum(x, axis=-1, keepdims=True) * (1.0 / width)

        def spread(r):
            kept[r] = (kept[r], jnp.sum(kept[r] * kept[r], axis=-1, keepdims=True) * (1.0 / width))

        def put(r):
            centred, variance = kept[r]
            fst_s[i % 2, rows_of(r), :] = (centred * lax.rsqrt(variance + EPS_NORM) * v[0] + v[1]).astype(BF)

        yield from staged(strips, LAG, mean, spread, put)

    def project(i, part):
        first_q = fst_s[i % 2]
        if part == 0:
            queries = nn(first_q, wq[...]).astype(BF)
            yield
            for r in range(qp // STRIP):
                for h in range(heads):
                    tile = cut(queries[:, tiles[h // half_heads]], r)
                    qm_s[i, h, rows_of(r), :] = tile * masks[h % half_heads] + one_lane
                yield
        elif part == 1:
            keys = nn(first_q, wk[...]).astype(BF)
            yield
            for r in range(strips):
                bias = bias_ref[i, rows_of(r), :]
                key_i[rows_of(r), :] = key_p[rows_of(r), :] + bias * cut(bias_lane, r)
                for t in range(2):
                    keys_s[rows_of(r), tiles[t]] = cut(keys[:, tiles[t]], r) + bias * one_lane
                yield
            kt_s[i] = keys.T
            yield
        else:
            values = nn(first_q, wv[...]).astype(BF)
            yield
            v_s[i] = values[:kp]
            vt_s[...] = values.T
            yield
            yield
            first_t[:, columns_at(i)] = first_q.T
            yield

    def head_rows(h):
        first_row = 128 * (h // half_heads) + hd * (h % half_heads)
        return slice(first_row, first_row + hd)


    def scores(i, h):
        s = nt(keys_s[:, tiles[h // half_heads]], qm_s[i, h])
        p = nn(key_i[...], query_p[h])
        m, pm = cut(s, 0), cut(p, 0)
        for r in range(strips):
            yield
            s_buf[h, rows_of(r), :] = cut(s, r)
            p_buf[h, rows_of(r), :] = cut(p, r)
            m = jnp.maximum(m, cut(s, r))
            pm = jnp.maximum(pm, cut(p, r))
        stat_s[4 * h : 4 * h + 1, :] = jnp.max(m, axis=0, keepdims=True)
        stat_s[4 * h + 1 : 4 * h + 2, :] = jnp.max(pm, axis=0, keepdims=True)

    def exponents(h):
        m, pm = stat_s[4 * h : 4 * h + 1, :], stat_s[4 * h + 1 : 4 * h + 2, :]
        z = jnp.zeros((STRIP, qp), F32)
        pz = jnp.zeros((STRIP, qp), F32)
        for r in range(strips):
            yield
            e = jnp.exp2((s_buf[h, rows_of(r), :] - m) * c_scale)
            pe = jnp.exp2(p_buf[h, rows_of(r), :] - pm)
            s_buf[h, rows_of(r), :] = e
            p_buf[h, rows_of(r), :] = pe
            z = z + e
            pz = pz + pe
        gate = gate_of(hp_s, h, qp)
        stat_s[4 * h + 2 : 4 * h + 3, :] = (1.0 - gate) / jnp.sum(z, axis=0, keepdims=True)
        stat_s[4 * h + 3 : 4 * h + 4, :] = gate / jnp.sum(pz, axis=0, keepdims=True)

    def mixing(i, h):
        a, b = stat_s[4 * h + 2 : 4 * h + 3, :], stat_s[4 * h + 3 : 4 * h + 4, :]
        for r in range(strips):
            yield
            content = s_buf[h, rows_of(r), :] * a
            located = p_buf[h, rows_of(r), :] * b
            soft_s[i, h, 0, rows_of(r), :] = content
            soft_s[i, h, 1, rows_of(r), :] = located
            att_buf[h % 2, rows_of(r), :] = (content + located).astype(BF)
        yield
        mix_t[h * hd : (h + 1) * hd, columns_at(i)] = nn(
            vt_s[head_rows(h), :], att_buf[h % 2]
        ).astype(BF)


    def strip_rows(i, r):
        return pl.ds(pl.multiple_of(i * qp + r * STRIP, 16), STRIP)

    def image_rows(i):
        return pl.ds(pl.multiple_of(i * qp, 16), kp)

    def start(i):
        attn = nt(mix_t[:, columns_at(i)].T[:kp], wo[...])
        for _ in range(WAIT + 2):
            yield
        kept = {}

        def mean(r):
            middle = x_ref[i, rows_of(r), :].astype(F32) + cut(attn, r) + v[4]
            mid_s[i, rows_of(r), :] = middle
            kept[r] = middle - jnp.sum(middle, axis=-1, keepdims=True) * (1.0 / width)

        def vary(r):
            kept[r] = (kept[r], jnp.sum(kept[r] * kept[r], axis=-1, keepdims=True) * (1.0 / width))

        def put(r):
            centred, variance = kept[r]
            spread = lax.rsqrt(variance + EPS_NORM)
            n2 = centred * spread
            n2_s[rows_of(r), :] = n2
            spr_s[rows_of(r), :] = spread
            sec_s[rows_of(r), 0:width] = (n2 * v[2] + v[3]).astype(BF)

        yield from staged(strips, LAG, mean, vary, put)
        left_t[0, :, columns_at(i)] = jnp.concatenate([inc_ref[i], gap], axis=0).T
        yield
        left_t[1, :, columns_at(i)] = jnp.concatenate([sec_s[:, 0:width], gap], axis=0).T

    def chunk(i, c, on):
        lanes = pl.ds(c * 256, 256)
        before = nn(sec_s[...], wi[:, lanes])
        back = nn(inc_ref[i], wn[:, lanes])
        total = jnp.zeros((8, 256), F32)
        for r in range(strips):
            yield
            gelu, slope = gelu_parts(cut(before, r))
            right_s[0, strip_rows(i, r), lanes] = gelu.astype(BF)
            grad_before = cut(back, r) * slope
            right_s[1, strip_rows(i, r), lanes] = grad_before.astype(BF)
            total = total + fold(grad_before)
        hid_g[:, lanes] += jnp.where(on, total, 0.0)

    def end(i, on):
        grad_second = nt(right_s[1, image_rows(i), :], wi[0:width, :])
        totals = [jnp.zeros((8, width), F32)] * 4
        mids = []
        for _ in range(WAIT):
            yield
        kept = {}

        def means(r):
            n2 = n2_s[rows_of(r), :]
            g = cut(grad_second, r)
            e = g * v[2]
            mean_e = jnp.sum(e, axis=-1, keepdims=True) * (1.0 / width)
            mean_en = jnp.sum(e * n2, axis=-1, keepdims=True) * (1.0 / width)
            kept[r] = (e, mean_e, mean_en)
            for k, term in enumerate((g * n2, g)):
                totals[k] = totals[k] + fold(term)

        def put(r):
            e, mean_e, mean_en = kept[r]
            n2 = n2_s[rows_of(r), :]
            incoming = inc_ref[i, rows_of(r), :].astype(F32)
            spread = spr_s[rows_of(r), :]
            grad_middle = incoming + spread * (e - mean_e - n2 * mean_en)
            gm_s[i, rows_of(r), :] = grad_middle
            mids.append(grad_middle.astype(BF))
            for k, term in enumerate((grad_middle, incoming)):
                totals[2 + k] = totals[2 + k] + fold(term)

        yield from staged(strips, LAG, means, put)
        for k in range(4):
            vec_g[k] += jnp.where(on, totals[k], 0.0)
        mid_low = jnp.concatenate([*mids, gap], axis=0)
        yield
        dm = nn(mid_low, wop[...]).astype(BF)
        for r in range(qp // STRIP):
            yield
            for h in range(heads):
                tile = cut(dm[:, tiles[h // half_heads]], r)
                dmm_s[i, h, rows_of(r), :] = tile * masks[h % half_heads]
        yield
        low_s[pl.ds(pl.multiple_of(i * qp, 16), qp), :] = mid_low

    blocks = hidden // 256

    def forward_step(i, carry):
        one, two = jnp.maximum(i - 1, 0), jnp.maximum(i - 2, 0)
        after = jnp.minimum(i + 1, images - 1)
        on_one, on_two = i > 0, i > 1
        interleave(scores(i, 0), exponents(3), mixing(one, 2), chunk(two, 1, on_two), first_norm(after))
        interleave(scores(i, 1), exponents(0), mixing(one, 3), chunk(two, 2, on_two))
        interleave(
            scores(i, 2),
            exponents(1),
            mixing(i, 0),
            end(two, on_two),
            start(one),
            project(i, 2),
        )
        interleave(
            scores(i, 3),
            exponents(2),
            mixing(i, 1),
            chunk(one, 0, on_one),
            project(after, 0),
            project(after, 1),
        )
        return carry

    interleave(first_norm(0))
    wi[0:width, pl.ds(0, wide)] = own_ref[0:width, :]
    wi[0:width, pl.ds(wide, wide)] = oth_ref[0:width, :]
    wn[:, pl.ds(0, wide)] = own_ref[width : 2 * width, :]
    wn[:, pl.ds(wide, wide)] = oth_ref[width : 2 * width, :]
    own_tri = own_ref[2 * width : 3 * width, :]
    oth_tri = oth_ref[2 * width : 3 * width, :]
    for k, w in enumerate((wq, wk, wv, wop)):
        lanes = slice(k * half, (k + 1) * half)
        w[...] = in_tiles(own_tri[:, lanes], oth_tri[:, lanes])
    wo[...] = jnp.concatenate([own_tri[:, 3 * half :], oth_tri[:, 3 * half :]], axis=1)
    small = []
    for ref in (own_ref, oth_ref):
        tail = ref[3 * width : 3 * width + 16, :].astype(F32)
        each = 1 + half_heads
        small.append(tail[0:each] + tail[each : 2 * each] + tail[2 * each : 3 * each])
    hb = jnp.concatenate([member[0:1] for member in small], axis=1)
    wi[width:, :] = jnp.concatenate(
        [*bf_parts(hb), jnp.zeros((256 - width - 3, hidden), F32)], axis=0
    ).astype(BF)
    hp_s[...] = jnp.concatenate(
        [member[1:, :128] for member in small] + [jnp.zeros((8 - heads, 128), F32)], axis=0
    )
    for h in range(heads):
        query_p[h, 0:16, :] = query_operand(hp_s, h, qp)
    for part in range(2):
        interleave(project(0, part))
    def leaving(first_image, count):
        rows = pl.ds(pl.multiple_of(first_image * qp, 16), count * qp)
        images_out = pl.ds(first_image, count)
        for k, (source, at_rows) in enumerate(
            ((right_s.at[0], rows), (mid_s, images_out), (gm_s, images_out))
        ):
            pltpu.make_async_copy(
                source.at[at_rows], far_refs[k].at[at_rows], sems.at[k]
            ).start()

    def forward_pair(j, carry):
        forward_step(2 * j + 1, forward_step(2 * j, carry))

        @pl.when(j > 0)
        def _():
            leaving(2 * j - 2, 2)

        return carry

    lax.fori_loop(0, images // 2, forward_pair, 0)


    def back_scores(i, h):
        da = nt(v_s[i, :, tiles[h // half_heads]], dmm_s[i, h])
        rc = jnp.zeros((STRIP, qp), F32)
        rl = jnp.zeros((STRIP, qp), F32)
        for r in range(strips):
            yield
            part = cut(da, r)
            da_buf[h % 2, rows_of(r), :] = part
            rc = rc + soft_s[i, h, 0, rows_of(r), :] * part
            rl = rl + soft_s[i, h, 1, rows_of(r), :] * part
        gate = gate_of(hp_s, h, qp)
        rc = jnp.sum(rc, axis=0, keepdims=True) / (1.0 - gate)
        rl = jnp.sum(rl, axis=0, keepdims=True) / gate
        back_s[2 * h : 2 * h + 1, :] = rc
        back_s[2 * h + 1 : 2 * h + 2, :] = rl
        gate_g[h : h + 1, :] += rl - rc

    def back_spread(i, h):
        rc, rl = back_s[2 * h : 2 * h + 1, :], back_s[2 * h + 1 : 2 * h + 2, :]
        lanes = pl.ds(h * qp, qp)
        for r in range(strips):
            yield
            rows = rows_of(r)
            c = soft_s[i, h, 0, rows, :]
            l = soft_s[i, h, 1, rows, :]
            part = da_buf[h % 2, rows, :]
            ds_s[rows, lanes] = (c * (part - rc)).astype(BF)
            att_s[rows, lanes] = (c + l).astype(BF)
            place_g[h, rows, :] += l * (part - rl)

    def products(i, t):
        lanes = slice(t * half_heads * qp, (t + 1) * half_heads * qp)
        heads_in = slice(t * half_heads, (t + 1) * half_heads)
        dk = nn(ds_s[:, lanes], qm_s[i, heads_in].reshape(half_heads * qp, 128))
        dv = nn(att_s[:, lanes], dmm_s[i, heads_in].reshape(half_heads * qp, 128))
        yield
        pad = jnp.zeros((qp - kp, qp), BF)
        dq_t = []
        for h in range(t * half_heads, (t + 1) * half_heads):
            ds = jnp.concatenate([ds_s[:, h * qp : (h + 1) * qp], pad], axis=0)
            dq_t.append(nn(kt_s[i, head_rows(h), :], ds))
        yield
        dp_s[1, image_rows(i), tiles[t]] = (dk * back_scale).astype(BF)
        yield
        dp_s[2, image_rows(i), tiles[t]] = dv.astype(BF)
        yield
        dq_t.append(jnp.zeros((128 - half, qp), F32))
        dq = (jnp.concatenate(dq_t, axis=0) * back_scale).astype(BF)
        dp_s[0, image_rows(i), tiles[t]] = dq.T[:kp]

    cut_at = (images - 2) * qp
    spans = (slice(0, cut_at), slice(cut_at, images * qp))

    def weight_gradient(unit, part):
        side = unit // blocks
        lanes = slice((unit % blocks) * 256, (unit % blocks) * 256 + 256)
        value = nn(left_t[side, :, spans[part]], right_s[side, spans[part], lanes])
        yield
        if part:
            wide_g[side, :, lanes] += value
        else:
            wide_g[side, :, lanes] = value

    def outward_gradient(part):
        value = nn(mix_t[:, spans[part]], low_s[spans[part], :])
        yield
        if part:
            out_g[...] += value
        else:
            out_g[...] = value

    def triple_gradient(c, part):
        value = nn(first_t[:, spans[part]], dp_s[c, spans[part], :])
        yield
        rows = pl.ds(c * width, width)
        for t in range(2):
            if part:
                tri_p[t, rows, :] += value[:, tiles[t]]
            else:
                tri_p[t, rows, :] = value[:, tiles[t]]

    last = images - 1
    on = True
    partial = [weight_gradient(unit, 0) for unit in range(2 * blocks)] + [outward_gradient(0)]
    interleave(
        exponents(3), mixing(last, 2), chunk(last - 1, 1, on), back_scores(0, 0), partial[0]
    )
    interleave(
        mixing(last, 3),
        chunk(last - 1, 2, on),
        back_scores(0, 1),
        back_spread(0, 0),
        partial[1],
    )
    interleave(
        end(last - 1, on), start(last), back_scores(0, 2), back_spread(0, 1), partial[2]
    )
    interleave(chunk(last, 0, on), back_scores(0, 3), back_spread(0, 2), partial[3])
    interleave(chunk(last, 1, on), back_spread(0, 3), partial[4])
    interleave(chunk(last, 2, on), products(0, 0), partial[5])
    interleave(end(last, on), products(0, 1), *partial[6:])

    leaving(images - 2, 2)


    def early_chunks():
        put_planes(nar_p, wide_g[0].T)
        put_planes(out_p, out_g[...])
        for side in range(2):
            for k, part in enumerate(even_odd_tiles(nar_p, side * wide, wide // 2)):
                nar_f[side, k] = part
            for k, part in enumerate(even_odd_tiles(out_p, side * half, half // 2)):
                out_f[side, k] = part
            yield
        for r in range(data_count):
            for side in range(2):
                yield
                piece = outs[0].at[r] if side == 0 else tmp.at[r]
                for k in range(3):
                    lanes = slice(side * wide + 128 * k, side * wide + 128 * (k + 1))
                    piece[k * wp : (k + 1) * wp, :] = wide_g[1, r * wp : (r + 1) * wp, lanes]
                    row = 3 * wp + k * np_
                    piece[row : row + np_, :] = nar_f[side, k, r * np_ : (r + 1) * np_, :]
                    row = 3 * (wp + np_) + k * op
                    piece[row : row + op, :] = out_f[side, k, r * op : (r + 1) * op, :]
                if side:
                    outs[1][r, 0:SENT_EARLY, :] = piece[0:SENT_EARLY, :].astype(BF)

    def late_chunks():
        early = jnp.sum(vec_g[...], axis=1)
        hidden_sum = jnp.sum(hid_g[...], axis=0, keepdims=True)
        vec_n, hid_n = 4 * width // data_count, wide // data_count
        rest = jnp.zeros((1, 128 - vec_n - hid_n), F32)
        groups = 3 * width // data_count // 4
        small_at = 3 * (wp + np_ + op)
        for side in range(2):
            for k, part in enumerate(four_row_tiles(tri_p, side, 0, 3 * width // 4)):
                tri_f[side, k] = part
            yield
        for r in range(data_count):
            for side in range(2):
                yield
                piece = outs[0].at[r] if side == 0 else tmp.at[r]
                row, lane = divmod(r * vec_n, width)
                at_hidden = side * wide + r * hid_n
                piece[small_at : small_at + 1, :] = jnp.concatenate(
                    [
                        early[row : row + 1, lane : lane + vec_n],
                        hidden_sum[:, at_hidden : at_hidden + hid_n],
                        rest,
                    ],
                    axis=1,
                )
                for k in range(3):
                    row = small_at + 1 + k * groups
                    piece[row : row + groups, :] = tri_f[side, k, r * groups : (r + 1) * groups, :]
                row = small_at + 1 + 3 * groups
                piece[row:SENT_ROWS, :] = jnp.zeros((SENT_ROWS - row, 128), F32)
                if side:
                    outs[1][r, SENT_EARLY:, :] = piece[SENT_EARLY:, :].astype(BF)

    if data_count:
        wp, np_, op = width // data_count, wide // data_count // 2, half // data_count // 2
    chunking = early_chunks() if data_count else iter(())
    def leaving_back(first_row, count):
        for c in range(3):
            rows = pl.ds(first_row, count)
            pltpu.make_async_copy(
                dp_s.at[c, rows], far_refs[3].at[c, rows], sems.at[3]
            ).start()

    def leaving_places(first, count):
        span = pl.ds(first, count)
        pltpu.make_async_copy(place_g.at[span], far_refs[4].at[span], sems.at[4]).start()

    for i in range(1, images):
        before = i > 1
        done = i == last
        interleave(
            back_scores(i, 0),
            back_spread(i - 1, 3) if before else None,
            outward_gradient(1) if i == 1 else None,
        )
        interleave(
            back_scores(i, 1),
            products(i - 1, 0) if before else None,
            back_spread(i, 0),
        )
        interleave(
            back_scores(i, 2),
            products(i - 1, 1) if before else None,
            back_spread(i, 1),
        )
        interleave(
            back_scores(i, 3),
            back_spread(i, 2),
            weight_gradient(i - 1, 1) if i <= 2 * blocks else triple_gradient(0, 0),
            triple_gradient(1, 0) if done else None,
            triple_gradient(2, 0) if done else None,
        )
        leaving_back((i - 1) * qp, qp)
        if done:
            leaving_places(0, heads - 1)
    for unit in range(last, 2 * blocks):
        interleave(weight_gradient(unit, 1))
    interleave(back_spread(last, 3))
    interleave(products(last, 0), products(last, 1))
    interleave(chunking)
    leaving_back(last * qp, qp)
    leaving_places(heads - 1, 1)
    gate_ref[...] = gate_g[...]
    hp_ref[...] = hp_s[...]
    for c in range(3):
        interleave(triple_gradient(c, 1))
    if data_count:
        interleave(late_chunks())
    else:
        outs[0][...] = wide_g[0].T
        outs[1][...] = wide_g[1]
        outs[2][...] = out_g[...]
        outs[3][...] = vec_g[...]
        outs[4][...] = hid_g[...]
        for c in range(3):
            rows = pl.ds(c * width, width)
            outs[5][rows, :] = jnp.concatenate(
                [tri_p[0, rows, 0:half], tri_p[1, rows, 0:half]], axis=1
            )
    for k, source in enumerate((right_s.at[0], mid_s, gm_s, dp_s, place_g)):
        pltpu.make_async_copy(source, far_refs[k], sems.at[k]).wait()


def run_layer(x, inc, bias, own, oth, vec, heads, patches, data_count):
    images, kp, width = x.shape
    qp = -(-patches // 128) * 128
    wide, half = own.shape[1], width // 2
    hidden = 2 * wide
    full = images * qp
    if data_count:
        outs = [
            pltpu.VMEM((data_count, SENT_ROWS, 128), F32),
            pltpu.VMEM((data_count, SENT_ROWS, 128), BF),
        ]
    else:
        outs = [
            sds(hidden, width),
            sds(width, hidden),
            sds(width, width),
            sds(4, 8, width),
            sds(8, hidden),
            sds(3 * width, width),
        ]

    def bf(*dims):
        return pltpu.VMEM(dims, BF)

    def f32(*dims):
        return pltpu.VMEM(dims, F32)

    scratch = [
        *[bf(width, 256)] * 3,
        bf(width, width),
        bf(width, 256),
        bf(256, hidden),
        bf(width, hidden),
        f32(8, 128),
        bf(kp, 128),
        bf(kp, 128),
        bf(heads, 128, qp),
        bf(2, qp, width),
        bf(kp, 256),
        bf(256, qp),
        bf(images, heads, qp, 128),
        bf(images, heads, qp, 128),
        bf(images, kp, 256),
        bf(images, 256, qp),
        f32(images, heads, 2, kp, qp),
        f32(images, kp, width),
        f32(kp, width),
        bf(kp, 256),
        f32(kp, 1),
        bf(full, width),
        f32(4 * heads, qp),
        f32(2 * heads, qp),
        bf(width, full),
        bf(width, full),
        bf(2, width, full),
        bf(2, full, hidden),
        f32(images, kp, width),
        bf(3, full, 256),
        f32(heads, kp, qp),
        f32(heads, kp, qp),
        bf(2, qp, qp),
        f32(heads, kp, qp),
        f32(8, qp),
        f32(2, kp, qp),
        bf(kp, heads * qp),
        bf(kp, heads * qp),
        f32(2, width, hidden),
        f32(width, width),
        f32(4, 8, width),
        f32(8, hidden),
        f32(2, 3 * width, 128),
        pltpu.SemaphoreType.DMA((5,)),
    ]
    if data_count:
        scratch += [f32(2, hidden, 128), f32(2, width, 128)]
        scratch += [f32(2, 3, wide // 2, 128), f32(2, 3, half // 2, 128)]
        scratch += [f32(2, 3, 3 * width // 4, 128), f32(data_count, SENT_ROWS, 128)]
    return pl.pallas_call(
        functools.partial(layer_kernel, patches=patches, heads=heads, data_count=data_count),
        out_shape=(
            sds(full, hidden, dtype=BF),
            sds(images, kp, width),
            sds(images, kp, width),
            sds(3, full, 256, dtype=BF),
            sds(heads, kp, qp),
            pltpu.VMEM((8, qp), F32),
            pltpu.VMEM((8, 128), F32),
            *outs,
        ),
        in_specs=[VM] * 6,
        out_specs=(ANYWHERE,) * 5 + (VM,) * (2 + len(outs)),
        scratch_shapes=scratch,
        compiler_params=pltpu.CompilerParams(vmem_limit_bytes=LAYER_VMEM),
        name="layer",
    )(*near(x, inc, bias, own, oth), vec)


def finish_kernel(*refs, patches, heads):
    (x_ref, own_ref, oth_ref, vec_ref, gate_ref, hp_ref), far_refs = refs[:6], refs[6:11]
    (res_out, gi_out, vec_out, head_ref) = refs[11:15]
    (act_s, mid_s, gm_s, dp_s, place_s), (w, wn, vec_g, rows_s, sems) = refs[15:20], refs[20:]
    images, kp, width = x_ref.shape
    qp = dp_s.shape[1] // images
    half = width // 2
    wide = own_ref.shape[1]
    copies = [
        pltpu.make_async_copy(source, target, sems.at[at])
        for at, (source, target) in enumerate(
            zip(far_refs, (act_s, mid_s, gm_s, dp_s, place_s))
        )
    ]
    for member in copies:
        member.start()
    own_tri = own_ref[2 * width : 3 * width, :]
    oth_tri = oth_ref[2 * width : 3 * width, :]
    for at in range(3):
        span = slice(at * half, (at + 1) * half)
        w[at] = in_tiles(own_tri[:, span], oth_tri[:, span])
    wn[:, 0:wide] = own_ref[width : 2 * width, :]
    wn[:, wide : 2 * wide] = oth_ref[width : 2 * width, :]
    vec_g[...] = jnp.zeros_like(vec_g)
    gain = vec_ref[0:1, :]
    shift = vec_ref[5:6, :]
    for member in copies[:2]:
        member.wait()
    for i in range(images):
        rows = mid_s[i] + nt(act_s[i * qp : i * qp + kp, :], wn[...]) + shift
        rows_s[i * patches : (i + 1) * patches, :] = rows[0:patches]
    res_out[...] = rows_s[...].T
    for member in copies[2:]:
        member.wait()
    for i in range(images):
        n1, spread = norm_parts(x_ref[i].astype(F32))
        g = sum(nt(dp_s[c, i * qp : i * qp + kp, :], w[c]) for c in range(3))
        vec_g[0] += fold(g * n1)
        vec_g[1] += fold(g)
        rows = gm_s[i] + norm_back(g * gain, n1, spread)
        rows_s[i * patches : (i + 1) * patches, :] = rows[0:patches]
    gi_out[...] = rows_s[...].T
    vec_out[...] = jnp.sum(vec_g[...], axis=1)
    parts = offsets(kp, qp)
    rank = lax.axis_index("tensor")
    lane = lax.broadcasted_iota(jnp.int32, (1, 128), 1)
    row = jnp.zeros((1, 128), F32)
    half_heads = heads // 2
    for h in range(heads):
        base = ((rank + h // half_heads) % 2) * (4 * half_heads) + h % half_heads
        g = place_s[h]
        for k in range(3):
            total = jnp.sum(g * parts[k])
            row = row + jnp.where(lane == base + k * half_heads, total, 0.0)
        gate = gate_of(hp_ref, h, 128)
        total = jnp.sum(gate_ref[h : h + 1, :])
        row = row + jnp.where(lane == base + 3 * half_heads, total * gate * (1.0 - gate), 0.0)
    head_ref[...] = row


def run_finish(x, own, oth, vec, gate, hp, act, mid, gm, dp, place, patches):
    images, kp, width = x.shape
    rows = images * patches
    fetched = (act, mid, gm, dp, place)
    return pl.pallas_call(
        functools.partial(finish_kernel, patches=patches, heads=place.shape[0]),
        out_shape=(sds(width, rows), sds(width, rows), sds(2, width), sds(1, 128)),
        in_specs=[VM] * 6 + [ANYWHERE] * 5,
        out_specs=(VM,) * 4,
        scratch_shapes=[
            *[pltpu.VMEM(member.shape, member.dtype) for member in fetched],
            pltpu.VMEM((3, width, 256), BF),
            pltpu.VMEM((width, 2 * own.shape[1]), BF),
            pltpu.VMEM((2, 8, width), F32),
            pltpu.VMEM((rows, width), F32),
            pltpu.SemaphoreType.DMA((5,)),
        ],
        compiler_params=pltpu.CompilerParams(vmem_limit_bytes=32 * 1024 * 1024),
        name="finish",
    )(*near(x, own, oth), vec, gate, hp, *far(*fetched))


def combine_kernel(own_ref, got_ref, out_ref):
    out_ref[...] = (own_ref[...] + got_ref[...].astype(F32)).astype(BF)


def run_combine(own, got):
    return pl.pallas_call(
        combine_kernel,
        out_shape=pltpu.VMEM(own.shape, BF),
        in_specs=[VM] * 2,
        out_specs=VM,
        compiler_params=PARAMS,
        name="combine",
    )(*near(own, got))


def pick_rows(ref, start, count, flip=False):
    total = ref.shape[1] if flip else ref.shape[0]
    row = lax.broadcasted_iota(jnp.int32, (count, total), 0) + start
    col = lax.broadcasted_iota(jnp.int32, (count, total), 1)
    chosen = (row == col).astype(F32)
    return lax.dot_general(
        chosen,
        ref[...],
        (((1,), (1 if flip else 0,)), ((), ())),
        preferred_element_type=F32,
        precision=lax.Precision.HIGHEST,
    )


def share_kernel(_, tri_ref, out_ref, wid_ref, nar_ref, *refs, data_count):
    (wt_f, wo_f, ww_f, wn_f, st, so, sw, sn) = refs
    width, wide = wid_ref.shape
    half = out_ref.shape[0]
    wp, np_, op = width // data_count, wide // data_count // 2, half // data_count // 2
    data_rank = lax.axis_index("dp")
    groups = tri_ref.shape[0] // data_count // 4
    st[0, :, 0 : tri_ref.shape[1]] = pick_rows(tri_ref, data_rank * 4 * groups, 4 * groups)
    put_planes(so, pick_rows(out_ref, data_rank * 2 * op, 2 * op))
    sw[...] = pick_rows(wid_ref, data_rank * wp, wp)
    put_planes(sn, pick_rows(nar_ref, data_rank * 2 * np_, 2 * np_, flip=True))
    tiles = four_row_tiles(st, 0, 0, groups)
    for p in range(groups):
        for k in range(3):
            tile = 128 * (3 * p + k)
            wt_f[0:1, tile : tile + 128] = tiles[k][p : p + 1, :]
    for ref, flat, pairs in ((so, wo_f, op), (sn, wn_f, np_)):
        tiles = even_odd_tiles(ref, 0, pairs)
        for p in range(pairs):
            for k in range(3):
                tile = 128 * (3 * p + k)
                flat[0:1, tile : tile + 128] = tiles[k][p : p + 1, :]
    for p in range(wp):
        ww_f[0:1, wide * p : wide * (p + 1)] = sw[p : p + 1, :]


def run_shares(after, tri, out, wid, nar_t, data_count):
    wide = wid.shape[1]
    share = [member.shape[0] // data_count for member in (tri, out, wid)]
    return pl.pallas_call(
        functools.partial(share_kernel, data_count=data_count),
        out_shape=tuple(sds(1, member.size // data_count) for member in (tri, out, wid, nar_t)),
        in_specs=[VM] * 5,
        out_specs=(VM,) * 4,
        scratch_shapes=[
            pltpu.VMEM((1, share[0], 128), F32),
            pltpu.VMEM((2, share[1], 128), F32),
            pltpu.VMEM((share[2], wide), F32),
            pltpu.VMEM((2, wide // data_count, 128), F32),
        ],
        compiler_params=PARAMS,
        name="weight_shares",
    )(after, tri, out, wid, nar_t)


def spread_rows(flat_ref, from_ref, base, blocks):
    for p in range(blocks):
        for k in range(3):
            at = base + k * blocks + p
            tile = 128 * (3 * p + k)
            flat_ref[0:1, tile : tile + 128] = from_ref[at : at + 1, :]


def sum_kernel(got_ref, late_ref, head_ref, _, *refs, blocks, span):
    (tri_f, out_f, wid_f, nar_f, pay_ref, tot) = refs
    tri_b, out_b, wid_b, nar_b = blocks
    vec_n, hid_n = span
    tot[...] = jnp.sum(got_ref[...].astype(F32), axis=0)
    spread_rows(wid_f, tot, 0, wid_b)
    spread_rows(nar_f, tot, 3 * wid_b, nar_b)
    spread_rows(out_f, tot, 3 * (wid_b + nar_b), out_b)
    at = 3 * (wid_b + nar_b + out_b)
    spread_rows(tri_f, tot, at + 1, tri_b)
    early = tot[0:at, :]
    late = tot[at + 1 : at + 1 + 3 * tri_b, :]
    small = tot[at : at + 1, :]
    hid = small[:, vec_n : vec_n + hid_n]
    squares = jnp.sum(early * early) + jnp.sum(late * late) + jnp.sum(hid * hid)
    lane = lax.broadcasted_iota(jnp.int32, (1, 128), 1)
    tails = jnp.concatenate([late_ref[0:1, 128:], late_ref[1:2, 128:]], axis=1)
    last = jnp.concatenate([head_ref[:, 0:SMALL_AT], small[:, 0 : 128 - SMALL_AT]], axis=1)
    payload = jnp.concatenate(
        [late_ref[:, :128], tails, jnp.where(lane == 127, squares, last)], axis=0
    )
    pay_ref[...] = jnp.broadcast_to(payload[None], pay_ref.shape)


def run_sums(got, late_vec, head, after, blocks, span):
    count = got.shape[0]
    return pl.pallas_call(
        functools.partial(sum_kernel, blocks=blocks, span=span),
        out_shape=(
            *[sds(1, 3 * 128 * member) for member in blocks],
            sds(2 * count, 4, 128),
        ),
        in_specs=[VM] * 4,
        out_specs=(VM,) * 5,
        scratch_shapes=[pltpu.VMEM((SENT_ROWS, 128), F32)],
        compiler_params=PARAMS,
        name="sums",
    )(got, late_vec, head, after)


def adam_parts(weight, gradient, moment, squares, rate, decay):
    moment_new = BETA_ONE * moment + (1.0 - BETA_ONE) * gradient
    squares_new = BETA_TWO * squares + (1.0 - BETA_TWO) * gradient * gradient
    quotient = (moment_new / (1.0 - BETA_ONE**STEP)) / (
        jnp.sqrt(squares_new / (1.0 - BETA_TWO**STEP)) + ADAM_EPS
    )
    return moment_new, squares_new, weight - rate * (quotient + decay * weight)


def gathered(last, width, wide):
    count = last.shape[0] // 2
    vec_n, hid_n = 4 * width // count, wide // count
    even = last[pl.ds(0, count, stride=2), :]
    odd = last[pl.ds(1, count, stride=2), :]
    mine = jnp.where(lax.axis_index("tensor") == 0, even, odd)

    def placed(part, times):
        n = part.shape[1]
        value = jnp.concatenate([part] * times, axis=1)
        row = lax.broadcasted_iota(jnp.int32, value.shape, 0)
        lane = lax.broadcasted_iota(jnp.int32, value.shape, 1)
        at = jnp.floor((lane.astype(F32) + 0.5) * (1.0 / n)).astype(jnp.int32)
        return value, row, at

    per_row = width // vec_n
    value, row, at = placed(even[:, SMALL_AT : SMALL_AT + vec_n], per_row)
    vector = jnp.concatenate(
        [
            jnp.sum(jnp.where(row == at + v * per_row, value, 0.0), axis=0, keepdims=True)
            for v in range(4)
        ],
        axis=0,
    )
    at_hidden = SMALL_AT + vec_n
    value, row, at = placed(mine[:, at_hidden : at_hidden + hid_n], count)
    return vector, jnp.sum(jnp.where(row == at, value, 0.0), axis=0, keepdims=True)


def adam_kernel(got_ref, hp_ref, vec_ref, hb_ref, *refs, given_sums):
    refs = list(refs)
    sums = [refs.pop(0) for _ in range(2 * given_sums)]
    grads = refs[0:4]
    weights = refs[4:8]
    states = refs[8:22]
    outs = refs[22:43]
    norm_ref, last = refs[43:45]
    width = vec_ref.shape[1]
    half_heads = hp_ref.shape[0]
    tail = width - 128
    total = jnp.sum(got_ref[...], axis=0)
    if given_sums:
        early, hid = sums[0][...], sums[1][...]
    else:
        last[...] = got_ref[:, 3, :]
        early, hid = gathered(last, width, hb_ref.shape[0])
    late = jnp.concatenate(
        [
            total[0:2, :],
            jnp.concatenate([total[2:3, :tail], total[2:3, tail : 2 * tail]], axis=0),
        ],
        axis=1,
    )
    vector = jnp.concatenate([late, early], axis=0)
    lane = lax.broadcasted_iota(jnp.int32, (1, 128), 1)
    heads_row = jnp.where(lane < 8 * half_heads, total[3:4, :], 0.0)
    squares = (
        jnp.sum(jnp.where(lane == 127, total[3:4, :], 0.0))
        + jnp.sum(vector * vector)
        + jnp.sum(heads_row * heads_row)
    )
    norm = jnp.sqrt(jnp.full((1, 128), squares))
    norm_ref[0] = jnp.sum(norm[:, 0:1])
    factor = (CLIP_AT / jnp.maximum(norm, CLIP_AT))[:, 0:1]
    span = 4 * half_heads
    mine = jnp.where(lax.axis_index("tensor") == 0, heads_row[:, :span], heads_row[:, span : 2 * span])
    head = jnp.concatenate(
        [
            jnp.concatenate(
                [mine[:, c * half_heads + h : c * half_heads + h + 1] for c in range(4)], axis=1
            )
            for h in range(half_heads)
        ],
        axis=0,
    )
    given = [ref[...] for ref in grads] + [vector, hid, head]
    wide = hid.shape[1]
    held = [ref[...] for ref in weights] + [vec_ref[...], hb_ref[...].reshape(1, wide), hp_ref[...]]
    for at in range(7):
        renewed = adam_parts(
            held[at],
            given[at] * factor,
            states[2 * at][...].reshape(held[at].shape),
            states[2 * at + 1][...].reshape(held[at].shape),
            RATES[at],
            DECAYS[at],
        )
        for step in range(3):
            out = outs[3 * at + step]
            out[...] = renewed[step].reshape(out.shape)


def run_adam(got, hp_t, vec, hb, sums, grads, weights, states):
    shapes = []
    for at in range(7):
        shapes += [sds(*states[2 * at].shape)] * 3
    return pl.pallas_call(
        functools.partial(adam_kernel, given_sums=len(sums) // 2),
        out_shape=(*shapes, sds(1)),
        in_specs=[VM] * (4 + len(sums) + 4 + 4 + 14),
        out_specs=(VM,) * 21 + (SM,),
        scratch_shapes=[pltpu.VMEM((got.shape[0], 128), F32)],
        compiler_params=PARAMS,
        name="adam",
    )(got, hp_t, vec, hb, *sums, *grads, *weights, *states)


def plain_chunks(halves, data_count, rows):
    sides = []
    for side in range(2):
        flat = jnp.concatenate([own_first[side].reshape(data_count, -1) for own_first in halves], axis=1)
        flat = jnp.pad(flat, ((0, 0), (0, rows * 128 - flat.shape[1])))
        sides.append(flat.reshape(data_count, rows, 128))
    return sides[0], sides[1].astype(BF)


def on_device(
    tokens,
    cotangent,
    keep_mask,
    triple_weight,
    outward_weight,
    widen_weight,
    narrow_weight,
    vectors,
    hidden_bias,
    head_params,
    triple_moment,
    triple_square,
    outward_moment,
    outward_square,
    widen_moment,
    widen_square,
    narrow_moment,
    narrow_square,
    vector_moment,
    vector_square,
    hidden_moment,
    hidden_square,
    head_moment,
    head_square,
):
    tensor_rank = lax.axis_index("tensor")
    data_rank = lax.axis_index("dp")
    data_count = lax.axis_size("dp")
    images = keep_mask.shape[0] // 2
    patches = keep_mask.shape[1]
    heads = 2 * head_params.shape[1]
    depth = triple_weight.shape[1]
    half = triple_weight.shape[2]
    wide = widen_weight.shape[1]
    triple_rows = triple_weight.reshape(3 * depth, half)
    narrow_t = narrow_weight.T
    head_t = head_params.T
    fast = (
        depth == 192
        and half == 96
        and wide == 384
        and depth % data_count == 0
        and wide % (2 * data_count) == 0
        and half % (2 * data_count) == 0
        and 3 * depth % (4 * data_count) == 0
    )
    if fast:
        early_rows = (2 * depth * wide + half * depth) // data_count // 128
        late_rows = 3 * depth * half // data_count // 128
        fast = SENT_EARLY <= early_rows and early_rows + 1 + late_rows <= SENT_ROWS
    chunked = data_count if fast else 0
    swap = [(0, 1), (1, 0)]

    own, *rows_near = run_pack(
        triple_weight,
        outward_weight,
        widen_weight,
        narrow_t,
        hidden_bias,
        head_t,
        tokens.T,
        cotangent.T,
        keep_mask,
    )
    other = lax.ppermute(own, "tensor", swap)
    x, inc, bias = run_prepare(*rows_near)
    act, middle, grad_middle, dp, place, gate, hp, *sums = run_layer(
        x, inc, bias, own, other, vectors, heads, patches, chunked
    )
    if fast:
        mine, theirs = sums
    else:
        nar_g, wid_g, out_g, vec_g, hid_g, tri_g = sums
        early_mine = jnp.sum(vec_g, axis=1).reshape(1, -1)
        early_both = jnp.broadcast_to(early_mine, (data_count, early_mine.size))
        hidden_both = jnp.broadcast_to(
            jnp.sum(hid_g, axis=0).reshape(2, 1, wide), (2, data_count, wide)
        )
        early = plain_chunks(
            [
                wid_g.reshape(depth, 2, wide).transpose(1, 0, 2),
                nar_g.reshape(2, -1),
                out_g.reshape(2, -1),
                (early_both, early_both),
                hidden_both,
            ],
            data_count,
            EARLY_ROWS,
        )
        late = plain_chunks(
            [tri_g.reshape(3 * depth, 2, half).transpose(1, 0, 2)], data_count, LATE_ROWS
        )
        mine, theirs = (jnp.concatenate(pair, axis=1) for pair in zip(early, late))
    received = lax.ppermute(theirs, "tensor", swap)
    chunks = run_combine(mine, received)
    got = lax.all_to_all(chunks, "dp", 0, 0, tiled=False)
    result_t, grad_input_t, late_vec, head_row = run_finish(
        x, own, other, vectors, gate, hp, act, middle, grad_middle, dp, place, patches
    )
    if fast:
        wt_f, wo_f, ww_f, wn_f = run_shares(
            gate, triple_rows, outward_weight, widen_weight, narrow_t, data_count
        )
        blocks = [
            member.size // data_count // 384
            for member in (triple_rows, outward_weight, widen_weight, narrow_t)
        ]
        span = (4 * depth // data_count, wide // data_count)
        tri_f, out_f, wid_f, nar_f, payload = run_sums(
            got, late_vec, head_row, wo_f, blocks, span
        )
        sums = ()
    else:
        total = jnp.sum(got.astype(F32), axis=0)
        early_sum = total[:EARLY_ROWS].reshape(1, -1)
        masters = (widen_weight, narrow_weight, outward_weight)
        sizes = [member.size // data_count for member in masters] + [4 * depth, wide]
        cuts = [sum(sizes[:at]) for at in range(6)]
        wid_f, nar_f, out_f, early_vec, hid = (
            early_sum[:, cuts[at] : cuts[at + 1]] for at in range(5)
        )
        early_vec = early_vec.reshape(4, depth)
        share = triple_rows.size // data_count
        tri_f = total[EARLY_ROWS:].reshape(1, -1)[:, :share]

        def weight_share(member):
            length = member.size // data_count
            return lax.dynamic_slice_in_dim(member.reshape(1, -1), data_rank * length, length, 1)

        ww_f, wn_f, wo_f = (weight_share(member) for member in masters)
        wt_f = weight_share(triple_rows)
        squares = sum(jnp.sum(member * member) for member in (wid_f, nar_f, out_f, tri_f))
        squares = squares + jnp.where(data_rank == 0, jnp.sum(hid * hid), 0.0)
        lane = lax.broadcasted_iota(jnp.int32, (1, 128), 1)
        payload = jnp.concatenate(
            [
                late_vec[:, :128],
                late_vec[:, 128:].reshape(1, 128),
                jnp.where(lane == 127, squares, head_row),
            ]
        )
        payload = jnp.broadcast_to(payload[None], (2 * data_count, 4, 128))
        sums = (early_vec, hid)
    last_got = lax.all_to_all(payload, ("dp", "tensor"), 0, 0, tiled=False)
    renewed = run_adam(
        last_got,
        head_t,
        vectors,
        hidden_bias,
        sums,
        (tri_f, out_f, wid_f, nar_f),
        (wt_f, wo_f, ww_f, wn_f),
        (
            triple_moment,
            triple_square,
            outward_moment,
            outward_square,
            widen_moment,
            widen_square,
            narrow_moment,
            narrow_square,
            vector_moment,
            vector_square,
            hidden_moment,
            hidden_square,
            head_moment.T,
            head_square.T,
        ),
    )
    hidden_new = renewed[15:18]
    head_new = [member.T for member in renewed[18:21]]
    return (result_t.T, grad_input_t.T, *renewed[:15], *hidden_new, *head_new, renewed[21].reshape(()))


def solution(mesh):
    return jax.shard_map(
        on_device,
        mesh=mesh,
        in_specs=(
            P(("dp", "tensor"), None),
            P(("dp", "tensor"), None),
            P("dp", None),
            P(None, None, "tensor"),
            P("tensor", None),
            P(None, "tensor"),
            P("tensor", None),
            P(),
            P("tensor"),
            P(None, "tensor"),
            P("tensor", "dp"),
            P("tensor", "dp"),
            P("tensor", "dp"),
            P("tensor", "dp"),
            P("tensor", "dp"),
            P("tensor", "dp"),
            P("tensor", "dp"),
            P("tensor", "dp"),
            P(),
            P(),
            P("tensor"),
            P("tensor"),
            P(None, "tensor"),
            P(None, "tensor"),
        ),
        out_specs=(
            P(("dp", "tensor"), None),
            P(("dp", "tensor"), None),
            P("tensor", "dp"),
            P("tensor", "dp"),
            P("tensor", "dp"),
            P("tensor", "dp"),
            P("tensor", "dp"),
            P("tensor", "dp"),
            P("tensor", "dp"),
            P("tensor", "dp"),
            P("tensor", "dp"),
            P("tensor", "dp"),
            P("tensor", "dp"),
            P("tensor", "dp"),
            P(),
            P(),
            P(),
            P("tensor"),
            P("tensor"),
            P("tensor"),
            P(None, "tensor"),
            P(None, "tensor"),
            P(None, "tensor"),
            P(),
        ),
        check_vma=False,
    )
```

```python
import functools
import math

import jax
import jax.numpy as jnp
from jax import lax
from jax.experimental import pallas as pl
from jax.experimental.pallas import tpu as pltpu
from jax.sharding import PartitionSpec as P

GRID = 14
STEP = 10
EPS_NORM = 1e-06
CLIP_AT = 1.0
BETA_ONE = 0.9
BETA_TWO = 0.95
ADAM_EPS = 1e-08
RATES = (0.1, 0.5, 0.1, 0.05, 0.3, 0.1, 0.3)
DECAYS = (0.05, 0.05, 0.05, 0.05, 0.0, 0.0, 0.0)
LOG2E = 1.4426950408889634
BF = jnp.bfloat16
F32 = jnp.float32
LAYER_VMEM = 52 * 1024 * 1024
SMALL_VMEM = 16 * 1024 * 1024
EARLY_ROWS = 96
LATE_ROWS = 32
SENT_EARLY = 80
SENT_ROWS = 112
SMALL_AT = 16
PAIR = 2
VM = pl.BlockSpec(memory_space=pltpu.VMEM)
ANYWHERE = pl.BlockSpec(memory_space=pl.ANY)
SM = pl.BlockSpec(memory_space=pltpu.SMEM)
PARAMS = pltpu.CompilerParams(vmem_limit_bytes=SMALL_VMEM)


def sds(*dims, dtype=F32):
    return jax.ShapeDtypeStruct(dims, dtype)


def near(*arrays):
    return [pltpu.with_memory_space_constraint(member, pltpu.VMEM) for member in arrays]


def far(*arrays):
    return [pltpu.with_memory_space_constraint(member, pltpu.HBM) for member in arrays]


def nn(a, b):
    return lax.dot_general(a, b, (((1,), (0,)), ((), ())), preferred_element_type=F32)


def nt(a, b):
    return lax.dot_general(a, b, (((1,), (1,)), ((), ())), preferred_element_type=F32)


def norm_parts(v):
    width = v.shape[-1]
    average = jnp.sum(v, axis=-1, keepdims=True) * (1.0 / width)
    centred = v - average
    variance = jnp.sum(centred * centred, axis=-1, keepdims=True) * (1.0 / width)
    spread = lax.rsqrt(variance + EPS_NORM)
    return centred * spread, spread


def norm_back(e, n, spread):
    width = e.shape[-1]
    mean_e = jnp.sum(e, axis=-1, keepdims=True) * (1.0 / width)
    mean_en = jnp.sum(e * n, axis=-1, keepdims=True) * (1.0 / width)
    return spread * (e - mean_e - n * mean_en)


def fold(v):
    rows = v.shape[0]
    return jnp.sum(v.reshape(rows // 8, 8, v.shape[1]), axis=0)


def gelu_parts(x):
    phi = 0.5 + 0.5 * lax.erf(x * math.sqrt(0.5))
    density = jnp.exp2((x * x) * (-0.5 * LOG2E)) * (1.0 / math.sqrt(2.0 * math.pi))
    return x * phi, phi + x * density


def places(count, lanes, dim):
    at = lax.broadcasted_iota(jnp.int32, (count, lanes), dim).astype(F32)
    row = jnp.floor((at + 0.5) * (1.0 / GRID))
    return at - row * GRID, row


def offsets(kp, qp):
    kc, kr = places(kp, qp, 0)
    qc, qr = places(kp, qp, 1)
    a = kc - qc
    b = kr - qr
    return a, b, a * a + b * b


def head_mask(hd, h):
    lane = lax.broadcasted_iota(jnp.int32, (STRIP, 128), 1)
    return ((lane >= h * hd) & (lane < (h + 1) * hd)).astype(BF)


def in_tiles(own, oth):
    gap = jnp.zeros((own.shape[0], 128 - own.shape[1]), own.dtype)
    return jnp.concatenate([own, gap, oth, gap], axis=1)


def gate_of(hp_ref, h, lanes):
    return 1.0 / (1.0 + jnp.exp(-jnp.broadcast_to(hp_ref[h : h + 1, 3:4], (1, lanes))))


def bf_parts(value, count=3):
    parts = []
    for _ in range(count):
        part = value.astype(BF).astype(F32)
        parts.append(part)
        value = value - part
    return parts


def key_operand(kp):
    kc, kr = places(kp, 128, 0)
    lane = lax.broadcasted_iota(jnp.int32, (kp, 128), 1)
    value = jnp.where(lane < 3, kc, jnp.where(lane < 6, kr, jnp.where(lane < 9, kc * kc, kr * kr)))
    return jnp.where(lane < 12, value, 0.0).astype(BF)


def query_operand(hp_ref, h, qp):
    p = [LOG2E * jnp.broadcast_to(hp_ref[h : h + 1, at : at + 1], (16, qp)) for at in range(3)]
    qc, qr = places(16, qp, 1)
    row = lax.broadcasted_iota(jnp.int32, (16, qp), 0)
    value = jnp.where(row < 3, p[0] - 2.0 * p[2] * qc, jnp.where(row < 6, p[1] - 2.0 * p[2] * qr, p[2]))
    parts = bf_parts(value)
    place = row - 3 * ((row >= 3).astype(jnp.int32) + (row >= 6) + (row >= 9))
    value = jnp.where(place == 0, parts[0], jnp.where(place == 1, parts[1], parts[2]))
    return jnp.where(row < 12, value, jnp.where(row == 12, 1.0, 0.0)).astype(BF)


STRIP = 16
LAG = 3
WAIT = 3


def interleave(*streams):
    streams = [member for member in streams if member is not None]
    while streams:
        alive = []
        for member in streams:
            try:
                next(member)
                alive.append(member)
            except StopIteration:
                pass
        streams = alive


def staged(count, lag, *stages):
    for t in range(count + lag * (len(stages) - 1)):
        for k, stage in enumerate(stages):
            if 0 <= t - k * lag < count:
                stage(t - k * lag)
        yield


def slow(stream, count):
    for _ in range(count):
        yield
        try:
            next(stream)
        except StopIteration:
            return


def cut(value, r):
    return value[r * STRIP : (r + 1) * STRIP]


def rows_of(r):
    return pl.ds(r * STRIP, STRIP)


def put_planes(ref, value):
    rows, width = value.shape
    ref[0, 0:rows, :] = value[:, :128]
    ref[1, 0:rows, 0 : width - 128] = value[:, 128:]


def even_odd_tiles(ref, start, pairs):
    even = [ref[at, pl.ds(start, pairs, stride=2), :] for at in range(2)]
    odd = [ref[at, pl.ds(start + 1, pairs, stride=2), :] for at in range(2)]
    return (
        even[0],
        jnp.concatenate([even[1][:, :64], odd[0][:, :64]], axis=1),
        jnp.concatenate([odd[0][:, 64:], odd[1][:, :64]], axis=1),
    )


def four_row_tiles(ref, plane, start, groups):
    r = [ref[plane, pl.ds(start + at, groups, stride=4), :] for at in range(4)]
    return (
        jnp.concatenate([r[0][:, :96], r[1][:, :32]], axis=1),
        jnp.concatenate([r[1][:, 32:96], r[2][:, :64]], axis=1),
        jnp.concatenate([r[2][:, 64:96], r[3][:, :96]], axis=1),
    )


def pack_kernel(*refs):
    given, pack_ref, passed, held, sems = refs[:9], refs[9], refs[10:13], refs[13:19], refs[19]
    copies = [
        pltpu.make_async_copy(source, target, sems.at[at])
        for at, (source, target) in enumerate(zip(given, [*held, *passed]))
    ]
    for member in copies:
        member.start()
    for member in copies[:6]:
        member.wait()
    tri_ref, out_ref, wid_ref, nar_ref, hb_ref, hp_ref = held
    depth, wide = wid_ref.shape
    pack_ref[0:depth, :] = wid_ref[...].astype(BF)
    pack_ref[depth : 2 * depth, :] = nar_ref[...].astype(BF)
    pack_ref[2 * depth : 3 * depth, :] = jnp.concatenate(
        [tri_ref[0], tri_ref[1], tri_ref[2], out_ref[...].T], axis=1
    ).astype(BF)
    heads_here = hp_ref.shape[0]
    hp = jnp.concatenate([hp_ref[...], jnp.zeros((heads_here, wide - 4), F32)], axis=1)
    left = jnp.concatenate([hb_ref[...].reshape(1, wide), hp], axis=0)
    parts = []
    for _ in range(3):
        part = left.astype(BF).astype(F32)
        parts.append(part)
        left = left - part
    parts.append(jnp.zeros((16 - 3 * (1 + heads_here), wide), F32))
    pack_ref[3 * depth : 3 * depth + 16, :] = jnp.concatenate(parts, axis=0).astype(BF)
    for member in copies[6:]:
        member.wait()


def run_pack(tri, out, wid, nar_t, hb, hp_t, *passed):
    depth, wide = wid.shape
    given = (tri, out, wid, nar_t, hb, hp_t)
    return pl.pallas_call(
        pack_kernel,
        out_shape=(
            pltpu.VMEM((3 * depth + 16, wide), BF),
            *[pltpu.VMEM(member.shape, member.dtype) for member in passed],
        ),
        in_specs=[pl.BlockSpec(memory_space=pltpu.HBM)] * 9,
        out_specs=(VM,) * 4,
        scratch_shapes=[
            *[pltpu.VMEM(member.shape, member.dtype) for member in given],
            pltpu.SemaphoreType.DMA((9,)),
        ],
        compiler_params=PARAMS,
        name="pack_weights",
    )(*far(*given, *passed))


def prepare_kernel(tok_ref, cot_ref, keep_ref, x_ref, inc_ref, bias_ref, xs, cs):
    images, kp, width = x_ref.shape
    patches = keep_ref.shape[1]
    rows = images * patches
    qp = -(-patches // 128) * 128
    mine = keep_ref[pl.ds(pl.multiple_of(lax.axis_index("tensor") * images, 8), images), :].astype(F32)
    columns = jnp.concatenate([mine, jnp.zeros((images, qp - patches), F32)], axis=1).T
    xs[0:rows, :] = tok_ref[...].T.astype(F32)
    cs[0:rows, :] = cot_ref[...].T.astype(F32)
    xs[rows : rows + 16, :] = jnp.zeros((16, width), F32)
    cs[rows : rows + 16, :] = jnp.zeros((16, width), F32)
    for i in range(images):
        span = slice(i * patches, i * patches + kp)
        keep = jnp.broadcast_to(columns[:kp, i : i + 1], (kp, 128))
        keep_wide = jnp.concatenate([keep, keep[:, : width - 128]], axis=1)
        x_ref[i] = xs[span, :].astype(BF)
        inc_ref[i] = (cs[span, :] * keep_wide).astype(BF)
        bias_ref[i] = ((keep - 1.0) * 1e30).astype(BF)


def run_prepare(tok_t, cot_t, keep_mask):
    images = keep_mask.shape[0] // 2
    kp = -(-keep_mask.shape[1] // 16) * 16
    width, rows_here = tok_t.shape
    rows = pltpu.VMEM((images, kp, width), BF)
    return pl.pallas_call(
        prepare_kernel,
        out_shape=(rows, rows, pltpu.VMEM((images, kp, 128), BF)),
        in_specs=[VM] * 3,
        out_specs=(VM,) * 3,
        scratch_shapes=[pltpu.VMEM((rows_here + 16, width), F32)] * 2,
        compiler_params=PARAMS,
        name="prepare",
    )(*near(tok_t, cot_t, keep_mask))


def layer_kernel(*refs, patches, heads, data_count):
    (x_ref, inc_ref, bias_ref, own_ref, oth_ref, vec_ref) = refs[:6]
    far_refs = refs[6:11]
    gate_ref, hp_ref = refs[11:13]
    outs = refs[13:15] if data_count else refs[13:19]
    at = 13 + len(outs)
    (wq, wk, wv, wo, wop, wi, wn, hp_s, key_p, key_i, query_p) = refs[at : at + 11]
    at += 11
    (fst_s, keys_s, vt_s, qm_s, dmm_s, v_s, kt_s, soft_s, mid_s, n2_s) = refs[at : at + 10]
    at += 10
    (sec_s, spr_s, low_s, stat_s, back_s) = refs[at : at + 5]
    at += 5
    (first_t, mix_t, left_t, right_s, gm_s, dp_s, s_buf, p_buf, att_buf) = refs[at : at + 9]
    at += 9
    (place_g, gate_g, da_buf, att_s, ds_s, wide_g, out_g, vec_g, hid_g, tri_p, sems) = refs[at : at + 11]
    at += 11
    if data_count:
        nar_p, out_p, nar_f, out_f, tri_f, tmp = refs[at : at + 6]
    images, kp, width = x_ref.shape
    qp = soft_s.shape[4]
    hd = width // heads
    half = width // 2
    half_heads = heads // 2
    wide = own_ref.shape[1]
    hidden = 2 * wide
    strips = kp // STRIP
    c_scale = LOG2E / math.sqrt(hd)
    back_scale = 1.0 / math.sqrt(hd)
    v = [vec_ref[k : k + 1, :] for k in range(6)]

    key_p[...] = key_operand(kp)
    query_p[...] = jnp.zeros_like(query_p)
    for ref in (hid_g, vec_g, place_g, gate_g):
        ref[...] = jnp.zeros_like(ref)
    for k in range(2):
        att_buf[k, kp:, :] = jnp.zeros((qp - kp, qp), BF)
    for k in range(2):
        fst_s[k, kp:, :] = jnp.zeros((qp - kp, width), BF)
    for k in range(images):
        for side in range(2):
            right_s[side, k * qp + kp : (k + 1) * qp, :] = jnp.zeros((qp - kp, hidden), BF)
        for c in range(3):
            dp_s[c, k * qp + kp : (k + 1) * qp, :] = jnp.zeros((qp - kp, 256), BF)
    sec_s[:, width:] = (lax.broadcasted_iota(jnp.int32, (kp, 256 - width), 1) < 3).astype(BF)
    gap = jnp.zeros((qp - kp, width), BF)
    one_lane = (lax.broadcasted_iota(jnp.int32, (STRIP, 128), 1) == half).astype(BF)
    masks = [head_mask(hd, h) for h in range(half_heads)]
    tiles = [slice(128 * t, 128 * (t + 1)) for t in range(2)]
    bias_lane = (lax.broadcasted_iota(jnp.int32, (kp, 128), 1) == 12).astype(BF)

    def columns_at(i):
        return pl.ds(pl.multiple_of(i * qp, 128), qp)


    def first_norm(i):
        kept = {}

        def mean(r):
            x = x_ref[i, rows_of(r), :].astype(F32)
            kept[r] = x - jnp.sum(x, axis=-1, keepdims=True) * (1.0 / width)

        def spread(r):
            kept[r] = (kept[r], jnp.sum(kept[r] * kept[r], axis=-1, keepdims=True) * (1.0 / width))

        def put(r):
            centred, variance = kept[r]
            fst_s[i % 2, rows_of(r), :] = (centred * lax.rsqrt(variance + EPS_NORM) * v[0] + v[1]).astype(BF)

        yield from staged(strips, LAG, mean, spread, put)

    def project(i, part):
        first_q = fst_s[i % 2]
        if part == 0:
            queries = nn(first_q, wq[...]).astype(BF)
            yield
            for r in range(qp // STRIP):
                for h in range(heads):
                    tile = cut(queries[:, tiles[h // half_heads]], r)
                    qm_s[i, h, rows_of(r), :] = tile * masks[h % half_heads] + one_lane
                yield
        elif part == 1:
            keys = nn(first_q, wk[...]).astype(BF)
            yield
            for r in range(strips):
                bias = bias_ref[i, rows_of(r), :]
                key_i[rows_of(r), :] = key_p[rows_of(r), :] + bias * cut(bias_lane, r)
                for t in range(2):
                    keys_s[rows_of(r), tiles[t]] = cut(keys[:, tiles[t]], r) + bias * one_lane
                yield
            kt_s[i] = keys.T
            yield
        else:
            values = nn(first_q, wv[...]).astype(BF)
            yield
            v_s[i] = values[:kp]
            vt_s[...] = values.T
            yield
            yield
            first_t[:, columns_at(i)] = first_q.T
            yield

    def head_rows(h):
        first_row = 128 * (h // half_heads) + hd * (h % half_heads)
        return slice(first_row, first_row + hd)


    def scores(i, h):
        s = nt(keys_s[:, tiles[h // half_heads]], qm_s[i, h])
        p = nn(key_i[...], query_p[h])
        m, pm = cut(s, 0), cut(p, 0)
        for r in range(strips):
            yield
            s_buf[h, rows_of(r), :] = cut(s, r)
            p_buf[h, rows_of(r), :] = cut(p, r)
            m = jnp.maximum(m, cut(s, r))
            pm = jnp.maximum(pm, cut(p, r))
        stat_s[4 * h : 4 * h + 1, :] = jnp.max(m, axis=0, keepdims=True)
        stat_s[4 * h + 1 : 4 * h + 2, :] = jnp.max(pm, axis=0, keepdims=True)

    def exponents(h):
        m, pm = stat_s[4 * h : 4 * h + 1, :], stat_s[4 * h + 1 : 4 * h + 2, :]
        z = jnp.zeros((STRIP, qp), F32)
        pz = jnp.zeros((STRIP, qp), F32)
        for r in range(strips):
            yield
            e = jnp.exp2((s_buf[h, rows_of(r), :] - m) * c_scale)
            pe = jnp.exp2(p_buf[h, rows_of(r), :] - pm)
            s_buf[h, rows_of(r), :] = e
            p_buf[h, rows_of(r), :] = pe
            z = z + e
            pz = pz + pe
        gate = gate_of(hp_s, h, qp)
        stat_s[4 * h + 2 : 4 * h + 3, :] = (1.0 - gate) / jnp.sum(z, axis=0, keepdims=True)
        stat_s[4 * h + 3 : 4 * h + 4, :] = gate / jnp.sum(pz, axis=0, keepdims=True)

    def mixing(i, h):
        a, b = stat_s[4 * h + 2 : 4 * h + 3, :], stat_s[4 * h + 3 : 4 * h + 4, :]
        for r in range(strips):
            yield
            content = s_buf[h, rows_of(r), :] * a
            located = p_buf[h, rows_of(r), :] * b
            soft_s[i, h, 0, rows_of(r), :] = content
            soft_s[i, h, 1, rows_of(r), :] = located
            att_buf[h % 2, rows_of(r), :] = (content + located).astype(BF)
        yield
        mix_t[h * hd : (h + 1) * hd, columns_at(i)] = nn(
            vt_s[head_rows(h), :], att_buf[h % 2]
        ).astype(BF)


    def strip_rows(i, r):
        return pl.ds(pl.multiple_of(i * qp + r * STRIP, 16), STRIP)

    def image_rows(i):
        return pl.ds(pl.multiple_of(i * qp, 16), kp)

    def start(i):
        attn = nt(mix_t[:, columns_at(i)].T[:kp], wo[...])
        for _ in range(WAIT + 2):
            yield
        kept = {}

        def mean(r):
            middle = x_ref[i, rows_of(r), :].astype(F32) + cut(attn, r) + v[4]
            mid_s[i, rows_of(r), :] = middle
            kept[r] = middle - jnp.sum(middle, axis=-1, keepdims=True) * (1.0 / width)

        def vary(r):
            kept[r] = (kept[r], jnp.sum(kept[r] * kept[r], axis=-1, keepdims=True) * (1.0 / width))

        def put(r):
            centred, variance = kept[r]
            spread = lax.rsqrt(variance + EPS_NORM)
            n2 = centred * spread
            n2_s[rows_of(r), :] = n2
            spr_s[rows_of(r), :] = spread
            sec_s[rows_of(r), 0:width] = (n2 * v[2] + v[3]).astype(BF)

        yield from staged(strips, LAG, mean, vary, put)
        left_t[0, :, columns_at(i)] = jnp.concatenate([inc_ref[i], gap], axis=0).T
        yield
        left_t[1, :, columns_at(i)] = jnp.concatenate([sec_s[:, 0:width], gap], axis=0).T

    def chunk(i, c, on):
        lanes = pl.ds(c * 256, 256)
        before = nn(sec_s[...], wi[:, lanes])
        back = nn(inc_ref[i], wn[:, lanes])
        total = jnp.zeros((8, 256), F32)
        for r in range(strips):
            yield
            gelu, slope = gelu_parts(cut(before, r))
            right_s[0, strip_rows(i, r), lanes] = gelu.astype(BF)
            grad_before = cut(back, r) * slope
            right_s[1, strip_rows(i, r), lanes] = grad_before.astype(BF)
            total = total + fold(grad_before)
        hid_g[:, lanes] += jnp.where(on, total, 0.0)

    def end(i, on):
        grad_second = nt(right_s[1, image_rows(i), :], wi[0:width, :])
        totals = [jnp.zeros((8, width), F32)] * 4
        mids = []
        for _ in range(WAIT):
            yield
        kept = {}

        def means(r):
            n2 = n2_s[rows_of(r), :]
            g = cut(grad_second, r)
            e = g * v[2]
            mean_e = jnp.sum(e, axis=-1, keepdims=True) * (1.0 / width)
            mean_en = jnp.sum(e * n2, axis=-1, keepdims=True) * (1.0 / width)
            kept[r] = (e, mean_e, mean_en)
            for k, term in enumerate((g * n2, g)):
                totals[k] = totals[k] + fold(term)

        def put(r):
            e, mean_e, mean_en = kept[r]
            n2 = n2_s[rows_of(r), :]
            incoming = inc_ref[i, rows_of(r), :].astype(F32)
            spread = spr_s[rows_of(r), :]
            grad_middle = incoming + spread * (e - mean_e - n2 * mean_en)
            gm_s[i, rows_of(r), :] = grad_middle
            mids.append(grad_middle.astype(BF))
            for k, term in enumerate((grad_middle, incoming)):
                totals[2 + k] = totals[2 + k] + fold(term)

        yield from staged(strips, LAG, means, put)
        for k in range(4):
            vec_g[k] += jnp.where(on, totals[k], 0.0)
        mid_low = jnp.concatenate([*mids, gap], axis=0)
        yield
        dm = nn(mid_low, wop[...]).astype(BF)
        for r in range(qp // STRIP):
            yield
            for h in range(heads):
                tile = cut(dm[:, tiles[h // half_heads]], r)
                dmm_s[i, h, rows_of(r), :] = tile * masks[h % half_heads]
        yield
        low_s[pl.ds(pl.multiple_of(i * qp, 16), qp), :] = mid_low

    blocks = hidden // 256

    def forward_step(i, carry):
        one, two = jnp.maximum(i - 1, 0), jnp.maximum(i - 2, 0)
        after = jnp.minimum(i + 1, images - 1)
        on_one, on_two = i > 0, i > 1
        interleave(scores(i, 0), exponents(3), mixing(one, 2), chunk(two, 1, on_two), first_norm(after))
        interleave(scores(i, 1), exponents(0), mixing(one, 3), chunk(two, 2, on_two))
        interleave(
            scores(i, 2),
            exponents(1),
            mixing(i, 0),
            end(two, on_two),
            start(one),
            project(i, 2),
        )
        interleave(
            scores(i, 3),
            exponents(2),
            mixing(i, 1),
            chunk(one, 0, on_one),
            project(after, 0),
            project(after, 1),
        )
        return carry

    interleave(first_norm(0))
    wi[0:width, pl.ds(0, wide)] = own_ref[0:width, :]
    wi[0:width, pl.ds(wide, wide)] = oth_ref[0:width, :]
    wn[:, pl.ds(0, wide)] = own_ref[width : 2 * width, :]
    wn[:, pl.ds(wide, wide)] = oth_ref[width : 2 * width, :]
    own_tri = own_ref[2 * width : 3 * width, :]
    oth_tri = oth_ref[2 * width : 3 * width, :]
    for k, w in enumerate((wq, wk, wv, wop)):
        lanes = slice(k * half, (k + 1) * half)
        w[...] = in_tiles(own_tri[:, lanes], oth_tri[:, lanes])
    wo[...] = jnp.concatenate([own_tri[:, 3 * half :], oth_tri[:, 3 * half :]], axis=1)
    small = []
    for ref in (own_ref, oth_ref):
        tail = ref[3 * width : 3 * width + 16, :].astype(F32)
        each = 1 + half_heads
        small.append(tail[0:each] + tail[each : 2 * each] + tail[2 * each : 3 * each])
    hb = jnp.concatenate([member[0:1] for member in small], axis=1)
    wi[width:, :] = jnp.concatenate(
        [*bf_parts(hb), jnp.zeros((256 - width - 3, hidden), F32)], axis=0
    ).astype(BF)
    hp_s[...] = jnp.concatenate(
        [member[1:, :128] for member in small] + [jnp.zeros((8 - heads, 128), F32)], axis=0
    )
    for h in range(heads):
        query_p[h, 0:16, :] = query_operand(hp_s, h, qp)
    for part in range(2):
        interleave(project(0, part))
    def leaving(first_image, count):
        rows = pl.ds(pl.multiple_of(first_image * qp, 16), count * qp)
        images_out = pl.ds(first_image, count)
        for k, (source, at_rows) in enumerate(
            ((right_s.at[0], rows), (mid_s, images_out), (gm_s, images_out))
        ):
            pltpu.make_async_copy(
                source.at[at_rows], far_refs[k].at[at_rows], sems.at[k]
            ).start()

    def forward_pair(j, carry):
        forward_step(2 * j + 1, forward_step(2 * j, carry))

        @pl.when(j > 0)
        def _():
            leaving(2 * j - 2, 2)

        return carry

    lax.fori_loop(0, images // 2, forward_pair, 0)


    def back_scores(i, h):
        da = nt(v_s[i, :, tiles[h // half_heads]], dmm_s[i, h])
        rc = jnp.zeros((STRIP, qp), F32)
        rl = jnp.zeros((STRIP, qp), F32)
        for r in range(strips):
            yield
            part = cut(da, r)
            da_buf[h % 2, rows_of(r), :] = part
            rc = rc + soft_s[i, h, 0, rows_of(r), :] * part
            rl = rl + soft_s[i, h, 1, rows_of(r), :] * part
        gate = gate_of(hp_s, h, qp)
        rc = jnp.sum(rc, axis=0, keepdims=True) / (1.0 - gate)
        rl = jnp.sum(rl, axis=0, keepdims=True) / gate
        back_s[2 * h : 2 * h + 1, :] = rc
        back_s[2 * h + 1 : 2 * h + 2, :] = rl
        gate_g[h : h + 1, :] += rl - rc

    def back_spread(i, h):
        rc, rl = back_s[2 * h : 2 * h + 1, :], back_s[2 * h + 1 : 2 * h + 2, :]
        lanes = pl.ds(h * qp, qp)
        for r in range(strips):
            yield
            rows = rows_of(r)
            c = soft_s[i, h, 0, rows, :]
            l = soft_s[i, h, 1, rows, :]
            part = da_buf[h % 2, rows, :]
            ds_s[rows, lanes] = (c * (part - rc)).astype(BF)
            att_s[rows, lanes] = (c + l).astype(BF)
            place_g[h, rows, :] += l * (part - rl)

    def products(i, t):
        lanes = slice(t * half_heads * qp, (t + 1) * half_heads * qp)
        heads_in = slice(t * half_heads, (t + 1) * half_heads)
        dk = nn(ds_s[:, lanes], qm_s[i, heads_in].reshape(half_heads * qp, 128))
        dv = nn(att_s[:, lanes], dmm_s[i, heads_in].reshape(half_heads * qp, 128))
        yield
        pad = jnp.zeros((qp - kp, qp), BF)
        dq_t = []
        for h in range(t * half_heads, (t + 1) * half_heads):
            ds = jnp.concatenate([ds_s[:, h * qp : (h + 1) * qp], pad], axis=0)
            dq_t.append(nn(kt_s[i, head_rows(h), :], ds))
        yield
        dp_s[1, image_rows(i), tiles[t]] = (dk * back_scale).astype(BF)
        yield
        dp_s[2, image_rows(i), tiles[t]] = dv.astype(BF)
        yield
        dq_t.append(jnp.zeros((128 - half, qp), F32))
        dq = (jnp.concatenate(dq_t, axis=0) * back_scale).astype(BF)
        dp_s[0, image_rows(i), tiles[t]] = dq.T[:kp]

    cut_at = (images - 2) * qp
    spans = (slice(0, cut_at), slice(cut_at, images * qp))

    def weight_gradient(unit, part):
        side = unit // blocks
        lanes = slice((unit % blocks) * 256, (unit % blocks) * 256 + 256)
        value = nn(left_t[side, :, spans[part]], right_s[side, spans[part], lanes])
        yield
        if part:
            wide_g[side, 0:width, lanes] += value
        else:
            wide_g[side, 0:width, lanes] = value

    def outward_gradient(part):
        value = nn(mix_t[:, spans[part]], low_s[spans[part], :])
        yield
        if part:
            out_g[...] += value
        else:
            out_g[...] = value

    def triple_gradient(c, part):
        value = nn(first_t[:, spans[part]], dp_s[c, spans[part], :])
        yield
        rows = pl.ds(c * width, width)
        for t in range(2):
            if part:
                tri_p[t, rows, :] += value[:, tiles[t]]
            else:
                tri_p[t, rows, :] = value[:, tiles[t]]

    last = images - 1
    on = True
    partial = [weight_gradient(unit, 0) for unit in range(2 * blocks)] + [outward_gradient(0)]
    interleave(
        exponents(3), mixing(last, 2), chunk(last - 1, 1, on), back_scores(0, 0), partial[0]
    )
    interleave(
        mixing(last, 3),
        chunk(last - 1, 2, on),
        back_scores(0, 1),
        back_spread(0, 0),
        partial[1],
    )
    interleave(
        end(last - 1, on), start(last), back_scores(0, 2), back_spread(0, 1), partial[2]
    )
    interleave(chunk(last, 0, on), back_scores(0, 3), back_spread(0, 2), partial[3])
    interleave(chunk(last, 1, on), back_spread(0, 3), partial[4])
    interleave(chunk(last, 2, on), products(0, 0), partial[5])
    interleave(end(last, on), products(0, 1), *partial[6:])

    leaving(images - 2, 2)


    def early_chunks():
        put_planes(nar_p, wide_g[0, 0:width, :].T)
        put_planes(out_p, out_g[...])
        for side in range(2):
            for k, part in enumerate(even_odd_tiles(nar_p, side * wide, wide // 2)):
                nar_f[side, k, 0 : wide // 2, :] = part
            for k, part in enumerate(even_odd_tiles(out_p, side * half, half // 2)):
                out_f[side, k, 0 : half // 2, :] = part
            yield
        for r in range(data_count):
            for side in range(2):
                yield
                piece = tmp.at[side, r]
                for k in range(3):
                    lanes = slice(side * wide + 128 * k, side * wide + 128 * (k + 1))
                    piece[k * wp : (k + 1) * wp, :] = wide_g[1, r * wp : (r + 1) * wp, lanes]
                    row = 3 * wp + k * np_
                    piece[row : row + np_, :] = nar_f[side, k, r * np_ : (r + 1) * np_, :]
                    row = 3 * (wp + np_) + k * op
                    piece[row : row + op, :] = out_f[side, k, r * op : (r + 1) * op, :]
                outs[side][r, 0:SENT_EARLY, :] = piece[0:SENT_EARLY, :].astype(outs[side].dtype)

    def late_chunks():
        early = jnp.sum(vec_g[...], axis=1)
        hidden_sum = jnp.sum(hid_g[...], axis=0, keepdims=True)
        vec_n, hid_n = 4 * width // data_count, wide // data_count
        rest = jnp.zeros((1, 128 - vec_n - hid_n), F32)
        groups = 3 * width // data_count // 4
        small_at = 3 * (wp + np_ + op)
        for side in range(2):
            for k, part in enumerate(four_row_tiles(tri_p, side, 0, 3 * width // 4)):
                tri_f[side, k, 0 : 3 * width // 4, :] = part
            yield
        for r in range(data_count):
            for side in range(2):
                yield
                piece = tmp.at[side, r]
                row, lane = divmod(r * vec_n, width)
                at_hidden = side * wide + r * hid_n
                piece[small_at : small_at + 1, :] = jnp.concatenate(
                    [
                        early[row : row + 1, lane : lane + vec_n],
                        hidden_sum[:, at_hidden : at_hidden + hid_n],
                        rest,
                    ],
                    axis=1,
                )
                for k in range(3):
                    row = small_at + 1 + k * groups
                    piece[row : row + groups, :] = tri_f[side, k, r * groups : (r + 1) * groups, :]
                row = small_at + 1 + 3 * groups
                piece[row:SENT_ROWS, :] = jnp.zeros((SENT_ROWS - row, 128), F32)
                outs[side][r, SENT_EARLY:, :] = piece[SENT_EARLY:SENT_ROWS, :].astype(
                    outs[side].dtype
                )

    if data_count:
        wp, np_, op = width // data_count, wide // data_count // 2, half // data_count // 2
    chunking = early_chunks() if data_count else iter(())
    def leaving_back(first_row, count):
        for c in range(3):
            rows = pl.ds(first_row, count)
            pltpu.make_async_copy(
                dp_s.at[c, rows], far_refs[3].at[c, rows], sems.at[3]
            ).start()

    def leaving_places(first, count):
        span = pl.ds(first, count)
        pltpu.make_async_copy(place_g.at[span], far_refs[4].at[span], sems.at[4]).start()

    for i in range(1, images):
        before = i > 1
        done = i == last
        interleave(
            back_scores(i, 0),
            back_spread(i - 1, 3) if before else None,
            outward_gradient(1) if i == 1 else None,
        )
        interleave(
            back_scores(i, 1),
            products(i - 1, 0) if before else None,
            back_spread(i, 0),
        )
        interleave(
            back_scores(i, 2),
            products(i - 1, 1) if before else None,
            back_spread(i, 1),
        )
        interleave(
            back_scores(i, 3),
            back_spread(i, 2),
            weight_gradient(i - 1, 1) if i <= 2 * blocks else triple_gradient(0, 0),
            triple_gradient(1, 0) if done else None,
            triple_gradient(2, 0) if done else None,
        )
        leaving_back((i - 1) * qp, qp)
        if done:
            leaving_places(0, heads - 1)
    for unit in range(last, 2 * blocks):
        interleave(weight_gradient(unit, 1))
    interleave(back_spread(last, 3))
    interleave(products(last, 0), products(last, 1))
    interleave(chunking)
    leaving_back(last * qp, qp)
    leaving_places(heads - 1, 1)
    gate_ref[...] = gate_g[...]
    hp_ref[...] = hp_s[...]
    for c in range(3):
        interleave(triple_gradient(c, 1))
    if data_count:
        interleave(late_chunks())
    else:
        outs[0][...] = wide_g[0, 0:width, :].T
        outs[1][...] = wide_g[1, 0:width, :]
        outs[2][...] = out_g[...]
        outs[3][...] = vec_g[...]
        outs[4][...] = hid_g[...]
        for c in range(3):
            rows = pl.ds(c * width, width)
            outs[5][rows, :] = jnp.concatenate(
                [tri_p[0, rows, 0:half], tri_p[1, rows, 0:half]], axis=1
            )
    for k, source in enumerate((right_s.at[0], mid_s, gm_s, dp_s, place_g)):
        pltpu.make_async_copy(source, far_refs[k], sems.at[k]).wait()


def run_layer(x, inc, bias, own, oth, vec, heads, patches, data_count):
    images, kp, width = x.shape
    qp = -(-patches // 128) * 128
    wide, half = own.shape[1], width // 2
    hidden = 2 * wide
    full = images * qp
    if data_count:
        outs = [
            pltpu.VMEM((data_count, SENT_ROWS, 128), F32),
            pltpu.VMEM((data_count, SENT_ROWS, 128), BF),
        ]
    else:
        outs = [
            sds(hidden, width),
            sds(width, hidden),
            sds(width, width),
            sds(4, 8, width),
            sds(8, hidden),
            sds(3 * width, width),
        ]

    def bf(*dims):
        return pltpu.VMEM(dims, BF)

    def f32(*dims):
        return pltpu.VMEM(dims, F32)

    scratch = [
        *[bf(width, 256)] * 3,
        bf(width, width),
        bf(width, 256),
        bf(256, hidden),
        bf(width, hidden),
        f32(8, 128),
        bf(kp, 128),
        bf(kp, 128),
        bf(heads, 128, qp),
        bf(2, qp, width),
        bf(kp, 256),
        bf(256, qp),
        bf(images, heads, qp, 128),
        bf(images, heads, qp, 128),
        bf(images, kp, 256),
        bf(images, 256, qp),
        f32(images, heads, 2, kp, qp),
        f32(images, kp, width),
        f32(kp, width),
        bf(kp, 256),
        f32(kp, 1),
        bf(full, width),
        f32(4 * heads, qp),
        f32(2 * heads, qp),
        bf(width, full),
        bf(width, full),
        bf(2, width, full),
        bf(2, full, hidden),
        f32(images, kp, width),
        bf(3, full, 256),
        f32(heads, kp, qp),
        f32(heads, kp, qp),
        bf(2, qp, qp),
        f32(heads, kp, qp),
        f32(8, qp),
        f32(2, kp, qp),
        bf(kp, heads * qp),
        bf(kp, heads * qp),
        f32(2, width + 8, hidden),
        f32(width, width),
        f32(4, 8, width),
        f32(8, hidden),
        f32(2, 3 * width, 128),
        pltpu.SemaphoreType.DMA((5,)),
    ]
    if data_count:
        scratch += [f32(2, hidden, 128), f32(2, width, 128)]
        scratch += [f32(2, 3, wide // 2 + 8, 128), f32(2, 3, half // 2 + 8, 128)]
        scratch += [f32(2, 3, 3 * width // 4 + 8, 128), f32(2, data_count, SENT_ROWS + 8, 128)]
    return pl.pallas_call(
        functools.partial(layer_kernel, patches=patches, heads=heads, data_count=data_count),
        out_shape=(
            sds(full, hidden, dtype=BF),
            sds(images, kp, width),
            sds(images, kp, width),
            sds(3, full, 256, dtype=BF),
            sds(heads, kp, qp),
            pltpu.VMEM((8, qp), F32),
            pltpu.VMEM((8, 128), F32),
            *outs,
        ),
        in_specs=[VM] * 6,
        out_specs=(ANYWHERE,) * 5 + (VM,) * (2 + len(outs)),
        scratch_shapes=scratch,
        compiler_params=pltpu.CompilerParams(vmem_limit_bytes=LAYER_VMEM),
        name="layer",
    )(*near(x, inc, bias, own, oth), vec)


def finish_kernel(*refs, patches, heads):
    (x_ref, own_ref, oth_ref, vec_ref, gate_ref, hp_ref), far_refs = refs[:6], refs[6:11]
    (res_out, gi_out, vec_out, head_ref) = refs[11:15]
    (act_s, mid_s, gm_s, dp_s, place_s), (w, wn, vec_g, rows_s, sems) = refs[15:20], refs[20:]
    images, kp, width = x_ref.shape
    qp = dp_s.shape[1] // images
    half = width // 2
    wide = own_ref.shape[1]
    copies = [
        pltpu.make_async_copy(source, target, sems.at[at])
        for at, (source, target) in enumerate(
            zip(far_refs, (act_s, mid_s, gm_s, dp_s, place_s))
        )
    ]
    for member in copies:
        member.start()
    own_tri = own_ref[2 * width : 3 * width, :]
    oth_tri = oth_ref[2 * width : 3 * width, :]
    for at in range(3):
        span = slice(at * half, (at + 1) * half)
        w[at] = in_tiles(own_tri[:, span], oth_tri[:, span])
    wn[:, 0:wide] = own_ref[width : 2 * width, :]
    wn[:, wide : 2 * wide] = oth_ref[width : 2 * width, :]
    vec_g[...] = jnp.zeros_like(vec_g)
    gain = vec_ref[0:1, :]
    shift = vec_ref[5:6, :]
    for member in copies[:2]:
        member.wait()
    for i in range(images):
        rows = mid_s[i] + nt(act_s[i * qp : i * qp + kp, :], wn[...]) + shift
        rows_s[i * patches : (i + 1) * patches, :] = rows[0:patches]
    res_out[...] = rows_s[0 : images * patches, :].T
    for member in copies[2:]:
        member.wait()
    for i in range(images):
        n1, spread = norm_parts(x_ref[i].astype(F32))
        g = sum(nt(dp_s[c, i * qp : i * qp + kp, :], w[c]) for c in range(3))
        vec_g[0] += fold(g * n1)
        vec_g[1] += fold(g)
        rows = gm_s[i] + norm_back(g * gain, n1, spread)
        rows_s[i * patches : (i + 1) * patches, :] = rows[0:patches]
    gi_out[...] = rows_s[0 : images * patches, :].T
    vec_out[...] = jnp.sum(vec_g[...], axis=1)
    parts = offsets(kp, qp)
    rank = lax.axis_index("tensor")
    lane = lax.broadcasted_iota(jnp.int32, (1, 128), 1)
    row = jnp.zeros((1, 128), F32)
    half_heads = heads // 2
    for h in range(heads):
        base = ((rank + h // half_heads) % 2) * (4 * half_heads) + h % half_heads
        g = place_s[h]
        for k in range(3):
            total = jnp.sum(g * parts[k])
            row = row + jnp.where(lane == base + k * half_heads, total, 0.0)
        gate = gate_of(hp_ref, h, 128)
        total = jnp.sum(gate_ref[h : h + 1, :])
        row = row + jnp.where(lane == base + 3 * half_heads, total * gate * (1.0 - gate), 0.0)
    head_ref[...] = row


def run_finish(x, own, oth, vec, gate, hp, act, mid, gm, dp, place, patches):
    images, kp, width = x.shape
    rows = images * patches
    fetched = (act, mid, gm, dp, place)
    return pl.pallas_call(
        functools.partial(finish_kernel, patches=patches, heads=place.shape[0]),
        out_shape=(sds(width, rows), sds(width, rows), sds(2, width), sds(1, 128)),
        in_specs=[VM] * 6 + [ANYWHERE] * 5,
        out_specs=(VM,) * 4,
        scratch_shapes=[
            *[pltpu.VMEM(member.shape, member.dtype) for member in fetched],
            pltpu.VMEM((3, width, 256), BF),
            pltpu.VMEM((width, 2 * own.shape[1]), BF),
            pltpu.VMEM((2, 8, width), F32),
            pltpu.VMEM((rows + 8, width), F32),
            pltpu.SemaphoreType.DMA((5,)),
        ],
        compiler_params=pltpu.CompilerParams(vmem_limit_bytes=32 * 1024 * 1024),
        name="finish",
    )(*near(x, own, oth), vec, gate, hp, *far(*fetched))


def combine_kernel(own_ref, got_ref, out_ref):
    out_ref[...] = (own_ref[...] + got_ref[...].astype(F32)).astype(BF)


def run_combine(own, got):
    return pl.pallas_call(
        combine_kernel,
        out_shape=pltpu.VMEM(own.shape, BF),
        in_specs=[VM] * 2,
        out_specs=VM,
        compiler_params=PARAMS,
        name="combine",
    )(*near(own, got))


def pick_rows(ref, start, count, flip=False):
    total = ref.shape[1] if flip else ref.shape[0]
    row = lax.broadcasted_iota(jnp.int32, (count, total), 0) + start
    col = lax.broadcasted_iota(jnp.int32, (count, total), 1)
    chosen = (row == col).astype(F32)
    return lax.dot_general(
        chosen,
        ref[...],
        (((1,), (1 if flip else 0,)), ((), ())),
        preferred_element_type=F32,
        precision=lax.Precision.HIGHEST,
    )


def share_kernel(_, tri_ref, out_ref, wid_ref, nar_ref, *refs, data_count):
    (wt_f, wo_f, ww_f, wn_f, st, so, sw, sn) = refs
    width, wide = wid_ref.shape
    half = out_ref.shape[0]
    wp, np_, op = width // data_count, wide // data_count // 2, half // data_count // 2
    data_rank = lax.axis_index("dp")
    groups = tri_ref.shape[0] // data_count // 4
    st[0, 0 : 4 * groups, 0 : tri_ref.shape[1]] = pick_rows(
        tri_ref, data_rank * 4 * groups, 4 * groups
    )
    put_planes(so, pick_rows(out_ref, data_rank * 2 * op, 2 * op))
    sw[0:wp, :] = pick_rows(wid_ref, data_rank * wp, wp)
    put_planes(sn, pick_rows(nar_ref, data_rank * 2 * np_, 2 * np_, flip=True))
    tiles = four_row_tiles(st, 0, 0, groups)
    for p in range(groups):
        for k in range(3):
            tile = 128 * (3 * p + k)
            wt_f[0:1, tile : tile + 128] = tiles[k][p : p + 1, :]
    for ref, flat, pairs in ((so, wo_f, op), (sn, wn_f, np_)):
        tiles = even_odd_tiles(ref, 0, pairs)
        for p in range(pairs):
            for k in range(3):
                tile = 128 * (3 * p + k)
                flat[0:1, tile : tile + 128] = tiles[k][p : p + 1, :]
    for p in range(wp):
        ww_f[0:1, wide * p : wide * (p + 1)] = sw[p : p + 1, :]


def run_shares(after, tri, out, wid, nar_t, data_count):
    wide = wid.shape[1]
    share = [member.shape[0] // data_count for member in (tri, out, wid)]
    return pl.pallas_call(
        functools.partial(share_kernel, data_count=data_count),
        out_shape=tuple(sds(1, member.size // data_count) for member in (tri, out, wid, nar_t)),
        in_specs=[VM] * 5,
        out_specs=(VM,) * 4,
        scratch_shapes=[
            pltpu.VMEM((1, share[0] + 40, 128), F32),
            pltpu.VMEM((2, share[1] + 18, 128), F32),
            pltpu.VMEM((share[2] + 12, wide), F32),
            pltpu.VMEM((2, wide // data_count + 16, 128), F32),
        ],
        compiler_params=PARAMS,
        name="weight_shares",
    )(after, tri, out, wid, nar_t)


def spread_rows(flat_ref, from_ref, base, blocks):
    for p in range(blocks):
        for k in range(3):
            at = base + k * blocks + p
            tile = 128 * (3 * p + k)
            flat_ref[0:1, tile : tile + 128] = from_ref[at : at + 1, :]


def sum_kernel(got_ref, late_ref, head_ref, _, *refs, blocks, span):
    (tri_f, out_f, wid_f, nar_f, pay_ref, tot) = refs
    tri_b, out_b, wid_b, nar_b = blocks
    vec_n, hid_n = span
    tot[0:SENT_ROWS, :] = jnp.sum(got_ref[...].astype(F32), axis=0)
    spread_rows(wid_f, tot, 0, wid_b)
    spread_rows(nar_f, tot, 3 * wid_b, nar_b)
    spread_rows(out_f, tot, 3 * (wid_b + nar_b), out_b)
    at = 3 * (wid_b + nar_b + out_b)
    spread_rows(tri_f, tot, at + 1, tri_b)
    early = tot[0:at, :]
    late = tot[at + 1 : at + 1 + 3 * tri_b, :]
    small = tot[at : at + 1, :]
    hid = small[:, vec_n : vec_n + hid_n]
    squares = jnp.sum(early * early) + jnp.sum(late * late) + jnp.sum(hid * hid)
    lane = lax.broadcasted_iota(jnp.int32, (1, 128), 1)
    tails = jnp.concatenate([late_ref[0:1, 128:], late_ref[1:2, 128:]], axis=1)
    last = jnp.concatenate([head_ref[:, 0:SMALL_AT], small[:, 0 : 128 - SMALL_AT]], axis=1)
    payload = jnp.concatenate(
        [late_ref[:, :128], tails, jnp.where(lane == 127, squares, last)], axis=0
    )
    pay_ref[...] = jnp.broadcast_to(payload[None], pay_ref.shape)


def run_sums(got, late_vec, head, after, blocks, span):
    count = got.shape[0]
    return pl.pallas_call(
        functools.partial(sum_kernel, blocks=blocks, span=span),
        out_shape=(
            *[sds(1, 3 * 128 * member) for member in blocks],
            sds(2 * count, 4, 128),
        ),
        in_specs=[VM] * 4,
        out_specs=(VM,) * 5,
        scratch_shapes=[pltpu.VMEM((SENT_ROWS + 8, 128), F32)],
        compiler_params=PARAMS,
        name="sums",
    )(got, late_vec, head, after)


def adam_parts(weight, gradient, moment, squares, rate, decay):
    moment_new = BETA_ONE * moment + (1.0 - BETA_ONE) * gradient
    squares_new = BETA_TWO * squares + (1.0 - BETA_TWO) * gradient * gradient
    quotient = (moment_new / (1.0 - BETA_ONE**STEP)) / (
        jnp.sqrt(squares_new / (1.0 - BETA_TWO**STEP)) + ADAM_EPS
    )
    return moment_new, squares_new, weight - rate * (quotient + decay * weight)


def gathered(last, width, wide):
    count = last.shape[0] // 2
    vec_n, hid_n = 4 * width // count, wide // count
    even = last[pl.ds(0, count, stride=2), :]
    odd = last[pl.ds(1, count, stride=2), :]
    mine = jnp.where(lax.axis_index("tensor") == 0, even, odd)

    def placed(part, times):
        n = part.shape[1]
        value = jnp.concatenate([part] * times, axis=1)
        row = lax.broadcasted_iota(jnp.int32, value.shape, 0)
        lane = lax.broadcasted_iota(jnp.int32, value.shape, 1)
        at = jnp.floor((lane.astype(F32) + 0.5) * (1.0 / n)).astype(jnp.int32)
        return value, row, at

    per_row = width // vec_n
    value, row, at = placed(even[:, SMALL_AT : SMALL_AT + vec_n], per_row)
    vector = jnp.concatenate(
        [
            jnp.sum(jnp.where(row == at + v * per_row, value, 0.0), axis=0, keepdims=True)
            for v in range(4)
        ],
        axis=0,
    )
    at_hidden = SMALL_AT + vec_n
    value, row, at = placed(mine[:, at_hidden : at_hidden + hid_n], count)
    return vector, jnp.sum(jnp.where(row == at, value, 0.0), axis=0, keepdims=True)


def adam_kernel(got_ref, hp_ref, vec_ref, hb_ref, *refs, given_sums):
    refs = list(refs)
    sums = [refs.pop(0) for _ in range(2 * given_sums)]
    grads = refs[0:4]
    weights = refs[4:8]
    states = refs[8:22]
    outs = refs[22:43]
    norm_ref, last = refs[43:45]
    width = vec_ref.shape[1]
    half_heads = hp_ref.shape[0]
    tail = width - 128
    total = jnp.sum(got_ref[...], axis=0)
    if given_sums:
        early, hid = sums[0][...], sums[1][...]
    else:
        last[...] = got_ref[:, 3, :]
        early, hid = gathered(last, width, hb_ref.shape[0])
    late = jnp.concatenate(
        [
            total[0:2, :],
            jnp.concatenate([total[2:3, :tail], total[2:3, tail : 2 * tail]], axis=0),
        ],
        axis=1,
    )
    vector = jnp.concatenate([late, early], axis=0)
    lane = lax.broadcasted_iota(jnp.int32, (1, 128), 1)
    heads_row = jnp.where(lane < 8 * half_heads, total[3:4, :], 0.0)
    squares = (
        jnp.sum(jnp.where(lane == 127, total[3:4, :], 0.0))
        + jnp.sum(vector * vector)
        + jnp.sum(heads_row * heads_row)
    )
    norm = jnp.sqrt(jnp.full((1, 128), squares))
    norm_ref[0] = jnp.sum(norm[:, 0:1])
    factor = (CLIP_AT / jnp.maximum(norm, CLIP_AT))[:, 0:1]
    span = 4 * half_heads
    mine = jnp.where(lax.axis_index("tensor") == 0, heads_row[:, :span], heads_row[:, span : 2 * span])
    head = jnp.concatenate(
        [
            jnp.concatenate(
                [mine[:, c * half_heads + h : c * half_heads + h + 1] for c in range(4)], axis=1
            )
            for h in range(half_heads)
        ],
        axis=0,
    )
    given = [ref[...] for ref in grads] + [vector, hid, head]
    wide = hid.shape[1]
    held = [ref[...] for ref in weights] + [vec_ref[...], hb_ref[...].reshape(1, wide), hp_ref[...]]
    for at in range(7):
        renewed = adam_parts(
            held[at],
            given[at] * factor,
            states[2 * at][...].reshape(held[at].shape),
            states[2 * at + 1][...].reshape(held[at].shape),
            RATES[at],
            DECAYS[at],
        )
        for step in range(3):
            out = outs[3 * at + step]
            out[...] = renewed[step].reshape(out.shape)


def run_adam(got, hp_t, vec, hb, sums, grads, weights, states):
    shapes = []
    for at in range(7):
        shapes += [sds(*states[2 * at].shape)] * 3
    return pl.pallas_call(
        functools.partial(adam_kernel, given_sums=len(sums) // 2),
        out_shape=(*shapes, sds(1)),
        in_specs=[VM] * (4 + len(sums) + 4 + 4 + 14),
        out_specs=(VM,) * 21 + (SM,),
        scratch_shapes=[pltpu.VMEM((got.shape[0], 128), F32)],
        compiler_params=PARAMS,
        name="adam",
    )(got, hp_t, vec, hb, *sums, *grads, *weights, *states)


def plain_chunks(halves, data_count, rows):
    sides = []
    for side in range(2):
        flat = jnp.concatenate([own_first[side].reshape(data_count, -1) for own_first in halves], axis=1)
        flat = jnp.pad(flat, ((0, 0), (0, rows * 128 - flat.shape[1])))
        sides.append(flat.reshape(data_count, rows, 128))
    return sides[0], sides[1].astype(BF)


def on_device(
    tokens,
    cotangent,
    keep_mask,
    triple_weight,
    outward_weight,
    widen_weight,
    narrow_weight,
    vectors,
    hidden_bias,
    head_params,
    triple_moment,
    triple_square,
    outward_moment,
    outward_square,
    widen_moment,
    widen_square,
    narrow_moment,
    narrow_square,
    vector_moment,
    vector_square,
    hidden_moment,
    hidden_square,
    head_moment,
    head_square,
):
    tensor_rank = lax.axis_index("tensor")
    data_rank = lax.axis_index("dp")
    data_count = lax.axis_size("dp")
    images = keep_mask.shape[0] // 2
    patches = keep_mask.shape[1]
    heads = 2 * head_params.shape[1]
    depth = triple_weight.shape[1]
    half = triple_weight.shape[2]
    wide = widen_weight.shape[1]
    triple_rows = triple_weight.reshape(3 * depth, half)
    narrow_t = narrow_weight.T
    head_t = head_params.T
    fast = (
        depth == 192
        and half == 96
        and wide == 384
        and depth % data_count == 0
        and wide % (2 * data_count) == 0
        and half % (2 * data_count) == 0
        and 3 * depth % (4 * data_count) == 0
    )
    if fast:
        early_rows = (2 * depth * wide + half * depth) // data_count // 128
        late_rows = 3 * depth * half // data_count // 128
        fast = SENT_EARLY <= early_rows and early_rows + 1 + late_rows <= SENT_ROWS
    chunked = data_count if fast else 0
    swap = [(0, 1), (1, 0)]

    own, *rows_near = run_pack(
        triple_weight,
        outward_weight,
        widen_weight,
        narrow_t,
        hidden_bias,
        head_t,
        tokens.T,
        cotangent.T,
        keep_mask,
    )
    other = lax.ppermute(own, "tensor", swap)
    x, inc, bias = run_prepare(*rows_near)
    act, middle, grad_middle, dp, place, gate, hp, *sums = run_layer(
        x, inc, bias, own, other, vectors, heads, patches, chunked
    )
    if fast:
        mine, theirs = sums
    else:
        nar_g, wid_g, out_g, vec_g, hid_g, tri_g = sums
        early_mine = jnp.sum(vec_g, axis=1).reshape(1, -1)
        early_both = jnp.broadcast_to(early_mine, (data_count, early_mine.size))
        hidden_both = jnp.broadcast_to(
            jnp.sum(hid_g, axis=0).reshape(2, 1, wide), (2, data_count, wide)
        )
        early = plain_chunks(
            [
                wid_g.reshape(depth, 2, wide).transpose(1, 0, 2),
                nar_g.reshape(2, -1),
                out_g.reshape(2, -1),
                (early_both, early_both),
                hidden_both,
            ],
            data_count,
            EARLY_ROWS,
        )
        late = plain_chunks(
            [tri_g.reshape(3 * depth, 2, half).transpose(1, 0, 2)], data_count, LATE_ROWS
        )
        mine, theirs = (jnp.concatenate(pair, axis=1) for pair in zip(early, late))
    received = lax.ppermute(theirs, "tensor", swap)
    chunks = run_combine(mine, received)
    got = lax.all_to_all(chunks, "dp", 0, 0, tiled=False)
    result_t, grad_input_t, late_vec, head_row = run_finish(
        x, own, other, vectors, gate, hp, act, middle, grad_middle, dp, place, patches
    )
    if fast:
        wt_f, wo_f, ww_f, wn_f = run_shares(
            gate, triple_rows, outward_weight, widen_weight, narrow_t, data_count
        )
        blocks = [
            member.size // data_count // 384
            for member in (triple_rows, outward_weight, widen_weight, narrow_t)
        ]
        span = (4 * depth // data_count, wide // data_count)
        tri_f, out_f, wid_f, nar_f, payload = run_sums(
            got, late_vec, head_row, wo_f, blocks, span
        )
        sums = ()
    else:
        total = jnp.sum(got.astype(F32), axis=0)
        early_sum = total[:EARLY_ROWS].reshape(1, -1)
        masters = (widen_weight, narrow_weight, outward_weight)
        sizes = [member.size // data_count for member in masters] + [4 * depth, wide]
        cuts = [sum(sizes[:at]) for at in range(6)]
        wid_f, nar_f, out_f, early_vec, hid = (
            early_sum[:, cuts[at] : cuts[at + 1]] for at in range(5)
        )
        early_vec = early_vec.reshape(4, depth)
        share = triple_rows.size // data_count
        tri_f = total[EARLY_ROWS:].reshape(1, -1)[:, :share]

        def weight_share(member):
            length = member.size // data_count
            return lax.dynamic_slice_in_dim(member.reshape(1, -1), data_rank * length, length, 1)

        ww_f, wn_f, wo_f = (weight_share(member) for member in masters)
        wt_f = weight_share(triple_rows)
        squares = sum(jnp.sum(member * member) for member in (wid_f, nar_f, out_f, tri_f))
        squares = squares + jnp.where(data_rank == 0, jnp.sum(hid * hid), 0.0)
        lane = lax.broadcasted_iota(jnp.int32, (1, 128), 1)
        payload = jnp.concatenate(
            [
                late_vec[:, :128],
                late_vec[:, 128:].reshape(1, 128),
                jnp.where(lane == 127, squares, head_row),
            ]
        )
        payload = jnp.broadcast_to(payload[None], (2 * data_count, 4, 128))
        sums = (early_vec, hid)
    last_got = lax.all_to_all(payload, ("dp", "tensor"), 0, 0, tiled=False)
    renewed = run_adam(
        last_got,
        head_t,
        vectors,
        hidden_bias,
        sums,
        (tri_f, out_f, wid_f, nar_f),
        (wt_f, wo_f, ww_f, wn_f),
        (
            triple_moment,
            triple_square,
            outward_moment,
            outward_square,
            widen_moment,
            widen_square,
            narrow_moment,
            narrow_square,
            vector_moment,
            vector_square,
            hidden_moment,
            hidden_square,
            head_moment.T,
            head_square.T,
        ),
    )
    hidden_new = renewed[15:18]
    head_new = [member.T for member in renewed[18:21]]
    return (result_t.T, grad_input_t.T, *renewed[:15], *hidden_new, *head_new, renewed[21].reshape(()))


def solution(mesh):
    return jax.shard_map(
        on_device,
        mesh=mesh,
        in_specs=(
            P(("dp", "tensor"), None),
            P(("dp", "tensor"), None),
            P("dp", None),
            P(None, None, "tensor"),
            P("tensor", None),
            P(None, "tensor"),
            P("tensor", None),
            P(),
            P("tensor"),
            P(None, "tensor"),
            P("tensor", "dp"),
            P("tensor", "dp"),
            P("tensor", "dp"),
            P("tensor", "dp"),
            P("tensor", "dp"),
            P("tensor", "dp"),
            P("tensor", "dp"),
            P("tensor", "dp"),
            P(),
            P(),
            P("tensor"),
            P("tensor"),
            P(None, "tensor"),
            P(None, "tensor"),
        ),
        out_specs=(
            P(("dp", "tensor"), None),
            P(("dp", "tensor"), None),
            P("tensor", "dp"),
            P("tensor", "dp"),
            P("tensor", "dp"),
            P("tensor", "dp"),
            P("tensor", "dp"),
            P("tensor", "dp"),
            P("tensor", "dp"),
            P("tensor", "dp"),
            P("tensor", "dp"),
            P("tensor", "dp"),
            P("tensor", "dp"),
            P("tensor", "dp"),
            P(),
            P(),
            P(),
            P("tensor"),
            P("tensor"),
            P("tensor"),
            P(None, "tensor"),
            P(None, "tensor"),
            P(None, "tensor"),
            P(),
        ),
        check_vma=False,
    )
```
